32 devices in a mesh: seq: 32 (over z, y, x, core), dp: 1.
Axes of the slice: x: 2, y: 2, z: 4, core: 2. Of those that a mesh axis runs over, the one named last changes fastest.
Arguments:
- queries: bfloat16 [4096, 1024], P(('dp', 'seq')), may hold values from -6 to 6
- keys: bfloat16 [4096, 1024], P(('dp', 'seq')), may hold values from -4 to 4
- values: bfloat16 [4096, 1024], P(('dp', 'seq')), may hold values from -6 to 6
- cotangent: bfloat16 [4096, 1024], P(('dp', 'seq')), may hold values from -6 to 6
- doc_ids: int32 [4096], P(('dp', 'seq')), may hold values from 0 to 7, never falling along the last dimension, each value on 1 to 2048 neighbouring positions
Outputs:
- attended: bfloat16 [4096, 1024], P(('dp', 'seq'))
- grad_queries: bfloat16 [4096, 1024], P(('dp', 'seq'))
- grad_keys: bfloat16 [4096, 1024], P(('dp', 'seq'))
- grad_values: bfloat16 [4096, 1024], P(('dp', 'seq'))
The draws below stay inside these ranges and needn't reach their ends.
Inputs may be any that keep to these rules, and one draw needn't show every extreme that they name: doc_ids never fall along the sequence; each document holds 1 to 2048 positions.
All inputs are finite; a program needn't handle non-finite values.
Results may differ from the reference program's by a relative error of at most 0.0058.
Values may be sent and summed in bfloat16 or wider, within the bound.
No kernel may reach another device: no remote copies, remote signals or barrier semaphores. Data moves between devices by JAX's collectives and lax.ppermute only.
A program may use at most 128 MiB of HBM per device.

```python
import math
import jax
import jax.numpy as jnp
import numpy as np
from jax import lax

H = 8
HD = 128
SEG = 1024
LEVELS = 2
SEQ_LEN = 4096
FINEST_DILATION = 2
DOCS = 8
DOC_MOST = 2048


def pair_draw(key):
    shape_full = (SEQ_LEN, H * HD)
    query_base = jax.random.truncated_normal(jax.random.fold_in(key, 11), -4.0, 4.0, shape_full, jnp.float32)
    key_base = jax.random.truncated_normal(jax.random.fold_in(key, 12), -4.0, 4.0, shape_full, jnp.float32)
    return (query_base, key_base)


def draw_queries(key, part):
    return pair_draw(key)[0].astype(jnp.bfloat16)


def draw_keys(key, part):
    return pair_draw(key)[1].astype(jnp.bfloat16)


def block_levels(stream_key, dims, cuts, least, high):
    level = 1.0
    for position, parts in cuts:
        heights = jax.random.uniform(jax.random.fold_in(jax.random.fold_in(stream_key, 6), position), (parts,), jnp.float32, least / len(cuts), high / len(cuts))
        level = level * jnp.repeat(jnp.exp(heights), dims[position] // parts).reshape((-1,) + (1,) * (len(dims) - 1 - position))
    return level


def profile(amount, total, limit, slope):
    loads = [(1 << 20) // math.isqrt(grade ** slope) + 1 for grade in range(2, amount + 1)]
    spare, counts = total - limit - (amount - 1), [1] * (amount - 1)
    while spare > 0:
        free = [i for i in range(amount - 1) if counts[i] < limit]
        pool, left = sum([loads[i] for i in free]), spare
        for i in free:
            more = min(limit - counts[i], max(1, left * loads[i] // pool), spare)
            counts[i] = counts[i] + more
            spare = spare - more
    return np.array([limit] + counts)


def ragged_sizes(own_key, amount, total, bound, lean):
    if amount == 2:
        one = jax.random.randint(own_key, (), max(1, total - bound), min(bound, total - 1) + 1)
        return jnp.stack([one, total - one])
    lengths = jnp.asarray(profile(amount, total, bound, lean), jnp.int32)
    pairs = (amount - 1) // 2
    source_of, taker = lengths[1:1 + 2 * pairs:2], lengths[2:2 + 2 * pairs:2]
    slack = jnp.minimum(source_of - 1, bound - taker)
    passed = jax.random.randint(jax.random.fold_in(own_key, 1), (pairs,), 0, 1 << 20) % (slack + 1)
    lengths = lengths.at[1:1 + 2 * pairs:2].set(source_of - passed).at[2:2 + 2 * pairs:2].set(taker + passed)
    return lengths[jax.random.permutation(jax.random.fold_in(own_key, 2), amount)]


def bell_draw(own_key, shape, scale, limit, split=(), kind=jnp.bfloat16):
    values = scale * jax.random.normal(own_key, shape, jnp.float32)
    if split:
        values = values * block_levels(own_key, shape, split, -0.22, 0.18)
    return jnp.clip(values, -limit, limit).astype(kind)


def setup_inputs(seed: int = 0, part: int = 0) -> dict:
    key_of = jax.random.split(jax.random.key(seed), 6)
    part_splits = jax.random.split(jax.random.fold_in(key_of[5], part), 6)
    queries = draw_queries(jax.random.fold_in(jax.random.fold_in(key_of[5], part), 71), part)
    keys = draw_keys(jax.random.fold_in(jax.random.fold_in(key_of[5], part), 71), part)
    values = bell_draw(part_splits[2], (SEQ_LEN, H * HD), 1.0, 6.0, ((0, 32),))
    cotangent = bell_draw(part_splits[3], (SEQ_LEN, H * HD), 1.0, 6.0, ((0, 32),))
    doc_ids = jnp.searchsorted(jnp.cumsum(ragged_sizes(part_splits[4], DOCS, SEQ_LEN, DOC_MOST, 2)), jnp.arange(SEQ_LEN), side="right").astype(jnp.int32)
    return {"queries": queries, "keys": keys, "values": values, "cotangent": cotangent, "doc_ids": doc_ids}


MASKED = -1e30


def dilate(array, dilation_step):
    heads = array.shape[1]
    rows = array.shape[0] // dilation_step
    shaped = array.reshape((rows, dilation_step) + array.shape[1:])
    return shaped[:, np.arange(heads) % dilation_step, np.arange(heads)]


def place_rows(array, dilation_step, filler):
    heads = array.shape[1]
    rows = array.shape[0]
    empty = jnp.full((rows, dilation_step) + array.shape[1:], filler, array.dtype)
    filled = empty.at[:, np.arange(heads) % dilation_step, np.arange(heads)].set(array)
    return filled.reshape((rows * dilation_step,) + array.shape[1:])


def coarsen(array):
    return lax.optimization_barrier(array.astype(jnp.bfloat16)).astype(jnp.float32)


def score_block(query_seg, key_segment, doc_seg):
    index = jnp.arange(query_seg.shape[0])
    allowed = (index[None, :] <= index[:, None])[None] & (doc_seg.T[:, :, None] == doc_seg.T[:, None, :])
    score = jnp.einsum("ihd,jhd->hij", query_seg, key_segment, precision=lax.Precision.HIGHEST) * (HD ** -0.5)
    return jnp.where(allowed, score, MASKED)


def segment_forward(item):
    query_seg, key_segment, value_seg, doc_seg = item
    score = score_block(query_seg, key_segment, doc_seg)
    top_score = jnp.max(score, -1)
    log_total = top_score + jnp.log(jnp.sum(jnp.exp(score - top_score[..., None]), -1))
    probs = jnp.exp(score - log_total[..., None])
    attended = jnp.einsum("hij,jhd->ihd", coarsen(probs), value_seg, precision=lax.Precision.HIGHEST)
    return log_total, attended


def segment_backward(item):
    query_seg, key_segment, value_seg, dout_seg, doc_seg, log_total, gain_segment, dot_seg = item
    highest = lax.Precision.HIGHEST
    probs = jnp.exp(score_block(query_seg, key_segment, doc_seg) - log_total[..., None])
    dprob = jnp.einsum("ihd,jhd->hij", dout_seg, value_seg, precision=highest)
    gain = gain_segment.T[:, :, None]
    dscore = coarsen(gain * probs * (dprob - dot_seg.T[:, :, None]))
    weighted = coarsen(gain * probs)
    level_queries = jnp.einsum("hij,jhd->ihd", dscore, key_segment, precision=highest) * (HD ** -0.5)
    level_k = jnp.einsum("hij,ihd->jhd", dscore, query_seg, precision=highest) * (HD ** -0.5)
    level_v = jnp.einsum("hij,ihd->jhd", weighted, dout_seg, precision=highest)
    return level_queries, level_k, level_v


def reference(queries, keys, values, cotangent, doc_ids):
    length_all = queries.shape[0]
    query_rows = queries.reshape(length_all, H, HD)
    key_rows = keys.reshape(length_all, H, HD)
    value_rows = values.reshape(length_all, H, HD)
    grad_rows = cotangent.reshape(length_all, H, HD)
    doc_heads = jnp.broadcast_to(doc_ids[:, None], (length_all, H))

    def segment_cut(array, dilation_step):
        segments = length_all // (SEG * dilation_step)
        return dilate(array, dilation_step).reshape((segments, SEG) + array.shape[1:])

    lse_full = []
    part_full = []
    lse_saved = []
    for index_of_level in range(LEVELS):
        dilation_step = FINEST_DILATION * 2 ** index_of_level
        inputs = (segment_cut(query_rows, dilation_step).astype(jnp.float32),
                  segment_cut(key_rows, dilation_step).astype(jnp.float32),
                  segment_cut(value_rows, dilation_step).astype(jnp.float32),
                  segment_cut(doc_heads, dilation_step))
        log_total, attended = lax.map(segment_forward, inputs)
        lse_full.append(place_rows(log_total.transpose(0, 2, 1).reshape(-1, H), dilation_step, MASKED))
        part_full.append(place_rows(attended.reshape(-1, H, HD), dilation_step, 0.0))
        lse_saved.append(log_total)
    top_level = lse_full[0]
    for index_of_level in range(1, LEVELS):
        top_level = jnp.maximum(top_level, lse_full[index_of_level])
    level_total = jnp.zeros_like(top_level)
    for index_of_level in range(LEVELS):
        level_total = level_total + jnp.exp(lse_full[index_of_level] - top_level)
    merged_log = top_level + jnp.log(level_total)
    weight_matrix = [jnp.exp(entry_lse - merged_log) for entry_lse in lse_full]
    combined = jnp.zeros((length_all, H, HD), jnp.float32)
    for index_of_level in range(LEVELS):
        combined = combined + weight_matrix[index_of_level][..., None] * part_full[index_of_level]
    dot_sum = jnp.sum(grad_rows.astype(jnp.float32) * combined, -1)
    grad_query = jnp.zeros((length_all, H, HD), jnp.float32)
    grad_key = jnp.zeros((length_all, H, HD), jnp.float32)
    grad_value = jnp.zeros((length_all, H, HD), jnp.float32)
    for index_of_level in range(LEVELS):
        dilation_step = FINEST_DILATION * 2 ** index_of_level
        inputs = (segment_cut(query_rows, dilation_step).astype(jnp.float32),
                  segment_cut(key_rows, dilation_step).astype(jnp.float32),
                  segment_cut(value_rows, dilation_step).astype(jnp.float32),
                  segment_cut(grad_rows, dilation_step).astype(jnp.float32),
                  segment_cut(doc_heads, dilation_step),
                  lse_saved[index_of_level],
                  segment_cut(weight_matrix[index_of_level], dilation_step),
                  segment_cut(dot_sum, dilation_step))
        level_queries, level_k, level_v = lax.map(segment_backward, inputs)
        grad_query = grad_query + place_rows(level_queries.reshape(-1, H, HD), dilation_step, 0.0)
        grad_key = grad_key + place_rows(level_k.reshape(-1, H, HD), dilation_step, 0.0)
        grad_value = grad_value + place_rows(level_v.reshape(-1, H, HD), dilation_step, 0.0)
    flattened_shape = (length_all, H * HD)
    return (combined.astype(jnp.bfloat16).reshape(flattened_shape),
            grad_query.astype(jnp.bfloat16).reshape(flattened_shape),
            grad_key.astype(jnp.bfloat16).reshape(flattened_shape),
            grad_value.astype(jnp.bfloat16).reshape(flattened_shape))
```

```python
import functools

import jax
import jax.numpy as jnp
import numpy as np
from jax import lax
from jax.experimental import pallas as pl
from jax.experimental.pallas import tpu as pltpu
from jax.sharding import Mesh
from jax.sharding import PartitionSpec as P

H = 8
HD = 128
SEG = 1024

MASKED = -1e30
SCALE = HD ** -0.5
LOG2E = float(np.log2(np.e))
VMEM = pl.BlockSpec(memory_space=pltpu.VMEM)
DOC_ROWS = 16


def dot_nn(a, b):
    return lax.dot_general(a, b, (((1,), (0,)), ((), ())), preferred_element_type=jnp.float32)


def dot_nt(a, b):
    return lax.dot_general(a, b, (((1,), (1,)), ((), ())), preferred_element_type=jnp.float32)


def selector(head, r0, rows, tokens, transposed):
    r1 = 2 * r0
    shape = (tokens, 2 * rows) if transposed else (2 * rows, tokens)
    k = lax.broadcasted_iota(jnp.int32, shape, 1 if transposed else 0)
    p = lax.broadcasted_iota(jnp.int32, shape, 0 if transposed else 1)
    coarse = head % r1
    other = (coarse + r0) % r1
    target = jnp.where(k < rows, r1 * k + coarse, r1 * (k - rows) + other)
    return (p == target).astype(jnp.float32).astype(jnp.bfloat16)


def pack_kernel(r0, rows, q_ref, k_ref, v_ref, g_ref, doc_ref, out_ref):
    tokens = q_ref.shape[0]
    docs = doc_ref[...].astype(jnp.float32).astype(jnp.bfloat16)
    docs = jnp.broadcast_to(docs, (DOC_ROWS, tokens))
    for h in range(H):
        sel = selector(h, r0, rows, tokens, False)
        cols = slice(h * HD, (h + 1) * HD)
        out_ref[h, 0:2 * rows] = dot_nn(sel, q_ref[:, cols]).astype(jnp.bfloat16)
        out_ref[h, 2 * rows:4 * rows] = dot_nn(sel, g_ref[:, cols]).astype(jnp.bfloat16)
        k = dot_nn(sel, k_ref[:, cols]).astype(jnp.bfloat16)
        v = dot_nn(sel, v_ref[:, cols]).astype(jnp.bfloat16)
        out_ref[h, 4 * rows:5 * rows] = k[rows:]
        out_ref[h, 5 * rows:6 * rows] = v[rows:]
        out_ref[h, 6 * rows:7 * rows] = k[:rows]
        out_ref[h, 7 * rows:8 * rows] = v[:rows]
        out_ref[h, 8 * rows:8 * rows + DOC_ROWS] = docs


def main_kernel(r0, rows, members, *refs):
    r1 = 2 * r0
    G = members
    own_ref = refs[0]
    swap_refs = refs[1:G]
    cross_refs = refs[G:2 * G]
    out_own, out_kv = refs[2 * G], refs[2 * G + 1]
    out_swap = refs[2 * G + 2:3 * G + 1]
    out_cross = refs[3 * G + 1:4 * G + 1]
    (k1, k2, kx, v1, v2, vx, d1, d2, dx, gk1, gk2, gv1, gv2, gkx, gvx) = refs[4 * G + 1:]
    bf16, f32 = jnp.bfloat16, jnp.float32
    tokens = HD
    half = lax.axis_index("half")
    head = lax.axis_index("head")
    member = lax.axis_index("member")

    sel = selector(head, r0, rows, tokens, False)
    for j in range(H):
        for g in range(G):
            at = pl.ds((j * G + g) * rows, rows)
            if g == 0:
                ref, base = own_ref, 4 * rows
            else:
                ref, base = swap_refs[g - 1], 0
            k2[at] = ref[j, base:base + rows]
            v2[at] = ref[j, base + rows:base + 2 * rows]
            k1[at] = ref[j, base + 2 * rows:base + 3 * rows]
            v1[at] = ref[j, base + 3 * rows:base + 4 * rows]
            doc = ref[j, base + 4 * rows:base + 4 * rows + DOC_ROWS][0:1]
            d1[at] = sel[:rows] * doc
            d2[at] = sel[rows:] * doc
            ref = cross_refs[g]
            kx[at] = ref[j, 0:rows]
            vx[at] = ref[j, rows:2 * rows]
            doc = ref[j, 2 * rows:2 * rows + DOC_ROWS][0:1]
            dx[at] = sel[:rows] * doc

    eye = (lax.broadcasted_iota(jnp.int32, (HD, HD), 0) == lax.broadcasted_iota(jnp.int32, (HD, HD), 1))
    eye = eye.astype(f32).astype(bf16)
    ones = jnp.ones((HD, HD), bf16)
    transposed = lambda x: dot_nt(eye, x).astype(bf16)
    doc_cols = lambda x: dot_nn(x, ones)[:, 0:1]
    k1t, k2t, kxt = transposed(k1[...]), transposed(k2[...]), transposed(kx[...])
    v1t, v2t, vxt = transposed(v1[...]), transposed(v2[...]), transposed(vx[...])
    docs1, docs2 = doc_cols(d1[...]), doc_cols(d2[...])
    docsx = doc_cols(dx[...]) + jnp.where(half == 0, 1000.0, 0.0)

    tiles = 2
    per = H // tiles
    nq = per * rows
    nd = per * G * rows
    lanes = 2 * nq
    xn = nq if nq % 128 == 0 else lanes

    coarse = head % r1
    other = (coarse + r0) % r1
    lane = lax.broadcasted_iota(jnp.int32, (1, lanes), 1)
    fine = lane >= nq
    ql = jnp.where(fine, lane - nq, lane)
    qpos = (ql // rows) * (G * tokens) + member * tokens + r1 * (ql % rows) + jnp.where(fine, other, coarse)
    kl = lax.broadcasted_iota(jnp.int32, (nd, 1), 0)
    kmember = member ^ ((kl // rows) % G)
    kpos = (kl // (rows * G)) * (G * tokens) + kmember * tokens + r1 * (kl % rows)
    causal1 = kpos + coarse <= qpos
    causal2 = kpos + other <= qpos
    both = jnp.where(fine, 0.0, 1.0)

    for u in reversed(range(tiles)):
        nk = (u + 1) * nd
        x0 = u * nd
        src = range(u * per, (u + 1) * per)
        qt = jnp.concatenate([own_ref[j, 0:rows] for j in src] + [own_ref[j, rows:2 * rows] for j in src], 0)
        gt = jnp.concatenate([own_ref[j, 2 * rows:3 * rows] for j in src] + [own_ref[j, 3 * rows:4 * rows] for j in src], 0)
        at = pl.ds(u * nd, nd)
        dq = jnp.concatenate(
            [sel[:rows] * own_ref[j, 8 * rows:8 * rows + DOC_ROWS][0:1] for j in src]
            + [sel[rows:] * own_ref[j, 8 * rows:8 * rows + DOC_ROWS][0:1] for j in src], 0)
        qdoc = dot_nt(jnp.ones((16, HD), bf16), dq)[0:1]

        def scores(key, docs, causal):
            s = dot_nt(key, qt)
            allow = docs == qdoc
            s = jnp.where(allow, s, MASKED)
            if u:
                return jnp.concatenate([s[:x0], jnp.where(causal, s[x0:], MASKED)], 0)
            return jnp.where(causal, s, MASKED)

        s1 = scores(k1[0:nk], docs1[0:nk], causal1)
        s2 = scores(k2[0:nk], docs2[0:nk], causal2)
        sx = dot_nt(kx[x0:], qt[:xn])
        allowx = docsx[x0:] == qdoc[:, :xn]
        if xn != nq:
            allowx = allowx & (lane[:, :xn] < nq)
        sx = jnp.where(allowx, sx, MASKED)
        top = jnp.maximum(jnp.max(s1, 0, keepdims=True), jnp.max(s2, 0, keepdims=True))
        topx = jnp.maximum(top[:, :xn], jnp.max(sx, 0, keepdims=True))
        top = topx if xn == lanes else jnp.concatenate([topx, top[:, xn:]], 1)
        c = SCALE * LOG2E
        base = top * c
        p1 = jnp.exp2(s1 * c - (base - both))
        p2 = jnp.exp2(s2 * c - base)
        px = jnp.exp2(sx * c - base[:, :xn])
        total = jnp.sum(p1, 0, keepdims=True) + jnp.sum(p2, 0, keepdims=True)
        totalx = total[:, :xn] + jnp.sum(px, 0, keepdims=True)
        total = totalx if xn == lanes else jnp.concatenate([totalx, total[:, xn:]], 1)
        inv = 1.0 / total
        out = dot_nn(v1t[:, :nk], p1.astype(bf16)) + dot_nn(v2t[:, :nk], p2.astype(bf16))
        outx = out[:, :xn] + dot_nn(vxt[:, x0:], px.astype(bf16))
        out = outx if xn == lanes else jnp.concatenate([outx, out[:, xn:]], 1)
        out = out * inv
        gtt = dot_nt(eye, gt)
        dot = jnp.sum(gtt * out, 0, keepdims=True)
        dinv = dot * inv

        def grads(p, value, gt, inv, dinv):
            ds = p * (dot_nt(value, gt) * inv - dinv)
            return ds.astype(bf16), (p * inv).astype(bf16)

        ds1, w1 = grads(p1, v1[0:nk], gt, inv, dinv)
        ds2, w2 = grads(p2, v2[0:nk], gt, inv, dinv)
        dsx, wx = grads(px, vx[x0:], gt[:xn], inv[:, :xn], dinv[:, :xn])
        gq = dot_nn(k1t[:, :nk], ds1) + dot_nn(k2t[:, :nk], ds2)
        gqx = gq[:, :xn] + dot_nn(kxt[:, x0:], dsx)
        gq = gqx if xn == lanes else jnp.concatenate([gqx, gq[:, xn:]], 1)
        gq = gq * SCALE

        def add(ref, lo, hi, value):
            if u == tiles - 1:
                ref[lo:hi] = value
                if ref is gkx or ref is gvx:
                    ref[0:lo] = jnp.zeros((lo, HD), f32)
            else:
                ref[lo:hi] = ref[lo:hi] + value

        add(gk1, 0, nk, dot_nn(ds1, qt))
        add(gk2, 0, nk, dot_nn(ds2, qt))
        add(gv1, 0, nk, dot_nn(w1, gt))
        add(gv2, 0, nk, dot_nn(w2, gt))
        add(gkx, x0, tiles * nd, dot_nn(dsx, qt[:xn]))
        add(gvx, x0, tiles * nd, dot_nn(wx, gt[:xn]))
        out = out.T.astype(bf16)
        gq = gq.T.astype(bf16)
        for i, j in enumerate(src):
            lo = i * rows
            out_own[j, 0:rows] = out[lo:lo + rows]
            out_own[j, rows:2 * rows] = out[nq + lo:nq + lo + rows]
            out_own[j, 2 * rows:3 * rows] = gq[lo:lo + rows]
            out_own[j, 3 * rows:4 * rows] = gq[nq + lo:nq + lo + rows]

    for j in range(H):
        for g in range(G):
            at = pl.ds((j * G + g) * rows, rows)
            ref = out_kv if g == 0 else out_swap[g - 1]
            ref[j, 0:rows] = (gk1[at] * SCALE).astype(ref.dtype)
            ref[j, rows:2 * rows] = (gk2[at] * SCALE).astype(ref.dtype)
            ref[j, 2 * rows:3 * rows] = gv1[at].astype(ref.dtype)
            ref[j, 3 * rows:4 * rows] = gv2[at].astype(ref.dtype)
            out_cross[g][j, 0:rows] = (gkx[at] * SCALE).astype(bf16)
            out_cross[g][j, rows:2 * rows] = gvx[at].astype(bf16)


def sum_kernel(rows, members, *refs):
    G = members
    own_ref, kv_ref = refs[0], refs[1]
    swap_refs = refs[2:G + 1]
    cross_refs = refs[G + 1:2 * G + 1]
    out_ref = refs[2 * G + 1]
    f32 = jnp.float32
    out_ref[:, 0:4 * rows] = own_ref[...]
    for j in range(H):
        total = kv_ref[j]
        for ref in swap_refs:
            total = total + ref[j].astype(f32)
        gk1, gv1 = total[0:rows], total[2 * rows:3 * rows]
        for ref in cross_refs:
            gk1 = gk1 + ref[j, 0:rows].astype(f32)
            gv1 = gv1 + ref[j, rows:2 * rows].astype(f32)
        out_ref[j, 4 * rows:5 * rows] = gk1.astype(jnp.bfloat16)
        out_ref[j, 5 * rows:6 * rows] = total[rows:2 * rows].astype(jnp.bfloat16)
        out_ref[j, 6 * rows:7 * rows] = gv1.astype(jnp.bfloat16)
        out_ref[j, 7 * rows:8 * rows] = total[3 * rows:4 * rows].astype(jnp.bfloat16)


def unpack_kernel(r0, rows, in_ref, *out_refs):
    tokens = out_refs[0].shape[0]
    for h in range(H):
        sel = selector(h, r0, rows, tokens, True)
        for i, ref in enumerate(out_refs):
            part = in_ref[h, 2 * i * rows:2 * (i + 1) * rows]
            ref[:, h * HD:(h + 1) * HD] = dot_nn(sel, part).astype(jnp.bfloat16)


def call(kernel, out_shape, scratch=()):
    return pl.pallas_call(
        kernel,
        out_shape=out_shape,
        scratch_shapes=list(scratch),
        compiler_params=pltpu.CompilerParams(vmem_limit_bytes=48 * 1024 * 1024),
    )


def per_device(members, queries, keys, values, cotangent, doc_ids):
    G = members
    tokens = queries.shape[0]
    devices = 2 * H * G
    r0 = tokens * devices // (2 * SEG)
    rows = tokens // (2 * r0)
    bf16, f32 = jnp.bfloat16, jnp.float32
    shape = jax.ShapeDtypeStruct
    n = H * G * rows

    packed = call(functools.partial(pack_kernel, r0, rows), shape((H, 8 * rows + DOC_ROWS, HD), bf16))(
        queries, keys, values, cotangent, doc_ids.reshape(1, tokens))
    own = lax.all_to_all(packed, "head", 0, 0, tiled=True)

    def to_member(x, g):
        return lax.ppermute(x, "member", [(i, i ^ g) for i in range(G)])

    def to_half(x):
        return lax.ppermute(x, "half", [(0, 1), (1, 0)])

    cross = to_half(own[:, 6 * rows:])
    swaps = [to_member(own[:, 4 * rows:], g) for g in range(1, G)]
    crosses = [cross] + [to_member(cross, g) for g in range(1, G)]
    outs = call(
        functools.partial(main_kernel, r0, rows, G),
        [shape((H, 4 * rows, HD), bf16), shape((H, 4 * rows, HD), f32)]
        + [shape((H, 4 * rows, HD), bf16)] * (G - 1) + [shape((H, 2 * rows, HD), bf16)] * G,
        [pltpu.VMEM((n, HD), bf16)] * 9 + [pltpu.VMEM((n, HD), f32)] * 6,
    )(own, *swaps, *crosses)
    out_own, out_kv = outs[0], outs[1]
    crosses = [to_half(x) for x in outs[G + 1:]]
    swaps = [to_member(outs[1 + g], g) for g in range(1, G)]
    crosses = [crosses[0]] + [to_member(crosses[g], g) for g in range(1, G)]
    back = call(functools.partial(sum_kernel, rows, G), shape((H, 8 * rows, HD), bf16))(
        out_own, out_kv, *swaps, *crosses)
    back = lax.all_to_all(back, "head", 0, 0, tiled=True)
    return tuple(call(functools.partial(unpack_kernel, r0, rows), [shape((tokens, H * HD), bf16)] * 4)(back))


def solution(mesh):
    members = mesh.shape["seq"] // (2 * H)
    parts = {"seq": [("half", 2), ("head", H), ("member", members)]}
    axes = [part for name in mesh.axis_names for part in parts.get(name, [(name, mesh.shape[name])])]
    inner = Mesh(mesh.devices.reshape([size for _, size in axes]), [name for name, _ in axes])
    split = ("dp", "half", "head", "member")
    in_specs = (P(split, None),) * 4 + (P(split),)
    return jax.shard_map(
        functools.partial(per_device, members), mesh=inner, in_specs=in_specs,
        out_specs=(P(split, None),) * 4, check_vma=False,
    )
```

```python
import functools

import jax
import jax.numpy as jnp
import numpy as np
from jax import lax
from jax.experimental import pallas as pl
from jax.experimental.pallas import tpu as pltpu
from jax.sharding import Mesh
from jax.sharding import PartitionSpec as P

H = 8
HD = 128
SEG = 1024

MASKED = -1e30
SCALE = HD ** -0.5
LOG2E = float(np.log2(np.e))
VMEM = pl.BlockSpec(memory_space=pltpu.VMEM)
DOC_ROWS = 16


def dot_nn(a, b):
    return lax.dot_general(a, b, (((1,), (0,)), ((), ())), preferred_element_type=jnp.float32)


def dot_nt(a, b):
    return lax.dot_general(a, b, (((1,), (1,)), ((), ())), preferred_element_type=jnp.float32)


def selector(head, r0, rows, tokens, transposed):
    r1 = 2 * r0
    shape = (tokens, 2 * rows) if transposed else (2 * rows, tokens)
    k = lax.broadcasted_iota(jnp.int32, shape, 1 if transposed else 0)
    p = lax.broadcasted_iota(jnp.int32, shape, 0 if transposed else 1)
    coarse = head % r1
    other = (coarse + r0) % r1
    target = jnp.where(k < rows, r1 * k + coarse, r1 * (k - rows) + other)
    return (p == target).astype(jnp.float32).astype(jnp.bfloat16)


def pack_kernel(r0, rows, q_in, k_in, v_in, g_in, doc_ref, qg_ref, kv_ref, q_ref, k_ref, v_ref, g_ref, sem):
    tokens = q_ref.shape[0]
    pairs = ((k_in, k_ref), (v_in, v_ref), (q_in, q_ref), (g_in, g_ref))
    copies = [pltpu.make_async_copy(src, dst, sem.at[i]) for i, (src, dst) in enumerate(pairs)]
    for copy in copies:
        copy.start()
    docs = doc_ref[...].astype(jnp.float32).astype(jnp.bfloat16)
    docs = jnp.broadcast_to(docs, (DOC_ROWS, tokens))
    cols = [slice(h * HD, (h + 1) * HD) for h in range(H)]
    sels = [selector(h, r0, rows, tokens, False) for h in range(min(H, 2 * r0))]
    pick = lambda h, ref: dot_nn(sels[h % (2 * r0)], ref[:, cols[h]]).astype(jnp.bfloat16)
    for i, copy in enumerate(copies[:2]):
        copy.wait()
        for h in range(H):
            x = pick(h, pairs[i][1])
            kv_ref[h, i * rows:(i + 1) * rows] = x[rows:]
            kv_ref[h, (2 + i) * rows:(3 + i) * rows] = x[:rows]
    for h in range(H):
        kv_ref[h, 4 * rows:4 * rows + DOC_ROWS] = docs
    for i, copy in enumerate(copies[2:]):
        copy.wait()
        for h in range(H):
            qg_ref[h, 2 * i * rows:2 * (i + 1) * rows] = pick(h, pairs[2 + i][1])


def main_kernel(r0, rows, members, *refs):
    r1 = 2 * r0
    G = members
    own_ref = refs[0]
    kv_refs = refs[1:G + 1]
    cross_refs = refs[G + 1:2 * G + 1]
    out_own, out_kv = refs[2 * G + 1], refs[2 * G + 2]
    out_swap = refs[2 * G + 3:3 * G + 2]
    out_cross = refs[3 * G + 2:4 * G + 2]
    (k1, k2, kx, v1, v2, vx, d1, d2, dx, gk1, gk2, gv1, gv2, gkx, gvx) = refs[4 * G + 2:]
    bf16, f32 = jnp.bfloat16, jnp.float32
    tokens = HD
    half = lax.axis_index("half")
    head = lax.axis_index("head")
    member = lax.axis_index("member")

    sel = selector(head, r0, rows, tokens, False)
    for j in range(H):
        for g in range(G):
            at = pl.ds((j * G + g) * rows, rows)
            ref = kv_refs[g]
            k2[at] = ref[j, 0:rows]
            v2[at] = ref[j, rows:2 * rows]
            k1[at] = ref[j, 2 * rows:3 * rows]
            v1[at] = ref[j, 3 * rows:4 * rows]
            doc = ref[j, 4 * rows:4 * rows + DOC_ROWS][0:1]
            d1[at] = sel[:rows] * doc
            d2[at] = sel[rows:] * doc
            ref = cross_refs[g]
            kx[at] = ref[j, 0:rows]
            vx[at] = ref[j, rows:2 * rows]
            doc = ref[j, 2 * rows:2 * rows + DOC_ROWS][0:1]
            dx[at] = sel[:rows] * doc

    eye = (lax.broadcasted_iota(jnp.int32, (HD, HD), 0) == lax.broadcasted_iota(jnp.int32, (HD, HD), 1))
    eye = eye.astype(f32).astype(bf16)
    ones = jnp.ones((HD, HD), bf16)
    transposed = lambda x: dot_nt(eye, x).astype(bf16)
    doc_cols = lambda x: dot_nn(x, ones)[:, 0:1]
    k1t, k2t, kxt = transposed(k1[...]), transposed(k2[...]), transposed(kx[...])
    v1t, v2t, vxt = transposed(v1[...]), transposed(v2[...]), transposed(vx[...])
    docs1, docs2 = doc_cols(d1[...]), doc_cols(d2[...])
    docsx = doc_cols(dx[...]) + jnp.where(half == 0, 1000.0, 0.0)

    tiles = 2
    per = H // tiles
    nq = per * rows
    nd = per * G * rows
    lanes = 2 * nq
    xn = nq if nq % 128 == 0 else lanes

    coarse = head % r1
    other = (coarse + r0) % r1
    lane = lax.broadcasted_iota(jnp.int32, (1, lanes), 1)
    fine = lane >= nq
    ql = jnp.where(fine, lane - nq, lane)
    qpos = (ql // rows) * (G * tokens) + member * tokens + r1 * (ql % rows) + jnp.where(fine, other, coarse)
    kl = lax.broadcasted_iota(jnp.int32, (nd, 1), 0)
    kmember = member ^ ((kl // rows) % G)
    kpos = (kl // (rows * G)) * (G * tokens) + kmember * tokens + r1 * (kl % rows)
    causal1 = kpos + coarse <= qpos
    causal2 = kpos + other <= qpos
    both = jnp.where(fine, 0.0, 1.0)

    for u in reversed(range(tiles)):
        nk = (u + 1) * nd
        x0 = u * nd
        src = range(u * per, (u + 1) * per)
        qt = jnp.concatenate([own_ref[j, 0:rows] for j in src] + [own_ref[j, rows:2 * rows] for j in src], 0)
        gt = jnp.concatenate([own_ref[j, 2 * rows:3 * rows] for j in src] + [own_ref[j, 3 * rows:4 * rows] for j in src], 0)
        at = pl.ds(u * nd, nd)
        dq = jnp.concatenate(
            [sel[:rows] * kv_refs[0][j, 4 * rows:4 * rows + DOC_ROWS][0:1] for j in src]
            + [sel[rows:] * kv_refs[0][j, 4 * rows:4 * rows + DOC_ROWS][0:1] for j in src], 0)
        qdoc = dot_nt(jnp.ones((16, HD), bf16), dq)[0:1]

        def scores(key, docs, causal):
            s = dot_nt(key, qt)
            allow = docs == qdoc
            s = jnp.where(allow, s, MASKED)
            if u:
                return jnp.concatenate([s[:x0], jnp.where(causal, s[x0:], MASKED)], 0)
            return jnp.where(causal, s, MASKED)

        s1 = scores(k1[0:nk], docs1[0:nk], causal1)
        s2 = scores(k2[0:nk], docs2[0:nk], causal2)
        sx = dot_nt(kx[x0:], qt[:xn])
        allowx = docsx[x0:] == qdoc[:, :xn]
        if xn != nq:
            allowx = allowx & (lane[:, :xn] < nq)
        sx = jnp.where(allowx, sx, MASKED)
        top = jnp.maximum(jnp.max(s1, 0, keepdims=True), jnp.max(s2, 0, keepdims=True))
        topx = jnp.maximum(top[:, :xn], jnp.max(sx, 0, keepdims=True))
        top = topx if xn == lanes else jnp.concatenate([topx, top[:, xn:]], 1)
        c = SCALE * LOG2E
        base = top * c
        p1 = jnp.exp2(s1 * c - (base - both))
        p2 = jnp.exp2(s2 * c - base)
        px = jnp.exp2(sx * c - base[:, :xn])
        total = jnp.sum(p1, 0, keepdims=True) + jnp.sum(p2, 0, keepdims=True)
        totalx = total[:, :xn] + jnp.sum(px, 0, keepdims=True)
        total = totalx if xn == lanes else jnp.concatenate([totalx, total[:, xn:]], 1)
        inv = 1.0 / total
        out = dot_nn(v1t[:, :nk], p1.astype(bf16)) + dot_nn(v2t[:, :nk], p2.astype(bf16))
        outx = out[:, :xn] + dot_nn(vxt[:, x0:], px.astype(bf16))
        out = outx if xn == lanes else jnp.concatenate([outx, out[:, xn:]], 1)
        out = out * inv
        gtt = dot_nt(eye, gt)
        dot = jnp.sum(gtt * out, 0, keepdims=True)
        dinv = dot * inv

        def grads(p, value, gt, inv, dinv):
            ds = p * (dot_nt(value, gt) * inv - dinv)
            return ds.astype(bf16), (p * inv).astype(bf16)

        ds1, w1 = grads(p1, v1[0:nk], gt, inv, dinv)
        ds2, w2 = grads(p2, v2[0:nk], gt, inv, dinv)
        dsx, wx = grads(px, vx[x0:], gt[:xn], inv[:, :xn], dinv[:, :xn])
        gq = dot_nn(k1t[:, :nk], ds1) + dot_nn(k2t[:, :nk], ds2)
        gqx = gq[:, :xn] + dot_nn(kxt[:, x0:], dsx)
        gq = gqx if xn == lanes else jnp.concatenate([gqx, gq[:, xn:]], 1)
        gq = gq * SCALE

        def add(ref, lo, hi, value):
            if u == tiles - 1:
                ref[lo:hi] = value
                if ref is gkx or ref is gvx:
                    ref[0:lo] = jnp.zeros((lo, HD), f32)
            else:
                ref[lo:hi] = ref[lo:hi] + value

        add(gk1, 0, nk, dot_nn(ds1, qt))
        add(gk2, 0, nk, dot_nn(ds2, qt))
        add(gv1, 0, nk, dot_nn(w1, gt))
        add(gv2, 0, nk, dot_nn(w2, gt))
        add(gkx, x0, tiles * nd, dot_nn(dsx, qt[:xn]))
        add(gvx, x0, tiles * nd, dot_nn(wx, gt[:xn]))
        out = out.T.astype(bf16)
        gq = gq.T.astype(bf16)
        for i, j in enumerate(src):
            lo = i * rows
            out_own[j, 0:rows] = out[lo:lo + rows]
            out_own[j, rows:2 * rows] = out[nq + lo:nq + lo + rows]
            out_own[j, 2 * rows:3 * rows] = gq[lo:lo + rows]
            out_own[j, 3 * rows:4 * rows] = gq[nq + lo:nq + lo + rows]

    for j in range(H):
        for g in range(G):
            at = pl.ds((j * G + g) * rows, rows)
            ref = out_kv if g == 0 else out_swap[g - 1]
            ref[j, 0:rows] = (gk1[at] * SCALE).astype(ref.dtype)
            ref[j, rows:2 * rows] = (gk2[at] * SCALE).astype(ref.dtype)
            ref[j, 2 * rows:3 * rows] = gv1[at].astype(ref.dtype)
            ref[j, 3 * rows:4 * rows] = gv2[at].astype(ref.dtype)
            out_cross[g][j, 0:rows] = (gkx[at] * SCALE).astype(bf16)
            out_cross[g][j, rows:2 * rows] = gvx[at].astype(bf16)


def sum_kernel(rows, members, *refs):
    G = members
    kv_ref = refs[0]
    swap_refs = refs[1:G]
    cross_refs = refs[G:2 * G]
    out_ref = refs[2 * G]
    f32 = jnp.float32
    for j in range(H):
        total = kv_ref[j]
        for ref in swap_refs:
            total = total + ref[j].astype(f32)
        gk1, gv1 = total[0:rows], total[2 * rows:3 * rows]
        for ref in cross_refs:
            gk1 = gk1 + ref[j, 0:rows].astype(f32)
            gv1 = gv1 + ref[j, rows:2 * rows].astype(f32)
        out_ref[j, 0:rows] = gk1.astype(jnp.bfloat16)
        out_ref[j, rows:2 * rows] = total[rows:2 * rows].astype(jnp.bfloat16)
        out_ref[j, 2 * rows:3 * rows] = gv1.astype(jnp.bfloat16)
        out_ref[j, 3 * rows:4 * rows] = total[3 * rows:4 * rows].astype(jnp.bfloat16)


def unpack_kernel(r0, rows, in_ref, *out_refs):
    tokens = out_refs[0].shape[0]
    for h in range(H):
        sel = selector(h, r0, rows, tokens, True)
        for i, ref in enumerate(out_refs):
            part = in_ref[h, 2 * i * rows:2 * (i + 1) * rows]
            ref[:, h * HD:(h + 1) * HD] = dot_nn(sel, part).astype(jnp.bfloat16)


def call(kernel, out_shape, scratch=(), limit=48, **more):
    return pl.pallas_call(
        kernel,
        out_shape=out_shape,
        scratch_shapes=list(scratch),
        compiler_params=pltpu.CompilerParams(vmem_limit_bytes=limit * 1024 * 1024),
        **more,
    )


def per_device(members, queries, keys, values, cotangent, doc_ids):
    G = members
    tokens = queries.shape[0]
    devices = 2 * H * G
    r0 = tokens * devices // (2 * SEG)
    rows = tokens // (2 * r0)
    bf16, f32 = jnp.bfloat16, jnp.float32
    shape = jax.ShapeDtypeStruct
    n = H * G * rows
    anywhere = pl.BlockSpec(memory_space=pltpu.HBM)

    qg, kv = call(
        functools.partial(pack_kernel, r0, rows),
        [shape((H, 4 * rows, HD), bf16), shape((H, 4 * rows + DOC_ROWS, HD), bf16)],
        [pltpu.VMEM((tokens, H * HD), bf16)] * 4 + [pltpu.SemaphoreType.DMA((4,))],
        limit=64, in_specs=[anywhere] * 4 + [VMEM],
    )(queries, keys, values, cotangent, doc_ids.reshape(1, tokens))

    def to_head(x):
        return lax.all_to_all(x, "head", 0, 0, tiled=True)

    def to_member(x, g):
        return lax.ppermute(x, "member", [(i, i ^ g) for i in range(G)])

    def to_half(x):
        return lax.ppermute(x, "half", [(0, 1), (1, 0)])

    kv = to_head(kv)
    cross = to_half(kv[:, 2 * rows:])
    kvs = [kv] + [to_member(kv, g) for g in range(1, G)]
    qg = to_head(qg)
    cross, qg = lax.optimization_barrier((cross, qg))
    crosses = [cross] + [to_member(cross, g) for g in range(1, G)]
    outs = call(
        functools.partial(main_kernel, r0, rows, G),
        [shape((H, 4 * rows, HD), bf16), shape((H, 4 * rows, HD), f32)]
        + [shape((H, 4 * rows, HD), bf16)] * (G - 1) + [shape((H, 2 * rows, HD), bf16)] * G,
        [pltpu.VMEM((n, HD), bf16)] * 9 + [pltpu.VMEM((n, HD), f32)] * 6,
    )(qg, *kvs, *crosses)
    out_own, out_kv = outs[0], outs[1]
    crosses = [to_half(x) for x in outs[G + 1:]]
    swaps = [to_member(outs[1 + g], g) for g in range(1, G)]
    out_own = to_head(out_own)
    *crosses, out_own = lax.optimization_barrier((*crosses, out_own))
    crosses = [crosses[0]] + [to_member(crosses[g], g) for g in range(1, G)]
    out_kv = call(functools.partial(sum_kernel, rows, G), shape((H, 4 * rows, HD), bf16))(
        out_kv, *swaps, *crosses)
    out_kv = to_head(out_kv)
    unpack = call(functools.partial(unpack_kernel, r0, rows), [shape((tokens, H * HD), bf16)] * 2)
    return tuple(unpack(out_own)) + tuple(unpack(out_kv))


def solution(mesh):
    members = mesh.shape["seq"] // (2 * H)
    parts = {"seq": [("half", 2), ("head", H), ("member", members)]}
    axes = [part for name in mesh.axis_names for part in parts.get(name, [(name, mesh.shape[name])])]
    inner = Mesh(mesh.devices.reshape([size for _, size in axes]), [name for name, _ in axes])
    split = ("dp", "half", "head", "member")
    in_specs = (P(split, None),) * 4 + (P(split),)
    return jax.shard_map(
        functools.partial(per_device, members), mesh=inner, in_specs=in_specs,
        out_specs=(P(split, None),) * 4, check_vma=False,
    )
```

```python
import functools

import jax
import jax.numpy as jnp
import numpy as np
from jax import lax
from jax.experimental import pallas as pl
from jax.experimental.pallas import tpu as pltpu
from jax.sharding import Mesh
from jax.sharding import PartitionSpec as P

H = 8
HD = 128
SEG = 1024

MASKED = -1e30
SCALE = HD ** -0.5
LOG2E = float(np.log2(np.e))
VMEM = pl.BlockSpec(memory_space=pltpu.VMEM)


def dot_nn(a, b):
    return lax.dot_general(a, b, (((1,), (0,)), ((), ())), preferred_element_type=jnp.float32)


def dot_nt(a, b):
    return lax.dot_general(a, b, (((1,), (1,)), ((), ())), preferred_element_type=jnp.float32)


def selector(head, r0, rows, tokens, transposed):
    r1 = 2 * r0
    shape = (tokens, 2 * rows) if transposed else (2 * rows, tokens)
    k = lax.broadcasted_iota(jnp.int32, shape, 1 if transposed else 0)
    p = lax.broadcasted_iota(jnp.int32, shape, 0 if transposed else 1)
    coarse = head % r1
    other = (coarse + r0) % r1
    target = jnp.where(k < rows, r1 * k + coarse, r1 * (k - rows) + other)
    return (p == target).astype(jnp.float32).astype(jnp.bfloat16)


def pack_kernel(r0, rows, q_in, k_in, v_in, g_in, coarse_out, rest_out, q_ref, k_ref, v_ref, g_ref, coarse, rest, sem):
    tokens = q_ref.shape[0]
    pairs = ((k_in, k_ref), (v_in, v_ref), (q_in, q_ref), (g_in, g_ref))
    copies = [pltpu.make_async_copy(src, dst, sem.at[i]) for i, (src, dst) in enumerate(pairs)]
    for copy in copies:
        copy.start()
    cols = [slice(h * HD, (h + 1) * HD) for h in range(H)]
    sels = [selector(h, r0, rows, tokens, False) for h in range(min(H, 2 * r0))]
    pick = lambda h, ref: dot_nn(sels[h % (2 * r0)], ref[:, cols[h]]).astype(jnp.bfloat16)
    for i, copy in enumerate(copies[:2]):
        copy.wait()
        for h in range(H):
            x = pick(h, pairs[i][1])
            coarse[h, i * rows:(i + 1) * rows] = x[:rows]
            rest[h, (4 + i) * rows:(5 + i) * rows] = x[rows:]
    sends = [pltpu.make_async_copy(coarse, coarse_out.at[pl.ds(i * H, H)], sem.at[4 + i]) for i in range(2)]
    for copy in sends:
        copy.start()
    for i, copy in enumerate(copies[2:]):
        copy.wait()
        for h in range(H):
            rest[h, 2 * i * rows:2 * (i + 1) * rows] = pick(h, pairs[2 + i][1])
    sends.append(pltpu.make_async_copy(rest, rest_out, sem.at[6]))
    sends[-1].start()
    for copy in sends:
        copy.wait()


def main_kernel(r0, rows, members, *refs):
    r1 = 2 * r0
    G = members
    docs_ref, own_ref = refs[0], refs[1]
    coarse_refs = refs[2:G + 2]
    fine_refs = (own_ref.at[:, 4 * rows:6 * rows],) + tuple(refs[G + 2:2 * G + 1])
    out_own, out_kv = refs[2 * G + 1], refs[2 * G + 2]
    out_swap = refs[2 * G + 3:3 * G + 2]
    (k1, k2, kx, v1, v2, vx, d1, d2, dx, gk1, gk2, gv1, gv2, gkx, gvx) = refs[3 * G + 2:]
    bf16, f32 = jnp.bfloat16, jnp.float32
    tokens = HD
    half = lax.axis_index("half")
    head = lax.axis_index("head")
    member = lax.axis_index("member")

    sel = selector(head, r0, rows, tokens, False)

    def doc_row(side, j, g):
        return docs_ref[pl.ds((side * H + j) * G + (member ^ g), 1)].astype(f32).astype(bf16)

    for j in range(H):
        for g in range(G):
            at = pl.ds((j * G + g) * rows, rows)
            k1[at] = coarse_refs[g][half * H + j, 0:rows]
            v1[at] = coarse_refs[g][half * H + j, rows:2 * rows]
            kx[at] = coarse_refs[g][(1 - half) * H + j, 0:rows]
            vx[at] = coarse_refs[g][(1 - half) * H + j, rows:2 * rows]
            k2[at] = fine_refs[g][j, 0:rows]
            v2[at] = fine_refs[g][j, rows:2 * rows]
            doc = doc_row(half, j, g)
            d1[at] = sel[:rows] * doc
            d2[at] = sel[rows:] * doc
            dx[at] = sel[:rows] * doc_row(0, j, g)

    eye = (lax.broadcasted_iota(jnp.int32, (HD, HD), 0) == lax.broadcasted_iota(jnp.int32, (HD, HD), 1))
    eye = eye.astype(f32).astype(bf16)
    ones = jnp.ones((HD, HD), bf16)
    transposed = lambda x: dot_nt(eye, x).astype(bf16)
    doc_cols = lambda x: dot_nn(x, ones)[:, 0:1]
    k1t, k2t, kxt = transposed(k1[...]), transposed(k2[...]), transposed(kx[...])
    v1t, v2t, vxt = transposed(v1[...]), transposed(v2[...]), transposed(vx[...])
    docs1, docs2 = doc_cols(d1[...]), doc_cols(d2[...])
    docsx = doc_cols(dx[...]) + jnp.where(half == 0, 1000.0, 0.0)

    tiles = 2
    per = H // tiles
    nq = per * rows
    nd = per * G * rows
    lanes = 2 * nq
    xn = nq if nq % 128 == 0 else lanes

    coarse = head % r1
    other = (coarse + r0) % r1
    lane = lax.broadcasted_iota(jnp.int32, (1, lanes), 1)
    fine = lane >= nq
    ql = jnp.where(fine, lane - nq, lane)
    qpos = (ql // rows) * (G * tokens) + member * tokens + r1 * (ql % rows) + jnp.where(fine, other, coarse)
    kl = lax.broadcasted_iota(jnp.int32, (nd, 1), 0)
    kmember = member ^ ((kl // rows) % G)
    kpos = (kl // (rows * G)) * (G * tokens) + kmember * tokens + r1 * (kl % rows)
    causal1 = kpos + coarse <= qpos
    causal2 = kpos + other <= qpos
    both = jnp.where(fine, 0.0, 1.0)

    for u in reversed(range(tiles)):
        nk = (u + 1) * nd
        x0 = u * nd
        src = range(u * per, (u + 1) * per)
        qt = jnp.concatenate([own_ref[j, 0:rows] for j in src] + [own_ref[j, rows:2 * rows] for j in src], 0)
        gt = jnp.concatenate([own_ref[j, 2 * rows:3 * rows] for j in src] + [own_ref[j, 3 * rows:4 * rows] for j in src], 0)
        at = pl.ds(u * nd, nd)
        dq = jnp.concatenate(
            [sel[:rows] * doc_row(half, j, 0) for j in src]
            + [sel[rows:] * doc_row(half, j, 0) for j in src], 0)
        qdoc = dot_nt(jnp.ones((16, HD), bf16), dq)[0:1]

        def scores(key, docs, causal):
            s = dot_nt(key, qt)
            allow = docs == qdoc
            s = jnp.where(allow, s, MASKED)
            if u:
                return jnp.concatenate([s[:x0], jnp.where(causal, s[x0:], MASKED)], 0)
            return jnp.where(causal, s, MASKED)

        s1 = scores(k1[0:nk], docs1[0:nk], causal1)
        s2 = scores(k2[0:nk], docs2[0:nk], causal2)
        sx = dot_nt(kx[x0:], qt[:xn])
        allowx = docsx[x0:] == qdoc[:, :xn]
        if xn != nq:
            allowx = allowx & (lane[:, :xn] < nq)
        sx = jnp.where(allowx, sx, MASKED)
        top = jnp.maximum(jnp.max(s1, 0, keepdims=True), jnp.max(s2, 0, keepdims=True))
        topx = jnp.maximum(top[:, :xn], jnp.max(sx, 0, keepdims=True))
        top = topx if xn == lanes else jnp.concatenate([topx, top[:, xn:]], 1)
        c = SCALE * LOG2E
        base = top * c
        p1 = jnp.exp2(s1 * c - (base - both))
        p2 = jnp.exp2(s2 * c - base)
        px = jnp.exp2(sx * c - base[:, :xn])
        total = jnp.sum(p1, 0, keepdims=True) + jnp.sum(p2, 0, keepdims=True)
        totalx = total[:, :xn] + jnp.sum(px, 0, keepdims=True)
        total = totalx if xn == lanes else jnp.concatenate([totalx, total[:, xn:]], 1)
        inv = 1.0 / total
        out = dot_nn(v1t[:, :nk], p1.astype(bf16)) + dot_nn(v2t[:, :nk], p2.astype(bf16))
        outx = out[:, :xn] + dot_nn(vxt[:, x0:], px.astype(bf16))
        out = outx if xn == lanes else jnp.concatenate([outx, out[:, xn:]], 1)
        out = out * inv
        gtt = dot_nt(eye, gt)
        dot = jnp.sum(gtt * out, 0, keepdims=True)
        dinv = dot * inv

        def grads(p, value, gt, inv, dinv):
            ds = p * (dot_nt(value, gt) * inv - dinv)
            return ds.astype(bf16), (p * inv).astype(bf16)

        ds1, w1 = grads(p1, v1[0:nk], gt, inv, dinv)
        ds2, w2 = grads(p2, v2[0:nk], gt, inv, dinv)
        dsx, wx = grads(px, vx[x0:], gt[:xn], inv[:, :xn], dinv[:, :xn])
        gq = dot_nn(k1t[:, :nk], ds1) + dot_nn(k2t[:, :nk], ds2)
        gqx = gq[:, :xn] + dot_nn(kxt[:, x0:], dsx)
        gq = gqx if xn == lanes else jnp.concatenate([gqx, gq[:, xn:]], 1)
        gq = gq * SCALE

        def add(ref, lo, hi, value):
            if u == tiles - 1:
                ref[lo:hi] = value
                if ref is gkx or ref is gvx:
                    ref[0:lo] = jnp.zeros((lo, HD), f32)
            else:
                ref[lo:hi] = ref[lo:hi] + value

        add(gk1, 0, nk, dot_nn(ds1, qt))
        add(gk2, 0, nk, dot_nn(ds2, qt))
        add(gv1, 0, nk, dot_nn(w1, gt))
        add(gv2, 0, nk, dot_nn(w2, gt))
        add(gkx, x0, tiles * nd, dot_nn(dsx, qt[:xn]))
        add(gvx, x0, tiles * nd, dot_nn(wx, gt[:xn]))
        out = out.T.astype(bf16)
        gq = gq.T.astype(bf16)
        for i, j in enumerate(src):
            lo = i * rows
            out_own[j, 0:rows] = out[lo:lo + rows]
            out_own[j, rows:2 * rows] = out[nq + lo:nq + lo + rows]
            out_own[j, 2 * rows:3 * rows] = gq[lo:lo + rows]
            out_own[j, 3 * rows:4 * rows] = gq[nq + lo:nq + lo + rows]

    for j in range(H):
        for g in range(G):
            at = pl.ds((j * G + g) * rows, rows)
            ref = out_kv if g == 0 else out_swap[g - 1]
            parts = (gk1[at] * SCALE, gv1[at], gkx[at] * SCALE, gvx[at], gk2[at] * SCALE, gv2[at])
            for i, part in enumerate(parts):
                ref[j, i * rows:(i + 1) * rows] = part.astype(ref.dtype)


def sum_kernel(rows, members, *refs):
    G = members
    own_ref, kv_ref = refs[0], refs[1]
    swap_refs = refs[2:G + 1]
    coarse_ref, rest_ref = refs[G + 1], refs[G + 2]
    half = lax.axis_index("half")
    bf16 = jnp.bfloat16
    rest_ref[:, 0:4 * rows] = own_ref[...]
    for j in range(H):
        total = kv_ref[j]
        for ref in swap_refs:
            total = total + ref[j].astype(jnp.float32)
        total = total.astype(bf16)
        coarse_ref[half * H + j] = total[0:2 * rows]
        coarse_ref[(1 - half) * H + j] = total[2 * rows:4 * rows]
        rest_ref[j, 4 * rows:6 * rows] = total[4 * rows:6 * rows]


def unpack_kernel(r0, rows, coarse_ref, rest_ref, *refs):
    outs, bufs, sem = refs[:4], refs[4:8], refs[8]
    tokens = bufs[0].shape[0]
    f32, bf16 = jnp.float32, jnp.bfloat16
    sels = [selector(h, r0, rows, tokens, True) for h in range(min(H, 2 * r0))]
    copies = []
    for i in range(4):
        for h in range(H):
            if i < 2:
                part = rest_ref[h, 2 * i * rows:2 * (i + 1) * rows]
            else:
                lo = (i - 2) * rows
                both = [coarse_ref[side * H + h, lo:lo + rows].astype(f32) for side in range(2)]
                fine = rest_ref[h, 4 * rows + lo:5 * rows + lo]
                part = jnp.concatenate([(both[0] + both[1]).astype(bf16), fine], 0)
            bufs[i][:, h * HD:(h + 1) * HD] = dot_nn(sels[h % (2 * r0)], part).astype(bf16)
        copies.append(pltpu.make_async_copy(bufs[i], outs[i], sem.at[i]))
        copies[-1].start()
    for copy in copies:
        copy.wait()


def call(kernel, out_shape, scratch=(), limit=16, **more):
    return pl.pallas_call(
        kernel,
        out_shape=out_shape,
        scratch_shapes=list(scratch),
        compiler_params=pltpu.CompilerParams(vmem_limit_bytes=limit * 1024 * 1024),
        **more,
    )


def per_device(members, queries, keys, values, cotangent, doc_ids):
    G = members
    tokens = queries.shape[0]
    devices = 2 * H * G
    r0 = tokens * devices // (2 * SEG)
    rows = tokens // (2 * r0)
    bf16, f32 = jnp.bfloat16, jnp.float32
    shape = jax.ShapeDtypeStruct
    n = H * G * rows
    anywhere = pl.BlockSpec(memory_space=pltpu.HBM)
    wide = pltpu.VMEM((tokens, H * HD), bf16)
    coarse_shape, rest_shape = (2 * H, 2 * rows, HD), (H, 6 * rows, HD)

    docs = lax.all_gather(doc_ids, ("half", "head", "member"))
    coarse, rest = call(
        functools.partial(pack_kernel, r0, rows),
        [shape(coarse_shape, bf16), shape(rest_shape, bf16)],
        [wide] * 4 + [pltpu.VMEM((H, 2 * rows, HD), bf16), pltpu.VMEM(rest_shape, bf16), pltpu.SemaphoreType.DMA((7,))],
        limit=64, in_specs=[anywhere] * 4, out_specs=[anywhere] * 2,
    )(queries, keys, values, cotangent)

    def to_head(x):
        return lax.all_to_all(x, "head", 0, 0, tiled=True)

    def to_half_head(x):
        return lax.all_to_all(x, ("half", "head"), 0, 0, tiled=True)

    def to_member(x, g):
        return lax.ppermute(x, "member", [(i, i ^ g) for i in range(G)])

    coarse = to_half_head(coarse)
    rest = to_head(rest)
    coarses = [coarse] + [to_member(coarse, g) for g in range(1, G)]
    fines = [to_member(rest[:, 4 * rows:], g) for g in range(1, G)]
    outs = call(
        functools.partial(main_kernel, r0, rows, G),
        [shape((H, 4 * rows, HD), bf16), shape(rest_shape, f32)] + [shape(rest_shape, bf16)] * (G - 1),
        [pltpu.VMEM((n, HD), bf16)] * 9 + [pltpu.VMEM((n, HD), f32)] * 6,
        limit=32,
    )(docs, rest, *coarses, *fines)
    swaps = [to_member(outs[1 + g], g) for g in range(1, G)]
    coarse, rest = call(
        functools.partial(sum_kernel, rows, G), [shape(coarse_shape, bf16), shape(rest_shape, bf16)],
    )(outs[0], outs[1], *swaps)
    coarse = to_half_head(coarse)
    rest = to_head(rest)
    return tuple(call(
        functools.partial(unpack_kernel, r0, rows), [shape((tokens, H * HD), bf16)] * 4,
        [wide] * 4 + [pltpu.SemaphoreType.DMA((4,))],
        in_specs=[VMEM] * 2, out_specs=[anywhere] * 4,
    )(coarse, rest))


def solution(mesh):
    members = mesh.shape["seq"] // (2 * H)
    parts = {"seq": [("half", 2), ("head", H), ("member", members)]}
    axes = [part for name in mesh.axis_names for part in parts.get(name, [(name, mesh.shape[name])])]
    inner = Mesh(mesh.devices.reshape([size for _, size in axes]), [name for name, _ in axes])
    split = ("dp", "half", "head", "member")
    in_specs = (P(split, None),) * 4 + (P(split),)
    return jax.shard_map(
        functools.partial(per_device, members), mesh=inner, in_specs=in_specs,
        out_specs=(P(split, None),) * 4, check_vma=False,
    )
```

```python
import functools

import jax
import jax.numpy as jnp
import numpy as np
from jax import lax
from jax.experimental import pallas as pl
from jax.experimental.pallas import tpu as pltpu
from jax.sharding import Mesh
from jax.sharding import PartitionSpec as P

H = 8
HD = 128
SEG = 1024

MASKED = -1e30
SCALE = HD ** -0.5
LOG2E = float(np.log2(np.e))
VMEM = pl.BlockSpec(memory_space=pltpu.VMEM)
DOC_ROWS = 16


def dot_nn(a, b):
    return lax.dot_general(a, b, (((1,), (0,)), ((), ())), preferred_element_type=jnp.float32)


def dot_nt(a, b):
    return lax.dot_general(a, b, (((1,), (1,)), ((), ())), preferred_element_type=jnp.float32)


def selector(head, r0, rows, tokens, transposed, fine_first=False):
    r1 = 2 * r0
    shape = (tokens, 2 * rows) if transposed else (2 * rows, tokens)
    k = lax.broadcasted_iota(jnp.int32, shape, 1 if transposed else 0)
    p = lax.broadcasted_iota(jnp.int32, shape, 0 if transposed else 1)
    coarse = head % r1
    other = (coarse + r0) % r1
    first, second = jnp.where(fine_first, other, coarse), jnp.where(fine_first, coarse, other)
    target = jnp.where(k < rows, r1 * k + first, r1 * (k - rows) + second)
    return (p == target).astype(jnp.float32).astype(jnp.bfloat16)


def takes_fine(members):
    return lax.axis_index("member") >= members // 2


def pack_kernel(r0, rows, members, q_in, k_in, v_in, g_in, doc_in, out, q_ref, k_ref, v_ref, g_ref, doc_ref, buf, sem):
    tokens = q_ref.shape[0]
    pairs = ((doc_in, doc_ref), (k_in, k_ref), (v_in, v_ref), (q_in, q_ref), (g_in, g_ref))
    copies = [pltpu.make_async_copy(src, dst, sem.at[i]) for i, (src, dst) in enumerate(pairs)]
    for copy in copies:
        copy.start()
    kinds = range(min(H, 2 * r0))
    key_sels = [selector(h, r0, rows, tokens, False) for h in kinds]
    query_sels = [selector(h, r0, rows, tokens, False, takes_fine(members)) for h in kinds]

    def pick(sels, h, ref):
        return dot_nn(sels[h % (2 * r0)], ref[:, h * HD:(h + 1) * HD]).astype(jnp.bfloat16)

    copies[0].wait()
    docs = jnp.broadcast_to(doc_ref[...].astype(jnp.float32).astype(jnp.bfloat16), (DOC_ROWS, tokens))
    for i, ref in enumerate((k_ref, v_ref)):
        copies[1 + i].wait()
        for h in range(H):
            x = pick(key_sels, h, ref)
            buf[h, (4 + i) * rows:(5 + i) * rows] = x[rows:]
            buf[h, (6 + i) * rows:(7 + i) * rows] = x[:rows]
    for i, ref in enumerate((q_ref, g_ref)):
        copies[3 + i].wait()
        for h in range(H):
            x = pick(query_sels, h, ref)
            buf[h, i * rows:(1 + i) * rows] = x[:rows]
            buf[h, (2 + i) * rows:(3 + i) * rows] = x[rows:]
    sends = []
    for h in range(H):
        buf[h, 8 * rows:8 * rows + DOC_ROWS] = docs
    sends.append(pltpu.make_async_copy(buf, out, sem.at[5]))
    for copy in sends:
        copy.start()
    for copy in sends:
        copy.wait()


def main_kernel(r0, rows, members, *refs):
    r1 = 2 * r0
    G = members
    own_ref, swap_refs, cross_refs = refs[0], refs[1:G], refs[G:2 * G]
    out_own, out_kv, out_swap, out_cross = refs[2 * G], refs[2 * G + 1], refs[2 * G + 2:3 * G + 1], refs[3 * G + 1:4 * G + 1]
    (k1, k2, kx, v1, v2, vx, d1, d2, dx, gk1, gk2, gv1, gv2, gkx, gvx) = refs[4 * G + 1:]
    bf16, f32 = jnp.bfloat16, jnp.float32
    tokens = HD
    half = lax.axis_index("half")
    head = lax.axis_index("head")
    member = lax.axis_index("member")
    fine = takes_fine(G)
    partner = G // 2
    partner_ref = swap_refs[partner - 1]

    sel = selector(head, r0, rows, tokens, False)
    query_sel = jnp.where(fine, sel[rows:].astype(f32), sel[:rows].astype(f32)).astype(bf16)
    source_docs = []
    for j in range(H):
        for g in range(G):
            at = pl.ds((j * G + g) * rows, rows)
            ref, base = (own_ref, 4 * rows) if g == 0 else (swap_refs[g - 1], 2 * rows if g == partner else 0)
            k2[at] = ref[j, base:base + rows]
            v2[at] = ref[j, base + rows:base + 2 * rows]
            k1[at] = ref[j, base + 2 * rows:base + 3 * rows]
            v1[at] = ref[j, base + 3 * rows:base + 4 * rows]
            doc = ref[j, base + 4 * rows:base + 4 * rows + DOC_ROWS][0:1]
            if g in (0, partner):
                source_docs.append(doc)
            d1[at] = sel[:rows] * doc
            d2[at] = sel[rows:] * doc
            ref = cross_refs[g]
            kx[at] = ref[2 * j * rows:(2 * j + 1) * rows]
            vx[at] = ref[(2 * j + 1) * rows:(2 * j + 2) * rows]
            dx[at] = sel[:rows] * ref[2 * H * rows:2 * H * rows + DOC_ROWS][j:j + 1]

    eye = (lax.broadcasted_iota(jnp.int32, (HD, HD), 0) == lax.broadcasted_iota(jnp.int32, (HD, HD), 1))
    eye = eye.astype(f32).astype(bf16)
    ones = jnp.ones((HD, HD), bf16)
    transposed = lambda x: dot_nt(eye, x).astype(bf16)
    doc_cols = lambda x: dot_nn(x, ones)[:, 0:1]
    k1t, k2t, kxt = transposed(k1[...]), transposed(k2[...]), transposed(kx[...])
    v1t, v2t, vxt = transposed(v1[...]), transposed(v2[...]), transposed(vx[...])
    docs1, docs2 = doc_cols(d1[...]), doc_cols(d2[...])
    docsx = doc_cols(dx[...]) + jnp.where((half == 0) | fine, 1000.0, 0.0)

    tiles = 2
    per = H // tiles
    nd = per * G * rows
    lanes = per * 2 * rows

    coarse = head % r1
    other = (coarse + r0) % r1
    lane = lax.broadcasted_iota(jnp.int32, (1, lanes), 1)
    qmember = member ^ (partner * ((lane // rows) % 2))
    qpos = (lane // (2 * rows)) * (G * tokens) + qmember * tokens + r1 * (lane % rows) + jnp.where(fine, other, coarse)
    kl = lax.broadcasted_iota(jnp.int32, (nd, 1), 0)
    kmember = member ^ ((kl // rows) % G)
    kpos = (kl // (rows * G)) * (G * tokens) + kmember * tokens + r1 * (kl % rows)
    causal1 = kpos + coarse <= qpos
    causal2 = kpos + other <= qpos
    both = jnp.where(fine, 0.0, 1.0)
    c = SCALE * LOG2E

    for u in reversed(range(tiles)):
        nk = (u + 1) * nd
        x0 = u * nd
        src = range(u * per, (u + 1) * per)
        gather = lambda lo: jnp.concatenate([ref[j, lo:lo + rows] for j in src for ref in (own_ref, partner_ref)], 0)
        qt, gt = gather(0), gather(rows)
        dq = jnp.concatenate([query_sel * source_docs[2 * j + e] for j in src for e in range(2)], 0)
        qdoc = dot_nt(jnp.ones((16, HD), bf16), dq)[0:1]

        def scores(key, docs, causal):
            s = jnp.where(docs == qdoc, dot_nt(key, qt), MASKED)
            if u:
                return jnp.concatenate([s[:x0], jnp.where(causal, s[x0:], MASKED)], 0)
            return jnp.where(causal, s, MASKED)

        s1 = scores(k1[0:nk], docs1[0:nk], causal1)
        s2 = scores(k2[0:nk], docs2[0:nk], causal2)
        sx = jnp.where(docsx[x0:] == qdoc, dot_nt(kx[x0:], qt), MASKED)
        top = jnp.maximum(jnp.maximum(jnp.max(s1, 0, keepdims=True), jnp.max(s2, 0, keepdims=True)), jnp.max(sx, 0, keepdims=True))
        base = top * c
        p1 = jnp.exp2(s1 * c - (base - both))
        p2 = jnp.exp2(s2 * c - base)
        px = jnp.exp2(sx * c - base)
        total = jnp.sum(p1, 0, keepdims=True) + jnp.sum(p2, 0, keepdims=True) + jnp.sum(px, 0, keepdims=True)
        inv = 1.0 / total
        out = dot_nn(v1t[:, :nk], p1.astype(bf16)) + dot_nn(v2t[:, :nk], p2.astype(bf16)) + dot_nn(vxt[:, x0:], px.astype(bf16))
        out = out * inv
        dinv = jnp.sum(dot_nt(eye, gt) * out, 0, keepdims=True) * inv

        def grads(p, value):
            ds = p * (dot_nt(value, gt) * inv - dinv)
            return ds.astype(bf16), (p * inv).astype(bf16)

        ds1, w1 = grads(p1, v1[0:nk])
        ds2, w2 = grads(p2, v2[0:nk])
        dsx, wx = grads(px, vx[x0:])
        gq = (dot_nn(k1t[:, :nk], ds1) + dot_nn(k2t[:, :nk], ds2) + dot_nn(kxt[:, x0:], dsx)) * SCALE

        def add(ref, lo, hi, value):
            if u == tiles - 1:
                ref[lo:hi] = value
                if lo:
                    ref[0:lo] = jnp.zeros((lo, HD), f32)
            else:
                ref[lo:hi] = ref[lo:hi] + value

        add(gk1, 0, nk, dot_nn(ds1, qt))
        add(gk2, 0, nk, dot_nn(ds2, qt))
        add(gv1, 0, nk, dot_nn(w1, gt))
        add(gv2, 0, nk, dot_nn(w2, gt))
        add(gkx, x0, tiles * nd, dot_nn(dsx, qt))
        add(gvx, x0, tiles * nd, dot_nn(wx, gt))
        out = out.T.astype(bf16)
        gq = gq.T.astype(bf16)
        for i, j in enumerate(src):
            for e, ref in enumerate((out_own, out_swap[partner - 1])):
                lo = (2 * i + e) * rows
                ref[j, 0:rows] = out[lo:lo + rows]
                ref[j, rows:2 * rows] = gq[lo:lo + rows]

    for j in range(H):
        for g in range(G):
            at = pl.ds((j * G + g) * rows, rows)
            ref = out_kv if g == 0 else out_swap[g - 1]
            base = 2 * rows if g == partner else 0
            for i, part in enumerate((gk2[at] * SCALE, gv2[at], gk1[at] * SCALE, gv1[at])):
                ref[j, base + i * rows:base + (i + 1) * rows] = part.astype(ref.dtype)
            out_cross[g][j, 0:rows] = (gkx[at] * SCALE).astype(bf16)
            out_cross[g][j, rows:2 * rows] = gvx[at].astype(bf16)


def sum_kernel(rows, members, *refs):
    G = members
    own_ref, kv_ref, swap_refs, cross_refs, out_ref = refs[0], refs[1], refs[2:G + 1], refs[G + 1:2 * G + 1], refs[2 * G + 1]
    f32, bf16 = jnp.float32, jnp.bfloat16
    out_ref[:, 0:2 * rows] = own_ref[...]
    out_ref[:, 2 * rows:4 * rows] = swap_refs[G // 2 - 1][:, 0:2 * rows]
    for j in range(H):
        total = kv_ref[j]
        for g, ref in enumerate(swap_refs, 1):
            base = 2 * rows if g == G // 2 else 0
            total = total + ref[j, base:base + 4 * rows].astype(f32)
        coarse = total[2 * rows:]
        for ref in cross_refs:
            coarse = coarse + ref[j].astype(f32)
        out_ref[j, 4 * rows:6 * rows] = total[:2 * rows].astype(bf16)
        out_ref[j, 6 * rows:8 * rows] = coarse.astype(bf16)


def unpack_kernel(r0, rows, members, in_ref, *refs):
    outs, bufs, sem = refs[:4], refs[4:8], refs[8]
    tokens = bufs[0].shape[0]
    bf16 = jnp.bfloat16
    kinds = range(min(H, 2 * r0))
    query_sels = [selector(h, r0, rows, tokens, True, takes_fine(members)) for h in kinds]
    key_sels = [selector(h, r0, rows, tokens, True, True) for h in kinds]
    copies = []
    for i, base in enumerate((0, 1, 4, 5)):
        for h in range(H):
            sels = query_sels if i < 2 else key_sels
            part = jnp.concatenate([in_ref[h, (base + e) * rows:(base + e + 1) * rows] for e in (0, 2)], 0)
            bufs[i][:, h * HD:(h + 1) * HD] = dot_nn(sels[h % (2 * r0)], part).astype(bf16)
        copies.append(pltpu.make_async_copy(bufs[i], outs[i], sem.at[i]))
        copies[-1].start()
    for copy in copies:
        copy.wait()


def call(kernel, out_shape, scratch=(), limit=16, **more):
    return pl.pallas_call(
        kernel,
        out_shape=out_shape,
        scratch_shapes=list(scratch),
        compiler_params=pltpu.CompilerParams(vmem_limit_bytes=limit * 1024 * 1024),
        **more,
    )


def per_device(members, queries, keys, values, cotangent, doc_ids):
    G = members
    tokens = queries.shape[0]
    devices = 2 * H * G
    r0 = tokens * devices // (2 * SEG)
    rows = tokens // (2 * r0)
    bf16, f32 = jnp.bfloat16, jnp.float32
    shape = jax.ShapeDtypeStruct
    n = H * G * rows
    anywhere = pl.BlockSpec(memory_space=pltpu.HBM)
    wide = pltpu.VMEM((tokens, H * HD), bf16)
    message = (H, 8 * rows + DOC_ROWS, HD)

    packed = call(
        functools.partial(pack_kernel, r0, rows, G), shape(message, bf16),
        [wide] * 4 + [pltpu.VMEM((1, tokens), jnp.int32), pltpu.VMEM(message, bf16), pltpu.SemaphoreType.DMA((6,))],
        limit=64, in_specs=[anywhere] * 5, out_specs=anywhere,
    )(queries, keys, values, cotangent, doc_ids.reshape(1, tokens))

    def to_head(x):
        return lax.all_to_all(x, "head", 0, 0, tiled=True)

    def to_member(x, g):
        return lax.ppermute(x, "member", [(i, i ^ g) for i in range(G)])

    def place(half, head, member):
        return (half * H + head) * G + member

    def across(x, g, back):
        pairs = [(place(0, h, m ^ g), place(1, h, m)) for h in range(H) for m in range(G // 2)]
        return lax.ppermute(x, ("half", "head", "member"), [pair[::-1] for pair in pairs] if back else pairs)

    own = to_head(packed)
    docs = jnp.pad(own[:, 8 * rows], ((0, DOC_ROWS - H), (0, 0)))
    cross = jnp.concatenate([own[:, 6 * rows:8 * rows].reshape(-1, HD), docs], 0)
    crosses = [across(cross, g, False) for g in range(G)]
    swaps = [to_member(own[:, (2 if g == G // 2 else 4) * rows:], g) for g in range(1, G)]
    sent = lambda g: (H, (6 if g == G // 2 else 4) * rows, HD)
    outs = call(
        functools.partial(main_kernel, r0, rows, G),
        [shape((H, 2 * rows, HD), bf16), shape((H, 4 * rows, HD), f32)]
        + [shape(sent(g), bf16) for g in range(1, G)] + [shape((H, 2 * rows, HD), bf16)] * G,
        [pltpu.VMEM((n, HD), bf16)] * 9 + [pltpu.VMEM((n, HD), f32)] * 6,
        limit=32,
    )(own, *swaps, *crosses)
    crosses = [across(outs[G + 1 + g], g, True) for g in range(G)]
    swaps = [to_member(outs[1 + g], g) for g in range(1, G)]
    back = call(functools.partial(sum_kernel, rows, G), shape((H, 8 * rows, HD), bf16))(
        outs[0], outs[1], *swaps, *crosses)
    back = to_head(back)
    return tuple(call(
        functools.partial(unpack_kernel, r0, rows, G), [shape((tokens, H * HD), bf16)] * 4,
        [wide] * 4 + [pltpu.SemaphoreType.DMA((4,))],
        in_specs=[VMEM], out_specs=[anywhere] * 4,
    )(back))


def solution(mesh):
    members = mesh.shape["seq"] // (2 * H)
    parts = {"seq": [("half", 2), ("head", H), ("member", members)]}
    axes = [part for name in mesh.axis_names for part in parts.get(name, [(name, mesh.shape[name])])]
    inner = Mesh(mesh.devices.reshape([size for _, size in axes]), [name for name, _ in axes])
    split = ("dp", "half", "head", "member")
    in_specs = (P(split, None),) * 4 + (P(split),)
    return jax.shard_map(
        functools.partial(per_device, members), mesh=inner, in_specs=in_specs,
        out_specs=(P(split, None),) * 4, check_vma=False,
    )
```

```python
import functools

import jax
import jax.numpy as jnp
import numpy as np
from jax import lax
from jax.experimental import pallas as pl
from jax.experimental.pallas import tpu as pltpu
from jax.sharding import Mesh
from jax.sharding import PartitionSpec as P

H = 8
HD = 128
SEG = 1024

MASKED = -1e30
SCALE = HD ** -0.5
LOG2E = float(np.log2(np.e))
VMEM = pl.BlockSpec(memory_space=pltpu.VMEM)
DOC_ROWS = 16


def dot_nn(a, b):
    return lax.dot_general(a, b, (((1,), (0,)), ((), ())), preferred_element_type=jnp.float32)


def dot_nt(a, b):
    return lax.dot_general(a, b, (((1,), (1,)), ((), ())), preferred_element_type=jnp.float32)


def selector(head, r0, rows, tokens, transposed, fine_first=False):
    r1 = 2 * r0
    shape = (tokens, 2 * rows) if transposed else (2 * rows, tokens)
    k = lax.broadcasted_iota(jnp.int32, shape, 1 if transposed else 0)
    p = lax.broadcasted_iota(jnp.int32, shape, 0 if transposed else 1)
    coarse = head % r1
    other = (coarse + r0) % r1
    first, second = jnp.where(fine_first, other, coarse), jnp.where(fine_first, coarse, other)
    target = jnp.where(k < rows, r1 * k + first, r1 * (k - rows) + second)
    return (p == target).astype(jnp.float32).astype(jnp.bfloat16)


def takes_fine(members):
    return lax.axis_index("member") >= members // 2


def pack_kernel(r0, rows, members, q_in, k_in, v_in, g_in, doc_in, out, q_ref, k_ref, v_ref, g_ref, doc_ref, buf, sem):
    tokens = q_ref.shape[0]
    pairs = ((doc_in, doc_ref), (k_in, k_ref), (v_in, v_ref), (q_in, q_ref), (g_in, g_ref))
    copies = [pltpu.make_async_copy(src, dst, sem.at[i]) for i, (src, dst) in enumerate(pairs)]
    for copy in copies:
        copy.start()
    kinds = range(min(H, 2 * r0))
    key_sels = [selector(h, r0, rows, tokens, False) for h in kinds]
    query_sels = [selector(h, r0, rows, tokens, False, takes_fine(members)) for h in kinds]

    def pick(sels, h, ref):
        return dot_nn(sels[h % (2 * r0)], ref[:, h * HD:(h + 1) * HD]).astype(jnp.bfloat16)

    copies[0].wait()
    docs = jnp.broadcast_to(doc_ref[...].astype(jnp.float32).astype(jnp.bfloat16), (DOC_ROWS, tokens))
    for i, ref in enumerate((k_ref, v_ref)):
        copies[1 + i].wait()
        for h in range(H):
            x = pick(key_sels, h, ref)
            buf[h, (4 + i) * rows:(5 + i) * rows] = x[rows:]
            buf[h, (6 + i) * rows:(7 + i) * rows] = x[:rows]
    for i, ref in enumerate((q_ref, g_ref)):
        copies[3 + i].wait()
        for h in range(H):
            x = pick(query_sels, h, ref)
            buf[h, i * rows:(1 + i) * rows] = x[:rows]
            buf[h, (2 + i) * rows:(3 + i) * rows] = x[rows:]
    sends = []
    for h in range(H):
        buf[h, 8 * rows:8 * rows + DOC_ROWS] = docs
    sends.append(pltpu.make_async_copy(buf, out, sem.at[5]))
    for copy in sends:
        copy.start()
    for copy in sends:
        copy.wait()


def main_kernel(r0, rows, members, *refs):
    r1 = 2 * r0
    G = members
    own_ref, swap_refs, cross_refs = refs[0], refs[1:G], refs[G:2 * G]
    out_own, out_kv, out_swap, out_cross = refs[2 * G], refs[2 * G + 1], refs[2 * G + 2:3 * G + 1], refs[3 * G + 1:4 * G + 1]
    (k1, k2, kx, v1, v2, vx, d1, d2, dx, gk1, gk2, gv1, gv2, gkx, gvx) = refs[4 * G + 1:]
    bf16, f32 = jnp.bfloat16, jnp.float32
    tokens = HD
    half = lax.axis_index("half")
    head = lax.axis_index("head")
    member = lax.axis_index("member")
    fine = takes_fine(G)
    partner = G // 2
    partner_ref = swap_refs[partner - 1]

    sel = selector(head, r0, rows, tokens, False)
    query_sel = jnp.where(fine, sel[rows:].astype(f32), sel[:rows].astype(f32)).astype(bf16)
    source_docs = []
    for j in range(H):
        for g in range(G):
            at = pl.ds((j * G + g) * rows, rows)
            ref, base = (own_ref, 4 * rows) if g == 0 else (swap_refs[g - 1], 2 * rows if g == partner else 0)
            k2[at] = ref[j, base:base + rows]
            v2[at] = ref[j, base + rows:base + 2 * rows]
            k1[at] = ref[j, base + 2 * rows:base + 3 * rows]
            v1[at] = ref[j, base + 3 * rows:base + 4 * rows]
            doc = ref[j, base + 4 * rows:base + 4 * rows + DOC_ROWS][0:1]
            if g in (0, partner):
                source_docs.append(doc)
            d1[at] = sel[:rows] * doc
            d2[at] = sel[rows:] * doc
            ref = cross_refs[g]
            kx[at] = ref[2 * j * rows:(2 * j + 1) * rows]
            vx[at] = ref[(2 * j + 1) * rows:(2 * j + 2) * rows]
            dx[at] = sel[:rows] * ref[2 * H * rows:2 * H * rows + DOC_ROWS][j:j + 1]

    eye = (lax.broadcasted_iota(jnp.int32, (HD, HD), 0) == lax.broadcasted_iota(jnp.int32, (HD, HD), 1))
    eye = eye.astype(f32).astype(bf16)
    ones = jnp.ones((HD, HD), bf16)
    transposed = lambda x: dot_nt(eye, x).astype(bf16)
    doc_cols = lambda x: dot_nn(x, ones)[:, 0:1]
    k1t, k2t, kxt = transposed(k1[...]), transposed(k2[...]), transposed(kx[...])
    v1t, v2t, vxt = transposed(v1[...]), transposed(v2[...]), transposed(vx[...])
    docs1, docs2 = doc_cols(d1[...]), doc_cols(d2[...])
    docsx = doc_cols(dx[...]) + jnp.where((half == 0) | fine, 1000.0, 0.0)

    tiles = 2
    per = H // tiles
    nd = per * G * rows
    lanes = per * 2 * rows

    coarse = head % r1
    other = (coarse + r0) % r1
    lane = lax.broadcasted_iota(jnp.int32, (1, lanes), 1)
    qmember = member ^ (partner * ((lane // rows) % 2))
    qpos = (lane // (2 * rows)) * (G * tokens) + qmember * tokens + r1 * (lane % rows) + jnp.where(fine, other, coarse)
    kl = lax.broadcasted_iota(jnp.int32, (nd, 1), 0)
    kmember = member ^ ((kl // rows) % G)
    kpos = (kl // (rows * G)) * (G * tokens) + kmember * tokens + r1 * (kl % rows)
    causal1 = kpos + coarse <= qpos
    causal2 = kpos + other <= qpos
    both = jnp.where(fine, 0.0, 1.0)
    c = SCALE * LOG2E

    for u in reversed(range(tiles)):
        nk = (u + 1) * nd
        x0 = u * nd
        src = range(u * per, (u + 1) * per)
        gather = lambda lo: jnp.concatenate([ref[j, lo:lo + rows] for j in src for ref in (own_ref, partner_ref)], 0)
        qt, gt = gather(0), gather(rows)
        dq = jnp.concatenate([query_sel * source_docs[2 * j + e] for j in src for e in range(2)], 0)
        qdoc = dot_nt(jnp.ones((16, HD), bf16), dq)[0:1]

        def scores(key, docs, causal):
            s = jnp.where(docs == qdoc, dot_nt(key, qt), MASKED)
            if u:
                return jnp.concatenate([s[:x0], jnp.where(causal, s[x0:], MASKED)], 0)
            return jnp.where(causal, s, MASKED)

        s1 = scores(k1[0:nk], docs1[0:nk], causal1)
        s2 = scores(k2[0:nk], docs2[0:nk], causal2)
        sx = jnp.where(docsx[x0:] == qdoc, dot_nt(kx[x0:], qt), MASKED)
        top = jnp.maximum(jnp.maximum(jnp.max(s1, 0, keepdims=True), jnp.max(s2, 0, keepdims=True)), jnp.max(sx, 0, keepdims=True))
        base = top * c
        p1 = jnp.exp2(s1 * c - (base - both))
        p2 = jnp.exp2(s2 * c - base)
        px = jnp.exp2(sx * c - base)
        total = jnp.sum(p1, 0, keepdims=True) + jnp.sum(p2, 0, keepdims=True) + jnp.sum(px, 0, keepdims=True)
        inv = 1.0 / total
        out = dot_nn(v1t[:, :nk], p1.astype(bf16)) + dot_nn(v2t[:, :nk], p2.astype(bf16)) + dot_nn(vxt[:, x0:], px.astype(bf16))
        out = out * inv
        dinv = jnp.sum(dot_nt(eye, gt) * out, 0, keepdims=True) * inv

        def grads(p, value):
            ds = p * (dot_nt(value, gt) * inv - dinv)
            return ds.astype(bf16), (p * inv).astype(bf16)

        ds1, w1 = grads(p1, v1[0:nk])
        ds2, w2 = grads(p2, v2[0:nk])
        dsx, wx = grads(px, vx[x0:])
        gq = (dot_nn(k1t[:, :nk], ds1) + dot_nn(k2t[:, :nk], ds2) + dot_nn(kxt[:, x0:], dsx)) * SCALE

        def add(ref, lo, hi, value):
            if u == tiles - 1:
                ref[lo:hi] = value
                if lo:
                    ref[0:lo] = jnp.zeros((lo, HD), f32)
            else:
                ref[lo:hi] = ref[lo:hi] + value

        add(gk1, 0, nk, dot_nn(ds1, qt))
        add(gk2, 0, nk, dot_nn(ds2, qt))
        add(gv1, 0, nk, dot_nn(w1, gt))
        add(gv2, 0, nk, dot_nn(w2, gt))
        add(gkx, x0, tiles * nd, dot_nn(dsx, qt))
        add(gvx, x0, tiles * nd, dot_nn(wx, gt))
        out = out.T.astype(bf16)
        gq = gq.T.astype(bf16)
        for i, j in enumerate(src):
            for e, ref in enumerate((out_own, out_swap[partner - 1])):
                lo = (2 * i + e) * rows
                ref[j, 0:rows] = out[lo:lo + rows]
                ref[j, rows:2 * rows] = gq[lo:lo + rows]

    for j in range(H):
        for g in range(G):
            at = pl.ds((j * G + g) * rows, rows)
            ref = out_kv if g == 0 else out_swap[g - 1]
            base = 2 * rows if g == partner else 0
            for i, part in enumerate((gk2[at] * SCALE, gv2[at], gk1[at] * SCALE, gv1[at])):
                ref[j, base + i * rows:base + (i + 1) * rows] = part.astype(ref.dtype)
            out_cross[g][j, 0:rows] = (gkx[at] * SCALE).astype(bf16)
            out_cross[g][j, rows:2 * rows] = gvx[at].astype(bf16)


def sum_kernel(rows, members, *refs):
    G = members
    own_ref, kv_ref, swap_refs, cross_refs, out_ref = refs[0], refs[1], refs[2:G + 1], refs[G + 1:2 * G + 1], refs[2 * G + 1]
    f32, bf16 = jnp.float32, jnp.bfloat16
    out_ref[:, 0:2 * rows] = own_ref[...]
    out_ref[:, 2 * rows:4 * rows] = swap_refs[G // 2 - 1][:, 0:2 * rows]
    for j in range(H):
        total = kv_ref[j]
        for g, ref in enumerate(swap_refs, 1):
            base = 2 * rows if g == G // 2 else 0
            total = total + ref[j, base:base + 4 * rows].astype(f32)
        coarse = total[2 * rows:]
        for ref in cross_refs:
            coarse = coarse + ref[j].astype(f32)
        out_ref[j, 4 * rows:6 * rows] = total[:2 * rows].astype(bf16)
        out_ref[j, 6 * rows:8 * rows] = coarse.astype(bf16)


def unpack_kernel(r0, rows, members, in_ref, *refs):
    outs, bufs, sem = refs[:4], refs[4:8], refs[8]
    tokens = bufs[0].shape[0]
    bf16 = jnp.bfloat16
    kinds = range(min(H, 2 * r0))
    query_sels = [selector(h, r0, rows, tokens, True, takes_fine(members)) for h in kinds]
    key_sels = [selector(h, r0, rows, tokens, True, True) for h in kinds]
    copies = []
    for i, base in enumerate((0, 1, 4, 5)):
        for h in range(H):
            sels = query_sels if i < 2 else key_sels
            part = jnp.concatenate([in_ref[h, (base + e) * rows:(base + e + 1) * rows] for e in (0, 2)], 0)
            bufs[i][:, h * HD:(h + 1) * HD] = dot_nn(sels[h % (2 * r0)], part).astype(bf16)
        copies.append(pltpu.make_async_copy(bufs[i], outs[i], sem.at[i]))
        copies[-1].start()
    for copy in copies:
        copy.wait()


def call(kernel, out_shape, scratch=(), limit=16, **more):
    return pl.pallas_call(
        kernel,
        out_shape=out_shape,
        scratch_shapes=list(scratch),
        compiler_params=pltpu.CompilerParams(vmem_limit_bytes=limit * 1024 * 1024),
        **more,
    )


def per_device(members, queries, keys, values, cotangent, doc_ids):
    G = members
    tokens = queries.shape[0]
    devices = 2 * H * G
    r0 = tokens * devices // (2 * SEG)
    rows = tokens // (2 * r0)
    bf16, f32 = jnp.bfloat16, jnp.float32
    shape = jax.ShapeDtypeStruct
    n = H * G * rows
    anywhere = pl.BlockSpec(memory_space=pltpu.HBM)
    wide = pltpu.VMEM((tokens, H * HD), bf16)
    message = (H, 8 * rows + DOC_ROWS, HD)

    packed = call(
        functools.partial(pack_kernel, r0, rows, G), shape(message, bf16),
        [wide] * 4 + [pltpu.VMEM((1, tokens), jnp.int32), pltpu.VMEM(message, bf16), pltpu.SemaphoreType.DMA((6,))],
        limit=64, in_specs=[anywhere] * 5, out_specs=anywhere,
    )(queries, keys, values, cotangent, doc_ids.reshape(1, tokens))

    def to_head(x):
        return lax.all_to_all(x, "head", 0, 0, tiled=True)

    def to_member(x, g):
        return lax.ppermute(x, "member", [(i, i ^ g) for i in range(G)])

    def place(half, head, member):
        return (half * H + head) * G + member

    def across(x, g):
        pairs = {place(0, h, m ^ g): place(1, h, m) for h in range(H) for m in range(G // 2)}
        pairs.update({b: a for a, b in pairs.items()})
        return lax.ppermute(x, ("half", "head", "member"), [(i, pairs.get(i, i)) for i in range(devices)])

    own = to_head(packed)
    docs = jnp.pad(own[:, 8 * rows], ((0, DOC_ROWS - H), (0, 0)))
    cross = jnp.concatenate([own[:, 6 * rows:8 * rows].reshape(-1, HD), docs], 0)
    crosses = [across(cross, g) for g in range(G)]
    swaps = [to_member(own[:, (2 if g == G // 2 else 4) * rows:], g) for g in range(1, G)]
    sent = lambda g: (H, (6 if g == G // 2 else 4) * rows, HD)
    outs = call(
        functools.partial(main_kernel, r0, rows, G),
        [shape((H, 2 * rows, HD), bf16), shape((H, 4 * rows, HD), f32)]
        + [shape(sent(g), bf16) for g in range(1, G)] + [shape((H, 2 * rows, HD), bf16)] * G,
        [pltpu.VMEM((n, HD), bf16)] * 9 + [pltpu.VMEM((n, HD), f32)] * 6,
        limit=32,
    )(own, *swaps, *crosses)
    crosses = [across(outs[G + 1 + g], g) for g in range(G)]
    swaps = [to_member(outs[1 + g], g) for g in range(1, G)]
    back = call(functools.partial(sum_kernel, rows, G), shape((H, 8 * rows, HD), bf16))(
        outs[0], outs[1], *swaps, *crosses)
    back = to_head(back)
    return tuple(call(
        functools.partial(unpack_kernel, r0, rows, G), [shape((tokens, H * HD), bf16)] * 4,
        [wide] * 4 + [pltpu.SemaphoreType.DMA((4,))],
        in_specs=[VMEM], out_specs=[anywhere] * 4,
    )(back))


def solution(mesh):
    members = mesh.shape["seq"] // (2 * H)
    parts = {"seq": [("half", 2), ("head", H), ("member", members)]}
    axes = [part for name in mesh.axis_names for part in parts.get(name, [(name, mesh.shape[name])])]
    inner = Mesh(mesh.devices.reshape([size for _, size in axes]), [name for name, _ in axes])
    split = ("dp", "half", "head", "member")
    in_specs = (P(split, None),) * 4 + (P(split),)
    return jax.shard_map(
        functools.partial(per_device, members), mesh=inner, in_specs=in_specs,
        out_specs=(P(split, None),) * 4, check_vma=False,
    )
```

```python
import functools

import jax
import jax.numpy as jnp
import numpy as np
from jax import lax
from jax.experimental import pallas as pl
from jax.experimental.pallas import tpu as pltpu
from jax.sharding import Mesh
from jax.sharding import PartitionSpec as P

H = 8
HD = 128
SEG = 1024

MASKED = -1e30
SCALE = HD ** -0.5
LOG2E = float(np.log2(np.e))
VMEM = pl.BlockSpec(memory_space=pltpu.VMEM)
DOC_ROWS = 16


def dot_nn(a, b):
    return lax.dot_general(a, b, (((1,), (0,)), ((), ())), preferred_element_type=jnp.float32)


def dot_nt(a, b):
    return lax.dot_general(a, b, (((1,), (1,)), ((), ())), preferred_element_type=jnp.float32)


def selector(head, r0, rows, tokens, transposed, fine_first=False):
    r1 = 2 * r0
    shape = (tokens, 2 * rows) if transposed else (2 * rows, tokens)
    k = lax.broadcasted_iota(jnp.int32, shape, 1 if transposed else 0)
    p = lax.broadcasted_iota(jnp.int32, shape, 0 if transposed else 1)
    coarse = head % r1
    other = (coarse + r0) % r1
    first, second = jnp.where(fine_first, other, coarse), jnp.where(fine_first, coarse, other)
    target = jnp.where(k < rows, r1 * k + first, r1 * (k - rows) + second)
    return (p == target).astype(jnp.float32).astype(jnp.bfloat16)


def takes_fine(members):
    return lax.axis_index("member") >= members // 2


def pack_kernel(r0, rows, members, q_in, k_in, v_in, g_in, doc_in, out, q_ref, k_ref, v_ref, g_ref, doc_ref, buf, sem):
    tokens = q_ref.shape[0]
    pairs = ((doc_in, doc_ref), (k_in, k_ref), (v_in, v_ref), (q_in, q_ref), (g_in, g_ref))
    copies = [pltpu.make_async_copy(src, dst, sem.at[i]) for i, (src, dst) in enumerate(pairs)]
    for copy in copies:
        copy.start()
    kinds = range(min(H, 2 * r0))
    key_sels = [selector(h, r0, rows, tokens, False) for h in kinds]
    query_sels = [selector(h, r0, rows, tokens, False, takes_fine(members)) for h in kinds]

    def pick(sels, h, ref):
        return dot_nn(sels[h % (2 * r0)], ref[:, h * HD:(h + 1) * HD]).astype(jnp.bfloat16)

    copies[0].wait()
    docs = jnp.broadcast_to(doc_ref[...].astype(jnp.float32).astype(jnp.bfloat16), (DOC_ROWS, tokens))
    for i, ref in enumerate((k_ref, v_ref)):
        copies[1 + i].wait()
        for h in range(H):
            x = pick(key_sels, h, ref)
            buf[h, (4 + i) * rows:(5 + i) * rows] = x[rows:]
            buf[h, (6 + i) * rows:(7 + i) * rows] = x[:rows]
    for i, ref in enumerate((q_ref, g_ref)):
        copies[3 + i].wait()
        for h in range(H):
            x = pick(query_sels, h, ref)
            buf[h, i * rows:(1 + i) * rows] = x[:rows]
            buf[h, (2 + i) * rows:(3 + i) * rows] = x[rows:]
    sends = []
    for h in range(H):
        buf[h, 8 * rows:8 * rows + DOC_ROWS] = docs
    sends.append(pltpu.make_async_copy(buf, out, sem.at[5]))
    for copy in sends:
        copy.start()
    for copy in sends:
        copy.wait()


TILES = 2


def tile_sizes(rows, members):
    per = H // TILES
    return per * members * rows, per * 2 * rows


def eye_matrix():
    shape = (HD, HD)
    same = lax.broadcasted_iota(jnp.int32, shape, 0) == lax.broadcasted_iota(jnp.int32, shape, 1)
    return same.astype(jnp.float32).astype(jnp.bfloat16)


def doc_cols(x):
    return dot_nn(x, jnp.ones((HD, HD), jnp.bfloat16))[:, 0:1]


def local_kernel(r0, rows, members, *refs):
    G = members
    r1 = 2 * r0
    own_ref, swap_refs = refs[0], refs[1:G]
    (k1, k2, q_all, g_all, stats, out_ref, gtt_ref), rest = refs[G:G + 7], refs[G + 7:]
    p_refs, dp_refs, (v1, v2, d1, d2) = rest[:2 * TILES], rest[2 * TILES:4 * TILES], rest[4 * TILES:]
    bf16, f32 = jnp.bfloat16, jnp.float32
    tokens = HD
    head = lax.axis_index("head")
    member = lax.axis_index("member")
    fine = takes_fine(G)
    partner = G // 2
    partner_ref = swap_refs[partner - 1]

    sel = selector(head, r0, rows, tokens, False)
    query_sel = jnp.where(fine, sel[rows:].astype(f32), sel[:rows].astype(f32)).astype(bf16)
    source_docs = []
    for j in range(H):
        for g in range(G):
            at = pl.ds((j * G + g) * rows, rows)
            ref, base = (own_ref, 4 * rows) if g == 0 else (swap_refs[g - 1], 2 * rows if g == partner else 0)
            k2[at] = ref[j, base:base + rows]
            v2[at] = ref[j, base + rows:base + 2 * rows]
            k1[at] = ref[j, base + 2 * rows:base + 3 * rows]
            v1[at] = ref[j, base + 3 * rows:base + 4 * rows]
            doc = ref[j, base + 4 * rows:base + 4 * rows + DOC_ROWS][0:1]
            if g in (0, partner):
                source_docs.append(doc)
            d1[at] = sel[:rows] * doc
            d2[at] = sel[rows:] * doc

    eye = eye_matrix()
    v1t, v2t = dot_nt(eye, v1[...]).astype(bf16), dot_nt(eye, v2[...]).astype(bf16)
    docs1, docs2 = doc_cols(d1[...]), doc_cols(d2[...])
    nd, lanes = tile_sizes(rows, G)
    per = H // TILES

    coarse = head % r1
    other = (coarse + r0) % r1
    lane = lax.broadcasted_iota(jnp.int32, (1, lanes), 1)
    qmember = member ^ (partner * ((lane // rows) % 2))
    qpos = (lane // (2 * rows)) * (G * tokens) + qmember * tokens + r1 * (lane % rows) + jnp.where(fine, other, coarse)
    kl = lax.broadcasted_iota(jnp.int32, (nd, 1), 0)
    kmember = member ^ ((kl // rows) % G)
    kpos = (kl // (rows * G)) * (G * tokens) + kmember * tokens + r1 * (kl % rows)
    causal1 = kpos + coarse <= qpos
    causal2 = kpos + other <= qpos
    both = jnp.where(fine, 0.0, 1.0)
    c = SCALE * LOG2E

    for u in range(TILES):
        nk = (u + 1) * nd
        x0 = u * nd
        src = range(u * per, (u + 1) * per)
        mine = slice(u * lanes, (u + 1) * lanes)
        gather = lambda lo: jnp.concatenate([ref[j, lo:lo + rows] for j in src for ref in (own_ref, partner_ref)], 0)
        qt, gt = gather(0), gather(rows)
        q_all[mine], g_all[mine] = qt, gt
        dq = jnp.concatenate([query_sel * source_docs[2 * j + e] for j in src for e in range(2)], 0)
        qdoc = dot_nt(jnp.ones((16, HD), bf16), dq)[0:1]

        def scores(key, docs, causal):
            s = jnp.where(docs == qdoc, dot_nt(key, qt), MASKED)
            if u:
                return jnp.concatenate([s[:x0], jnp.where(causal, s[x0:], MASKED)], 0)
            return jnp.where(causal, s, MASKED)

        s1 = scores(k1[0:nk], docs1[0:nk], causal1)
        s2 = scores(k2[0:nk], docs2[0:nk], causal2)
        top = jnp.maximum(jnp.max(s1, 0, keepdims=True), jnp.max(s2, 0, keepdims=True))
        base = top * c
        p1 = jnp.exp2(s1 * c - (base - both))
        p2 = jnp.exp2(s2 * c - base)
        stats[0:1, mine] = top
        stats[1:2, mine] = jnp.sum(p1, 0, keepdims=True) + jnp.sum(p2, 0, keepdims=True)
        stats[2:3, mine] = qdoc
        out_ref[:, mine] = dot_nn(v1t[:, :nk], p1.astype(bf16)) + dot_nn(v2t[:, :nk], p2.astype(bf16))
        gtt_ref[:, mine] = dot_nt(eye, gt)
        p_refs[2 * u][...], p_refs[2 * u + 1][...] = p1, p2
        dp_refs[2 * u][...], dp_refs[2 * u + 1][...] = dot_nt(v1[0:nk], gt), dot_nt(v2[0:nk], gt)


def cross_kernel(r0, rows, members, *refs):
    G = members
    cross_refs = refs[0:G]
    q_all, g_all, stats, local_out, gtt_ref = refs[G:G + 5]
    out_cross, (out_ref, gq_ref, new_stats) = refs[G + 5:2 * G + 5], refs[2 * G + 5:2 * G + 8]
    kx, vx, dx, gkx, gvx = refs[2 * G + 8:]
    bf16, f32 = jnp.bfloat16, jnp.float32
    half = lax.axis_index("half")
    head = lax.axis_index("head")
    sel = selector(head, r0, rows, HD, False)
    for j in range(H):
        for g in range(G):
            at = pl.ds((j * G + g) * rows, rows)
            ref = cross_refs[g]
            kx[at] = ref[2 * j * rows:(2 * j + 1) * rows]
            vx[at] = ref[(2 * j + 1) * rows:(2 * j + 2) * rows]
            dx[at] = sel[:rows] * ref[2 * H * rows:2 * H * rows + DOC_ROWS][j:j + 1]
    eye = eye_matrix()
    kxt, vxt = dot_nt(eye, kx[...]).astype(bf16), dot_nt(eye, vx[...]).astype(bf16)
    docsx = doc_cols(dx[...]) + jnp.where((half == 0) | takes_fine(G), 1000.0, 0.0)
    nd, lanes = tile_sizes(rows, G)
    c = SCALE * LOG2E
    for u in range(TILES):
        x0 = u * nd
        mine = slice(u * lanes, (u + 1) * lanes)
        qt, gt = q_all[mine], g_all[mine]
        top0, total0, qdoc = stats[0:1, mine], stats[1:2, mine], stats[2:3, mine]
        sx = jnp.where(docsx[x0:] == qdoc, dot_nt(kx[x0:], qt), MASKED)
        top = jnp.maximum(top0, jnp.max(sx, 0, keepdims=True))
        px = jnp.exp2(sx * c - top * c)
        shrink = jnp.exp2(top0 * c - top * c)
        inv = 1.0 / (total0 * shrink + jnp.sum(px, 0, keepdims=True))
        local_inv = shrink * inv
        out = local_out[:, mine] * local_inv + dot_nn(vxt[:, x0:], px.astype(bf16)) * inv
        dot = jnp.sum(gtt_ref[:, mine] * out, 0, keepdims=True)
        wx = px * inv
        ds = (wx * (dot_nt(vx[x0:], gt) - dot)).astype(bf16)
        wx = wx.astype(bf16)
        new_stats[0:1, mine] = local_inv
        new_stats[1:2, mine] = dot
        out_ref[mine] = out.T.astype(bf16)
        gq_ref[:, mine] = dot_nn(kxt[:, x0:], ds)
        gk, gv = dot_nn(ds, qt), dot_nn(wx, gt)
        if u == 0:
            gkx[...], gvx[...] = gk, gv
        else:
            gkx[x0:] += gk
            gvx[x0:] += gv
    for j in range(H):
        for g in range(G):
            at = pl.ds((j * G + g) * rows, rows)
            out_cross[g][j, 0:rows] = (gkx[at] * SCALE).astype(bf16)
            out_cross[g][j, rows:2 * rows] = gvx[at].astype(bf16)


def grad_kernel(rows, members, *refs):
    G = members
    k1, k2, q_all, g_all, out_ref, gq_ref, stats = refs[:7]
    p_refs, dp_refs = refs[7:7 + 2 * TILES], refs[7 + 2 * TILES:7 + 4 * TILES]
    rest = refs[7 + 4 * TILES:]
    partner = G // 2
    out_own, out_kv, (gk1, gk2, gv1, gv2) = rest[0], rest[1], rest[-4:]
    out_swap = rest[2:-4]
    bf16, f32 = jnp.bfloat16, jnp.float32
    eye = eye_matrix()
    nd, lanes = tile_sizes(rows, G)
    per = H // TILES
    k1t, k2t = dot_nt(eye, k1[...]).astype(bf16), dot_nt(eye, k2[...]).astype(bf16)
    for u in reversed(range(TILES)):
        nk = (u + 1) * nd
        mine = slice(u * lanes, (u + 1) * lanes)
        qt, gt = q_all[mine], g_all[mine]
        inv, dot = stats[0:1, mine], stats[1:2, mine]
        gq = gq_ref[:, mine]
        for i, (kt, gk, gv) in enumerate(((k1t, gk1, gv1), (k2t, gk2, gv2))):
            w = p_refs[2 * u + i][...] * inv
            ds = (w * (dp_refs[2 * u + i][...] - dot)).astype(bf16)
            gq = gq + dot_nn(kt[:, :nk], ds)
            new_k, new_v = dot_nn(ds, qt), dot_nn(w.astype(bf16), gt)
            if u == TILES - 1:
                gk[...], gv[...] = new_k, new_v
            else:
                gk[0:nk] += new_k
                gv[0:nk] += new_v
        gq = (gq * SCALE).T.astype(bf16)
        for i in range(per):
            j = u * per + i
            for e, ref in enumerate((out_own, out_swap[partner - 1])):
                lo = (2 * i + e) * rows
                ref[j, 0:rows] = out_ref[u * lanes + lo:u * lanes + lo + rows]
                ref[j, rows:2 * rows] = gq[lo:lo + rows]
    for j in range(H):
        for g in range(G):
            at = pl.ds((j * G + g) * rows, rows)
            ref = out_kv if g == 0 else out_swap[g - 1]
            base = 2 if g == partner else 0
            for i, part in enumerate((gk2[at] * SCALE, gv2[at], gk1[at] * SCALE, gv1[at]), base):
                ref[j, i * rows:(i + 1) * rows] = part.astype(ref.dtype)


def add_kernel(*refs):
    total = refs[0][...].astype(jnp.float32)
    for ref in refs[1:-1]:
        total = total + ref[...].astype(jnp.float32)
    refs[-1][...] = total


def sum_kernel(rows, members, own_ref, kv_ref, coarse_ref, *refs):
    swap_refs, out_ref = refs[:-1], refs[-1]
    partner = members // 2
    out_ref[:, 0:2 * rows] = own_ref[...]
    out_ref[:, 2 * rows:4 * rows] = swap_refs[partner - 1][:, 0:2 * rows]
    for i in range(2):
        total = kv_ref[:, 2 * i * rows:2 * (i + 1) * rows]
        for g, ref in enumerate(swap_refs, 1):
            base = 2 * (i + (g == partner))
            total = total + ref[:, base * rows:(base + 2) * rows].astype(jnp.float32)
        if i == 1:
            total = total + coarse_ref[...]
        out_ref[:, (4 + 2 * i) * rows:(6 + 2 * i) * rows] = total.astype(jnp.bfloat16)


def unpack_kernel(r0, rows, members, in_ref, *refs):
    outs, bufs, sem = refs[:4], refs[4:8], refs[8]
    tokens = bufs[0].shape[0]
    bf16 = jnp.bfloat16
    kinds = range(min(H, 2 * r0))
    query_sels = [selector(h, r0, rows, tokens, True, takes_fine(members)) for h in kinds]
    key_sels = [selector(h, r0, rows, tokens, True, True) for h in kinds]
    copies = []
    for i, base in enumerate((0, 1, 4, 5)):
        for h in range(H):
            sels = query_sels if i < 2 else key_sels
            part = jnp.concatenate([in_ref[h, (base + e) * rows:(base + e + 1) * rows] for e in (0, 2)], 0)
            bufs[i][:, h * HD:(h + 1) * HD] = dot_nn(sels[h % (2 * r0)], part).astype(bf16)
        copies.append(pltpu.make_async_copy(bufs[i], outs[i], sem.at[i]))
        copies[-1].start()
    for copy in copies:
        copy.wait()


def call(kernel, out_shape, scratch=(), limit=16, **more):
    return pl.pallas_call(
        kernel,
        out_shape=out_shape,
        scratch_shapes=list(scratch),
        compiler_params=pltpu.CompilerParams(vmem_limit_bytes=limit * 1024 * 1024),
        **more,
    )


def per_device(members, queries, keys, values, cotangent, doc_ids):
    G = members
    tokens = queries.shape[0]
    devices = 2 * H * G
    r0 = tokens * devices // (2 * SEG)
    rows = tokens // (2 * r0)
    bf16, f32 = jnp.bfloat16, jnp.float32
    shape = jax.ShapeDtypeStruct
    n = H * G * rows
    anywhere = pl.BlockSpec(memory_space=pltpu.HBM)
    wide = pltpu.VMEM((tokens, H * HD), bf16)
    message = (H, 8 * rows + DOC_ROWS, HD)

    packed = call(
        functools.partial(pack_kernel, r0, rows, G), shape(message, bf16),
        [wide] * 4 + [pltpu.VMEM((1, tokens), jnp.int32), pltpu.VMEM(message, bf16), pltpu.SemaphoreType.DMA((6,))],
        limit=64, in_specs=[anywhere] * 5, out_specs=anywhere,
    )(queries, keys, values, cotangent, doc_ids.reshape(1, tokens))

    def to_head(x):
        return lax.all_to_all(x, "head", 0, 0, tiled=True)

    def to_member(x, g):
        return lax.ppermute(x, "member", [(i, i ^ g) for i in range(G)])

    def place(half, head, member):
        return (half * H + head) * G + member

    def across(x):
        return lax.ppermute(x, "half", [(0, 1), (1, 0)])

    def back_across(x, g):
        pairs = [(place(1, h, m), place(0, h, m ^ g)) for h in range(H) for m in range(G // 2)]
        return lax.ppermute(x, ("half", "head", "member"), pairs)

    nd, lanes = tile_sizes(rows, G)
    nq = TILES * lanes
    tile = [shape(((u + 1) * nd, lanes), f32) for u in range(TILES) for _ in range(2)]
    pairs = 2 * nd * lanes * TILES * (TILES + 1) // 2
    work = pl.CostEstimate(flops=6 * pairs * HD, bytes_accessed=16 * pairs, transcendentals=pairs)
    keys_scratch, wide_row = pltpu.VMEM((n, HD), bf16), shape((8, nq), f32)

    own = to_head(packed)
    docs = jnp.pad(own[:, 8 * rows], ((0, DOC_ROWS - H), (0, 0)))
    cross = across(jnp.concatenate([own[:, 6 * rows:8 * rows].reshape(-1, HD), docs], 0))
    swaps = [to_member(own[:, (2 if g == G // 2 else 4) * rows:], g) for g in range(1, G)]
    local = call(
        functools.partial(local_kernel, r0, rows, G),
        [shape((n, HD), bf16)] * 2 + [shape((nq, HD), bf16)] * 2 + [wide_row]
        + [shape((HD, nq), f32)] * 2 + tile * 2,
        [keys_scratch] * 4, limit=32, cost_estimate=work,
    )(own, *swaps)
    k1, k2, q_all, g_all, stats, out, gtt = local[:7]
    cross, stats = lax.optimization_barrier((cross, stats))
    crosses = [cross] + [to_member(cross, g) for g in range(1, G)]
    outs = call(
        functools.partial(cross_kernel, r0, rows, G),
        [shape((H, 2 * rows, HD), bf16)] * G + [shape((nq, HD), bf16), shape((HD, nq), f32), wide_row],
        [keys_scratch] * 3 + [pltpu.VMEM((n, HD), f32)] * 2, limit=32,
    )(*crosses, q_all, g_all, stats, out, gtt)
    crosses = [back_across(outs[g], g) for g in range(G)]
    sent = lambda g: (H, (6 if g == G // 2 else 4) * rows, HD)
    outs = call(
        functools.partial(grad_kernel, rows, G),
        [shape((H, 2 * rows, HD), bf16), shape((H, 4 * rows, HD), f32)] + [shape(sent(g), bf16) for g in range(1, G)],
        [pltpu.VMEM((n, HD), f32)] * 4, limit=32, cost_estimate=work,
    )(k1, k2, q_all, g_all, *outs[G:], *local[7:])
    swaps = [to_member(outs[1 + g], g) for g in range(1, G)]
    coarse = call(add_kernel, shape((H, 2 * rows, HD), f32))(*crosses)
    coarse, *swaps = lax.optimization_barrier((coarse, *swaps))
    back = call(functools.partial(sum_kernel, rows, G), shape((H, 8 * rows, HD), bf16))(
        outs[0], outs[1], coarse, *swaps)
    back = to_head(back)
    return tuple(call(
        functools.partial(unpack_kernel, r0, rows, G), [shape((tokens, H * HD), bf16)] * 4,
        [wide] * 4 + [pltpu.SemaphoreType.DMA((4,))],
        in_specs=[VMEM], out_specs=[anywhere] * 4,
    )(back))


def solution(mesh):
    members = mesh.shape["seq"] // (2 * H)
    parts = {"seq": [("half", 2), ("head", H), ("member", members)]}
    axes = [part for name in mesh.axis_names for part in parts.get(name, [(name, mesh.shape[name])])]
    inner = Mesh(mesh.devices.reshape([size for _, size in axes]), [name for name, _ in axes])
    split = ("dp", "half", "head", "member")
    in_specs = (P(split, None),) * 4 + (P(split),)
    return jax.shard_map(
        functools.partial(per_device, members), mesh=inner, in_specs=in_specs,
        out_specs=(P(split, None),) * 4, check_vma=False,
    )
```

```python
import functools

import jax
import jax.numpy as jnp
import numpy as np
from jax import lax
from jax.experimental import pallas as pl
from jax.experimental.pallas import tpu as pltpu
from jax.sharding import Mesh
from jax.sharding import PartitionSpec as P

H = 8
HD = 128
SEG = 1024

MASKED = -1e30
SCALE = HD ** -0.5
LOG2E = float(np.log2(np.e))
VMEM = pl.BlockSpec(memory_space=pltpu.VMEM)
DOC_ROWS = 16
PLANE = 4


def dot_nn(a, b):
    return lax.dot_general(a, b, (((1,), (0,)), ((), ())), preferred_element_type=jnp.float32)


def dot_nt(a, b):
    return lax.dot_general(a, b, (((1,), (1,)), ((), ())), preferred_element_type=jnp.float32)


def selector(head, r0, rows, tokens, transposed, fine_first=False):
    r1 = 2 * r0
    shape = (tokens, 2 * rows) if transposed else (2 * rows, tokens)
    k = lax.broadcasted_iota(jnp.int32, shape, 1 if transposed else 0)
    p = lax.broadcasted_iota(jnp.int32, shape, 0 if transposed else 1)
    coarse = head % r1
    other = (coarse + r0) % r1
    first, second = jnp.where(fine_first, other, coarse), jnp.where(fine_first, coarse, other)
    target = jnp.where(k < rows, r1 * k + first, r1 * (k - rows) + second)
    return (p == target).astype(jnp.float32).astype(jnp.bfloat16)


def takes_fine(members):
    return lax.axis_index("member") >= members // 2


def pack_kernel(r0, rows, members, q_in, k_in, v_in, g_in, doc_in, out, far_out, q_ref, k_ref, v_ref, g_ref, doc_ref, buf, far, sem):
    tokens = q_ref.shape[0]
    chip = lax.axis_index("head")
    pairs = ((doc_in, doc_ref), (k_in, k_ref), (v_in, v_ref), (q_in, q_ref), (g_in, g_ref))
    copies = [pltpu.make_async_copy(src, dst, sem.at[i]) for i, (src, dst) in enumerate(pairs)]
    for copy in copies:
        copy.start()
    kinds = range(min(H, 2 * r0))
    key_sels = [selector(h, r0, rows, tokens, False) for h in kinds]
    query_sels = [selector(h, r0, rows, tokens, False, takes_fine(members)) for h in kinds]

    def pick(sels, h, ref):
        return dot_nn(sels[h % (2 * r0)], ref[:, h * HD:(h + 1) * HD]).astype(jnp.bfloat16)

    copies[0].wait()
    docs = jnp.broadcast_to(doc_ref[...].astype(jnp.float32).astype(jnp.bfloat16), (DOC_ROWS, tokens))
    for i, ref in enumerate((k_ref, v_ref)):
        copies[1 + i].wait()
        for h in range(H):
            x = pick(key_sels, h, ref)
            buf[h, (4 + i) * rows:(5 + i) * rows] = x[rows:]
            buf[h, (6 + i) * rows:(7 + i) * rows] = x[:rows]
            hop = chip ^ h
            base = pl.multiple_of((hop // PLANE == 0) * (2 * rows + DOC_ROWS) + i * rows, 16)
            far[hop % PLANE, pl.ds(base, rows)] = x[:rows]
    for k in range(PLANE):
        far[k, 2 * rows:2 * rows + DOC_ROWS] = docs
    sends = [pltpu.make_async_copy(far, far_out, sem.at[6])]
    sends[0].start()
    for i, ref in enumerate((q_ref, g_ref)):
        copies[3 + i].wait()
        for h in range(H):
            x = pick(query_sels, h, ref)
            buf[h, i * rows:(1 + i) * rows] = x[:rows]
            buf[h, (2 + i) * rows:(3 + i) * rows] = x[rows:]
    for h in range(H):
        buf[h, 8 * rows:8 * rows + DOC_ROWS] = docs
    sends.append(pltpu.make_async_copy(buf, out, sem.at[5]))
    sends[1].start()
    for copy in sends:
        copy.wait()


TILES = 2


def tile_sizes(rows, members):
    per = H // TILES
    return per * members * rows, per * 2 * rows


def eye_matrix():
    shape = (HD, HD)
    same = lax.broadcasted_iota(jnp.int32, shape, 0) == lax.broadcasted_iota(jnp.int32, shape, 1)
    return same.astype(jnp.float32).astype(jnp.bfloat16)


def doc_cols(x):
    return dot_nn(x, jnp.ones((HD, HD), jnp.bfloat16))[:, 0:1]


def local_kernel(r0, rows, members, *refs):
    G = members
    r1 = 2 * r0
    own_ref, swap_refs = refs[0], refs[1:G]
    (k1, k2, q_all, g_all, stats, out_ref, gtt_ref), rest = refs[G:G + 7], refs[G + 7:]
    p_refs, dp_refs, (v1, v2, d1, d2) = rest[:2 * TILES], rest[2 * TILES:4 * TILES], rest[4 * TILES:]
    bf16, f32 = jnp.bfloat16, jnp.float32
    tokens = HD
    head = lax.axis_index("head")
    member = lax.axis_index("member")
    fine = takes_fine(G)
    partner = G // 2
    partner_ref = swap_refs[partner - 1]

    sel = selector(head, r0, rows, tokens, False)
    query_sel = jnp.where(fine, sel[rows:].astype(f32), sel[:rows].astype(f32)).astype(bf16)
    source_docs = []
    for j in range(H):
        for g in range(G):
            at = pl.ds((j * G + g) * rows, rows)
            ref, base = (own_ref, 4 * rows) if g == 0 else (swap_refs[g - 1], 2 * rows if g == partner else 0)
            k2[at] = ref[j, base:base + rows]
            v2[at] = ref[j, base + rows:base + 2 * rows]
            k1[at] = ref[j, base + 2 * rows:base + 3 * rows]
            v1[at] = ref[j, base + 3 * rows:base + 4 * rows]
            doc = ref[j, base + 4 * rows:base + 4 * rows + DOC_ROWS][0:1]
            if g in (0, partner):
                source_docs.append(doc)
            d1[at] = sel[:rows] * doc
            d2[at] = sel[rows:] * doc

    eye = eye_matrix()
    v1t, v2t = dot_nt(eye, v1[...]).astype(bf16), dot_nt(eye, v2[...]).astype(bf16)
    docs1, docs2 = doc_cols(d1[...]), doc_cols(d2[...])
    nd, lanes = tile_sizes(rows, G)
    per = H // TILES

    coarse = head % r1
    other = (coarse + r0) % r1
    lane = lax.broadcasted_iota(jnp.int32, (1, lanes), 1)
    qmember = member ^ (partner * ((lane // rows) % 2))
    qpos = (lane // (2 * rows)) * (G * tokens) + qmember * tokens + r1 * (lane % rows) + jnp.where(fine, other, coarse)
    kl = lax.broadcasted_iota(jnp.int32, (nd, 1), 0)
    kmember = member ^ ((kl // rows) % G)
    kpos = (kl // (rows * G)) * (G * tokens) + kmember * tokens + r1 * (kl % rows)
    causal1 = kpos + coarse <= qpos
    causal2 = kpos + other <= qpos
    both = jnp.where(fine, 0.0, 1.0)
    c = SCALE * LOG2E

    for u in range(TILES):
        nk = (u + 1) * nd
        x0 = u * nd
        src = range(u * per, (u + 1) * per)
        mine = slice(u * lanes, (u + 1) * lanes)
        gather = lambda lo: jnp.concatenate([ref[j, lo:lo + rows] for j in src for ref in (own_ref, partner_ref)], 0)
        qt, gt = gather(0), gather(rows)
        q_all[mine], g_all[mine] = qt, gt
        dq = jnp.concatenate([query_sel * source_docs[2 * j + e] for j in src for e in range(2)], 0)
        qdoc = dot_nt(jnp.ones((16, HD), bf16), dq)[0:1]

        def scores(key, docs, causal):
            s = jnp.where(docs == qdoc, dot_nt(key, qt), MASKED)
            if u:
                return jnp.concatenate([s[:x0], jnp.where(causal, s[x0:], MASKED)], 0)
            return jnp.where(causal, s, MASKED)

        s1 = scores(k1[0:nk], docs1[0:nk], causal1)
        s2 = scores(k2[0:nk], docs2[0:nk], causal2)
        top = jnp.maximum(jnp.max(s1, 0, keepdims=True), jnp.max(s2, 0, keepdims=True))
        base = top * c
        p1 = jnp.exp2(s1 * c - (base - both))
        p2 = jnp.exp2(s2 * c - base)
        stats[0:1, mine] = top
        stats[1:2, mine] = jnp.sum(p1, 0, keepdims=True) + jnp.sum(p2, 0, keepdims=True)
        stats[2:3, mine] = qdoc
        out_ref[:, mine] = dot_nn(v1t[:, :nk], p1.astype(bf16)) + dot_nn(v2t[:, :nk], p2.astype(bf16))
        gtt_ref[:, mine] = dot_nt(eye, gt)
        p_refs[2 * u][...], p_refs[2 * u + 1][...] = p1, p2
        dp_refs[2 * u][...], dp_refs[2 * u + 1][...] = dot_nt(v1[0:nk], gt), dot_nt(v2[0:nk], gt)


def handoff_kernel(rows, *refs):
    far_refs, near, beyond = refs[:PLANE], refs[PLANE], refs[PLANE + 1]
    for k, ref in enumerate(far_refs):
        near[k, 0:2 * rows] = ref[2 * rows + DOC_ROWS:]
        near[k, 2 * rows:] = ref[2 * rows:2 * rows + DOC_ROWS]
        beyond[k] = ref[0:2 * rows + DOC_ROWS]


def cross_kernel(r0, rows, members, *refs):
    G = members
    far_refs = refs[0:2 * G]
    q_all, g_all, stats, local_out, gtt_ref = refs[2 * G:2 * G + 5]
    out_cross, (out_ref, gq_ref, new_stats) = refs[2 * G + 5:3 * G + 5], refs[3 * G + 5:3 * G + 8]
    kx, vx, dx, gkx, gvx = refs[3 * G + 8:]
    bf16, f32 = jnp.bfloat16, jnp.float32
    half = lax.axis_index("half")
    head = lax.axis_index("head")
    sel = selector(head, r0, rows, HD, False)
    for hop in range(H):
        for g in range(G):
            at = pl.ds(pl.multiple_of(((head ^ hop) * G + g) * rows, rows), rows)
            ref, k = far_refs[2 * g + hop // PLANE], hop % PLANE
            kx[at] = ref[k, 0:rows]
            vx[at] = ref[k, rows:2 * rows]
            dx[at] = sel[:rows] * ref[k, 2 * rows:2 * rows + DOC_ROWS][0:1]
    eye = eye_matrix()
    kxt, vxt = dot_nt(eye, kx[...]).astype(bf16), dot_nt(eye, vx[...]).astype(bf16)
    docsx = doc_cols(dx[...]) + jnp.where((half == 0) | takes_fine(G), 1000.0, 0.0)
    nd, lanes = tile_sizes(rows, G)
    c = SCALE * LOG2E
    for u in range(TILES):
        x0 = u * nd
        mine = slice(u * lanes, (u + 1) * lanes)
        qt, gt = q_all[mine], g_all[mine]
        top0, total0, qdoc = stats[0:1, mine], stats[1:2, mine], stats[2:3, mine]
        sx = jnp.where(docsx[x0:] == qdoc, dot_nt(kx[x0:], qt), MASKED)
        top = jnp.maximum(top0, jnp.max(sx, 0, keepdims=True))
        px = jnp.exp2(sx * c - top * c)
        shrink = jnp.exp2(top0 * c - top * c)
        inv = 1.0 / (total0 * shrink + jnp.sum(px, 0, keepdims=True))
        local_inv = shrink * inv
        out = local_out[:, mine] * local_inv + dot_nn(vxt[:, x0:], px.astype(bf16)) * inv
        dot = jnp.sum(gtt_ref[:, mine] * out, 0, keepdims=True)
        wx = px * inv
        ds = (wx * (dot_nt(vx[x0:], gt) - dot)).astype(bf16)
        wx = wx.astype(bf16)
        new_stats[0:1, mine] = local_inv
        new_stats[1:2, mine] = dot
        out_ref[mine] = out.T.astype(bf16)
        gq_ref[:, mine] = dot_nn(kxt[:, x0:], ds)
        gk, gv = dot_nn(ds, qt), dot_nn(wx, gt)
        if u == 0:
            gkx[...], gvx[...] = gk, gv
        else:
            gkx[x0:] += gk
            gvx[x0:] += gv
    for j in range(H):
        for g in range(G):
            at = pl.ds((j * G + g) * rows, rows)
            out_cross[g][j, 0:rows] = (gkx[at] * SCALE).astype(bf16)
            out_cross[g][j, rows:2 * rows] = gvx[at].astype(bf16)


def grad_kernel(rows, members, *refs):
    G = members
    k1, k2, q_all, g_all, out_ref, gq_ref, stats = refs[:7]
    p_refs, dp_refs = refs[7:7 + 2 * TILES], refs[7 + 2 * TILES:7 + 4 * TILES]
    rest = refs[7 + 4 * TILES:]
    partner = G // 2
    out_own, out_kv, (gk1, gk2, gv1, gv2) = rest[0], rest[1], rest[-4:]
    out_swap = rest[2:-4]
    bf16, f32 = jnp.bfloat16, jnp.float32
    eye = eye_matrix()
    nd, lanes = tile_sizes(rows, G)
    per = H // TILES
    k1t, k2t = dot_nt(eye, k1[...]).astype(bf16), dot_nt(eye, k2[...]).astype(bf16)
    for u in reversed(range(TILES)):
        nk = (u + 1) * nd
        mine = slice(u * lanes, (u + 1) * lanes)
        qt, gt = q_all[mine], g_all[mine]
        inv, dot = stats[0:1, mine], stats[1:2, mine]
        gq = gq_ref[:, mine]
        for i, (kt, gk, gv) in enumerate(((k1t, gk1, gv1), (k2t, gk2, gv2))):
            w = p_refs[2 * u + i][...] * inv
            ds = (w * (dp_refs[2 * u + i][...] - dot)).astype(bf16)
            gq = gq + dot_nn(kt[:, :nk], ds)
            new_k, new_v = dot_nn(ds, qt), dot_nn(w.astype(bf16), gt)
            if u == TILES - 1:
                gk[...], gv[...] = new_k, new_v
            else:
                gk[0:nk] += new_k
                gv[0:nk] += new_v
        gq = (gq * SCALE).T.astype(bf16)
        for i in range(per):
            j = u * per + i
            for e, ref in enumerate((out_own, out_swap[partner - 1])):
                lo = (2 * i + e) * rows
                ref[j, 0:rows] = out_ref[u * lanes + lo:u * lanes + lo + rows]
                ref[j, rows:2 * rows] = gq[lo:lo + rows]
    for j in range(H):
        for g in range(G):
            at = pl.ds((j * G + g) * rows, rows)
            ref = out_kv if g == 0 else out_swap[g - 1]
            base = 2 if g == partner else 0
            for i, part in enumerate((gk2[at] * SCALE, gv2[at], gk1[at] * SCALE, gv1[at]), base):
                ref[j, i * rows:(i + 1) * rows] = part.astype(ref.dtype)


def add_kernel(*refs):
    total = refs[0][...].astype(jnp.float32)
    for ref in refs[1:-1]:
        total = total + ref[...].astype(jnp.float32)
    refs[-1][...] = total


def sum_kernel(rows, members, own_ref, kv_ref, coarse_ref, *refs):
    swap_refs, out_ref = refs[:-1], refs[-1]
    partner = members // 2
    out_ref[:, 0:2 * rows] = own_ref[...]
    out_ref[:, 2 * rows:4 * rows] = swap_refs[partner - 1][:, 0:2 * rows]
    for i in range(2):
        total = kv_ref[:, 2 * i * rows:2 * (i + 1) * rows]
        for g, ref in enumerate(swap_refs, 1):
            base = 2 * (i + (g == partner))
            total = total + ref[:, base * rows:(base + 2) * rows].astype(jnp.float32)
        if i == 1:
            total = total + coarse_ref[...]
        out_ref[:, (4 + 2 * i) * rows:(6 + 2 * i) * rows] = total.astype(jnp.bfloat16)


def unpack_kernel(r0, rows, members, in_ref, *refs):
    outs, bufs, sem = refs[:4], refs[4:8], refs[8]
    tokens = bufs[0].shape[0]
    bf16 = jnp.bfloat16
    kinds = range(min(H, 2 * r0))
    query_sels = [selector(h, r0, rows, tokens, True, takes_fine(members)) for h in kinds]
    key_sels = [selector(h, r0, rows, tokens, True, True) for h in kinds]
    copies = []
    for i, base in enumerate((0, 1, 4, 5)):
        for h in range(H):
            sels = query_sels if i < 2 else key_sels
            part = jnp.concatenate([in_ref[h, (base + e) * rows:(base + e + 1) * rows] for e in (0, 2)], 0)
            bufs[i][:, h * HD:(h + 1) * HD] = dot_nn(sels[h % (2 * r0)], part).astype(bf16)
        copies.append(pltpu.make_async_copy(bufs[i], outs[i], sem.at[i]))
        copies[-1].start()
    for copy in copies:
        copy.wait()


def call(kernel, out_shape, scratch=(), limit=16, **more):
    return pl.pallas_call(
        kernel,
        out_shape=out_shape,
        scratch_shapes=list(scratch),
        compiler_params=pltpu.CompilerParams(vmem_limit_bytes=limit * 1024 * 1024),
        **more,
    )


def per_device(members, queries, keys, values, cotangent, doc_ids):
    G = members
    tokens = queries.shape[0]
    devices = 2 * H * G
    r0 = tokens * devices // (2 * SEG)
    rows = tokens // (2 * r0)
    bf16, f32 = jnp.bfloat16, jnp.float32
    shape = jax.ShapeDtypeStruct
    n = H * G * rows
    anywhere = pl.BlockSpec(memory_space=pltpu.HBM)
    wide = pltpu.VMEM((tokens, H * HD), bf16)
    message, far_shape = (H, 8 * rows + DOC_ROWS, HD), (PLANE, 4 * rows + DOC_ROWS, HD)

    packed, far = call(
        functools.partial(pack_kernel, r0, rows, G), [shape(message, bf16), shape(far_shape, bf16)],
        [wide] * 4 + [pltpu.VMEM((1, tokens), jnp.int32), pltpu.VMEM(message, bf16), pltpu.VMEM(far_shape, bf16),
                      pltpu.SemaphoreType.DMA((7,))],
        limit=64, in_specs=[anywhere] * 5, out_specs=[anywhere] * 2,
    )(queries, keys, values, cotangent, doc_ids.reshape(1, tokens))

    def to_head(x):
        return lax.all_to_all(x, "head", 0, 0, tiled=True)

    def to_member(x, g):
        return lax.ppermute(x, "member", [(i, i ^ g) for i in range(G)])

    def place(half, head, member):
        return (half * H + head) * G + member

    def to_chip(x, g):
        return lax.ppermute(x, "head", [(i, i ^ g) for i in range(H)])

    def spread(far):
        far = lax.ppermute(far, "half", [(0, 1), (1, 0)])
        hops = [far[0]] + [to_chip(far[g], g) for g in range(1, PLANE)]
        part = shape((PLANE, 2 * rows + DOC_ROWS, HD), bf16)
        near, beyond = call(functools.partial(handoff_kernel, rows), [part, part])(*hops)
        return near, to_chip(beyond, PLANE)

    def back_across(x, g):
        pairs = [(place(1, h, m), place(0, h, m ^ g)) for h in range(H) for m in range(G // 2)]
        return lax.ppermute(x, ("half", "head", "member"), pairs)

    nd, lanes = tile_sizes(rows, G)
    nq = TILES * lanes
    tile = [shape(((u + 1) * nd, lanes), f32) for u in range(TILES) for _ in range(2)]
    pairs = 2 * nd * lanes * TILES * (TILES + 1) // 2
    work = pl.CostEstimate(flops=6 * pairs * HD, bytes_accessed=16 * pairs, transcendentals=pairs)
    keys_scratch, wide_row = pltpu.VMEM((n, HD), bf16), shape((8, nq), f32)

    far = spread(far)
    own = to_head(packed)
    fars = list(far) + [to_member(x, g) for g in range(1, G) for x in far]
    swaps = [to_member(own[:, (2 if g == G // 2 else 4) * rows:], g) for g in range(1, G)]
    local = call(
        functools.partial(local_kernel, r0, rows, G),
        [shape((n, HD), bf16)] * 2 + [shape((nq, HD), bf16)] * 2 + [wide_row]
        + [shape((HD, nq), f32)] * 2 + tile * 2,
        [keys_scratch] * 4, limit=32, cost_estimate=work,
    )(own, *swaps)
    k1, k2, q_all, g_all, stats, out, gtt = local[:7]
    outs = call(
        functools.partial(cross_kernel, r0, rows, G),
        [shape((H, 2 * rows, HD), bf16)] * G + [shape((nq, HD), bf16), shape((HD, nq), f32), wide_row],
        [keys_scratch] * 3 + [pltpu.VMEM((n, HD), f32)] * 2, limit=32,
    )(*fars, q_all, g_all, stats, out, gtt)
    crosses = [back_across(outs[g], g) for g in range(G)]
    sent = lambda g: (H, (6 if g == G // 2 else 4) * rows, HD)
    outs = call(
        functools.partial(grad_kernel, rows, G),
        [shape((H, 2 * rows, HD), bf16), shape((H, 4 * rows, HD), f32)] + [shape(sent(g), bf16) for g in range(1, G)],
        [pltpu.VMEM((n, HD), f32)] * 4, limit=32, cost_estimate=work,
    )(k1, k2, q_all, g_all, *outs[G:], *local[7:])
    swaps = [to_member(outs[1 + g], g) for g in range(1, G)]
    coarse = call(add_kernel, shape((H, 2 * rows, HD), f32))(*crosses)
    coarse, *swaps = lax.optimization_barrier((coarse, *swaps))
    back = call(functools.partial(sum_kernel, rows, G), shape((H, 8 * rows, HD), bf16))(
        outs[0], outs[1], coarse, *swaps)
    back = to_head(back)
    return tuple(call(
        functools.partial(unpack_kernel, r0, rows, G), [shape((tokens, H * HD), bf16)] * 4,
        [wide] * 4 + [pltpu.SemaphoreType.DMA((4,))],
        in_specs=[VMEM], out_specs=[anywhere] * 4,
    )(back))


def solution(mesh):
    members = mesh.shape["seq"] // (2 * H)
    parts = {"seq": [("half", 2), ("head", H), ("member", members)]}
    axes = [part for name in mesh.axis_names for part in parts.get(name, [(name, mesh.shape[name])])]
    inner = Mesh(mesh.devices.reshape([size for _, size in axes]), [name for name, _ in axes])
    split = ("dp", "half", "head", "member")
    in_specs = (P(split, None),) * 4 + (P(split),)
    return jax.shard_map(
        functools.partial(per_device, members), mesh=inner, in_specs=in_specs,
        out_specs=(P(split, None),) * 4, check_vma=False,
    )
```

```python
import functools

import jax
import jax.numpy as jnp
import numpy as np
from jax import lax
from jax.experimental import pallas as pl
from jax.experimental.pallas import tpu as pltpu
from jax.sharding import Mesh
from jax.sharding import PartitionSpec as P

H = 8
HD = 128
SEG = 1024

MASKED = -1e30
SCALE = HD ** -0.5
LOG2E = float(np.log2(np.e))
VMEM = pl.BlockSpec(memory_space=pltpu.VMEM)
DOC_ROWS = 16
PLANE = 4


def dot_nn(a, b):
    return lax.dot_general(a, b, (((1,), (0,)), ((), ())), preferred_element_type=jnp.float32)


def dot_nt(a, b):
    return lax.dot_general(a, b, (((1,), (1,)), ((), ())), preferred_element_type=jnp.float32)


def selector(head, r0, rows, tokens, transposed, fine_first=False):
    r1 = 2 * r0
    shape = (tokens, 2 * rows) if transposed else (2 * rows, tokens)
    k = lax.broadcasted_iota(jnp.int32, shape, 1 if transposed else 0)
    p = lax.broadcasted_iota(jnp.int32, shape, 0 if transposed else 1)
    coarse = head % r1
    other = (coarse + r0) % r1
    first, second = jnp.where(fine_first, other, coarse), jnp.where(fine_first, coarse, other)
    target = jnp.where(k < rows, r1 * k + first, r1 * (k - rows) + second)
    return (p == target).astype(jnp.float32).astype(jnp.bfloat16)


def takes_fine(members):
    return lax.axis_index("member") >= members // 2


def pack_kernel(r0, rows, members, q_in, k_in, v_in, g_in, doc_in, *refs):
    outs, far_out, (q_ref, k_ref, v_ref, g_ref, doc_ref, buf, far, sem) = refs[:H], refs[H], refs[H + 1:]
    tokens = q_ref.shape[0]
    chip = lax.axis_index("head")
    pairs = ((doc_in, doc_ref), (k_in, k_ref), (v_in, v_ref), (q_in, q_ref), (g_in, g_ref))
    copies = [pltpu.make_async_copy(src, dst, sem.at[i]) for i, (src, dst) in enumerate(pairs)]
    for copy in copies:
        copy.start()
    kinds = range(min(H, 2 * r0))
    key_sels = [selector(h, r0, rows, tokens, False) for h in kinds]
    query_sels = [selector(h, r0, rows, tokens, False, takes_fine(members)) for h in kinds]

    def pick(sels, h, ref):
        return dot_nn(sels[h % (2 * r0)], ref[:, h * HD:(h + 1) * HD]).astype(jnp.bfloat16)

    copies[0].wait()
    docs = jnp.broadcast_to(doc_ref[...].astype(jnp.float32).astype(jnp.bfloat16), (DOC_ROWS, tokens))
    for i, ref in enumerate((k_ref, v_ref)):
        copies[1 + i].wait()
        for h in range(H):
            x = pick(key_sels, h, ref)
            hop = chip ^ h
            buf[hop, (4 + i) * rows:(5 + i) * rows] = x[rows:]
            buf[hop, (6 + i) * rows:(7 + i) * rows] = x[:rows]
            base = pl.multiple_of((hop // PLANE == 0) * (2 * rows + DOC_ROWS) + i * rows, 16)
            far[hop % PLANE, pl.ds(base, rows)] = x[:rows]
    for k in range(PLANE):
        far[k, 2 * rows:2 * rows + DOC_ROWS] = docs
    sends = [pltpu.make_async_copy(far, far_out, sem.at[6])]
    sends[0].start()
    for i, ref in enumerate((q_ref, g_ref)):
        copies[3 + i].wait()
        for h in range(H):
            x = pick(query_sels, h, ref)
            buf[chip ^ h, i * rows:(1 + i) * rows] = x[:rows]
            buf[chip ^ h, (2 + i) * rows:(3 + i) * rows] = x[rows:]
    for h in range(H):
        buf[h, 8 * rows:8 * rows + DOC_ROWS] = docs
    for h in range(H):
        sends.append(pltpu.make_async_copy(buf.at[h], outs[h], sem.at[7 + h]))
        sends[-1].start()
    for copy in sends:
        copy.wait()


TILES = 2


def tile_sizes(rows, members):
    per = H // TILES
    return per * members * rows, per * 2 * rows


def eye_matrix():
    shape = (HD, HD)
    same = lax.broadcasted_iota(jnp.int32, shape, 0) == lax.broadcasted_iota(jnp.int32, shape, 1)
    return same.astype(jnp.float32).astype(jnp.bfloat16)


def doc_cols(x):
    return dot_nn(x, jnp.ones((HD, HD), jnp.bfloat16))[:, 0:1]


def local_kernel(r0, rows, members, *refs):
    G = members
    r1 = 2 * r0
    own_refs, swap_refs, refs = refs[:H], refs[H:H + G - 1], refs[H + G - 1:]
    (k1, k2, q_all, g_all, stats, out_ref, gtt_ref), rest = refs[:7], refs[7:]
    p_refs, dp_refs, (v1, v2, d1, d2, dq) = rest[:2 * TILES], rest[2 * TILES:4 * TILES], rest[4 * TILES:]
    bf16, f32 = jnp.bfloat16, jnp.float32
    tokens = HD
    head = lax.axis_index("head")
    member = lax.axis_index("member")
    fine = takes_fine(G)
    partner = G // 2

    sel = selector(head, r0, rows, tokens, False)
    query_sel = jnp.where(fine, sel[rows:].astype(f32), sel[:rows].astype(f32)).astype(bf16)
    for hop in range(H):
        for g in range(G):
            at = pl.ds(pl.multiple_of(((head ^ hop) * G + g) * rows, rows), rows)
            ref = own_refs[hop] if g == 0 else swap_refs[g - 1].at[hop]
            base = 4 * rows if g == 0 else 2 * rows if g == partner else 0
            k2[at] = ref[base:base + rows]
            v2[at] = ref[base + rows:base + 2 * rows]
            k1[at] = ref[base + 2 * rows:base + 3 * rows]
            v1[at] = ref[base + 3 * rows:base + 4 * rows]
            doc = ref[base + 4 * rows:base + 4 * rows + DOC_ROWS][0:1]
            d1[at] = sel[:rows] * doc
            d2[at] = sel[rows:] * doc
            if g in (0, partner):
                at = pl.ds(pl.multiple_of(((head ^ hop) * 2 + (g != 0)) * rows, rows), rows)
                q_all[at] = ref[0:rows]
                g_all[at] = ref[rows:2 * rows]
                dq[at] = query_sel * doc

    eye = eye_matrix()
    v1t, v2t = dot_nt(eye, v1[...]).astype(bf16), dot_nt(eye, v2[...]).astype(bf16)
    docs1, docs2 = doc_cols(d1[...]), doc_cols(d2[...])
    nd, lanes = tile_sizes(rows, G)

    coarse = head % r1
    other = (coarse + r0) % r1
    lane = lax.broadcasted_iota(jnp.int32, (1, lanes), 1)
    qmember = member ^ (partner * ((lane // rows) % 2))
    qpos = (lane // (2 * rows)) * (G * tokens) + qmember * tokens + r1 * (lane % rows) + jnp.where(fine, other, coarse)
    kl = lax.broadcasted_iota(jnp.int32, (nd, 1), 0)
    kmember = member ^ ((kl // rows) % G)
    kpos = (kl // (rows * G)) * (G * tokens) + kmember * tokens + r1 * (kl % rows)
    causal1 = kpos + coarse <= qpos
    causal2 = kpos + other <= qpos
    both = jnp.where(fine, 0.0, 1.0)
    c = SCALE * LOG2E

    for u in range(TILES):
        nk = (u + 1) * nd
        x0 = u * nd
        mine = slice(u * lanes, (u + 1) * lanes)
        qt, gt = q_all[mine], g_all[mine]
        qdoc = dot_nt(jnp.ones((16, HD), bf16), dq[mine])[0:1]

        def scores(key, docs, causal):
            s = jnp.where(docs == qdoc, dot_nt(key, qt), MASKED)
            if u:
                return jnp.concatenate([s[:x0], jnp.where(causal, s[x0:], MASKED)], 0)
            return jnp.where(causal, s, MASKED)

        s1 = scores(k1[0:nk], docs1[0:nk], causal1)
        s2 = scores(k2[0:nk], docs2[0:nk], causal2)
        top = jnp.maximum(jnp.max(s1, 0, keepdims=True), jnp.max(s2, 0, keepdims=True))
        base = top * c
        p1 = jnp.exp2(s1 * c - (base - both))
        p2 = jnp.exp2(s2 * c - base)
        stats[0:1, mine] = top
        stats[1:2, mine] = jnp.sum(p1, 0, keepdims=True) + jnp.sum(p2, 0, keepdims=True)
        stats[2:3, mine] = qdoc
        out_ref[:, mine] = dot_nn(v1t[:, :nk], p1.astype(bf16)) + dot_nn(v2t[:, :nk], p2.astype(bf16))
        gtt_ref[:, mine] = dot_nt(eye, gt)
        p_refs[2 * u][...], p_refs[2 * u + 1][...] = p1, p2
        dp_refs[2 * u][...], dp_refs[2 * u + 1][...] = dot_nt(v1[0:nk], gt), dot_nt(v2[0:nk], gt)


def gather_kernel(rows, members, *refs):
    for g, out in enumerate(refs[H:], 1):
        base = (2 if g == members // 2 else 4) * rows
        for hop in range(H):
            out[hop] = refs[hop][base:]


def handoff_kernel(rows, *refs):
    far_refs, near, beyond = refs[:PLANE], refs[PLANE], refs[PLANE + 1]
    for k, ref in enumerate(far_refs):
        near[k, 0:2 * rows] = ref[2 * rows + DOC_ROWS:]
        near[k, 2 * rows:] = ref[2 * rows:2 * rows + DOC_ROWS]
        beyond[k] = ref[0:2 * rows + DOC_ROWS]


def cross_kernel(r0, rows, members, *refs):
    G = members
    far_refs = refs[0:2 * G]
    q_all, g_all, stats, local_out, gtt_ref = refs[2 * G:2 * G + 5]
    out_cross, (out_ref, gq_ref, new_stats) = refs[2 * G + 5:3 * G + 5], refs[3 * G + 5:3 * G + 8]
    kx, vx, dx, gkx, gvx = refs[3 * G + 8:]
    bf16, f32 = jnp.bfloat16, jnp.float32
    half = lax.axis_index("half")
    head = lax.axis_index("head")
    sel = selector(head, r0, rows, HD, False)
    for hop in range(H):
        for g in range(G):
            at = pl.ds(pl.multiple_of(((head ^ hop) * G + g) * rows, rows), rows)
            ref, k = far_refs[2 * g + hop // PLANE], hop % PLANE
            kx[at] = ref[k, 0:rows]
            vx[at] = ref[k, rows:2 * rows]
            dx[at] = sel[:rows] * ref[k, 2 * rows:2 * rows + DOC_ROWS][0:1]
    eye = eye_matrix()
    kxt, vxt = dot_nt(eye, kx[...]).astype(bf16), dot_nt(eye, vx[...]).astype(bf16)
    docsx = doc_cols(dx[...]) + jnp.where((half == 0) | takes_fine(G), 1000.0, 0.0)
    nd, lanes = tile_sizes(rows, G)
    c = SCALE * LOG2E
    for u in range(TILES):
        x0 = u * nd
        mine = slice(u * lanes, (u + 1) * lanes)
        qt, gt = q_all[mine], g_all[mine]
        top0, total0, qdoc = stats[0:1, mine], stats[1:2, mine], stats[2:3, mine]
        sx = jnp.where(docsx[x0:] == qdoc, dot_nt(kx[x0:], qt), MASKED)
        top = jnp.maximum(top0, jnp.max(sx, 0, keepdims=True))
        px = jnp.exp2(sx * c - top * c)
        shrink = jnp.exp2(top0 * c - top * c)
        inv = 1.0 / (total0 * shrink + jnp.sum(px, 0, keepdims=True))
        local_inv = shrink * inv
        out = local_out[:, mine] * local_inv + dot_nn(vxt[:, x0:], px.astype(bf16)) * inv
        dot = jnp.sum(gtt_ref[:, mine] * out, 0, keepdims=True)
        wx = px * inv
        ds = (wx * (dot_nt(vx[x0:], gt) - dot)).astype(bf16)
        wx = wx.astype(bf16)
        new_stats[0:1, mine] = local_inv
        new_stats[1:2, mine] = dot
        out_ref[mine] = out.T.astype(bf16)
        gq_ref[:, mine] = dot_nn(kxt[:, x0:], ds)
        gk, gv = dot_nn(ds, qt), dot_nn(wx, gt)
        if u == 0:
            gkx[...], gvx[...] = gk, gv
        else:
            gkx[x0:] += gk
            gvx[x0:] += gv
    for j in range(H):
        for g in range(G):
            at = pl.ds((j * G + g) * rows, rows)
            out_cross[g][j, 0:rows] = (gkx[at] * SCALE).astype(bf16)
            out_cross[g][j, rows:2 * rows] = gvx[at].astype(bf16)


def grad_kernel(rows, members, *refs):
    G = members
    k1, k2, q_all, g_all, out_ref, gq_ref, stats = refs[:7]
    p_refs, dp_refs = refs[7:7 + 2 * TILES], refs[7 + 2 * TILES:7 + 4 * TILES]
    rest = refs[7 + 4 * TILES:]
    partner = G // 2
    out_own, out_kv, (gk1, gk2, gv1, gv2) = rest[0], rest[1], rest[-4:]
    out_swap = rest[2:-4]
    bf16, f32 = jnp.bfloat16, jnp.float32
    eye = eye_matrix()
    nd, lanes = tile_sizes(rows, G)
    per = H // TILES
    k1t, k2t = dot_nt(eye, k1[...]).astype(bf16), dot_nt(eye, k2[...]).astype(bf16)
    for u in reversed(range(TILES)):
        nk = (u + 1) * nd
        mine = slice(u * lanes, (u + 1) * lanes)
        qt, gt = q_all[mine], g_all[mine]
        inv, dot = stats[0:1, mine], stats[1:2, mine]
        gq = gq_ref[:, mine]
        for i, (kt, gk, gv) in enumerate(((k1t, gk1, gv1), (k2t, gk2, gv2))):
            w = p_refs[2 * u + i][...] * inv
            ds = (w * (dp_refs[2 * u + i][...] - dot)).astype(bf16)
            gq = gq + dot_nn(kt[:, :nk], ds)
            new_k, new_v = dot_nn(ds, qt), dot_nn(w.astype(bf16), gt)
            if u == TILES - 1:
                gk[...], gv[...] = new_k, new_v
            else:
                gk[0:nk] += new_k
                gv[0:nk] += new_v
        gq = (gq * SCALE).T.astype(bf16)
        for i in range(per):
            j = u * per + i
            for e, ref in enumerate((out_own, out_swap[partner - 1])):
                lo = (2 * i + e) * rows
                ref[j, 0:rows] = out_ref[u * lanes + lo:u * lanes + lo + rows]
                ref[j, rows:2 * rows] = gq[lo:lo + rows]
    for j in range(H):
        for g in range(G):
            at = pl.ds((j * G + g) * rows, rows)
            ref = out_kv if g == 0 else out_swap[g - 1]
            base = 2 if g == partner else 0
            for i, part in enumerate((gk2[at] * SCALE, gv2[at], gk1[at] * SCALE, gv1[at]), base):
                ref[j, i * rows:(i + 1) * rows] = part.astype(ref.dtype)


def add_kernel(*refs):
    total = refs[0][...].astype(jnp.float32)
    for ref in refs[1:-1]:
        total = total + ref[...].astype(jnp.float32)
    refs[-1][...] = total


def sum_kernel(rows, members, own_ref, kv_ref, coarse_ref, *refs):
    swap_refs, out_ref = refs[:-1], refs[-1]
    partner = members // 2
    out_ref[:, 0:2 * rows] = own_ref[...]
    out_ref[:, 2 * rows:4 * rows] = swap_refs[partner - 1][:, 0:2 * rows]
    for i in range(2):
        total = kv_ref[:, 2 * i * rows:2 * (i + 1) * rows]
        for g, ref in enumerate(swap_refs, 1):
            base = 2 * (i + (g == partner))
            total = total + ref[:, base * rows:(base + 2) * rows].astype(jnp.float32)
        if i == 1:
            total = total + coarse_ref[...]
        out_ref[:, (4 + 2 * i) * rows:(6 + 2 * i) * rows] = total.astype(jnp.bfloat16)


def unpack_kernel(r0, rows, members, in_ref, *refs):
    outs, bufs, sem = refs[:4], refs[4:8], refs[8]
    tokens = bufs[0].shape[0]
    bf16 = jnp.bfloat16
    kinds = range(min(H, 2 * r0))
    query_sels = [selector(h, r0, rows, tokens, True, takes_fine(members)) for h in kinds]
    key_sels = [selector(h, r0, rows, tokens, True, True) for h in kinds]
    copies = []
    for i, base in enumerate((0, 1, 4, 5)):
        for h in range(H):
            sels = query_sels if i < 2 else key_sels
            part = jnp.concatenate([in_ref[h, (base + e) * rows:(base + e + 1) * rows] for e in (0, 2)], 0)
            bufs[i][:, h * HD:(h + 1) * HD] = dot_nn(sels[h % (2 * r0)], part).astype(bf16)
        copies.append(pltpu.make_async_copy(bufs[i], outs[i], sem.at[i]))
        copies[-1].start()
    for copy in copies:
        copy.wait()


def call(kernel, out_shape, scratch=(), limit=16, **more):
    return pl.pallas_call(
        kernel,
        out_shape=out_shape,
        scratch_shapes=list(scratch),
        compiler_params=pltpu.CompilerParams(vmem_limit_bytes=limit * 1024 * 1024),
        **more,
    )


def per_device(members, queries, keys, values, cotangent, doc_ids):
    G = members
    tokens = queries.shape[0]
    devices = 2 * H * G
    r0 = tokens * devices // (2 * SEG)
    rows = tokens // (2 * r0)
    bf16, f32 = jnp.bfloat16, jnp.float32
    shape = jax.ShapeDtypeStruct
    n = H * G * rows
    anywhere = pl.BlockSpec(memory_space=pltpu.HBM)
    wide = pltpu.VMEM((tokens, H * HD), bf16)
    message, far_shape = (H, 8 * rows + DOC_ROWS, HD), (PLANE, 4 * rows + DOC_ROWS, HD)

    *packed, far = call(
        functools.partial(pack_kernel, r0, rows, G), [shape(message[1:], bf16)] * H + [shape(far_shape, bf16)],
        [wide] * 4 + [pltpu.VMEM((1, tokens), jnp.int32), pltpu.VMEM(message, bf16), pltpu.VMEM(far_shape, bf16),
                      pltpu.SemaphoreType.DMA((7 + H,))],
        limit=64, in_specs=[anywhere] * 5, out_specs=[anywhere] * (H + 1),
    )(queries, keys, values, cotangent, doc_ids.reshape(1, tokens))

    def to_head(x):
        return lax.all_to_all(x, "head", 0, 0, tiled=True)

    def to_member(x, g):
        return lax.ppermute(x, "member", [(i, i ^ g) for i in range(G)])

    def place(half, head, member):
        return (half * H + head) * G + member

    def to_chip(x, g):
        return lax.ppermute(x, "head", [(i, i ^ g) for i in range(H)])

    def spread(far):
        far = lax.ppermute(far, "half", [(0, 1), (1, 0)])
        hops = [far[0]] + [to_chip(far[g], g) for g in range(1, PLANE)]
        part = shape((PLANE, 2 * rows + DOC_ROWS, HD), bf16)
        near, beyond = call(functools.partial(handoff_kernel, rows), [part, part])(*hops)
        return near, to_chip(beyond, PLANE)

    def back_across(x, g):
        pairs = [(place(1, h, m), place(0, h, m ^ g)) for h in range(H) for m in range(G // 2)]
        return lax.ppermute(x, ("half", "head", "member"), pairs)

    nd, lanes = tile_sizes(rows, G)
    nq = TILES * lanes
    tile = [shape(((u + 1) * nd, lanes), f32) for u in range(TILES) for _ in range(2)]
    pairs = 2 * nd * lanes * TILES * (TILES + 1) // 2
    work = pl.CostEstimate(flops=6 * pairs * HD, bytes_accessed=16 * pairs, transcendentals=pairs)
    keys_scratch, wide_row = pltpu.VMEM((n, HD), bf16), shape((8, nq), f32)

    far = spread(far)
    own = [packed[0]] + [to_chip(packed[g], g) for g in range(1, H)]
    fars = list(far) + [to_member(x, g) for g in range(1, G) for x in far]
    sent = lambda g: (6 if g == G // 2 else 4) * rows
    gathered = call(
        functools.partial(gather_kernel, rows, G), [shape((H, sent(g) + DOC_ROWS, HD), bf16) for g in range(1, G)])(*own)
    swaps = [to_member(x, g) for g, x in enumerate(gathered, 1)]
    local = call(
        functools.partial(local_kernel, r0, rows, G),
        [shape((n, HD), bf16)] * 2 + [shape((nq, HD), bf16)] * 2 + [wide_row]
        + [shape((HD, nq), f32)] * 2 + tile * 2,
        [keys_scratch] * 4 + [pltpu.VMEM((nq, HD), bf16)], limit=32, cost_estimate=work,
    )(*own, *swaps)
    k1, k2, q_all, g_all, stats, out, gtt = local[:7]
    outs = call(
        functools.partial(cross_kernel, r0, rows, G),
        [shape((H, 2 * rows, HD), bf16)] * G + [shape((nq, HD), bf16), shape((HD, nq), f32), wide_row],
        [keys_scratch] * 3 + [pltpu.VMEM((n, HD), f32)] * 2, limit=32,
    )(*fars, q_all, g_all, stats, out, gtt)
    crosses = [back_across(outs[g], g) for g in range(G)]
    outs = call(
        functools.partial(grad_kernel, rows, G),
        [shape((H, 2 * rows, HD), bf16), shape((H, 4 * rows, HD), f32)] + [shape((H, sent(g), HD), bf16) for g in range(1, G)],
        [pltpu.VMEM((n, HD), f32)] * 4, limit=32, cost_estimate=work,
    )(k1, k2, q_all, g_all, *outs[G:], *local[7:])
    swaps = [to_member(outs[1 + g], g) for g in range(1, G)]
    coarse = call(add_kernel, shape((H, 2 * rows, HD), f32))(*crosses)
    coarse, *swaps = lax.optimization_barrier((coarse, *swaps))
    back = call(functools.partial(sum_kernel, rows, G), shape((H, 8 * rows, HD), bf16))(
        outs[0], outs[1], coarse, *swaps)
    back = to_head(back)
    return tuple(call(
        functools.partial(unpack_kernel, r0, rows, G), [shape((tokens, H * HD), bf16)] * 4,
        [wide] * 4 + [pltpu.SemaphoreType.DMA((4,))],
        in_specs=[VMEM], out_specs=[anywhere] * 4,
    )(back))


def solution(mesh):
    members = mesh.shape["seq"] // (2 * H)
    parts = {"seq": [("half", 2), ("head", H), ("member", members)]}
    axes = [part for name in mesh.axis_names for part in parts.get(name, [(name, mesh.shape[name])])]
    inner = Mesh(mesh.devices.reshape([size for _, size in axes]), [name for name, _ in axes])
    split = ("dp", "half", "head", "member")
    in_specs = (P(split, None),) * 4 + (P(split),)
    return jax.shard_map(
        functools.partial(per_device, members), mesh=inner, in_specs=in_specs,
        out_specs=(P(split, None),) * 4, check_vma=False,
    )
```

```python
import functools

import jax
import jax.numpy as jnp
import numpy as np
from jax import lax
from jax.experimental import pallas as pl
from jax.experimental.pallas import tpu as pltpu
from jax.sharding import Mesh
from jax.sharding import PartitionSpec as P

H = 8
HD = 128
SEG = 1024

MASKED = -1e30
SCALE = HD ** -0.5
LOG2E = float(np.log2(np.e))
VMEM = pl.BlockSpec(memory_space=pltpu.VMEM)
DOC_ROWS = 16


def dot_nn(a, b):
    return lax.dot_general(a, b, (((1,), (0,)), ((), ())), preferred_element_type=jnp.float32)


def dot_nt(a, b):
    return lax.dot_general(a, b, (((1,), (1,)), ((), ())), preferred_element_type=jnp.float32)


def selector(head, r0, rows, tokens, transposed, fine_first=False):
    r1 = 2 * r0
    shape = (tokens, 2 * rows) if transposed else (2 * rows, tokens)
    k = lax.broadcasted_iota(jnp.int32, shape, 1 if transposed else 0)
    p = lax.broadcasted_iota(jnp.int32, shape, 0 if transposed else 1)
    coarse = head % r1
    other = (coarse + r0) % r1
    first, second = jnp.where(fine_first, other, coarse), jnp.where(fine_first, coarse, other)
    target = jnp.where(k < rows, r1 * k + first, r1 * (k - rows) + second)
    return (p == target).astype(jnp.float32).astype(jnp.bfloat16)


def takes_fine(members):
    return lax.axis_index("member") >= members // 2


def pack_kernel(r0, rows, members, q_in, k_in, v_in, g_in, doc_in, out, far_out, q_ref, k_ref, v_ref, g_ref, doc_ref, buf, far, sem):
    tokens = q_ref.shape[0]
    pairs = ((doc_in, doc_ref), (k_in, k_ref), (v_in, v_ref), (q_in, q_ref), (g_in, g_ref))
    copies = [pltpu.make_async_copy(src, dst, sem.at[i]) for i, (src, dst) in enumerate(pairs)]
    for copy in copies:
        copy.start()
    kinds = range(min(H, 2 * r0))
    key_sels = [selector(h, r0, rows, tokens, False) for h in kinds]
    query_sels = [selector(h, r0, rows, tokens, False, takes_fine(members)) for h in kinds]

    def pick(sels, h, ref):
        return dot_nn(sels[h % (2 * r0)], ref[:, h * HD:(h + 1) * HD]).astype(jnp.bfloat16)

    copies[0].wait()
    docs = jnp.broadcast_to(doc_ref[...].astype(jnp.float32).astype(jnp.bfloat16), (DOC_ROWS, tokens))
    for i, ref in enumerate((k_ref, v_ref)):
        copies[1 + i].wait()
        for h in range(H):
            x = pick(key_sels, h, ref)
            buf[h, (4 + i) * rows:(5 + i) * rows] = x[rows:]
            buf[h, (6 + i) * rows:(7 + i) * rows] = x[:rows]
            far[h, i * rows:(i + 1) * rows] = x[:rows]
    for h in range(H):
        far[h, 2 * rows:] = docs
    sends = [pltpu.make_async_copy(far, far_out, sem.at[6])]
    sends[0].start()
    for i, ref in enumerate((q_ref, g_ref)):
        copies[3 + i].wait()
        for h in range(H):
            x = pick(query_sels, h, ref)
            buf[h, i * rows:(1 + i) * rows] = x[:rows]
            buf[h, (2 + i) * rows:(3 + i) * rows] = x[rows:]
    for h in range(H):
        buf[h, 8 * rows:8 * rows + DOC_ROWS] = docs
    sends.append(pltpu.make_async_copy(buf, out, sem.at[5]))
    sends[1].start()
    for copy in sends:
        copy.wait()


TILES = 2


def tile_sizes(rows, members):
    per = H // TILES
    return per * members * rows, per * 2 * rows


def eye_matrix():
    shape = (HD, HD)
    same = lax.broadcasted_iota(jnp.int32, shape, 0) == lax.broadcasted_iota(jnp.int32, shape, 1)
    return same.astype(jnp.float32).astype(jnp.bfloat16)


def doc_cols(x):
    return dot_nn(x, jnp.ones((HD, HD), jnp.bfloat16))[:, 0:1]


def local_kernel(r0, rows, members, *refs):
    G = members
    r1 = 2 * r0
    own_ref, swap_refs = refs[0], refs[1:G]
    (k1, k2, q_all, g_all, stats, out_ref, gtt_ref), rest = refs[G:G + 7], refs[G + 7:]
    p_refs, dp_refs, (v1, v2, d1, d2) = rest[:2 * TILES], rest[2 * TILES:4 * TILES], rest[4 * TILES:]
    bf16, f32 = jnp.bfloat16, jnp.float32
    tokens = HD
    head = lax.axis_index("head")
    member = lax.axis_index("member")
    fine = takes_fine(G)
    partner = G // 2
    partner_ref = swap_refs[partner - 1]

    sel = selector(head, r0, rows, tokens, False)
    query_sel = jnp.where(fine, sel[rows:].astype(f32), sel[:rows].astype(f32)).astype(bf16)
    source_docs = []
    for j in range(H):
        for g in range(G):
            at = pl.ds((j * G + g) * rows, rows)
            ref, base = (own_ref, 4 * rows) if g == 0 else (swap_refs[g - 1], 2 * rows if g == partner else 0)
            k2[at] = ref[j, base:base + rows]
            v2[at] = ref[j, base + rows:base + 2 * rows]
            k1[at] = ref[j, base + 2 * rows:base + 3 * rows]
            v1[at] = ref[j, base + 3 * rows:base + 4 * rows]
            doc = ref[j, base + 4 * rows:base + 4 * rows + DOC_ROWS][0:1]
            if g in (0, partner):
                source_docs.append(doc)
            d1[at] = sel[:rows] * doc
            d2[at] = sel[rows:] * doc

    eye = eye_matrix()
    v1t, v2t = dot_nt(eye, v1[...]).astype(bf16), dot_nt(eye, v2[...]).astype(bf16)
    docs1, docs2 = doc_cols(d1[...]), doc_cols(d2[...])
    nd, lanes = tile_sizes(rows, G)
    per = H // TILES

    coarse = head % r1
    other = (coarse + r0) % r1
    lane = lax.broadcasted_iota(jnp.int32, (1, lanes), 1)
    qmember = member ^ (partner * ((lane // rows) % 2))
    qpos = (lane // (2 * rows)) * (G * tokens) + qmember * tokens + r1 * (lane % rows) + jnp.where(fine, other, coarse)
    kl = lax.broadcasted_iota(jnp.int32, (nd, 1), 0)
    kmember = member ^ ((kl // rows) % G)
    kpos = (kl // (rows * G)) * (G * tokens) + kmember * tokens + r1 * (kl % rows)
    causal1 = kpos + coarse <= qpos
    causal2 = kpos + other <= qpos
    both = jnp.where(fine, 0.0, 1.0)
    c = SCALE * LOG2E

    for u in range(TILES):
        nk = (u + 1) * nd
        x0 = u * nd
        src = range(u * per, (u + 1) * per)
        mine = slice(u * lanes, (u + 1) * lanes)
        gather = lambda lo: jnp.concatenate([ref[j, lo:lo + rows] for j in src for ref in (own_ref, partner_ref)], 0)
        qt, gt = gather(0), gather(rows)
        q_all[mine], g_all[mine] = qt, gt
        dq = jnp.concatenate([query_sel * source_docs[2 * j + e] for j in src for e in range(2)], 0)
        qdoc = dot_nt(jnp.ones((16, HD), bf16), dq)[0:1]

        def scores(key, docs, causal):
            s = jnp.where(docs == qdoc, dot_nt(key, qt), MASKED)
            if u:
                return jnp.concatenate([s[:x0], jnp.where(causal, s[x0:], MASKED)], 0)
            return jnp.where(causal, s, MASKED)

        s1 = scores(k1[0:nk], docs1[0:nk], causal1)
        s2 = scores(k2[0:nk], docs2[0:nk], causal2)
        top = jnp.maximum(jnp.max(s1, 0, keepdims=True), jnp.max(s2, 0, keepdims=True))
        base = top * c
        p1 = jnp.exp2(s1 * c - (base - both))
        p2 = jnp.exp2(s2 * c - base)
        stats[0:1, mine] = top
        stats[1:2, mine] = jnp.sum(p1, 0, keepdims=True) + jnp.sum(p2, 0, keepdims=True)
        stats[2:3, mine] = qdoc
        out_ref[:, mine] = dot_nn(v1t[:, :nk], p1.astype(bf16)) + dot_nn(v2t[:, :nk], p2.astype(bf16))
        gtt_ref[:, mine] = dot_nt(eye, gt)
        p_refs[2 * u][...], p_refs[2 * u + 1][...] = p1, p2
        dp_refs[2 * u][...], dp_refs[2 * u + 1][...] = dot_nt(v1[0:nk], gt), dot_nt(v2[0:nk], gt)


def cross_kernel(r0, rows, members, *refs):
    G = members
    far_refs = refs[0:G]
    q_all, g_all, stats, local_out, gtt_ref = refs[G:G + 5]
    out_cross, (out_ref, gq_ref, new_stats) = refs[G + 5:2 * G + 5], refs[2 * G + 5:2 * G + 8]
    kx, vx, dx, gkx, gvx = refs[2 * G + 8:]
    bf16, f32 = jnp.bfloat16, jnp.float32
    half = lax.axis_index("half")
    head = lax.axis_index("head")
    sel = selector(head, r0, rows, HD, False)
    for j in range(H):
        for g in range(G):
            at = pl.ds((j * G + g) * rows, rows)
            ref = far_refs[g]
            kx[at] = ref[j, 0:rows]
            vx[at] = ref[j, rows:2 * rows]
            dx[at] = sel[:rows] * ref[j, 2 * rows:2 * rows + DOC_ROWS][0:1]
    eye = eye_matrix()
    kxt, vxt = dot_nt(eye, kx[...]).astype(bf16), dot_nt(eye, vx[...]).astype(bf16)
    docsx = doc_cols(dx[...]) + jnp.where((half == 0) | takes_fine(G), 1000.0, 0.0)
    nd, lanes = tile_sizes(rows, G)
    c = SCALE * LOG2E
    for u in range(TILES):
        x0 = u * nd
        mine = slice(u * lanes, (u + 1) * lanes)
        qt, gt = q_all[mine], g_all[mine]
        top0, total0, qdoc = stats[0:1, mine], stats[1:2, mine], stats[2:3, mine]
        sx = jnp.where(docsx[x0:] == qdoc, dot_nt(kx[x0:], qt), MASKED)
        top = jnp.maximum(top0, jnp.max(sx, 0, keepdims=True))
        px = jnp.exp2(sx * c - top * c)
        shrink = jnp.exp2(top0 * c - top * c)
        inv = 1.0 / (total0 * shrink + jnp.sum(px, 0, keepdims=True))
        local_inv = shrink * inv
        out = local_out[:, mine] * local_inv + dot_nn(vxt[:, x0:], px.astype(bf16)) * inv
        dot = jnp.sum(gtt_ref[:, mine] * out, 0, keepdims=True)
        wx = px * inv
        ds = (wx * (dot_nt(vx[x0:], gt) - dot)).astype(bf16)
        wx = wx.astype(bf16)
        new_stats[0:1, mine] = local_inv
        new_stats[1:2, mine] = dot
        out_ref[mine] = out.T.astype(bf16)
        gq_ref[:, mine] = dot_nn(kxt[:, x0:], ds)
        gk, gv = dot_nn(ds, qt), dot_nn(wx, gt)
        if u == 0:
            gkx[...], gvx[...] = gk, gv
        else:
            gkx[x0:] += gk
            gvx[x0:] += gv
    for j in range(H):
        for g in range(G):
            at = pl.ds((j * G + g) * rows, rows)
            out_cross[g][j, 0:rows] = (gkx[at] * SCALE).astype(bf16)
            out_cross[g][j, rows:2 * rows] = gvx[at].astype(bf16)


def grad_kernel(rows, members, *refs):
    G = members
    k1, k2, q_all, g_all, out_ref, gq_ref, stats = refs[:7]
    p_refs, dp_refs = refs[7:7 + 2 * TILES], refs[7 + 2 * TILES:7 + 4 * TILES]
    rest = refs[7 + 4 * TILES:]
    partner = G // 2
    out_own, out_kv, (gk1, gk2, gv1, gv2) = rest[0], rest[1], rest[-4:]
    out_swap = rest[2:-4]
    bf16, f32 = jnp.bfloat16, jnp.float32
    eye = eye_matrix()
    nd, lanes = tile_sizes(rows, G)
    per = H // TILES
    k1t, k2t = dot_nt(eye, k1[...]).astype(bf16), dot_nt(eye, k2[...]).astype(bf16)
    for u in reversed(range(TILES)):
        nk = (u + 1) * nd
        mine = slice(u * lanes, (u + 1) * lanes)
        qt, gt = q_all[mine], g_all[mine]
        inv, dot = stats[0:1, mine], stats[1:2, mine]
        gq = gq_ref[:, mine]
        for i, (kt, gk, gv) in enumerate(((k1t, gk1, gv1), (k2t, gk2, gv2))):
            w = p_refs[2 * u + i][...] * inv
            ds = (w * (dp_refs[2 * u + i][...] - dot)).astype(bf16)
            gq = gq + dot_nn(kt[:, :nk], ds)
            new_k, new_v = dot_nn(ds, qt), dot_nn(w.astype(bf16), gt)
            if u == TILES - 1:
                gk[...], gv[...] = new_k, new_v
            else:
                gk[0:nk] += new_k
                gv[0:nk] += new_v
        gq = (gq * SCALE).T.astype(bf16)
        for i in range(per):
            j = u * per + i
            for e, ref in enumerate((out_own, out_swap[partner - 1])):
                lo = (2 * i + e) * rows
                ref[j, 0:rows] = out_ref[u * lanes + lo:u * lanes + lo + rows]
                ref[j, rows:2 * rows] = gq[lo:lo + rows]
    for j in range(H):
        for g in range(G):
            at = pl.ds((j * G + g) * rows, rows)
            ref = out_kv if g == 0 else out_swap[g - 1]
            base = 2 if g == partner else 0
            for i, part in enumerate((gk2[at] * SCALE, gv2[at], gk1[at] * SCALE, gv1[at]), base):
                ref[j, i * rows:(i + 1) * rows] = part.astype(ref.dtype)


def add_kernel(*refs):
    total = refs[0][...].astype(jnp.float32)
    for ref in refs[1:-1]:
        total = total + ref[...].astype(jnp.float32)
    refs[-1][...] = total


def sum_kernel(rows, members, own_ref, kv_ref, coarse_ref, *refs):
    swap_refs, out_ref = refs[:-1], refs[-1]
    partner = members // 2
    out_ref[:, 0:2 * rows] = own_ref[...]
    out_ref[:, 2 * rows:4 * rows] = swap_refs[partner - 1][:, 0:2 * rows]
    for i in range(2):
        total = kv_ref[:, 2 * i * rows:2 * (i + 1) * rows]
        for g, ref in enumerate(swap_refs, 1):
            base = 2 * (i + (g == partner))
            total = total + ref[:, base * rows:(base + 2) * rows].astype(jnp.float32)
        if i == 1:
            total = total + coarse_ref[...]
        out_ref[:, (4 + 2 * i) * rows:(6 + 2 * i) * rows] = total.astype(jnp.bfloat16)


def unpack_kernel(r0, rows, members, in_ref, *refs):
    outs, bufs, sem = refs[:4], refs[4:8], refs[8]
    tokens = bufs[0].shape[0]
    bf16 = jnp.bfloat16
    kinds = range(min(H, 2 * r0))
    query_sels = [selector(h, r0, rows, tokens, True, takes_fine(members)) for h in kinds]
    key_sels = [selector(h, r0, rows, tokens, True, True) for h in kinds]
    copies = []
    for i, base in enumerate((0, 1, 4, 5)):
        for h in range(H):
            sels = query_sels if i < 2 else key_sels
            part = jnp.concatenate([in_ref[h, (base + e) * rows:(base + e + 1) * rows] for e in (0, 2)], 0)
            bufs[i][:, h * HD:(h + 1) * HD] = dot_nn(sels[h % (2 * r0)], part).astype(bf16)
        copies.append(pltpu.make_async_copy(bufs[i], outs[i], sem.at[i]))
        copies[-1].start()
    for copy in copies:
        copy.wait()


def call(kernel, out_shape, scratch=(), limit=16, **more):
    return pl.pallas_call(
        kernel,
        out_shape=out_shape,
        scratch_shapes=list(scratch),
        compiler_params=pltpu.CompilerParams(vmem_limit_bytes=limit * 1024 * 1024),
        **more,
    )


def per_device(members, queries, keys, values, cotangent, doc_ids):
    G = members
    tokens = queries.shape[0]
    devices = 2 * H * G
    r0 = tokens * devices // (2 * SEG)
    rows = tokens // (2 * r0)
    bf16, f32 = jnp.bfloat16, jnp.float32
    shape = jax.ShapeDtypeStruct
    n = H * G * rows
    anywhere = pl.BlockSpec(memory_space=pltpu.HBM)
    wide = pltpu.VMEM((tokens, H * HD), bf16)
    message, far_shape = (H, 8 * rows + DOC_ROWS, HD), (H, 2 * rows + DOC_ROWS, HD)

    packed, far = call(
        functools.partial(pack_kernel, r0, rows, G), [shape(message, bf16), shape(far_shape, bf16)],
        [wide] * 4 + [pltpu.VMEM((1, tokens), jnp.int32), pltpu.VMEM(message, bf16), pltpu.VMEM(far_shape, bf16),
                      pltpu.SemaphoreType.DMA((7,))],
        limit=64, in_specs=[anywhere] * 5, out_specs=[anywhere] * 2,
    )(queries, keys, values, cotangent, doc_ids.reshape(1, tokens))

    def to_head(x):
        return lax.all_to_all(x, "head", 0, 0, tiled=True)

    def to_member(x, g):
        return lax.ppermute(x, "member", [(i, i ^ g) for i in range(G)])

    def place(half, head, member):
        return (half * H + head) * G + member

    def back_across(x, g):
        pairs = [(place(1, h, m), place(0, h, m ^ g)) for h in range(H) for m in range(G // 2)]
        return lax.ppermute(x, ("half", "head", "member"), pairs)

    nd, lanes = tile_sizes(rows, G)
    nq = TILES * lanes
    tile = [shape(((u + 1) * nd, lanes), f32) for u in range(TILES) for _ in range(2)]
    pairs = 2 * nd * lanes * TILES * (TILES + 1) // 2
    work = pl.CostEstimate(flops=6 * pairs * HD, bytes_accessed=16 * pairs, transcendentals=pairs)
    keys_scratch, wide_row = pltpu.VMEM((n, HD), bf16), shape((8, nq), f32)

    far = lax.ppermute(far, "half", [(0, 1), (1, 0)])
    own = to_head(packed)
    own, far = lax.optimization_barrier((own, far))
    far = to_head(far)
    fars = [far] + [to_member(far, g) for g in range(1, G)]
    swaps = [to_member(own[:, (2 if g == G // 2 else 4) * rows:], g) for g in range(1, G)]
    local = call(
        functools.partial(local_kernel, r0, rows, G),
        [shape((n, HD), bf16)] * 2 + [shape((nq, HD), bf16)] * 2 + [wide_row]
        + [shape((HD, nq), f32)] * 2 + tile * 2,
        [keys_scratch] * 4, limit=32, cost_estimate=work,
    )(own, *swaps)
    k1, k2, q_all, g_all, stats, out, gtt = local[:7]
    outs = call(
        functools.partial(cross_kernel, r0, rows, G),
        [shape((H, 2 * rows, HD), bf16)] * G + [shape((nq, HD), bf16), shape((HD, nq), f32), wide_row],
        [keys_scratch] * 3 + [pltpu.VMEM((n, HD), f32)] * 2, limit=32,
    )(*fars, q_all, g_all, stats, out, gtt)
    crosses = [back_across(outs[g], g) for g in range(G)]
    sent = lambda g: (H, (6 if g == G // 2 else 4) * rows, HD)
    outs = call(
        functools.partial(grad_kernel, rows, G),
        [shape((H, 2 * rows, HD), bf16), shape((H, 4 * rows, HD), f32)] + [shape(sent(g), bf16) for g in range(1, G)],
        [pltpu.VMEM((n, HD), f32)] * 4, limit=32, cost_estimate=work,
    )(k1, k2, q_all, g_all, *outs[G:], *local[7:])
    swaps = [to_member(outs[1 + g], g) for g in range(1, G)]
    coarse = call(add_kernel, shape((H, 2 * rows, HD), f32))(*crosses)
    coarse, *swaps = lax.optimization_barrier((coarse, *swaps))
    back = call(functools.partial(sum_kernel, rows, G), shape((H, 8 * rows, HD), bf16))(
        outs[0], outs[1], coarse, *swaps)
    back = to_head(back)
    return tuple(call(
        functools.partial(unpack_kernel, r0, rows, G), [shape((tokens, H * HD), bf16)] * 4,
        [wide] * 4 + [pltpu.SemaphoreType.DMA((4,))],
        in_specs=[VMEM], out_specs=[anywhere] * 4,
    )(back))


def solution(mesh):
    members = mesh.shape["seq"] // (2 * H)
    parts = {"seq": [("half", 2), ("head", H), ("member", members)]}
    axes = [part for name in mesh.axis_names for part in parts.get(name, [(name, mesh.shape[name])])]
    inner = Mesh(mesh.devices.reshape([size for _, size in axes]), [name for name, _ in axes])
    split = ("dp", "half", "head", "member")
    in_specs = (P(split, None),) * 4 + (P(split),)
    return jax.shard_map(
        functools.partial(per_device, members), mesh=inner, in_specs=in_specs,
        out_specs=(P(split, None),) * 4, check_vma=False,
    )
```

```python
import functools

import jax
import jax.numpy as jnp
import numpy as np
from jax import lax
from jax.experimental import pallas as pl
from jax.experimental.pallas import tpu as pltpu
from jax.sharding import Mesh
from jax.sharding import PartitionSpec as P

H = 8
HD = 128
SEG = 1024

MASKED = -1e30
SCALE = HD ** -0.5
LOG2E = float(np.log2(np.e))
VMEM = pl.BlockSpec(memory_space=pltpu.VMEM)
DOC_ROWS = 16


def dot_nn(a, b):
    return lax.dot_general(a, b, (((1,), (0,)), ((), ())), preferred_element_type=jnp.float32)


def dot_nt(a, b):
    return lax.dot_general(a, b, (((1,), (1,)), ((), ())), preferred_element_type=jnp.float32)


def selector(head, r0, rows, tokens, transposed, fine_first=False):
    r1 = 2 * r0
    shape = (tokens, 2 * rows) if transposed else (2 * rows, tokens)
    k = lax.broadcasted_iota(jnp.int32, shape, 1 if transposed else 0)
    p = lax.broadcasted_iota(jnp.int32, shape, 0 if transposed else 1)
    coarse = head % r1
    other = (coarse + r0) % r1
    first, second = jnp.where(fine_first, other, coarse), jnp.where(fine_first, coarse, other)
    target = jnp.where(k < rows, r1 * k + first, r1 * (k - rows) + second)
    return (p == target).astype(jnp.float32).astype(jnp.bfloat16)


def takes_fine(members):
    return lax.axis_index("member") >= members // 2


def pack_keys_kernel(r0, rows, k_in, v_in, doc_in, out, fine_out, k_ref, v_ref, doc_ref, buf, fine, sem):
    tokens = k_ref.shape[0]
    pairs = ((doc_in, doc_ref), (k_in, k_ref), (v_in, v_ref))
    copies = [pltpu.make_async_copy(src, dst, sem.at[i]) for i, (src, dst) in enumerate(pairs)]
    for copy in copies:
        copy.start()
    sels = [selector(h, r0, rows, tokens, False) for h in range(min(H, 2 * r0))]
    for copy in copies:
        copy.wait()
    docs = jnp.broadcast_to(doc_ref[...].astype(jnp.float32).astype(jnp.bfloat16), (DOC_ROWS, tokens))
    for h in range(H):
        for i, ref in enumerate((k_ref, v_ref)):
            x = dot_nn(sels[h % (2 * r0)], ref[:, h * HD:(h + 1) * HD]).astype(jnp.bfloat16)
            buf[h, i * rows:(i + 1) * rows] = x[:rows]
            fine[h, i * rows:(i + 1) * rows] = x[rows:]
        buf[h, 2 * rows:2 * rows + DOC_ROWS] = docs
    sends = [pltpu.make_async_copy(buf, out, sem.at[3]), pltpu.make_async_copy(fine, fine_out, sem.at[4])]
    for copy in sends:
        copy.start()
    for copy in sends:
        copy.wait()


def pack_rest_kernel(r0, rows, members, q_in, g_in, fine_in, out, q_ref, g_ref, buf, sem):
    tokens = q_ref.shape[0]
    pairs = ((q_in, q_ref), (g_in, g_ref), (fine_in, buf.at[:, 4 * rows:6 * rows]))
    copies = [pltpu.make_async_copy(src, dst, sem.at[i]) for i, (src, dst) in enumerate(pairs)]
    for copy in copies:
        copy.start()
    sels = [selector(h, r0, rows, tokens, False, takes_fine(members)) for h in range(min(H, 2 * r0))]
    for copy in copies:
        copy.wait()
    for h in range(H):
        for i, ref in enumerate((q_ref, g_ref)):
            x = dot_nn(sels[h % (2 * r0)], ref[:, h * HD:(h + 1) * HD]).astype(jnp.bfloat16)
            buf[h, i * rows:(1 + i) * rows] = x[:rows]
            buf[h, (2 + i) * rows:(3 + i) * rows] = x[rows:]
    copy = pltpu.make_async_copy(buf, out, sem.at[3])
    copy.start()
    copy.wait()


def main_kernel(r0, rows, members, *refs):
    r1 = 2 * r0
    G = members
    coarse_refs, (own_ref, *swap_refs), cross_refs = refs[:G], refs[G:2 * G], refs[2 * G:3 * G]
    refs = refs[3 * G:]
    out_own, out_kv, out_swap, out_cross = refs[0], refs[1], refs[2:G + 1], refs[G + 1:2 * G + 1]
    (k1, k2, kx, v1, v2, vx, d1, d2, dx, gk1, gk2, gv1, gv2, gkx, gvx) = refs[2 * G + 1:]
    bf16, f32 = jnp.bfloat16, jnp.float32
    tokens = HD
    half = lax.axis_index("half")
    head = lax.axis_index("head")
    member = lax.axis_index("member")
    fine = takes_fine(G)
    partner = G // 2
    partner_ref = swap_refs[partner - 1]

    sel = selector(head, r0, rows, tokens, False)
    query_sel = jnp.where(fine, sel[rows:].astype(f32), sel[:rows].astype(f32)).astype(bf16)
    source_docs = []
    for j in range(H):
        for g in range(G):
            at = pl.ds((j * G + g) * rows, rows)
            ref, base = (own_ref, 4 * rows) if g == 0 else (swap_refs[g - 1], 2 * rows if g == partner else 0)
            k2[at] = ref[j, base:base + rows]
            v2[at] = ref[j, base + rows:base + 2 * rows]
            ref = coarse_refs[g]
            k1[at] = ref[j, 0:rows]
            v1[at] = ref[j, rows:2 * rows]
            doc = ref[j, 2 * rows:2 * rows + DOC_ROWS][0:1]
            if g in (0, partner):
                source_docs.append(doc)
            d1[at] = sel[:rows] * doc
            d2[at] = sel[rows:] * doc
            ref = cross_refs[g]
            kx[at] = ref[2 * j * rows:(2 * j + 1) * rows]
            vx[at] = ref[(2 * j + 1) * rows:(2 * j + 2) * rows]
            dx[at] = sel[:rows] * ref[2 * H * rows:2 * H * rows + DOC_ROWS][j:j + 1]

    eye = (lax.broadcasted_iota(jnp.int32, (HD, HD), 0) == lax.broadcasted_iota(jnp.int32, (HD, HD), 1))
    eye = eye.astype(f32).astype(bf16)
    ones = jnp.ones((HD, HD), bf16)
    transposed = lambda x: dot_nt(eye, x).astype(bf16)
    doc_cols = lambda x: dot_nn(x, ones)[:, 0:1]
    k1t, k2t, kxt = transposed(k1[...]), transposed(k2[...]), transposed(kx[...])
    v1t, v2t, vxt = transposed(v1[...]), transposed(v2[...]), transposed(vx[...])
    docs1, docs2 = doc_cols(d1[...]), doc_cols(d2[...])
    docsx = doc_cols(dx[...]) + jnp.where((half == 0) | fine, 1000.0, 0.0)

    tiles = 2
    per = H // tiles
    nd = per * G * rows
    lanes = per * 2 * rows

    coarse = head % r1
    other = (coarse + r0) % r1
    lane = lax.broadcasted_iota(jnp.int32, (1, lanes), 1)
    qmember = member ^ (partner * ((lane // rows) % 2))
    qpos = (lane // (2 * rows)) * (G * tokens) + qmember * tokens + r1 * (lane % rows) + jnp.where(fine, other, coarse)
    kl = lax.broadcasted_iota(jnp.int32, (nd, 1), 0)
    kmember = member ^ ((kl // rows) % G)
    kpos = (kl // (rows * G)) * (G * tokens) + kmember * tokens + r1 * (kl % rows)
    causal1 = kpos + coarse <= qpos
    causal2 = kpos + other <= qpos
    both = jnp.where(fine, 0.0, 1.0)
    c = SCALE * LOG2E

    for u in reversed(range(tiles)):
        nk = (u + 1) * nd
        x0 = u * nd
        src = range(u * per, (u + 1) * per)
        gather = lambda lo: jnp.concatenate([ref[j, lo:lo + rows] for j in src for ref in (own_ref, partner_ref)], 0)
        qt, gt = gather(0), gather(rows)
        dq = jnp.concatenate([query_sel * source_docs[2 * j + e] for j in src for e in range(2)], 0)
        qdoc = dot_nt(jnp.ones((16, HD), bf16), dq)[0:1]

        def scores(key, docs, causal):
            s = jnp.where(docs == qdoc, dot_nt(key, qt), MASKED)
            if u:
                return jnp.concatenate([s[:x0], jnp.where(causal, s[x0:], MASKED)], 0)
            return jnp.where(causal, s, MASKED)

        s1 = scores(k1[0:nk], docs1[0:nk], causal1)
        s2 = scores(k2[0:nk], docs2[0:nk], causal2)
        sx = jnp.where(docsx[x0:] == qdoc, dot_nt(kx[x0:], qt), MASKED)
        top = jnp.maximum(jnp.maximum(jnp.max(s1, 0, keepdims=True), jnp.max(s2, 0, keepdims=True)), jnp.max(sx, 0, keepdims=True))
        base = top * c
        p1 = jnp.exp2(s1 * c - (base - both))
        p2 = jnp.exp2(s2 * c - base)
        px = jnp.exp2(sx * c - base)
        total = jnp.sum(p1, 0, keepdims=True) + jnp.sum(p2, 0, keepdims=True) + jnp.sum(px, 0, keepdims=True)
        inv = 1.0 / total
        out = dot_nn(v1t[:, :nk], p1.astype(bf16)) + dot_nn(v2t[:, :nk], p2.astype(bf16)) + dot_nn(vxt[:, x0:], px.astype(bf16))
        out = out * inv
        dinv = jnp.sum(dot_nt(eye, gt) * out, 0, keepdims=True) * inv

        def grads(p, value):
            ds = p * (dot_nt(value, gt) * inv - dinv)
            return ds.astype(bf16), (p * inv).astype(bf16)

        ds1, w1 = grads(p1, v1[0:nk])
        ds2, w2 = grads(p2, v2[0:nk])
        dsx, wx = grads(px, vx[x0:])
        gq = (dot_nn(k1t[:, :nk], ds1) + dot_nn(k2t[:, :nk], ds2) + dot_nn(kxt[:, x0:], dsx)) * SCALE

        def add(ref, lo, hi, value):
            if u == tiles - 1:
                ref[lo:hi] = value
                if lo:
                    ref[0:lo] = jnp.zeros((lo, HD), f32)
            else:
                ref[lo:hi] = ref[lo:hi] + value

        add(gk1, 0, nk, dot_nn(ds1, qt))
        add(gk2, 0, nk, dot_nn(ds2, qt))
        add(gv1, 0, nk, dot_nn(w1, gt))
        add(gv2, 0, nk, dot_nn(w2, gt))
        add(gkx, x0, tiles * nd, dot_nn(dsx, qt))
        add(gvx, x0, tiles * nd, dot_nn(wx, gt))
        out = out.T.astype(bf16)
        gq = gq.T.astype(bf16)
        for i, j in enumerate(src):
            for e, ref in enumerate((out_own, out_swap[partner - 1])):
                lo = (2 * i + e) * rows
                ref[j, 0:rows] = out[lo:lo + rows]
                ref[j, rows:2 * rows] = gq[lo:lo + rows]

    for j in range(H):
        for g in range(G):
            at = pl.ds((j * G + g) * rows, rows)
            ref = out_kv if g == 0 else out_swap[g - 1]
            base = 2 * rows if g == partner else 0
            for i, part in enumerate((gk2[at] * SCALE, gv2[at], gk1[at] * SCALE, gv1[at])):
                ref[j, base + i * rows:base + (i + 1) * rows] = part.astype(ref.dtype)
            out_cross[g][j, 0:rows] = (gkx[at] * SCALE).astype(bf16)
            out_cross[g][j, rows:2 * rows] = gvx[at].astype(bf16)


def sum_kernel(rows, members, *refs):
    G = members
    own_ref, kv_ref, swap_refs, cross_refs, out_ref = refs[0], refs[1], refs[2:G + 1], refs[G + 1:2 * G + 1], refs[2 * G + 1]
    f32, bf16 = jnp.float32, jnp.bfloat16
    out_ref[:, 0:2 * rows] = own_ref[...]
    out_ref[:, 2 * rows:4 * rows] = swap_refs[G // 2 - 1][:, 0:2 * rows]
    for j in range(H):
        total = kv_ref[j]
        for g, ref in enumerate(swap_refs, 1):
            base = 2 * rows if g == G // 2 else 0
            total = total + ref[j, base:base + 4 * rows].astype(f32)
        coarse = total[2 * rows:]
        for ref in cross_refs:
            coarse = coarse + ref[j].astype(f32)
        out_ref[j, 4 * rows:6 * rows] = total[:2 * rows].astype(bf16)
        out_ref[j, 6 * rows:8 * rows] = coarse.astype(bf16)


def unpack_kernel(r0, rows, members, in_ref, *refs):
    outs, bufs, sem = refs[:4], refs[4:8], refs[8]
    tokens = bufs[0].shape[0]
    bf16 = jnp.bfloat16
    kinds = range(min(H, 2 * r0))
    query_sels = [selector(h, r0, rows, tokens, True, takes_fine(members)) for h in kinds]
    key_sels = [selector(h, r0, rows, tokens, True, True) for h in kinds]
    copies = []
    for i, base in enumerate((0, 1, 4, 5)):
        for h in range(H):
            sels = query_sels if i < 2 else key_sels
            part = jnp.concatenate([in_ref[h, (base + e) * rows:(base + e + 1) * rows] for e in (0, 2)], 0)
            bufs[i][:, h * HD:(h + 1) * HD] = dot_nn(sels[h % (2 * r0)], part).astype(bf16)
        copies.append(pltpu.make_async_copy(bufs[i], outs[i], sem.at[i]))
        copies[-1].start()
    for copy in copies:
        copy.wait()


def call(kernel, out_shape, scratch=(), limit=16, **more):
    return pl.pallas_call(
        kernel,
        out_shape=out_shape,
        scratch_shapes=list(scratch),
        compiler_params=pltpu.CompilerParams(vmem_limit_bytes=limit * 1024 * 1024),
        **more,
    )


def per_device(members, queries, keys, values, cotangent, doc_ids):
    G = members
    tokens = queries.shape[0]
    devices = 2 * H * G
    r0 = tokens * devices // (2 * SEG)
    rows = tokens // (2 * r0)
    bf16, f32 = jnp.bfloat16, jnp.float32
    shape = jax.ShapeDtypeStruct
    n = H * G * rows
    anywhere = pl.BlockSpec(memory_space=pltpu.HBM)
    wide = pltpu.VMEM((tokens, H * HD), bf16)
    coarse_shape, fine_shape, rest_shape = (H, 2 * rows + DOC_ROWS, HD), (H, 2 * rows, HD), (H, 6 * rows, HD)

    coarse, fine = call(
        functools.partial(pack_keys_kernel, r0, rows), [shape(coarse_shape, bf16), shape(fine_shape, bf16)],
        [wide] * 2 + [pltpu.VMEM((1, tokens), jnp.int32), pltpu.VMEM(coarse_shape, bf16), pltpu.VMEM(fine_shape, bf16),
                      pltpu.SemaphoreType.DMA((5,))],
        limit=64, in_specs=[anywhere] * 3, out_specs=[anywhere] * 2,
    )(keys, values, doc_ids.reshape(1, tokens))
    rest = call(
        functools.partial(pack_rest_kernel, r0, rows, G), shape(rest_shape, bf16),
        [wide] * 2 + [pltpu.VMEM(rest_shape, bf16), pltpu.SemaphoreType.DMA((4,))],
        limit=64, in_specs=[anywhere] * 3, out_specs=anywhere,
    )(queries, cotangent, fine)

    def to_head(x):
        return lax.all_to_all(x, "head", 0, 0, tiled=True)

    def to_member(x, g):
        return lax.ppermute(x, "member", [(i, i ^ g) for i in range(G)])

    def place(half, head, member):
        return (half * H + head) * G + member

    def across(x, g, back):
        pairs = [(place(0, h, m ^ g), place(1, h, m)) for h in range(H) for m in range(G // 2)]
        return lax.ppermute(x, ("half", "head", "member"), [pair[::-1] for pair in pairs] if back else pairs)

    coarse = to_head(coarse)
    docs = jnp.pad(coarse[:, 2 * rows], ((0, DOC_ROWS - H), (0, 0)))
    cross = jnp.concatenate([coarse[:, :2 * rows].reshape(-1, HD), docs], 0)
    crosses = [across(cross, g, False) for g in range(G)]
    coarses = [coarse] + [to_member(coarse, g) for g in range(1, G)]
    own = to_head(rest)
    own, *crosses = lax.optimization_barrier((own, *crosses))
    swaps = [to_member(own[:, (2 if g == G // 2 else 4) * rows:], g) for g in range(1, G)]
    sent = lambda g: (H, (6 if g == G // 2 else 4) * rows, HD)
    outs = call(
        functools.partial(main_kernel, r0, rows, G),
        [shape((H, 2 * rows, HD), bf16), shape((H, 4 * rows, HD), f32)]
        + [shape(sent(g), bf16) for g in range(1, G)] + [shape((H, 2 * rows, HD), bf16)] * G,
        [pltpu.VMEM((n, HD), bf16)] * 9 + [pltpu.VMEM((n, HD), f32)] * 6,
        limit=32,
    )(*coarses, own, *swaps, *crosses)
    crosses = [across(outs[G + 1 + g], g, True) for g in range(G)]
    swaps = [to_member(outs[1 + g], g) for g in range(1, G)]
    back = call(functools.partial(sum_kernel, rows, G), shape((H, 8 * rows, HD), bf16))(
        outs[0], outs[1], *swaps, *crosses)
    back = to_head(back)
    return tuple(call(
        functools.partial(unpack_kernel, r0, rows, G), [shape((tokens, H * HD), bf16)] * 4,
        [wide] * 4 + [pltpu.SemaphoreType.DMA((4,))],
        in_specs=[VMEM], out_specs=[anywhere] * 4,
    )(back))


def solution(mesh):
    members = mesh.shape["seq"] // (2 * H)
    parts = {"seq": [("half", 2), ("head", H), ("member", members)]}
    axes = [part for name in mesh.axis_names for part in parts.get(name, [(name, mesh.shape[name])])]
    inner = Mesh(mesh.devices.reshape([size for _, size in axes]), [name for name, _ in axes])
    split = ("dp", "half", "head", "member")
    in_specs = (P(split, None),) * 4 + (P(split),)
    return jax.shard_map(
        functools.partial(per_device, members), mesh=inner, in_specs=in_specs,
        out_specs=(P(split, None),) * 4, check_vma=False,
    )
```

```python
import functools

import jax
import jax.numpy as jnp
import numpy as np
from jax import lax
from jax.experimental import pallas as pl
from jax.experimental.pallas import tpu as pltpu
from jax.sharding import Mesh
from jax.sharding import PartitionSpec as P

H = 8
HD = 128
SEG = 1024

MASKED = -1e30
SCALE = HD ** -0.5
LOG2E = float(np.log2(np.e))
VMEM = pl.BlockSpec(memory_space=pltpu.VMEM)
DOC_ROWS = 16


def dot_nn(a, b):
    return lax.dot_general(a, b, (((1,), (0,)), ((), ())), preferred_element_type=jnp.float32)


def dot_nt(a, b):
    return lax.dot_general(a, b, (((1,), (1,)), ((), ())), preferred_element_type=jnp.float32)


def selector(head, r0, rows, tokens, transposed, fine_first=False):
    r1 = 2 * r0
    shape = (tokens, 2 * rows) if transposed else (2 * rows, tokens)
    k = lax.broadcasted_iota(jnp.int32, shape, 1 if transposed else 0)
    p = lax.broadcasted_iota(jnp.int32, shape, 0 if transposed else 1)
    coarse = head % r1
    other = (coarse + r0) % r1
    first, second = jnp.where(fine_first, other, coarse), jnp.where(fine_first, coarse, other)
    target = jnp.where(k < rows, r1 * k + first, r1 * (k - rows) + second)
    return (p == target).astype(jnp.float32).astype(jnp.bfloat16)


def takes_fine(members):
    return lax.axis_index("member") >= members // 2


def pack_kernel(r0, rows, members, q_in, k_in, v_in, g_in, doc_in, out, q_ref, k_ref, v_ref, g_ref, doc_ref, buf, sem):
    tokens = q_ref.shape[0]
    pairs = ((doc_in, doc_ref), (k_in, k_ref), (v_in, v_ref), (q_in, q_ref), (g_in, g_ref))
    copies = [pltpu.make_async_copy(src, dst, sem.at[i]) for i, (src, dst) in enumerate(pairs)]
    for copy in copies:
        copy.start()
    kinds = range(min(H, 2 * r0))
    key_sels = [selector(h, r0, rows, tokens, False) for h in kinds]
    query_sels = [selector(h, r0, rows, tokens, False, takes_fine(members)) for h in kinds]

    def pick(sels, h, ref):
        return dot_nn(sels[h % (2 * r0)], ref[:, h * HD:(h + 1) * HD]).astype(jnp.bfloat16)

    for copy in copies:
        copy.wait()
    docs = jnp.broadcast_to(doc_ref[...].astype(jnp.float32).astype(jnp.bfloat16), (DOC_ROWS, tokens))
    sends = []
    for h in range(H):
        for i, ref in enumerate((q_ref, g_ref)):
            x = pick(query_sels, h, ref)
            buf[h, i * rows:(1 + i) * rows] = x[:rows]
            buf[h, (2 + i) * rows:(3 + i) * rows] = x[rows:]
        for i, ref in enumerate((k_ref, v_ref)):
            x = pick(key_sels, h, ref)
            buf[h, (4 + i) * rows:(5 + i) * rows] = x[rows:]
            buf[h, (6 + i) * rows:(7 + i) * rows] = x[:rows]
        buf[h, 8 * rows:8 * rows + DOC_ROWS] = docs
        sends.append(pltpu.make_async_copy(buf.at[h], out.at[h], sem.at[5 + h]))
        sends[-1].start()
    for copy in sends:
        copy.wait()


TILES = 2


def tile_sizes(rows, members):
    per = H // TILES
    return per * members * rows, per * 2 * rows


def eye_matrix():
    shape = (HD, HD)
    same = lax.broadcasted_iota(jnp.int32, shape, 0) == lax.broadcasted_iota(jnp.int32, shape, 1)
    return same.astype(jnp.float32).astype(jnp.bfloat16)


def doc_cols(x):
    return dot_nn(x, jnp.ones((HD, HD), jnp.bfloat16))[:, 0:1]


def local_kernel(r0, rows, members, *refs):
    G = members
    r1 = 2 * r0
    own_ref, swap_refs = refs[0], refs[1:G]
    (k1, k2, q_all, g_all, stats, out_ref, gtt_ref), rest = refs[G:G + 7], refs[G + 7:]
    p_refs, dp_refs, (v1, v2, d1, d2) = rest[:2 * TILES], rest[2 * TILES:4 * TILES], rest[4 * TILES:]
    bf16, f32 = jnp.bfloat16, jnp.float32
    tokens = HD
    head = lax.axis_index("head")
    member = lax.axis_index("member")
    fine = takes_fine(G)
    partner = G // 2
    partner_ref = swap_refs[partner - 1]

    sel = selector(head, r0, rows, tokens, False)
    query_sel = jnp.where(fine, sel[rows:].astype(f32), sel[:rows].astype(f32)).astype(bf16)
    source_docs = []
    for j in range(H):
        for g in range(G):
            at = pl.ds((j * G + g) * rows, rows)
            ref, base = (own_ref, 4 * rows) if g == 0 else (swap_refs[g - 1], 2 * rows if g == partner else 0)
            k2[at] = ref[j, base:base + rows]
            v2[at] = ref[j, base + rows:base + 2 * rows]
            k1[at] = ref[j, base + 2 * rows:base + 3 * rows]
            v1[at] = ref[j, base + 3 * rows:base + 4 * rows]
            doc = ref[j, base + 4 * rows:base + 4 * rows + DOC_ROWS][0:1]
            if g in (0, partner):
                source_docs.append(doc)
            d1[at] = sel[:rows] * doc
            d2[at] = sel[rows:] * doc

    eye = eye_matrix()
    v1t, v2t = dot_nt(eye, v1[...]).astype(bf16), dot_nt(eye, v2[...]).astype(bf16)
    docs1, docs2 = doc_cols(d1[...]), doc_cols(d2[...])
    nd, lanes = tile_sizes(rows, G)
    per = H // TILES

    coarse = head % r1
    other = (coarse + r0) % r1
    lane = lax.broadcasted_iota(jnp.int32, (1, lanes), 1)
    qmember = member ^ (partner * ((lane // rows) % 2))
    qpos = (lane // (2 * rows)) * (G * tokens) + qmember * tokens + r1 * (lane % rows) + jnp.where(fine, other, coarse)
    kl = lax.broadcasted_iota(jnp.int32, (nd, 1), 0)
    kmember = member ^ ((kl // rows) % G)
    kpos = (kl // (rows * G)) * (G * tokens) + kmember * tokens + r1 * (kl % rows)
    causal1 = kpos + coarse <= qpos
    causal2 = kpos + other <= qpos
    both = jnp.where(fine, 0.0, 1.0)
    c = SCALE * LOG2E

    for u in range(TILES):
        nk = (u + 1) * nd
        x0 = u * nd
        src = range(u * per, (u + 1) * per)
        mine = slice(u * lanes, (u + 1) * lanes)
        gather = lambda lo: jnp.concatenate([ref[j, lo:lo + rows] for j in src for ref in (own_ref, partner_ref)], 0)
        qt, gt = gather(0), gather(rows)
        q_all[mine], g_all[mine] = qt, gt
        dq = jnp.concatenate([query_sel * source_docs[2 * j + e] for j in src for e in range(2)], 0)
        qdoc = dot_nt(jnp.ones((16, HD), bf16), dq)[0:1]

        def scores(key, docs, causal):
            s = jnp.where(docs == qdoc, dot_nt(key, qt), MASKED)
            if u:
                return jnp.concatenate([s[:x0], jnp.where(causal, s[x0:], MASKED)], 0)
            return jnp.where(causal, s, MASKED)

        s1 = scores(k1[0:nk], docs1[0:nk], causal1)
        s2 = scores(k2[0:nk], docs2[0:nk], causal2)
        top = jnp.maximum(jnp.max(s1, 0, keepdims=True), jnp.max(s2, 0, keepdims=True))
        base = top * c
        p1 = jnp.exp2(s1 * c - (base - both))
        p2 = jnp.exp2(s2 * c - base)
        stats[0:1, mine] = top
        stats[1:2, mine] = jnp.sum(p1, 0, keepdims=True) + jnp.sum(p2, 0, keepdims=True)
        stats[2:3, mine] = qdoc
        out_ref[:, mine] = dot_nn(v1t[:, :nk], p1.astype(bf16)) + dot_nn(v2t[:, :nk], p2.astype(bf16))
        gtt_ref[:, mine] = dot_nt(eye, gt)
        p_refs[2 * u][...], p_refs[2 * u + 1][...] = p1, p2
        dp_refs[2 * u][...], dp_refs[2 * u + 1][...] = dot_nt(v1[0:nk], gt), dot_nt(v2[0:nk], gt)


def cross_kernel(r0, rows, members, *refs):
    G = members
    cross_refs = refs[0:G]
    q_all, g_all, stats, local_out, gtt_ref = refs[G:G + 5]
    out_cross, (out_ref, gq_ref, new_stats) = refs[G + 5:2 * G + 5], refs[2 * G + 5:2 * G + 8]
    kx, vx, dx, gkx, gvx = refs[2 * G + 8:]
    bf16, f32 = jnp.bfloat16, jnp.float32
    half = lax.axis_index("half")
    head = lax.axis_index("head")
    sel = selector(head, r0, rows, HD, False)
    for j in range(H):
        for g in range(G):
            at = pl.ds((j * G + g) * rows, rows)
            ref = cross_refs[g]
            kx[at] = ref[2 * j * rows:(2 * j + 1) * rows]
            vx[at] = ref[(2 * j + 1) * rows:(2 * j + 2) * rows]
            dx[at] = sel[:rows] * ref[2 * H * rows:2 * H * rows + DOC_ROWS][j:j + 1]
    eye = eye_matrix()
    kxt, vxt = dot_nt(eye, kx[...]).astype(bf16), dot_nt(eye, vx[...]).astype(bf16)
    docsx = doc_cols(dx[...]) + jnp.where((half == 0) | takes_fine(G), 1000.0, 0.0)
    nd, lanes = tile_sizes(rows, G)
    c = SCALE * LOG2E
    for u in range(TILES):
        x0 = u * nd
        mine = slice(u * lanes, (u + 1) * lanes)
        qt, gt = q_all[mine], g_all[mine]
        top0, total0, qdoc = stats[0:1, mine], stats[1:2, mine], stats[2:3, mine]
        sx = jnp.where(docsx[x0:] == qdoc, dot_nt(kx[x0:], qt), MASKED)
        top = jnp.maximum(top0, jnp.max(sx, 0, keepdims=True))
        px = jnp.exp2(sx * c - top * c)
        shrink = jnp.exp2(top0 * c - top * c)
        inv = 1.0 / (total0 * shrink + jnp.sum(px, 0, keepdims=True))
        local_inv = shrink * inv
        out = local_out[:, mine] * local_inv + dot_nn(vxt[:, x0:], px.astype(bf16)) * inv
        dot = jnp.sum(gtt_ref[:, mine] * out, 0, keepdims=True)
        wx = px * inv
        ds = (wx * (dot_nt(vx[x0:], gt) - dot)).astype(bf16)
        wx = wx.astype(bf16)
        new_stats[0:1, mine] = local_inv
        new_stats[1:2, mine] = dot
        out_ref[mine] = out.T.astype(bf16)
        gq_ref[:, mine] = dot_nn(kxt[:, x0:], ds)
        gk, gv = dot_nn(ds, qt), dot_nn(wx, gt)
        if u == 0:
            gkx[...], gvx[...] = gk, gv
        else:
            gkx[x0:] += gk
            gvx[x0:] += gv
    for j in range(H):
        for g in range(G):
            at = pl.ds((j * G + g) * rows, rows)
            out_cross[g][j, 0:rows] = (gkx[at] * SCALE).astype(bf16)
            out_cross[g][j, rows:2 * rows] = gvx[at].astype(bf16)


def grad_kernel(rows, members, *refs):
    G = members
    k1, k2, q_all, g_all, out_ref, gq_ref, stats = refs[:7]
    p_refs, dp_refs = refs[7:7 + 2 * TILES], refs[7 + 2 * TILES:7 + 4 * TILES]
    rest = refs[7 + 4 * TILES:]
    partner = G // 2
    out_own, out_kv, (gk1, gk2, gv1, gv2) = rest[0], rest[1], rest[-4:]
    out_swap = rest[2:-4]
    bf16, f32 = jnp.bfloat16, jnp.float32
    eye = eye_matrix()
    nd, lanes = tile_sizes(rows, G)
    per = H // TILES
    k1t, k2t = dot_nt(eye, k1[...]).astype(bf16), dot_nt(eye, k2[...]).astype(bf16)
    for u in reversed(range(TILES)):
        nk = (u + 1) * nd
        mine = slice(u * lanes, (u + 1) * lanes)
        qt, gt = q_all[mine], g_all[mine]
        inv, dot = stats[0:1, mine], stats[1:2, mine]
        gq = gq_ref[:, mine]
        for i, (kt, gk, gv) in enumerate(((k1t, gk1, gv1), (k2t, gk2, gv2))):
            w = p_refs[2 * u + i][...] * inv
            ds = (w * (dp_refs[2 * u + i][...] - dot)).astype(bf16)
            gq = gq + dot_nn(kt[:, :nk], ds)
            new_k, new_v = dot_nn(ds, qt), dot_nn(w.astype(bf16), gt)
            if u == TILES - 1:
                gk[...], gv[...] = new_k, new_v
            else:
                gk[0:nk] += new_k
                gv[0:nk] += new_v
        gq = (gq * SCALE).T.astype(bf16)
        for i in range(per):
            j = u * per + i
            for e, ref in enumerate((out_own, out_swap[partner - 1])):
                lo = (2 * i + e) * rows
                ref[j, 0:rows] = out_ref[u * lanes + lo:u * lanes + lo + rows]
                ref[j, rows:2 * rows] = gq[lo:lo + rows]
    for j in range(H):
        for g in range(G):
            at = pl.ds((j * G + g) * rows, rows)
            ref = out_kv if g == 0 else out_swap[g - 1]
            base = 2 if g == partner else 0
            for i, part in enumerate((gk2[at] * SCALE, gv2[at], gk1[at] * SCALE, gv1[at]), base):
                ref[j, i * rows:(i + 1) * rows] = part.astype(ref.dtype)


def finish_kernel(r0, rows, members, *refs):
    G = members
    crosses, (q_all, g_all, stats, local_out, gtt, k1, k2), refs = refs[:G], refs[G:G + 7], refs[G + 7:]
    products, refs = refs[:4 * TILES], refs[4 * TILES:]
    out_cross, results, scratch = refs[:G], refs[G:2 * G + 1], refs[2 * G + 1:]
    out, gq, new_stats = scratch[:3]
    cross_kernel(r0, rows, G, *crosses, q_all, g_all, stats, local_out, gtt, *out_cross, *scratch[:8])
    grad_kernel(rows, G, k1, k2, q_all, g_all, out, gq, new_stats, *products, *results, *scratch[8:])


def sum_kernel(rows, members, *refs):
    G = members
    own_ref, kv_ref, swap_refs, cross_refs, out_ref = refs[0], refs[1], refs[2:G + 1], refs[G + 1:2 * G + 1], refs[2 * G + 1]
    f32, bf16 = jnp.float32, jnp.bfloat16
    out_ref[:, 0:2 * rows] = own_ref[...]
    out_ref[:, 2 * rows:4 * rows] = swap_refs[G // 2 - 1][:, 0:2 * rows]
    for j in range(H):
        total = kv_ref[j]
        for g, ref in enumerate(swap_refs, 1):
            base = 2 * rows if g == G // 2 else 0
            total = total + ref[j, base:base + 4 * rows].astype(f32)
        coarse = total[2 * rows:]
        for ref in cross_refs:
            coarse = coarse + ref[j].astype(f32)
        out_ref[j, 4 * rows:6 * rows] = total[:2 * rows].astype(bf16)
        out_ref[j, 6 * rows:8 * rows] = coarse.astype(bf16)


def unpack_kernel(r0, rows, members, in_ref, *refs):
    outs, bufs, sem = refs[:4], refs[4:8], refs[8]
    tokens = bufs[0].shape[0]
    bf16 = jnp.bfloat16
    kinds = range(min(H, 2 * r0))
    query_sels = [selector(h, r0, rows, tokens, True, takes_fine(members)) for h in kinds]
    key_sels = [selector(h, r0, rows, tokens, True, True) for h in kinds]
    copies = []
    for i, base in enumerate((0, 1, 4, 5)):
        for h in range(H):
            sels = query_sels if i < 2 else key_sels
            part = jnp.concatenate([in_ref[h, (base + e) * rows:(base + e + 1) * rows] for e in (0, 2)], 0)
            bufs[i][:, h * HD:(h + 1) * HD] = dot_nn(sels[h % (2 * r0)], part).astype(bf16)
        copies.append(pltpu.make_async_copy(bufs[i], outs[i], sem.at[i]))
        copies[-1].start()
    for copy in copies:
        copy.wait()


def call(kernel, out_shape, scratch=(), limit=16, **more):
    return pl.pallas_call(
        kernel,
        out_shape=out_shape,
        scratch_shapes=list(scratch),
        compiler_params=pltpu.CompilerParams(vmem_limit_bytes=limit * 1024 * 1024),
        **more,
    )


def per_device(members, queries, keys, values, cotangent, doc_ids):
    G = members
    tokens = queries.shape[0]
    devices = 2 * H * G
    r0 = tokens * devices // (2 * SEG)
    rows = tokens // (2 * r0)
    bf16, f32 = jnp.bfloat16, jnp.float32
    shape = jax.ShapeDtypeStruct
    n = H * G * rows
    anywhere = pl.BlockSpec(memory_space=pltpu.HBM)
    wide = pltpu.VMEM((tokens, H * HD), bf16)
    message = (H, 8 * rows + DOC_ROWS, HD)

    packed = call(
        functools.partial(pack_kernel, r0, rows, G), shape(message, bf16),
        [wide] * 4 + [pltpu.VMEM((1, tokens), jnp.int32), pltpu.VMEM(message, bf16), pltpu.SemaphoreType.DMA((5 + H,))],
        limit=64, in_specs=[anywhere] * 5, out_specs=anywhere,
    )(queries, keys, values, cotangent, doc_ids.reshape(1, tokens))

    def to_head(x):
        return lax.all_to_all(x, "head", 0, 0, tiled=True)

    def to_member(x, g):
        return lax.ppermute(x, "member", [(i, i ^ g) for i in range(G)])

    def place(half, head, member):
        return (half * H + head) * G + member

    def across(x, g, back):
        pairs = [(place(0, h, m ^ g), place(1, h, m)) for h in range(H) for m in range(G // 2)]
        return lax.ppermute(x, ("half", "head", "member"), [pair[::-1] for pair in pairs] if back else pairs)

    own = to_head(packed)
    docs = jnp.pad(own[:, 8 * rows], ((0, DOC_ROWS - H), (0, 0)))
    cross = jnp.concatenate([own[:, 6 * rows:8 * rows].reshape(-1, HD), docs], 0)
    crosses = [across(cross, g, False) for g in range(G)]
    swaps = [to_member(own[:, (2 if g == G // 2 else 4) * rows:], g) for g in range(1, G)]
    nd, lanes = tile_sizes(rows, G)
    nq = TILES * lanes
    tile = [shape(((u + 1) * nd, lanes), f32) for u in range(TILES) for _ in range(2)]
    key_rows, key_sums = pltpu.VMEM((n, HD), bf16), pltpu.VMEM((n, HD), f32)
    k1, k2, q_all, g_all, *rest = call(
        functools.partial(local_kernel, r0, rows, G),
        [shape((n, HD), bf16)] * 2 + [shape((nq, HD), bf16)] * 2 + [shape((8, nq), f32)]
        + [shape((HD, nq), f32)] * 2 + tile * 2,
        [key_rows] * 4, limit=32,
    )(own, *swaps)
    sent = lambda g: (H, (6 if g == G // 2 else 4) * rows, HD)
    outs = call(
        functools.partial(finish_kernel, r0, rows, G),
        [shape((H, 2 * rows, HD), bf16)] * G + [shape((H, 2 * rows, HD), bf16), shape((H, 4 * rows, HD), f32)]
        + [shape(sent(g), bf16) for g in range(1, G)],
        [pltpu.VMEM((nq, HD), bf16), pltpu.VMEM((HD, nq), f32), pltpu.VMEM((8, nq), f32)]
        + [key_rows] * 3 + [key_sums] * 6, limit=32,
    )(*crosses, q_all, g_all, *rest[:3], k1, k2, *rest[3:])
    crosses = [across(outs[g], g, True) for g in range(G)]
    swaps = [to_member(outs[G + 1 + g], g) for g in range(1, G)]
    back = call(functools.partial(sum_kernel, rows, G), shape((H, 8 * rows, HD), bf16))(
        outs[G], outs[G + 1], *swaps, *crosses)
    back = to_head(back)
    return tuple(call(
        functools.partial(unpack_kernel, r0, rows, G), [shape((tokens, H * HD), bf16)] * 4,
        [wide] * 4 + [pltpu.SemaphoreType.DMA((4,))],
        in_specs=[VMEM], out_specs=[anywhere] * 4,
    )(back))


def solution(mesh):
    members = mesh.shape["seq"] // (2 * H)
    parts = {"seq": [("half", 2), ("head", H), ("member", members)]}
    axes = [part for name in mesh.axis_names for part in parts.get(name, [(name, mesh.shape[name])])]
    inner = Mesh(mesh.devices.reshape([size for _, size in axes]), [name for name, _ in axes])
    split = ("dp", "half", "head", "member")
    in_specs = (P(split, None),) * 4 + (P(split),)
    return jax.shard_map(
        functools.partial(per_device, members), mesh=inner, in_specs=in_specs,
        out_specs=(P(split, None),) * 4, check_vma=False,
    )
```

```python
import functools

import jax
import jax.numpy as jnp
import numpy as np
from jax import lax
from jax.experimental import pallas as pl
from jax.experimental.pallas import tpu as pltpu
from jax.sharding import Mesh
from jax.sharding import PartitionSpec as P

H = 8
HD = 128
SEG = 1024

MASKED = -1e30
SCALE = HD ** -0.5
LOG2E = float(np.log2(np.e))
VMEM = pl.BlockSpec(memory_space=pltpu.VMEM)
DOC_ROWS = 16


def dot_nn(a, b):
    return lax.dot_general(a, b, (((1,), (0,)), ((), ())), preferred_element_type=jnp.float32)


def dot_nt(a, b):
    return lax.dot_general(a, b, (((1,), (1,)), ((), ())), preferred_element_type=jnp.float32)


def selector(head, r0, rows, tokens, transposed, fine_first=False):
    r1 = 2 * r0
    shape = (tokens, 2 * rows) if transposed else (2 * rows, tokens)
    k = lax.broadcasted_iota(jnp.int32, shape, 1 if transposed else 0)
    p = lax.broadcasted_iota(jnp.int32, shape, 0 if transposed else 1)
    coarse = head % r1
    other = (coarse + r0) % r1
    first, second = jnp.where(fine_first, other, coarse), jnp.where(fine_first, coarse, other)
    target = jnp.where(k < rows, r1 * k + first, r1 * (k - rows) + second)
    return (p == target).astype(jnp.float32).astype(jnp.bfloat16)


def takes_fine(members):
    return lax.axis_index("member") >= members // 2


def pack_kernel(r0, rows, members, q_in, k_in, v_in, g_in, doc_in, out, q_ref, k_ref, v_ref, g_ref, doc_ref, buf, sem):
    tokens = q_ref.shape[0]
    pairs = ((doc_in, doc_ref), (k_in, k_ref), (v_in, v_ref), (q_in, q_ref), (g_in, g_ref))
    copies = [pltpu.make_async_copy(src, dst, sem.at[i]) for i, (src, dst) in enumerate(pairs)]
    for copy in copies:
        copy.start()
    kinds = range(min(H, 2 * r0))
    key_sels = [selector(h, r0, rows, tokens, False) for h in kinds]
    query_sels = [selector(h, r0, rows, tokens, False, takes_fine(members)) for h in kinds]

    def pick(sels, h, ref):
        return dot_nn(sels[h % (2 * r0)], ref[:, h * HD:(h + 1) * HD]).astype(jnp.bfloat16)

    for copy in copies:
        copy.wait()
    docs = jnp.broadcast_to(doc_ref[...].astype(jnp.float32).astype(jnp.bfloat16), (DOC_ROWS, tokens))
    sends = []
    for h in range(H):
        for i, ref in enumerate((q_ref, g_ref)):
            x = pick(query_sels, h, ref)
            buf[h, i * rows:(1 + i) * rows] = x[:rows]
            buf[h, (2 + i) * rows:(3 + i) * rows] = x[rows:]
        for i, ref in enumerate((k_ref, v_ref)):
            x = pick(key_sels, h, ref)
            buf[h, (4 + i) * rows:(5 + i) * rows] = x[rows:]
            buf[h, (6 + i) * rows:(7 + i) * rows] = x[:rows]
        buf[h, 8 * rows:8 * rows + DOC_ROWS] = docs
        sends.append(pltpu.make_async_copy(buf.at[h], out.at[h], sem.at[5 + h]))
        sends[-1].start()
    for copy in sends:
        copy.wait()


TILES = 2


def tile_sizes(rows, members):
    per = H // TILES
    return per * members * rows, per * 2 * rows


def eye_matrix():
    shape = (HD, HD)
    same = lax.broadcasted_iota(jnp.int32, shape, 0) == lax.broadcasted_iota(jnp.int32, shape, 1)
    return same.astype(jnp.float32).astype(jnp.bfloat16)


def doc_cols(x):
    return dot_nn(x, jnp.ones((HD, HD), jnp.bfloat16))[:, 0:1]


def local_kernel(r0, rows, members, *refs):
    G = members
    r1 = 2 * r0
    own_ref, swap_refs = refs[0], refs[1:G]
    (k1, k2, q_all, g_all, stats, out_ref, gtt_ref), rest = refs[G:G + 7], refs[G + 7:]
    p_refs, dp_refs, (v1, v2, d1, d2) = rest[:2 * TILES], rest[2 * TILES:4 * TILES], rest[4 * TILES:]
    bf16, f32 = jnp.bfloat16, jnp.float32
    tokens = HD
    head = lax.axis_index("head")
    member = lax.axis_index("member")
    fine = takes_fine(G)
    partner = G // 2
    partner_ref = swap_refs[partner - 1]

    sel = selector(head, r0, rows, tokens, False)
    query_sel = jnp.where(fine, sel[rows:].astype(f32), sel[:rows].astype(f32)).astype(bf16)
    source_docs = []
    for j in range(H):
        for g in range(G):
            at = pl.ds((j * G + g) * rows, rows)
            ref, base = (own_ref, 4 * rows) if g == 0 else (swap_refs[g - 1], 2 * rows if g == partner else 0)
            k2[at] = ref[j, base:base + rows]
            v2[at] = ref[j, base + rows:base + 2 * rows]
            k1[at] = ref[j, base + 2 * rows:base + 3 * rows]
            v1[at] = ref[j, base + 3 * rows:base + 4 * rows]
            doc = ref[j, base + 4 * rows:base + 4 * rows + DOC_ROWS][0:1]
            if g in (0, partner):
                source_docs.append(doc)
            d1[at] = sel[:rows] * doc
            d2[at] = sel[rows:] * doc

    eye = eye_matrix()
    v1t, v2t = dot_nt(eye, v1[...]).astype(bf16), dot_nt(eye, v2[...]).astype(bf16)
    docs1, docs2 = doc_cols(d1[...]), doc_cols(d2[...])
    nd, lanes = tile_sizes(rows, G)
    per = H // TILES

    coarse = head % r1
    other = (coarse + r0) % r1
    lane = lax.broadcasted_iota(jnp.int32, (1, lanes), 1)
    qmember = member ^ (partner * ((lane // rows) % 2))
    qpos = (lane // (2 * rows)) * (G * tokens) + qmember * tokens + r1 * (lane % rows) + jnp.where(fine, other, coarse)
    kl = lax.broadcasted_iota(jnp.int32, (nd, 1), 0)
    kmember = member ^ ((kl // rows) % G)
    kpos = (kl // (rows * G)) * (G * tokens) + kmember * tokens + r1 * (kl % rows)
    causal1 = kpos + coarse <= qpos
    causal2 = kpos + other <= qpos
    both = jnp.where(fine, 0.0, 1.0)
    c = SCALE * LOG2E

    for u in range(TILES):
        nk = (u + 1) * nd
        x0 = u * nd
        src = range(u * per, (u + 1) * per)
        mine = slice(u * lanes, (u + 1) * lanes)
        gather = lambda lo: jnp.concatenate([ref[j, lo:lo + rows] for j in src for ref in (own_ref, partner_ref)], 0)
        qt, gt = gather(0), gather(rows)
        q_all[mine], g_all[mine] = qt, gt
        dq = jnp.concatenate([query_sel * source_docs[2 * j + e] for j in src for e in range(2)], 0)
        qdoc = dot_nt(jnp.ones((16, HD), bf16), dq)[0:1]

        def scores(key, docs, causal):
            s = jnp.where(docs == qdoc, dot_nt(key, qt), MASKED)
            if u:
                return jnp.concatenate([s[:x0], jnp.where(causal, s[x0:], MASKED)], 0)
            return jnp.where(causal, s, MASKED)

        s1 = scores(k1[0:nk], docs1[0:nk], causal1)
        s2 = scores(k2[0:nk], docs2[0:nk], causal2)
        top = jnp.maximum(jnp.max(s1, 0, keepdims=True), jnp.max(s2, 0, keepdims=True))
        base = top * c
        p1 = jnp.exp2(s1 * c - (base - both))
        p2 = jnp.exp2(s2 * c - base)
        stats[0:1, mine] = top
        stats[1:2, mine] = jnp.sum(p1, 0, keepdims=True) + jnp.sum(p2, 0, keepdims=True)
        stats[2:3, mine] = qdoc
        out_ref[:, mine] = dot_nn(v1t[:, :nk], p1.astype(bf16)) + dot_nn(v2t[:, :nk], p2.astype(bf16))
        gtt_ref[:, mine] = dot_nt(eye, gt)
        p_refs[2 * u][...], p_refs[2 * u + 1][...] = p1, p2
        dp_refs[2 * u][...], dp_refs[2 * u + 1][...] = dot_nt(v1[0:nk], gt), dot_nt(v2[0:nk], gt)


def cross_kernel(r0, rows, members, *refs):
    G = members
    cross_refs = refs[0:G]
    q_all, g_all, stats, local_out, gtt_ref = refs[G:G + 5]
    out_cross, (out_ref, gq_ref, new_stats) = refs[G + 5:2 * G + 5], refs[2 * G + 5:2 * G + 8]
    kx, vx, dx, gkx, gvx = refs[2 * G + 8:]
    bf16, f32 = jnp.bfloat16, jnp.float32
    half = lax.axis_index("half")
    head = lax.axis_index("head")
    sel = selector(head, r0, rows, HD, False)
    for j in range(H):
        for g in range(G):
            at = pl.ds((j * G + g) * rows, rows)
            ref = cross_refs[g]
            kx[at] = ref[2 * j * rows:(2 * j + 1) * rows]
            vx[at] = ref[(2 * j + 1) * rows:(2 * j + 2) * rows]
            dx[at] = sel[:rows] * ref[2 * H * rows:2 * H * rows + DOC_ROWS][j:j + 1]
    eye = eye_matrix()
    kxt, vxt = dot_nt(eye, kx[...]).astype(bf16), dot_nt(eye, vx[...]).astype(bf16)
    docsx = doc_cols(dx[...]) + jnp.where((half == 0) | takes_fine(G), 1000.0, 0.0)
    nd, lanes = tile_sizes(rows, G)
    c = SCALE * LOG2E
    for u in range(TILES):
        x0 = u * nd
        mine = slice(u * lanes, (u + 1) * lanes)
        qt, gt = q_all[mine], g_all[mine]
        top0, total0, qdoc = stats[0:1, mine], stats[1:2, mine], stats[2:3, mine]
        sx = jnp.where(docsx[x0:] == qdoc, dot_nt(kx[x0:], qt), MASKED)
        top = jnp.maximum(top0, jnp.max(sx, 0, keepdims=True))
        px = jnp.exp2(sx * c - top * c)
        shrink = jnp.exp2(top0 * c - top * c)
        inv = 1.0 / (total0 * shrink + jnp.sum(px, 0, keepdims=True))
        local_inv = shrink * inv
        out = local_out[:, mine] * local_inv + dot_nn(vxt[:, x0:], px.astype(bf16)) * inv
        dot = jnp.sum(gtt_ref[:, mine] * out, 0, keepdims=True)
        wx = px * inv
        ds = (wx * (dot_nt(vx[x0:], gt) - dot)).astype(bf16)
        wx = wx.astype(bf16)
        new_stats[0:1, mine] = local_inv
        new_stats[1:2, mine] = dot
        out_ref[mine] = out.T.astype(bf16)
        gq_ref[:, mine] = dot_nn(kxt[:, x0:], ds)
        gk, gv = dot_nn(ds, qt), dot_nn(wx, gt)
        if u == 0:
            gkx[...], gvx[...] = gk, gv
        else:
            gkx[x0:] += gk
            gvx[x0:] += gv
    for j in range(H):
        for g in range(G):
            at = pl.ds((j * G + g) * rows, rows)
            out_cross[g][j, 0:rows] = (gkx[at] * SCALE).astype(bf16)
            out_cross[g][j, rows:2 * rows] = gvx[at].astype(bf16)


def grad_kernel(rows, members, *refs):
    G = members
    k1, k2, q_all, g_all, out_ref, gq_ref, stats = refs[:7]
    p_refs, dp_refs = refs[7:7 + 2 * TILES], refs[7 + 2 * TILES:7 + 4 * TILES]
    rest = refs[7 + 4 * TILES:]
    partner = G // 2
    out_own, out_kv, (gk1, gk2, gv1, gv2) = rest[0], rest[1], rest[-4:]
    out_swap = rest[2:-4]
    bf16, f32 = jnp.bfloat16, jnp.float32
    eye = eye_matrix()
    nd, lanes = tile_sizes(rows, G)
    per = H // TILES
    k1t, k2t = dot_nt(eye, k1[...]).astype(bf16), dot_nt(eye, k2[...]).astype(bf16)
    for u in reversed(range(TILES)):
        nk = (u + 1) * nd
        mine = slice(u * lanes, (u + 1) * lanes)
        qt, gt = q_all[mine], g_all[mine]
        inv, dot = stats[0:1, mine], stats[1:2, mine]
        gq = gq_ref[:, mine]
        for i, (kt, gk, gv) in enumerate(((k1t, gk1, gv1), (k2t, gk2, gv2))):
            w = p_refs[2 * u + i][...] * inv
            ds = (w * (dp_refs[2 * u + i][...] - dot)).astype(bf16)
            gq = gq + dot_nn(kt[:, :nk], ds)
            new_k, new_v = dot_nn(ds, qt), dot_nn(w.astype(bf16), gt)
            if u == TILES - 1:
                gk[...], gv[...] = new_k, new_v
            else:
                gk[0:nk] += new_k
                gv[0:nk] += new_v
        gq = (gq * SCALE).T.astype(bf16)
        for i in range(per):
            j = u * per + i
            for e, ref in enumerate((out_own, out_swap[partner - 1])):
                lo = (2 * i + e) * rows
                ref[j, 0:rows] = out_ref[u * lanes + lo:u * lanes + lo + rows]
                ref[j, rows:2 * rows] = gq[lo:lo + rows]
    for j in range(H):
        for g in range(G):
            at = pl.ds((j * G + g) * rows, rows)
            ref = out_kv if g == 0 else out_swap[g - 1]
            base = 2 if g == partner else 0
            for i, part in enumerate((gk2[at] * SCALE, gv2[at], gk1[at] * SCALE, gv1[at]), base):
                ref[j, i * rows:(i + 1) * rows] = part.astype(ref.dtype)


def finish_kernel(r0, rows, members, *refs):
    G = members
    crosses, (q_all, g_all, stats, local_out, gtt, k1, k2), refs = refs[:G], refs[G:G + 7], refs[G + 7:]
    products, refs = refs[:4 * TILES], refs[4 * TILES:]
    out_cross, results, scratch = refs[:G], refs[G:2 * G + 1], refs[2 * G + 1:]
    out, gq, new_stats = scratch[:3]
    cross_kernel(r0, rows, G, *crosses, q_all, g_all, stats, local_out, gtt, *out_cross, *scratch[:8])
    grad_kernel(rows, G, k1, k2, q_all, g_all, out, gq, new_stats, *products, *results, *scratch[8:])


def sum_kernel(rows, members, kv_ref, *refs):
    G = members
    swap_refs, cross_refs, out_ref = refs[:G - 1], refs[G - 1:-1], refs[-1]
    f32 = jnp.float32
    for i in range(2):
        total = kv_ref[:, 2 * i * rows:2 * (i + 1) * rows]
        for g, ref in enumerate(swap_refs, 1):
            base = 2 * (i + (g == G // 2))
            total = total + ref[:, base * rows:(base + 2) * rows].astype(f32)
        if i == 1:
            for ref in cross_refs:
                total = total + ref[...].astype(f32)
        out_ref[:, 2 * i * rows:2 * (i + 1) * rows] = total.astype(jnp.bfloat16)


def unpack_kernel(r0, rows, members, query_ref, key_ref, *refs):
    outs, bufs, sem = refs[:4], refs[4:8], refs[8]
    tokens = bufs[0].shape[0]
    bf16 = jnp.bfloat16
    kinds = range(min(H, 2 * r0))
    query_sels = [selector(h, r0, rows, tokens, True, takes_fine(members)) for h in kinds]
    key_sels = [selector(h, r0, rows, tokens, True, True) for h in kinds]
    copies = []
    for i in range(4):
        ref, sels, base = (query_ref, query_sels, i) if i < 2 else (key_ref, key_sels, i - 2)
        for h in range(H):
            part = jnp.concatenate([ref[h, (base + e) * rows:(base + e + 1) * rows] for e in (0, 2)], 0)
            bufs[i][:, h * HD:(h + 1) * HD] = dot_nn(sels[h % (2 * r0)], part).astype(bf16)
        copies.append(pltpu.make_async_copy(bufs[i], outs[i], sem.at[i]))
        copies[-1].start()
    for copy in copies:
        copy.wait()


def call(kernel, out_shape, scratch=(), limit=16, **more):
    return pl.pallas_call(
        kernel,
        out_shape=out_shape,
        scratch_shapes=list(scratch),
        compiler_params=pltpu.CompilerParams(vmem_limit_bytes=limit * 1024 * 1024),
        **more,
    )


def per_device(members, queries, keys, values, cotangent, doc_ids):
    G = members
    tokens = queries.shape[0]
    devices = 2 * H * G
    r0 = tokens * devices // (2 * SEG)
    rows = tokens // (2 * r0)
    bf16, f32 = jnp.bfloat16, jnp.float32
    shape = jax.ShapeDtypeStruct
    n = H * G * rows
    anywhere = pl.BlockSpec(memory_space=pltpu.HBM)
    wide = pltpu.VMEM((tokens, H * HD), bf16)
    message = (H, 8 * rows + DOC_ROWS, HD)

    packed = call(
        functools.partial(pack_kernel, r0, rows, G), shape(message, bf16),
        [wide] * 4 + [pltpu.VMEM((1, tokens), jnp.int32), pltpu.VMEM(message, bf16), pltpu.SemaphoreType.DMA((5 + H,))],
        limit=64, in_specs=[anywhere] * 5, out_specs=anywhere,
    )(queries, keys, values, cotangent, doc_ids.reshape(1, tokens))

    def to_head(x):
        return lax.all_to_all(x, "head", 0, 0, tiled=True)

    def to_member(x, g):
        return lax.ppermute(x, "member", [(i, i ^ g) for i in range(G)])

    def place(half, head, member):
        return (half * H + head) * G + member

    def across(x, g, back):
        pairs = [(place(0, h, m ^ g), place(1, h, m)) for h in range(H) for m in range(G // 2)]
        return lax.ppermute(x, ("half", "head", "member"), [pair[::-1] for pair in pairs] if back else pairs)

    own = to_head(packed)
    docs = jnp.pad(own[:, 8 * rows], ((0, DOC_ROWS - H), (0, 0)))
    cross = jnp.concatenate([own[:, 6 * rows:8 * rows].reshape(-1, HD), docs], 0)
    crosses = [across(cross, g, False) for g in range(G)]
    swaps = [to_member(own[:, (2 if g == G // 2 else 4) * rows:], g) for g in range(1, G)]
    nd, lanes = tile_sizes(rows, G)
    nq = TILES * lanes
    tile = [shape(((u + 1) * nd, lanes), f32) for u in range(TILES) for _ in range(2)]
    key_rows, key_sums = pltpu.VMEM((n, HD), bf16), pltpu.VMEM((n, HD), f32)
    k1, k2, q_all, g_all, *rest = call(
        functools.partial(local_kernel, r0, rows, G),
        [shape((n, HD), bf16)] * 2 + [shape((nq, HD), bf16)] * 2 + [shape((8, nq), f32)]
        + [shape((HD, nq), f32)] * 2 + tile * 2,
        [key_rows] * 4, limit=32,
    )(own, *swaps)
    sent = lambda g: (H, (6 if g == G // 2 else 4) * rows, HD)
    outs = call(
        functools.partial(finish_kernel, r0, rows, G),
        [shape((H, 2 * rows, HD), bf16)] * G + [shape((H, 2 * rows, HD), bf16), shape((H, 4 * rows, HD), f32)]
        + [shape(sent(g), bf16) for g in range(1, G)],
        [pltpu.VMEM((nq, HD), bf16), pltpu.VMEM((HD, nq), f32), pltpu.VMEM((8, nq), f32)]
        + [key_rows] * 3 + [key_sums] * 6, limit=32,
    )(*crosses, q_all, g_all, *rest[:3], k1, k2, *rest[3:])
    crosses = [across(outs[g], g, True) for g in range(G)]
    swaps = [to_member(outs[G + 1 + g], g) for g in range(1, G)]
    from_queries = jnp.concatenate([outs[G], swaps[G // 2 - 1][:, :2 * rows]], 1)
    first_half = lax.axis_index("half") == 0
    early = lax.cond(first_half, to_head, jnp.zeros_like, from_queries)
    early, *crosses = lax.optimization_barrier((early, *crosses))
    from_keys = call(functools.partial(sum_kernel, rows, G), shape((H, 4 * rows, HD), bf16))(
        outs[G + 1], *swaps, *crosses)

    def keys_alone(early, from_queries, from_keys):
        return early, to_head(from_keys)

    def all_at_once(early, from_queries, from_keys):
        back = to_head(jnp.concatenate([from_queries, from_keys], 1))
        return back[:, :4 * rows], back[:, 4 * rows:]

    back = lax.cond(first_half, keys_alone, all_at_once, early, from_queries, from_keys)
    return tuple(call(
        functools.partial(unpack_kernel, r0, rows, G), [shape((tokens, H * HD), bf16)] * 4,
        [wide] * 4 + [pltpu.SemaphoreType.DMA((4,))],
        in_specs=[VMEM] * 2, out_specs=[anywhere] * 4,
    )(*back))


def solution(mesh):
    members = mesh.shape["seq"] // (2 * H)
    parts = {"seq": [("half", 2), ("head", H), ("member", members)]}
    axes = [part for name in mesh.axis_names for part in parts.get(name, [(name, mesh.shape[name])])]
    inner = Mesh(mesh.devices.reshape([size for _, size in axes]), [name for name, _ in axes])
    split = ("dp", "half", "head", "member")
    in_specs = (P(split, None),) * 4 + (P(split),)
    return jax.shard_map(
        functools.partial(per_device, members), mesh=inner, in_specs=in_specs,
        out_specs=(P(split, None),) * 4, check_vma=False,
    )
```

```python
import functools

import jax
import jax.numpy as jnp
import numpy as np
from jax import lax
from jax.experimental import pallas as pl
from jax.experimental.pallas import tpu as pltpu
from jax.sharding import Mesh
from jax.sharding import PartitionSpec as P

H = 8
HD = 128
SEG = 1024

MASKED = -1e30
SCALE = HD ** -0.5
LOG2E = float(np.log2(np.e))
VMEM = pl.BlockSpec(memory_space=pltpu.VMEM)
DOC_ROWS = 16


def dot_nn(a, b):
    return lax.dot_general(a, b, (((1,), (0,)), ((), ())), preferred_element_type=jnp.float32)


def dot_nt(a, b):
    return lax.dot_general(a, b, (((1,), (1,)), ((), ())), preferred_element_type=jnp.float32)


def selector(head, r0, rows, tokens, transposed, fine_first=False):
    r1 = 2 * r0
    shape = (tokens, 2 * rows) if transposed else (2 * rows, tokens)
    k = lax.broadcasted_iota(jnp.int32, shape, 1 if transposed else 0)
    p = lax.broadcasted_iota(jnp.int32, shape, 0 if transposed else 1)
    coarse = head % r1
    other = (coarse + r0) % r1
    first, second = jnp.where(fine_first, other, coarse), jnp.where(fine_first, coarse, other)
    target = jnp.where(k < rows, r1 * k + first, r1 * (k - rows) + second)
    return (p == target).astype(jnp.float32).astype(jnp.bfloat16)


def takes_fine(members):
    return lax.axis_index("member") >= members // 2


def pack_kernel(r0, rows, members, q_in, k_in, v_in, g_in, doc_in, out, q_ref, k_ref, v_ref, g_ref, doc_ref, buf, sem):
    tokens = q_ref.shape[0]
    pairs = ((doc_in, doc_ref), (k_in, k_ref), (v_in, v_ref), (q_in, q_ref), (g_in, g_ref))
    copies = [pltpu.make_async_copy(src, dst, sem.at[i]) for i, (src, dst) in enumerate(pairs)]
    for copy in copies:
        copy.start()
    kinds = range(min(H, 2 * r0))
    key_sels = [selector(h, r0, rows, tokens, False) for h in kinds]
    query_sels = [selector(h, r0, rows, tokens, False, takes_fine(members)) for h in kinds]

    def pick(sels, h, ref):
        return dot_nn(sels[h % (2 * r0)], ref[:, h * HD:(h + 1) * HD]).astype(jnp.bfloat16)

    for copy in copies:
        copy.wait()
    docs = jnp.broadcast_to(doc_ref[...].astype(jnp.float32).astype(jnp.bfloat16), (DOC_ROWS, tokens))
    sends = []
    for h in range(H):
        for i, ref in enumerate((q_ref, g_ref)):
            x = pick(query_sels, h, ref)
            buf[h, i * rows:(1 + i) * rows] = x[:rows]
            buf[h, (2 + i) * rows:(3 + i) * rows] = x[rows:]
        for i, ref in enumerate((k_ref, v_ref)):
            x = pick(key_sels, h, ref)
            buf[h, (4 + i) * rows:(5 + i) * rows] = x[rows:]
            buf[h, (6 + i) * rows:(7 + i) * rows] = x[:rows]
        buf[h, 8 * rows:8 * rows + DOC_ROWS] = docs
        sends.append(pltpu.make_async_copy(buf.at[h], out.at[h], sem.at[5 + h]))
        sends[-1].start()
    for copy in sends:
        copy.wait()


TILES = 2


def tile_sizes(rows, members):
    per = H // TILES
    return per * members * rows, per * 2 * rows


def eye_matrix():
    shape = (HD, HD)
    same = lax.broadcasted_iota(jnp.int32, shape, 0) == lax.broadcasted_iota(jnp.int32, shape, 1)
    return same.astype(jnp.float32).astype(jnp.bfloat16)


def doc_cols(x):
    return dot_nn(x, jnp.ones((HD, HD), jnp.bfloat16))[:, 0:1]


def local_kernel(r0, rows, members, *refs):
    G = members
    r1 = 2 * r0
    own_ref, swap_refs = refs[0], refs[1:G]
    (k1, k2, q_all, g_all, stats, out_ref, gtt_ref), rest = refs[G:G + 7], refs[G + 7:]
    p_refs, dp_refs, (v1, v2, d1, d2) = rest[:2 * TILES], rest[2 * TILES:4 * TILES], rest[4 * TILES:]
    bf16, f32 = jnp.bfloat16, jnp.float32
    tokens = HD
    head = lax.axis_index("head")
    member = lax.axis_index("member")
    fine = takes_fine(G)
    partner = G // 2
    partner_ref = swap_refs[partner - 1]

    sel = selector(head, r0, rows, tokens, False)
    query_sel = jnp.where(fine, sel[rows:].astype(f32), sel[:rows].astype(f32)).astype(bf16)
    source_docs = []
    for j in range(H):
        for g in range(G):
            at = pl.ds((j * G + g) * rows, rows)
            ref, base = (own_ref, 4 * rows) if g == 0 else (swap_refs[g - 1], 2 * rows if g == partner else 0)
            k2[at] = ref[j, base:base + rows]
            v2[at] = ref[j, base + rows:base + 2 * rows]
            k1[at] = ref[j, base + 2 * rows:base + 3 * rows]
            v1[at] = ref[j, base + 3 * rows:base + 4 * rows]
            doc = ref[j, base + 4 * rows:base + 4 * rows + DOC_ROWS][0:1]
            if g in (0, partner):
                source_docs.append(doc)
            d1[at] = sel[:rows] * doc
            d2[at] = sel[rows:] * doc

    eye = eye_matrix()
    v1t, v2t = dot_nt(eye, v1[...]).astype(bf16), dot_nt(eye, v2[...]).astype(bf16)
    docs1, docs2 = doc_cols(d1[...]), doc_cols(d2[...])
    nd, lanes = tile_sizes(rows, G)
    per = H // TILES

    coarse = head % r1
    other = (coarse + r0) % r1
    lane = lax.broadcasted_iota(jnp.int32, (1, lanes), 1)
    qmember = member ^ (partner * ((lane // rows) % 2))
    qpos = (lane // (2 * rows)) * (G * tokens) + qmember * tokens + r1 * (lane % rows) + jnp.where(fine, other, coarse)
    kl = lax.broadcasted_iota(jnp.int32, (nd, 1), 0)
    kmember = member ^ ((kl // rows) % G)
    kpos = (kl // (rows * G)) * (G * tokens) + kmember * tokens + r1 * (kl % rows)
    causal1 = kpos + coarse <= qpos
    causal2 = kpos + other <= qpos
    both = jnp.where(fine, 0.0, 1.0)
    c = SCALE * LOG2E

    for u in range(TILES):
        nk = (u + 1) * nd
        x0 = u * nd
        src = range(u * per, (u + 1) * per)
        mine = slice(u * lanes, (u + 1) * lanes)
        gather = lambda lo: jnp.concatenate([ref[j, lo:lo + rows] for j in src for ref in (own_ref, partner_ref)], 0)
        qt, gt = gather(0), gather(rows)
        q_all[mine], g_all[mine] = qt, gt
        dq = jnp.concatenate([query_sel * source_docs[2 * j + e] for j in src for e in range(2)], 0)
        qdoc = dot_nt(jnp.ones((16, HD), bf16), dq)[0:1]

        def scores(key, docs, causal):
            s = jnp.where(docs == qdoc, dot_nt(key, qt), MASKED)
            if u:
                return jnp.concatenate([s[:x0], jnp.where(causal, s[x0:], MASKED)], 0)
            return jnp.where(causal, s, MASKED)

        s1 = scores(k1[0:nk], docs1[0:nk], causal1)
        s2 = scores(k2[0:nk], docs2[0:nk], causal2)
        top = jnp.maximum(jnp.max(s1, 0, keepdims=True), jnp.max(s2, 0, keepdims=True))
        base = top * c
        p1 = jnp.exp2(s1 * c - (base - both))
        p2 = jnp.exp2(s2 * c - base)
        stats[0:1, mine] = top
        stats[1:2, mine] = jnp.sum(p1, 0, keepdims=True) + jnp.sum(p2, 0, keepdims=True)
        stats[2:3, mine] = qdoc
        out_ref[:, mine] = dot_nn(v1t[:, :nk], p1.astype(bf16)) + dot_nn(v2t[:, :nk], p2.astype(bf16))
        gtt_ref[:, mine] = dot_nt(eye, gt)
        p_refs[2 * u][...], p_refs[2 * u + 1][...] = p1, p2
        dp_refs[2 * u][...], dp_refs[2 * u + 1][...] = dot_nt(v1[0:nk], gt), dot_nt(v2[0:nk], gt)


def cross_kernel(r0, rows, members, *refs):
    G = members
    cross_refs = refs[0:G]
    q_all, g_all, stats, local_out, gtt_ref = refs[G:G + 5]
    far_stats, out_ref, gq_ref, new_stats, kx, vx, dx = refs[G + 5:]
    bf16, f32 = jnp.bfloat16, jnp.float32
    half = lax.axis_index("half")
    head = lax.axis_index("head")
    sel = selector(head, r0, rows, HD, False)
    for j in range(H):
        for g in range(G):
            at = pl.ds((j * G + g) * rows, rows)
            ref = cross_refs[g]
            kx[at] = ref[2 * j * rows:(2 * j + 1) * rows]
            vx[at] = ref[(2 * j + 1) * rows:(2 * j + 2) * rows]
            dx[at] = sel[:rows] * ref[2 * H * rows:2 * H * rows + DOC_ROWS][j:j + 1]
    eye = eye_matrix()
    kxt, vxt = dot_nt(eye, kx[...]).astype(bf16), dot_nt(eye, vx[...]).astype(bf16)
    docsx = doc_cols(dx[...]) + jnp.where((half == 0) | takes_fine(G), 1000.0, 0.0)
    nd, lanes = tile_sizes(rows, G)
    c = SCALE * LOG2E
    for u in range(TILES):
        x0 = u * nd
        mine = slice(u * lanes, (u + 1) * lanes)
        qt, gt = q_all[mine], g_all[mine]
        top0, total0, qdoc = stats[0:1, mine], stats[1:2, mine], stats[2:3, mine]
        sx = jnp.where(docsx[x0:] == qdoc, dot_nt(kx[x0:], qt), MASKED)
        top = jnp.maximum(top0, jnp.max(sx, 0, keepdims=True))
        px = jnp.exp2(sx * c - top * c)
        shrink = jnp.exp2(top0 * c - top * c)
        total = total0 * shrink + jnp.sum(px, 0, keepdims=True)
        inv = 1.0 / total
        local_inv = shrink * inv
        out = local_out[:, mine] * local_inv + dot_nn(vxt[:, x0:], px.astype(bf16)) * inv
        dot = jnp.sum(gtt_ref[:, mine] * out, 0, keepdims=True)
        ds = (px * inv * (dot_nt(vx[x0:], gt) - dot)).astype(bf16)
        new_stats[0:1, mine] = local_inv
        new_stats[1:2, mine] = dot
        far_stats[0:1, mine] = top * c + jnp.log(total) * LOG2E
        far_stats[1:2, mine] = dot
        far_stats[2:3, mine] = qdoc
        out_ref[mine] = out.T.astype(bf16)
        gq_ref[:, mine] = dot_nn(kxt[:, x0:], ds)


def grad_kernel(rows, members, *refs):
    G = members
    k1, k2, q_all, g_all, out_ref, gq_ref, stats = refs[:7]
    p_refs, dp_refs = refs[7:7 + 2 * TILES], refs[7 + 2 * TILES:7 + 4 * TILES]
    rest = refs[7 + 4 * TILES:]
    partner = G // 2
    out_own, out_kv, (gk1, gk2, gv1, gv2) = rest[0], rest[1], rest[-4:]
    out_swap = rest[2:-4]
    bf16, f32 = jnp.bfloat16, jnp.float32
    eye = eye_matrix()
    nd, lanes = tile_sizes(rows, G)
    per = H // TILES
    k1t, k2t = dot_nt(eye, k1[...]).astype(bf16), dot_nt(eye, k2[...]).astype(bf16)
    for u in reversed(range(TILES)):
        nk = (u + 1) * nd
        mine = slice(u * lanes, (u + 1) * lanes)
        qt, gt = q_all[mine], g_all[mine]
        inv, dot = stats[0:1, mine], stats[1:2, mine]
        gq = gq_ref[:, mine]
        for i, (kt, gk, gv) in enumerate(((k1t, gk1, gv1), (k2t, gk2, gv2))):
            w = p_refs[2 * u + i][...] * inv
            ds = (w * (dp_refs[2 * u + i][...] - dot)).astype(bf16)
            gq = gq + dot_nn(kt[:, :nk], ds)
            new_k, new_v = dot_nn(ds, qt), dot_nn(w.astype(bf16), gt)
            if u == TILES - 1:
                gk[...], gv[...] = new_k, new_v
            else:
                gk[0:nk] += new_k
                gv[0:nk] += new_v
        gq = (gq * SCALE).T.astype(bf16)
        for i in range(per):
            j = u * per + i
            for e, ref in enumerate((out_own, out_swap[partner - 1])):
                lo = (2 * i + e) * rows
                ref[j, 0:rows] = out_ref[u * lanes + lo:u * lanes + lo + rows]
                ref[j, rows:2 * rows] = gq[lo:lo + rows]
    for j in range(H):
        for g in range(G):
            at = pl.ds((j * G + g) * rows, rows)
            ref = out_kv if g == 0 else out_swap[g - 1]
            base = 2 if g == partner else 0
            for i, part in enumerate((gk2[at] * SCALE, gv2[at], gk1[at] * SCALE, gv1[at]), base):
                ref[j, i * rows:(i + 1) * rows] = part.astype(ref.dtype)


def finish_kernel(r0, rows, members, *refs):
    G = members
    crosses, (q_all, g_all, stats, local_out, gtt, k1, k2), refs = refs[:G], refs[G:G + 7], refs[G + 7:]
    products, refs = refs[:4 * TILES], refs[4 * TILES:]
    far_stats, results, scratch = refs[0], refs[1:G + 2], refs[G + 2:]
    out, gq, new_stats = scratch[:3]
    cross_kernel(r0, rows, G, *crosses, q_all, g_all, stats, local_out, gtt, far_stats, *scratch[:6])
    grad_kernel(rows, G, k1, k2, q_all, g_all, out, gq, new_stats, *products, *results, *scratch[6:])


def far_grads(r0, rows, members, own_ref, query_refs, stat_refs, gk, gv):
    G = members
    bf16 = jnp.bfloat16
    head, member = lax.axis_index("head"), lax.axis_index("member")
    sel = selector(head, r0, rows, HD, False)[:rows]
    per = H // TILES
    nd, lanes = per * rows, per * 2 * rows
    c = SCALE * LOG2E
    gk[...], gv[...] = jnp.zeros_like(gk), jnp.zeros_like(gv)
    keys, values = (jnp.concatenate([own_ref[j, lo * rows:(lo + 1) * rows] for j in range(H)], 0) for lo in (6, 7))
    docs = doc_cols(jnp.concatenate([sel * own_ref[j, 8 * rows:8 * rows + DOC_ROWS][0:1] for j in range(H)], 0))
    for g in range(G):

        @pl.when((lax.axis_index("half") == 0) & ((member ^ g) < G // 2))
        def _(g=g):
            pair = (query_refs[g], query_refs[g ^ (G // 2)])
            for u in range(TILES):
                x0 = u * nd
                mine = slice(u * lanes, (u + 1) * lanes)
                qt, gt = (
                    jnp.concatenate([ref[(2 * j + lo) * rows:(2 * j + lo + 1) * rows]
                                     for j in range(u * per, (u + 1) * per) for ref in pair], 0)
                    for lo in range(2))
                lse, dot, qdoc = (stat_refs[g][i:i + 1, mine] for i in range(3))
                p = jnp.where(docs[x0:] == qdoc, jnp.exp2(dot_nt(keys[x0:], qt) * c - lse), 0.0)
                ds = p * (dot_nt(values[x0:], gt) - dot)
                gk[x0:] += dot_nn(ds.astype(bf16), qt) * SCALE
                gv[x0:] += dot_nn(p.astype(bf16), gt)


def sum_kernel(r0, rows, members, *refs):
    G = members
    message_ref, query_refs, stat_refs, refs = refs[0], refs[1:G + 1], refs[G + 1:2 * G + 1], refs[2 * G + 1:]
    own_ref, kv_ref, swap_refs, (out_ref, gk, gv) = refs[0], refs[1], refs[2:G + 1], refs[G + 1:]
    f32, bf16 = jnp.float32, jnp.bfloat16
    far_grads(r0, rows, G, message_ref, query_refs, stat_refs, gk, gv)
    out_ref[:, 0:2 * rows] = own_ref[...]
    out_ref[:, 2 * rows:4 * rows] = swap_refs[G // 2 - 1][:, 0:2 * rows]
    for j in range(H):
        total = kv_ref[j]
        for g, ref in enumerate(swap_refs, 1):
            base = 2 * rows if g == G // 2 else 0
            total = total + ref[j, base:base + 4 * rows].astype(f32)
        mine = slice(j * rows, (j + 1) * rows)
        out_ref[j, 4 * rows:6 * rows] = total[:2 * rows].astype(bf16)
        out_ref[j, 6 * rows:7 * rows] = (total[2 * rows:3 * rows] + gk[mine]).astype(bf16)
        out_ref[j, 7 * rows:8 * rows] = (total[3 * rows:] + gv[mine]).astype(bf16)


def unpack_kernel(r0, rows, members, in_ref, *refs):
    outs, bufs, sem = refs[:4], refs[4:8], refs[8]
    tokens = bufs[0].shape[0]
    bf16 = jnp.bfloat16
    kinds = range(min(H, 2 * r0))
    query_sels = [selector(h, r0, rows, tokens, True, takes_fine(members)) for h in kinds]
    key_sels = [selector(h, r0, rows, tokens, True, True) for h in kinds]
    copies = []
    for i, base in enumerate((0, 1, 4, 5)):
        for h in range(H):
            sels = query_sels if i < 2 else key_sels
            part = jnp.concatenate([in_ref[h, (base + e) * rows:(base + e + 1) * rows] for e in (0, 2)], 0)
            bufs[i][:, h * HD:(h + 1) * HD] = dot_nn(sels[h % (2 * r0)], part).astype(bf16)
        copies.append(pltpu.make_async_copy(bufs[i], outs[i], sem.at[i]))
        copies[-1].start()
    for copy in copies:
        copy.wait()


def call(kernel, out_shape, scratch=(), limit=16, **more):
    return pl.pallas_call(
        kernel,
        out_shape=out_shape,
        scratch_shapes=list(scratch),
        compiler_params=pltpu.CompilerParams(vmem_limit_bytes=limit * 1024 * 1024),
        **more,
    )


def per_device(members, queries, keys, values, cotangent, doc_ids):
    G = members
    tokens = queries.shape[0]
    devices = 2 * H * G
    r0 = tokens * devices // (2 * SEG)
    rows = tokens // (2 * r0)
    bf16, f32 = jnp.bfloat16, jnp.float32
    shape = jax.ShapeDtypeStruct
    n = H * G * rows
    anywhere = pl.BlockSpec(memory_space=pltpu.HBM)
    wide = pltpu.VMEM((tokens, H * HD), bf16)
    message = (H, 8 * rows + DOC_ROWS, HD)

    packed = call(
        functools.partial(pack_kernel, r0, rows, G), shape(message, bf16),
        [wide] * 4 + [pltpu.VMEM((1, tokens), jnp.int32), pltpu.VMEM(message, bf16), pltpu.SemaphoreType.DMA((5 + H,))],
        limit=64, in_specs=[anywhere] * 5, out_specs=anywhere,
    )(queries, keys, values, cotangent, doc_ids.reshape(1, tokens))

    def to_head(x):
        return lax.all_to_all(x, "head", 0, 0, tiled=True)

    def to_member(x, g):
        return lax.ppermute(x, "member", [(i, i ^ g) for i in range(G)])

    def place(half, head, member):
        return (half * H + head) * G + member

    def across(x, g):
        pairs = [(place(half, h, m), place(1 - half, h, m ^ g)) for half in range(2) for h in range(H) for m in range(G)]
        return lax.ppermute(x, ("half", "head", "member"), pairs)

    own = to_head(packed)
    queries_here = jnp.where(takes_fine(G), own[:, 2 * rows:4 * rows], own[:, :2 * rows])
    sent_across = jnp.where(lax.axis_index("half") == 0, own[:, 6 * rows:8 * rows], queries_here)
    docs = jnp.pad(own[:, 8 * rows], ((0, DOC_ROWS - H), (0, 0)))
    cross = across(jnp.concatenate([sent_across.reshape(-1, HD), docs], 0), 0)
    crosses = [cross] + [to_member(cross, g) for g in range(1, G)]
    swaps = [to_member(own[:, (2 if g == G // 2 else 4) * rows:], g) for g in range(1, G)]
    nd, lanes = tile_sizes(rows, G)
    nq = TILES * lanes
    tile = [shape(((u + 1) * nd, lanes), f32) for u in range(TILES) for _ in range(2)]
    key_rows, key_sums = pltpu.VMEM((n, HD), bf16), pltpu.VMEM((n, HD), f32)
    k1, k2, q_all, g_all, *rest = call(
        functools.partial(local_kernel, r0, rows, G),
        [shape((n, HD), bf16)] * 2 + [shape((nq, HD), bf16)] * 2 + [shape((8, nq), f32)]
        + [shape((HD, nq), f32)] * 2 + tile * 2,
        [key_rows] * 4, limit=32,
    )(own, *swaps)
    sent = lambda g: (H, (6 if g == G // 2 else 4) * rows, HD)
    outs = call(
        functools.partial(finish_kernel, r0, rows, G),
        [shape((8, nq), f32), shape((H, 2 * rows, HD), bf16), shape((H, 4 * rows, HD), f32)]
        + [shape(sent(g), bf16) for g in range(1, G)],
        [pltpu.VMEM((nq, HD), bf16), pltpu.VMEM((HD, nq), f32), pltpu.VMEM((8, nq), f32)]
        + [key_rows] * 3 + [key_sums] * 4, limit=32,
    )(*crosses, q_all, g_all, *rest[:3], k1, k2, *rest[3:])
    far_stats = [across(outs[0], g) for g in range(G)]
    swaps = [to_member(outs[2 + g], g) for g in range(1, G)]
    back = call(
        functools.partial(sum_kernel, r0, rows, G), shape((H, 8 * rows, HD), bf16),
        [pltpu.VMEM((H * rows, HD), f32)] * 2,
    )(own, *crosses, *far_stats, outs[1], outs[2], *swaps)
    back = to_head(back)
    return tuple(call(
        functools.partial(unpack_kernel, r0, rows, G), [shape((tokens, H * HD), bf16)] * 4,
        [wide] * 4 + [pltpu.SemaphoreType.DMA((4,))],
        in_specs=[VMEM], out_specs=[anywhere] * 4,
    )(back))


def solution(mesh):
    members = mesh.shape["seq"] // (2 * H)
    parts = {"seq": [("half", 2), ("head", H), ("member", members)]}
    axes = [part for name in mesh.axis_names for part in parts.get(name, [(name, mesh.shape[name])])]
    inner = Mesh(mesh.devices.reshape([size for _, size in axes]), [name for name, _ in axes])
    split = ("dp", "half", "head", "member")
    in_specs = (P(split, None),) * 4 + (P(split),)
    return jax.shard_map(
        functools.partial(per_device, members), mesh=inner, in_specs=in_specs,
        out_specs=(P(split, None),) * 4, check_vma=False,
    )
```

```python
import functools

import jax
import jax.numpy as jnp
import numpy as np
from jax import lax
from jax.experimental import pallas as pl
from jax.experimental.pallas import tpu as pltpu
from jax.sharding import Mesh
from jax.sharding import PartitionSpec as P

H = 8
HD = 128
SEG = 1024

MASKED = -1e30
SCALE = HD ** -0.5
LOG2E = float(np.log2(np.e))
VMEM = pl.BlockSpec(memory_space=pltpu.VMEM)
DOC_ROWS = 16


def dot_nn(a, b):
    return lax.dot_general(a, b, (((1,), (0,)), ((), ())), preferred_element_type=jnp.float32)


def dot_nt(a, b):
    return lax.dot_general(a, b, (((1,), (1,)), ((), ())), preferred_element_type=jnp.float32)


def selector(head, r0, rows, tokens, transposed, fine_first=False):
    r1 = 2 * r0
    shape = (tokens, 2 * rows) if transposed else (2 * rows, tokens)
    k = lax.broadcasted_iota(jnp.int32, shape, 1 if transposed else 0)
    p = lax.broadcasted_iota(jnp.int32, shape, 0 if transposed else 1)
    coarse = head % r1
    other = (coarse + r0) % r1
    first, second = jnp.where(fine_first, other, coarse), jnp.where(fine_first, coarse, other)
    target = jnp.where(k < rows, r1 * k + first, r1 * (k - rows) + second)
    return (p == target).astype(jnp.float32).astype(jnp.bfloat16)


def takes_fine(members):
    return lax.axis_index("member") >= members // 2


def pack_kernel(r0, rows, members, q_in, k_in, v_in, g_in, doc_in, out, q_ref, k_ref, v_ref, g_ref, doc_ref, buf, sem):
    tokens = q_ref.shape[0]
    pairs = ((doc_in, doc_ref), (k_in, k_ref), (v_in, v_ref), (q_in, q_ref), (g_in, g_ref))
    copies = [pltpu.make_async_copy(src, dst, sem.at[i]) for i, (src, dst) in enumerate(pairs)]
    for copy in copies:
        copy.start()
    kinds = range(min(H, 2 * r0))
    key_sels = [selector(h, r0, rows, tokens, False) for h in kinds]
    query_sels = [selector(h, r0, rows, tokens, False, takes_fine(members)) for h in kinds]

    def pick(sels, h, ref):
        return dot_nn(sels[h % (2 * r0)], ref[:, h * HD:(h + 1) * HD]).astype(jnp.bfloat16)

    for copy in copies:
        copy.wait()
    docs = jnp.broadcast_to(doc_ref[...].astype(jnp.float32).astype(jnp.bfloat16), (DOC_ROWS, tokens))
    sends = []
    for h in range(H):
        for i, ref in enumerate((q_ref, g_ref)):
            x = pick(query_sels, h, ref)
            buf[h, i * rows:(1 + i) * rows] = x[:rows]
            buf[h, (2 + i) * rows:(3 + i) * rows] = x[rows:]
        for i, ref in enumerate((k_ref, v_ref)):
            x = pick(key_sels, h, ref)
            buf[h, (4 + i) * rows:(5 + i) * rows] = x[rows:]
            buf[h, (6 + i) * rows:(7 + i) * rows] = x[:rows]
        buf[h, 8 * rows:8 * rows + DOC_ROWS] = docs
        sends.append(pltpu.make_async_copy(buf.at[h], out.at[h], sem.at[5 + h]))
        sends[-1].start()
    for copy in sends:
        copy.wait()


TILES = 2


def tile_sizes(rows, members):
    per = H // TILES
    return per * members * rows, per * 2 * rows


def eye_matrix():
    shape = (HD, HD)
    same = lax.broadcasted_iota(jnp.int32, shape, 0) == lax.broadcasted_iota(jnp.int32, shape, 1)
    return same.astype(jnp.float32).astype(jnp.bfloat16)


def doc_cols(x):
    return dot_nn(x, jnp.ones((HD, HD), jnp.bfloat16))[:, 0:1]


def local_kernel(r0, rows, members, *refs):
    G = members
    r1 = 2 * r0
    own_ref, swap_refs = refs[0], refs[1:G]
    (k1, k2, q_all, g_all, stats, out_ref, gtt_ref), rest = refs[G:G + 7], refs[G + 7:]
    p_refs, dp_refs, (v1, v2, d1, d2) = rest[:2 * TILES], rest[2 * TILES:4 * TILES], rest[4 * TILES:]
    bf16, f32 = jnp.bfloat16, jnp.float32
    tokens = HD
    head = lax.axis_index("head")
    member = lax.axis_index("member")
    fine = takes_fine(G)
    partner = G // 2
    partner_ref = swap_refs[partner - 1]

    sel = selector(head, r0, rows, tokens, False)
    query_sel = jnp.where(fine, sel[rows:].astype(f32), sel[:rows].astype(f32)).astype(bf16)
    source_docs = []
    for j in range(H):
        for g in range(G):
            at = pl.ds((j * G + g) * rows, rows)
            ref, base = (own_ref, 4 * rows) if g == 0 else (swap_refs[g - 1], 2 * rows if g == partner else 0)
            k2[at] = ref[j, base:base + rows]
            v2[at] = ref[j, base + rows:base + 2 * rows]
            k1[at] = ref[j, base + 2 * rows:base + 3 * rows]
            v1[at] = ref[j, base + 3 * rows:base + 4 * rows]
            doc = ref[j, base + 4 * rows:base + 4 * rows + DOC_ROWS][0:1]
            if g in (0, partner):
                source_docs.append(doc)
            d1[at] = sel[:rows] * doc
            d2[at] = sel[rows:] * doc

    eye = eye_matrix()
    v1t, v2t = dot_nt(eye, v1[...]).astype(bf16), dot_nt(eye, v2[...]).astype(bf16)
    docs1, docs2 = doc_cols(d1[...]), doc_cols(d2[...])
    nd, lanes = tile_sizes(rows, G)
    per = H // TILES

    coarse = head % r1
    other = (coarse + r0) % r1
    lane = lax.broadcasted_iota(jnp.int32, (1, lanes), 1)
    qmember = member ^ (partner * ((lane // rows) % 2))
    qpos = (lane // (2 * rows)) * (G * tokens) + qmember * tokens + r1 * (lane % rows) + jnp.where(fine, other, coarse)
    kl = lax.broadcasted_iota(jnp.int32, (nd, 1), 0)
    kmember = member ^ ((kl // rows) % G)
    kpos = (kl // (rows * G)) * (G * tokens) + kmember * tokens + r1 * (kl % rows)
    causal1 = kpos + coarse <= qpos
    causal2 = kpos + other <= qpos
    both = jnp.where(fine, 0.0, 1.0)
    c = SCALE * LOG2E

    for u in range(TILES):
        nk = (u + 1) * nd
        x0 = u * nd
        src = range(u * per, (u + 1) * per)
        mine = slice(u * lanes, (u + 1) * lanes)
        gather = lambda lo: jnp.concatenate([ref[j, lo:lo + rows] for j in src for ref in (own_ref, partner_ref)], 0)
        qt, gt = gather(0), gather(rows)
        q_all[mine], g_all[mine] = qt, gt
        dq = jnp.concatenate([query_sel * source_docs[2 * j + e] for j in src for e in range(2)], 0)
        qdoc = dot_nt(jnp.ones((16, HD), bf16), dq)[0:1]

        def scores(key, docs, causal):
            s = jnp.where(docs == qdoc, dot_nt(key, qt), MASKED)
            if u:
                return jnp.concatenate([s[:x0], jnp.where(causal, s[x0:], MASKED)], 0)
            return jnp.where(causal, s, MASKED)

        s1 = scores(k1[0:nk], docs1[0:nk], causal1)
        s2 = scores(k2[0:nk], docs2[0:nk], causal2)
        top = jnp.maximum(jnp.max(s1, 0, keepdims=True), jnp.max(s2, 0, keepdims=True))
        base = top * c
        p1 = jnp.exp2(s1 * c - (base - both))
        p2 = jnp.exp2(s2 * c - base)
        stats[0:1, mine] = top
        stats[1:2, mine] = jnp.sum(p1, 0, keepdims=True) + jnp.sum(p2, 0, keepdims=True)
        stats[2:3, mine] = qdoc
        out_ref[:, mine] = dot_nn(v1t[:, :nk], p1.astype(bf16)) + dot_nn(v2t[:, :nk], p2.astype(bf16))
        gtt_ref[:, mine] = dot_nt(eye, gt)
        p_refs[2 * u][...], p_refs[2 * u + 1][...] = p1, p2
        dp_refs[2 * u][...], dp_refs[2 * u + 1][...] = dot_nt(v1[0:nk], gt), dot_nt(v2[0:nk], gt)


def cross_kernel(r0, rows, members, *refs):
    G = members
    cross_refs = refs[0:G]
    q_all, g_all, stats, local_out, gtt_ref = refs[G:G + 5]
    far_stats, out_ref, gq_ref, new_stats, kx, vx, dx = refs[G + 5:]
    bf16, f32 = jnp.bfloat16, jnp.float32
    half = lax.axis_index("half")
    head = lax.axis_index("head")
    sel = selector(head, r0, rows, HD, False)
    for j in range(H):
        for g in range(G):
            at = pl.ds((j * G + g) * rows, rows)
            ref = cross_refs[g]
            kx[at] = ref[2 * j * rows:(2 * j + 1) * rows]
            vx[at] = ref[(2 * j + 1) * rows:(2 * j + 2) * rows]
            dx[at] = sel[:rows] * ref[2 * H * rows:2 * H * rows + DOC_ROWS][j:j + 1]
    eye = eye_matrix()
    kxt, vxt = dot_nt(eye, kx[...]).astype(bf16), dot_nt(eye, vx[...]).astype(bf16)
    docsx = doc_cols(dx[...]) + jnp.where((half == 0) | takes_fine(G), 1000.0, 0.0)
    nd, lanes = tile_sizes(rows, G)
    c = SCALE * LOG2E
    for u in range(TILES):
        x0 = u * nd
        mine = slice(u * lanes, (u + 1) * lanes)
        qt, gt = q_all[mine], g_all[mine]
        top0, total0, qdoc = stats[0:1, mine], stats[1:2, mine], stats[2:3, mine]
        sx = jnp.where(docsx[x0:] == qdoc, dot_nt(kx[x0:], qt), MASKED)
        top = jnp.maximum(top0, jnp.max(sx, 0, keepdims=True))
        px = jnp.exp2(sx * c - top * c)
        shrink = jnp.exp2(top0 * c - top * c)
        total = total0 * shrink + jnp.sum(px, 0, keepdims=True)
        inv = 1.0 / total
        local_inv = shrink * inv
        out = local_out[:, mine] * local_inv + dot_nn(vxt[:, x0:], px.astype(bf16)) * inv
        dot = jnp.sum(gtt_ref[:, mine] * out, 0, keepdims=True)
        ds = (px * inv * (dot_nt(vx[x0:], gt) - dot)).astype(bf16)
        new_stats[0:1, mine] = local_inv
        new_stats[1:2, mine] = dot
        far_stats[0:1, mine] = top * c + jnp.log(total) * LOG2E
        far_stats[1:2, mine] = dot
        far_stats[2:3, mine] = qdoc
        out_ref[mine] = out.T.astype(bf16)
        gq_ref[:, mine] = dot_nn(kxt[:, x0:], ds)


def grad_kernel(rows, members, *refs):
    G = members
    k1, k2, q_all, g_all, out_ref, gq_ref, stats = refs[:7]
    p_refs, dp_refs = refs[7:7 + 2 * TILES], refs[7 + 2 * TILES:7 + 4 * TILES]
    rest = refs[7 + 4 * TILES:]
    partner = G // 2
    out_own, out_kv, (gk1, gk2, gv1, gv2) = rest[0], rest[1], rest[-4:]
    out_swap = rest[2:-4]
    bf16, f32 = jnp.bfloat16, jnp.float32
    eye = eye_matrix()
    nd, lanes = tile_sizes(rows, G)
    per = H // TILES
    k1t, k2t = dot_nt(eye, k1[...]).astype(bf16), dot_nt(eye, k2[...]).astype(bf16)
    for u in reversed(range(TILES)):
        nk = (u + 1) * nd
        mine = slice(u * lanes, (u + 1) * lanes)
        qt, gt = q_all[mine], g_all[mine]
        inv, dot = stats[0:1, mine], stats[1:2, mine]
        gq = gq_ref[:, mine]
        for i, (kt, gk, gv) in enumerate(((k1t, gk1, gv1), (k2t, gk2, gv2))):
            w = p_refs[2 * u + i][...] * inv
            ds = (w * (dp_refs[2 * u + i][...] - dot)).astype(bf16)
            gq = gq + dot_nn(kt[:, :nk], ds)
            new_k, new_v = dot_nn(ds, qt), dot_nn(w.astype(bf16), gt)
            if u == TILES - 1:
                gk[...], gv[...] = new_k, new_v
            else:
                gk[0:nk] += new_k
                gv[0:nk] += new_v
        gq = (gq * SCALE).T.astype(bf16)
        for i in range(per):
            j = u * per + i
            for e, ref in enumerate((out_own, out_swap[partner - 1])):
                lo = (2 * i + e) * rows
                ref[j, 0:rows] = out_ref[u * lanes + lo:u * lanes + lo + rows]
                ref[j, rows:2 * rows] = gq[lo:lo + rows]
    for j in range(H):
        for g in range(G):
            at = pl.ds((j * G + g) * rows, rows)
            ref = out_kv if g == 0 else out_swap[g - 1]
            base = 2 if g == partner else 0
            for i, part in enumerate((gk2[at] * SCALE, gv2[at], gk1[at] * SCALE, gv1[at]), base):
                ref[j, i * rows:(i + 1) * rows] = part.astype(ref.dtype)


def finish_kernel(r0, rows, members, *refs):
    G = members
    crosses, (q_all, g_all, stats, local_out, gtt, k1, k2), refs = refs[:G], refs[G:G + 7], refs[G + 7:]
    products, refs = refs[:4 * TILES], refs[4 * TILES:]
    far_stats, results, scratch = refs[0], refs[1:G + 2], refs[G + 2:]
    out, gq, new_stats = scratch[:3]
    cross_kernel(r0, rows, G, *crosses, q_all, g_all, stats, local_out, gtt, far_stats, *scratch[:6])
    grad_kernel(rows, G, k1, k2, q_all, g_all, out, gq, new_stats, *products, *results, *scratch[6:])


def far_grads(r0, rows, members, own_ref, query_refs, stat_refs, gk, gv):
    G = members
    bf16 = jnp.bfloat16
    head, member = lax.axis_index("head"), lax.axis_index("member")
    sel = selector(head, r0, rows, HD, False)[:rows]
    per = H // TILES
    nd, lanes = per * rows, per * 2 * rows
    c = SCALE * LOG2E
    gk[...], gv[...] = jnp.zeros_like(gk), jnp.zeros_like(gv)
    keys, values = (jnp.concatenate([own_ref[j, lo * rows:(lo + 1) * rows] for j in range(H)], 0) for lo in (6, 7))
    docs = doc_cols(jnp.concatenate([sel * own_ref[j, 8 * rows:8 * rows + DOC_ROWS][0:1] for j in range(H)], 0))
    for g in range(G):

        @pl.when((lax.axis_index("half") == 0) & ((member ^ g) < G // 2))
        def _(g=g):
            pair = (query_refs[g], query_refs[g ^ (G // 2)])
            for u in range(TILES):
                x0 = u * nd
                mine = slice(u * lanes, (u + 1) * lanes)
                qt, gt = (
                    jnp.concatenate([ref[(2 * j + lo) * rows:(2 * j + lo + 1) * rows]
                                     for j in range(u * per, (u + 1) * per) for ref in pair], 0)
                    for lo in range(2))
                lse, dot, qdoc = (stat_refs[g][i:i + 1, mine] for i in range(3))
                p = jnp.where(docs[x0:] == qdoc, jnp.exp2(dot_nt(keys[x0:], qt) * c - lse), 0.0)
                ds = p * (dot_nt(values[x0:], gt) - dot)
                gk[x0:] += dot_nn(ds.astype(bf16), qt) * SCALE
                gv[x0:] += dot_nn(p.astype(bf16), gt)


def sum_kernel(r0, rows, members, *refs):
    G = members
    message_ref, query_refs, stat_refs, refs = refs[0], refs[1:G + 1], refs[G + 1:2 * G + 1], refs[2 * G + 1:]
    own_ref, kv_ref, swap_refs, (out_ref, gk, gv) = refs[0], refs[1], refs[2:G + 1], refs[G + 1:]
    f32, bf16 = jnp.float32, jnp.bfloat16
    far_grads(r0, rows, G, message_ref, query_refs, stat_refs, gk, gv)
    out_ref[:, 0:2 * rows] = own_ref[...]
    out_ref[:, 2 * rows:4 * rows] = swap_refs[G // 2 - 1][:, 0:2 * rows]
    for j in range(H):
        total = kv_ref[j]
        for g, ref in enumerate(swap_refs, 1):
            base = 2 * rows if g == G // 2 else 0
            total = total + ref[j, base:base + 4 * rows].astype(f32)
        mine = slice(j * rows, (j + 1) * rows)
        out_ref[j, 4 * rows:6 * rows] = total[:2 * rows].astype(bf16)
        out_ref[j, 6 * rows:7 * rows] = (total[2 * rows:3 * rows] + gk[mine]).astype(bf16)
        out_ref[j, 7 * rows:8 * rows] = (total[3 * rows:] + gv[mine]).astype(bf16)


def unpack_kernel(r0, rows, members, in_ref, *refs):
    outs, bufs, sem = refs[:4], refs[4:8], refs[8]
    tokens = bufs[0].shape[0]
    bf16 = jnp.bfloat16
    kinds = range(min(H, 2 * r0))
    query_sels = [selector(h, r0, rows, tokens, True, takes_fine(members)) for h in kinds]
    key_sels = [selector(h, r0, rows, tokens, True, True) for h in kinds]
    copies = []
    for i, base in enumerate((0, 1, 4, 5)):
        for h in range(H):
            sels = query_sels if i < 2 else key_sels
            part = jnp.concatenate([in_ref[h, (base + e) * rows:(base + e + 1) * rows] for e in (0, 2)], 0)
            bufs[i][:, h * HD:(h + 1) * HD] = dot_nn(sels[h % (2 * r0)], part).astype(bf16)
        copies.append(pltpu.make_async_copy(bufs[i], outs[i], sem.at[i]))
        copies[-1].start()
    for copy in copies:
        copy.wait()


def call(kernel, out_shape, scratch=(), limit=16, **more):
    return pl.pallas_call(
        kernel,
        out_shape=out_shape,
        scratch_shapes=list(scratch),
        compiler_params=pltpu.CompilerParams(vmem_limit_bytes=limit * 1024 * 1024),
        **more,
    )


def per_device(members, queries, keys, values, cotangent, doc_ids):
    G = members
    tokens = queries.shape[0]
    devices = 2 * H * G
    r0 = tokens * devices // (2 * SEG)
    rows = tokens // (2 * r0)
    bf16, f32 = jnp.bfloat16, jnp.float32
    shape = jax.ShapeDtypeStruct
    n = H * G * rows
    anywhere = pl.BlockSpec(memory_space=pltpu.HBM)
    wide = pltpu.VMEM((tokens, H * HD), bf16)
    message = (H, 8 * rows + DOC_ROWS, HD)

    packed = call(
        functools.partial(pack_kernel, r0, rows, G), shape(message, bf16),
        [wide] * 4 + [pltpu.VMEM((1, tokens), jnp.int32), pltpu.VMEM(message, bf16), pltpu.SemaphoreType.DMA((5 + H,))],
        limit=64, in_specs=[anywhere] * 5, out_specs=anywhere,
    )(queries, keys, values, cotangent, doc_ids.reshape(1, tokens))

    def to_head(x):
        return lax.all_to_all(x, "head", 0, 0, tiled=True)

    def to_member(x, g):
        return lax.ppermute(x, "member", [(i, i ^ g) for i in range(G)])

    def across(x):
        return lax.ppermute(x, "half", [(0, 1), (1, 0)])

    own = to_head(packed)
    queries_here = jnp.where(takes_fine(G), own[:, 2 * rows:4 * rows], own[:, :2 * rows])
    sent_across = jnp.where(lax.axis_index("half") == 0, own[:, 6 * rows:8 * rows], queries_here)
    docs = jnp.pad(own[:, 8 * rows], ((0, DOC_ROWS - H), (0, 0)))
    cross = across(jnp.concatenate([sent_across.reshape(-1, HD), docs], 0))
    swaps = [to_member(own[:, (2 if g == G // 2 else 4) * rows:], g) for g in range(1, G)]
    nd, lanes = tile_sizes(rows, G)
    nq = TILES * lanes
    tile = [shape(((u + 1) * nd, lanes), f32) for u in range(TILES) for _ in range(2)]
    key_rows, key_sums = pltpu.VMEM((n, HD), bf16), pltpu.VMEM((n, HD), f32)
    k1, k2, q_all, g_all, *rest = call(
        functools.partial(local_kernel, r0, rows, G),
        [shape((n, HD), bf16)] * 2 + [shape((nq, HD), bf16)] * 2 + [shape((8, nq), f32)]
        + [shape((HD, nq), f32)] * 2 + tile * 2,
        [key_rows] * 4, limit=32,
    )(own, *swaps)
    cross, k1 = lax.optimization_barrier((cross, k1))
    crosses = [cross] + [to_member(cross, g) for g in range(1, G)]
    sent = lambda g: (H, (6 if g == G // 2 else 4) * rows, HD)
    outs = call(
        functools.partial(finish_kernel, r0, rows, G),
        [shape((8, nq), f32), shape((H, 2 * rows, HD), bf16), shape((H, 4 * rows, HD), f32)]
        + [shape(sent(g), bf16) for g in range(1, G)],
        [pltpu.VMEM((nq, HD), bf16), pltpu.VMEM((HD, nq), f32), pltpu.VMEM((8, nq), f32)]
        + [key_rows] * 3 + [key_sums] * 4, limit=32,
    )(*crosses, q_all, g_all, *rest[:3], k1, k2, *rest[3:])
    far_stats = across(outs[0])
    far_stats = [far_stats] + [to_member(far_stats, g) for g in range(1, G)]
    swaps = [to_member(outs[2 + g], g) for g in range(1, G)]
    back = call(
        functools.partial(sum_kernel, r0, rows, G), shape((H, 8 * rows, HD), bf16),
        [pltpu.VMEM((H * rows, HD), f32)] * 2,
    )(own, *crosses, *far_stats, outs[1], outs[2], *swaps)
    back = to_head(back)
    return tuple(call(
        functools.partial(unpack_kernel, r0, rows, G), [shape((tokens, H * HD), bf16)] * 4,
        [wide] * 4 + [pltpu.SemaphoreType.DMA((4,))],
        in_specs=[VMEM], out_specs=[anywhere] * 4,
    )(back))


def solution(mesh):
    members = mesh.shape["seq"] // (2 * H)
    parts = {"seq": [("half", 2), ("head", H), ("member", members)]}
    axes = [part for name in mesh.axis_names for part in parts.get(name, [(name, mesh.shape[name])])]
    inner = Mesh(mesh.devices.reshape([size for _, size in axes]), [name for name, _ in axes])
    split = ("dp", "half", "head", "member")
    in_specs = (P(split, None),) * 4 + (P(split),)
    return jax.shard_map(
        functools.partial(per_device, members), mesh=inner, in_specs=in_specs,
        out_specs=(P(split, None),) * 4, check_vma=False,
    )
```

```python
import functools

import jax
import jax.numpy as jnp
import numpy as np
from jax import lax
from jax.experimental import pallas as pl
from jax.experimental.pallas import tpu as pltpu
from jax.sharding import Mesh
from jax.sharding import PartitionSpec as P

H = 8
HD = 128
SEG = 1024

MASKED = -1e30
SCALE = HD ** -0.5
LOG2E = float(np.log2(np.e))
VMEM = pl.BlockSpec(memory_space=pltpu.VMEM)
DOC_ROWS = 16


def dot_nn(a, b):
    return lax.dot_general(a, b, (((1,), (0,)), ((), ())), preferred_element_type=jnp.float32)


def dot_nt(a, b):
    return lax.dot_general(a, b, (((1,), (1,)), ((), ())), preferred_element_type=jnp.float32)


def selector(head, r0, rows, tokens, transposed, fine_first=False):
    r1 = 2 * r0
    shape = (tokens, 2 * rows) if transposed else (2 * rows, tokens)
    k = lax.broadcasted_iota(jnp.int32, shape, 1 if transposed else 0)
    p = lax.broadcasted_iota(jnp.int32, shape, 0 if transposed else 1)
    coarse = head % r1
    other = (coarse + r0) % r1
    first, second = jnp.where(fine_first, other, coarse), jnp.where(fine_first, coarse, other)
    target = jnp.where(k < rows, r1 * k + first, r1 * (k - rows) + second)
    return (p == target).astype(jnp.float32).astype(jnp.bfloat16)


def takes_fine(members):
    return lax.axis_index("member") >= members // 2


def pack_kernel(r0, rows, members, q_in, k_in, v_in, g_in, doc_in, out, q_ref, k_ref, v_ref, g_ref, doc_ref, buf, sem):
    tokens = q_ref.shape[0]
    pairs = ((doc_in, doc_ref), (k_in, k_ref), (v_in, v_ref), (q_in, q_ref), (g_in, g_ref))
    copies = [pltpu.make_async_copy(src, dst, sem.at[i]) for i, (src, dst) in enumerate(pairs)]
    for copy in copies:
        copy.start()
    kinds = range(min(H, 2 * r0))
    key_sels = [selector(h, r0, rows, tokens, False) for h in kinds]
    query_sels = [selector(h, r0, rows, tokens, False, takes_fine(members)) for h in kinds]

    def pick(sels, h, ref):
        return dot_nn(sels[h % (2 * r0)], ref[:, h * HD:(h + 1) * HD]).astype(jnp.bfloat16)

    for copy in copies:
        copy.wait()
    docs = jnp.broadcast_to(doc_ref[...].astype(jnp.float32).astype(jnp.bfloat16), (DOC_ROWS, tokens))
    sends = []
    for h in range(H):
        for i, ref in enumerate((q_ref, g_ref)):
            x = pick(query_sels, h, ref)
            buf[h, i * rows:(1 + i) * rows] = x[:rows]
            buf[h, (2 + i) * rows:(3 + i) * rows] = x[rows:]
        for i, ref in enumerate((k_ref, v_ref)):
            x = pick(key_sels, h, ref)
            buf[h, (4 + i) * rows:(5 + i) * rows] = x[rows:]
            buf[h, (6 + i) * rows:(7 + i) * rows] = x[:rows]
        buf[h, 8 * rows:8 * rows + DOC_ROWS] = docs
        sends.append(pltpu.make_async_copy(buf.at[h], out.at[h], sem.at[5 + h]))
        sends[-1].start()
    for copy in sends:
        copy.wait()


TILES = 2


def tile_sizes(rows, members):
    per = H // TILES
    return per * members * rows, per * 2 * rows


def eye_matrix():
    shape = (HD, HD)
    same = lax.broadcasted_iota(jnp.int32, shape, 0) == lax.broadcasted_iota(jnp.int32, shape, 1)
    return same.astype(jnp.float32).astype(jnp.bfloat16)


def doc_cols(x):
    return dot_nn(x, jnp.ones((HD, HD), jnp.bfloat16))[:, 0:1]


def local_kernel(r0, rows, members, *refs):
    G = members
    r1 = 2 * r0
    own_ref, swap_refs = refs[0], refs[1:G]
    (k1, k2, q_all, g_all, stats, out_ref, gtt_ref), rest = refs[G:G + 7], refs[G + 7:]
    p_refs, dp_refs, (v1, v2, d1, d2) = rest[:2 * TILES], rest[2 * TILES:4 * TILES], rest[4 * TILES:]
    bf16, f32 = jnp.bfloat16, jnp.float32
    tokens = HD
    head = lax.axis_index("head")
    member = lax.axis_index("member")
    fine = takes_fine(G)
    partner = G // 2
    partner_ref = swap_refs[partner - 1]

    sel = selector(head, r0, rows, tokens, False)
    query_sel = jnp.where(fine, sel[rows:].astype(f32), sel[:rows].astype(f32)).astype(bf16)
    source_docs = []
    for j in range(H):
        for g in range(G):
            at = pl.ds((j * G + g) * rows, rows)
            ref, base = (own_ref, 4 * rows) if g == 0 else (swap_refs[g - 1], 2 * rows if g == partner else 0)
            k2[at] = ref[j, base:base + rows]
            v2[at] = ref[j, base + rows:base + 2 * rows]
            k1[at] = ref[j, base + 2 * rows:base + 3 * rows]
            v1[at] = ref[j, base + 3 * rows:base + 4 * rows]
            doc = ref[j, base + 4 * rows:base + 4 * rows + DOC_ROWS][0:1]
            if g in (0, partner):
                source_docs.append(doc)
            d1[at] = sel[:rows] * doc
            d2[at] = sel[rows:] * doc

    eye = eye_matrix()
    v1t, v2t = dot_nt(eye, v1[...]).astype(bf16), dot_nt(eye, v2[...]).astype(bf16)
    docs1, docs2 = doc_cols(d1[...]), doc_cols(d2[...])
    nd, lanes = tile_sizes(rows, G)
    per = H // TILES

    coarse = head % r1
    other = (coarse + r0) % r1
    lane = lax.broadcasted_iota(jnp.int32, (1, lanes), 1)
    qmember = member ^ (partner * ((lane // rows) % 2))
    qpos = (lane // (2 * rows)) * (G * tokens) + qmember * tokens + r1 * (lane % rows) + jnp.where(fine, other, coarse)
    kl = lax.broadcasted_iota(jnp.int32, (nd, 1), 0)
    kmember = member ^ ((kl // rows) % G)
    kpos = (kl // (rows * G)) * (G * tokens) + kmember * tokens + r1 * (kl % rows)
    causal1 = kpos + coarse <= qpos
    causal2 = kpos + other <= qpos
    both = jnp.where(fine, 0.0, 1.0)
    c = SCALE * LOG2E

    for u in range(TILES):
        nk = (u + 1) * nd
        x0 = u * nd
        src = range(u * per, (u + 1) * per)
        mine = slice(u * lanes, (u + 1) * lanes)
        gather = lambda lo: jnp.concatenate([ref[j, lo:lo + rows] for j in src for ref in (own_ref, partner_ref)], 0)
        qt, gt = gather(0), gather(rows)
        q_all[mine], g_all[mine] = qt, gt
        dq = jnp.concatenate([query_sel * source_docs[2 * j + e] for j in src for e in range(2)], 0)
        qdoc = dot_nt(jnp.ones((16, HD), bf16), dq)[0:1]

        def scores(key, docs, causal):
            s = jnp.where(docs == qdoc, dot_nt(key, qt), MASKED)
            if u:
                return jnp.concatenate([s[:x0], jnp.where(causal, s[x0:], MASKED)], 0)
            return jnp.where(causal, s, MASKED)

        s1 = scores(k1[0:nk], docs1[0:nk], causal1)
        s2 = scores(k2[0:nk], docs2[0:nk], causal2)
        top = jnp.maximum(jnp.max(s1, 0, keepdims=True), jnp.max(s2, 0, keepdims=True))
        base = top * c
        p1 = jnp.exp2(s1 * c - (base - both))
        p2 = jnp.exp2(s2 * c - base)
        stats[0:1, mine] = top
        stats[1:2, mine] = jnp.sum(p1, 0, keepdims=True) + jnp.sum(p2, 0, keepdims=True)
        stats[2:3, mine] = qdoc
        out_ref[:, mine] = dot_nn(v1t[:, :nk], p1.astype(bf16)) + dot_nn(v2t[:, :nk], p2.astype(bf16))
        gtt_ref[:, mine] = dot_nt(eye, gt)
        p_refs[2 * u][...], p_refs[2 * u + 1][...] = p1, p2
        dp_refs[2 * u][...], dp_refs[2 * u + 1][...] = dot_nt(v1[0:nk], gt), dot_nt(v2[0:nk], gt)


def cross_kernel(r0, rows, members, *refs):
    G = members
    cross_refs = refs[0:G]
    q_all, g_all, stats, local_out, gtt_ref = refs[G:G + 5]
    far_stats, out_ref, gq_ref, new_stats, kx, vx, dx = refs[G + 5:]
    bf16, f32 = jnp.bfloat16, jnp.float32
    half = lax.axis_index("half")
    head = lax.axis_index("head")
    sel = selector(head, r0, rows, HD, False)
    for j in range(H):
        for g in range(G):
            at = pl.ds((j * G + g) * rows, rows)
            ref = cross_refs[g]
            kx[at] = ref[2 * j * rows:(2 * j + 1) * rows]
            vx[at] = ref[(2 * j + 1) * rows:(2 * j + 2) * rows]
            dx[at] = sel[:rows] * ref[2 * H * rows:2 * H * rows + DOC_ROWS][j:j + 1]
    eye = eye_matrix()
    kxt, vxt = dot_nt(eye, kx[...]).astype(bf16), dot_nt(eye, vx[...]).astype(bf16)
    docsx = doc_cols(dx[...]) + jnp.where((half == 0) | takes_fine(G), 1000.0, 0.0)
    nd, lanes = tile_sizes(rows, G)
    c = SCALE * LOG2E
    for u in range(TILES):
        x0 = u * nd
        mine = slice(u * lanes, (u + 1) * lanes)
        qt, gt = q_all[mine], g_all[mine]
        top0, total0, qdoc = stats[0:1, mine], stats[1:2, mine], stats[2:3, mine]
        sx = jnp.where(docsx[x0:] == qdoc, dot_nt(kx[x0:], qt), MASKED)
        top = jnp.maximum(top0, jnp.max(sx, 0, keepdims=True))
        px = jnp.exp2(sx * c - top * c)
        shrink = jnp.exp2(top0 * c - top * c)
        total = total0 * shrink + jnp.sum(px, 0, keepdims=True)
        inv = 1.0 / total
        local_inv = shrink * inv
        out = local_out[:, mine] * local_inv + dot_nn(vxt[:, x0:], px.astype(bf16)) * inv
        dot = jnp.sum(gtt_ref[:, mine] * out, 0, keepdims=True)
        ds = (px * inv * (dot_nt(vx[x0:], gt) - dot)).astype(bf16)
        new_stats[0:1, mine] = local_inv
        new_stats[1:2, mine] = dot
        far_stats[0:1, mine] = top * c + jnp.log(total) * LOG2E
        far_stats[1:2, mine] = dot
        out_ref[mine] = out.T.astype(bf16)
        gq_ref[:, mine] = dot_nn(kxt[:, x0:], ds)


def grad_kernel(rows, members, *refs):
    G = members
    k1, k2, q_all, g_all, out_ref, gq_ref, stats = refs[:7]
    p_refs, dp_refs = refs[7:7 + 2 * TILES], refs[7 + 2 * TILES:7 + 4 * TILES]
    rest = refs[7 + 4 * TILES:]
    partner = G // 2
    out_own, out_kv, (gk1, gk2, gv1, gv2) = rest[0], rest[1], rest[-4:]
    out_swap = rest[2:-4]
    bf16, f32 = jnp.bfloat16, jnp.float32
    eye = eye_matrix()
    nd, lanes = tile_sizes(rows, G)
    per = H // TILES
    k1t, k2t = dot_nt(eye, k1[...]).astype(bf16), dot_nt(eye, k2[...]).astype(bf16)
    for u in reversed(range(TILES)):
        nk = (u + 1) * nd
        mine = slice(u * lanes, (u + 1) * lanes)
        qt, gt = q_all[mine], g_all[mine]
        inv, dot = stats[0:1, mine], stats[1:2, mine]
        gq = gq_ref[:, mine]
        for i, (kt, gk, gv) in enumerate(((k1t, gk1, gv1), (k2t, gk2, gv2))):
            w = p_refs[2 * u + i][...] * inv
            ds = (w * (dp_refs[2 * u + i][...] - dot)).astype(bf16)
            gq = gq + dot_nn(kt[:, :nk], ds)
            new_k, new_v = dot_nn(ds, qt), dot_nn(w.astype(bf16), gt)
            if u == TILES - 1:
                gk[...], gv[...] = new_k, new_v
            else:
                gk[0:nk] += new_k
                gv[0:nk] += new_v
        gq = (gq * SCALE).T.astype(bf16)
        for i in range(per):
            j = u * per + i
            for e, ref in enumerate((out_own, out_swap[partner - 1])):
                lo = (2 * i + e) * rows
                ref[j, 0:rows] = out_ref[u * lanes + lo:u * lanes + lo + rows]
                ref[j, rows:2 * rows] = gq[lo:lo + rows]
    for j in range(H):
        for g in range(G):
            at = pl.ds((j * G + g) * rows, rows)
            ref = out_kv if g == 0 else out_swap[g - 1]
            base = 2 if g == partner else 0
            for i, part in enumerate((gk2[at] * SCALE, gv2[at], gk1[at] * SCALE, gv1[at]), base):
                ref[j, i * rows:(i + 1) * rows] = part.astype(ref.dtype)


def finish_kernel(r0, rows, members, *refs):
    G = members
    crosses, (q_all, g_all, stats, local_out, gtt, k1, k2), refs = refs[:G], refs[G:G + 7], refs[G + 7:]
    products, refs = refs[:4 * TILES], refs[4 * TILES:]
    far_stats, results, scratch = refs[0], refs[1:G + 2], refs[G + 2:]
    out, gq, new_stats = scratch[:3]
    cross_kernel(r0, rows, G, *crosses, q_all, g_all, stats, local_out, gtt, far_stats, *scratch[:6])
    grad_kernel(rows, G, k1, k2, q_all, g_all, out, gq, new_stats, *products, *results, *scratch[6:])


def far_rows(query_refs, g, members, u, rows, lo):
    per = H // TILES
    pair = (query_refs[g], query_refs[g ^ (members // 2)])
    return jnp.concatenate([ref[(2 * j + lo) * rows:(2 * j + lo + 1) * rows]
                            for j in range(u * per, (u + 1) * per) for ref in pair], 0)


def far_slots(members, body):
    for g in range(members):
        slot = lax.axis_index("member") ^ g

        @pl.when((lax.axis_index("half") == 0) & (slot < members // 2))
        def _(g=g, slot=slot):
            body(g, slot)


def far_kernel(r0, rows, members, own_ref, *refs):
    G = members
    query_refs, products = refs[:G], refs[G:]
    sel = selector(lax.axis_index("head"), r0, rows, HD, False)[:rows]
    per = H // TILES
    keys, values = (jnp.concatenate([own_ref[j, lo * rows:(lo + 1) * rows] for j in range(H)], 0) for lo in (6, 7))
    docs = doc_cols(jnp.concatenate([sel * own_ref[j, 8 * rows:8 * rows + DOC_ROWS][0:1] for j in range(H)], 0))

    def body(g, slot):
        pair = (query_refs[g], query_refs[g ^ (G // 2)])
        for u in range(TILES):
            x0 = u * per * rows
            dq = jnp.concatenate([sel * ref[2 * H * rows:2 * H * rows + DOC_ROWS][j:j + 1]
                                  for j in range(u * per, (u + 1) * per) for ref in pair], 0)
            qdoc = dot_nt(jnp.ones((16, HD), jnp.bfloat16), dq)[0:1]
            s = dot_nt(keys[x0:], far_rows(query_refs, g, G, u, rows, 0)) * (SCALE * LOG2E)
            products[2 * u][slot] = jnp.where(docs[x0:] == qdoc, s, MASKED)
            products[2 * u + 1][slot] = dot_nt(values[x0:], far_rows(query_refs, g, G, u, rows, 1))

    far_slots(G, body)


def far_grads(rows, members, query_refs, stat_ref, products, gk, gv):
    G = members
    per = H // TILES
    gk[...], gv[...] = jnp.zeros_like(gk), jnp.zeros_like(gv)

    def body(g, slot):
        for u in range(TILES):
            x0 = u * per * rows
            mine = slice(u * per * 2 * rows, (u + 1) * per * 2 * rows)
            lse, dot = (stat_ref[8 * g + i:8 * g + i + 1, mine] for i in range(2))
            p = jnp.exp2(products[2 * u][slot] - lse)
            ds = p * (products[2 * u + 1][slot] - dot)
            gk[x0:] += dot_nn(ds.astype(jnp.bfloat16), far_rows(query_refs, g, G, u, rows, 0)) * SCALE
            gv[x0:] += dot_nn(p.astype(jnp.bfloat16), far_rows(query_refs, g, G, u, rows, 1))

    far_slots(G, body)


def sum_kernel(rows, members, *refs):
    G = members
    query_refs, stat_ref, products, refs = refs[:G], refs[G], refs[G + 1:G + 1 + 2 * TILES], refs[G + 1 + 2 * TILES:]
    own_ref, kv_ref, swap_refs, (out_ref, gk, gv) = refs[0], refs[1], refs[2:G + 1], refs[G + 1:]
    f32, bf16 = jnp.float32, jnp.bfloat16
    far_grads(rows, G, query_refs, stat_ref, products, gk, gv)
    out_ref[:, 0:2 * rows] = own_ref[...]
    out_ref[:, 2 * rows:4 * rows] = swap_refs[G // 2 - 1][:, 0:2 * rows]
    for j in range(H):
        total = kv_ref[j]
        for g, ref in enumerate(swap_refs, 1):
            base = 2 * rows if g == G // 2 else 0
            total = total + ref[j, base:base + 4 * rows].astype(f32)
        mine = slice(j * rows, (j + 1) * rows)
        out_ref[j, 4 * rows:6 * rows] = total[:2 * rows].astype(bf16)
        out_ref[j, 6 * rows:7 * rows] = (total[2 * rows:3 * rows] + gk[mine]).astype(bf16)
        out_ref[j, 7 * rows:8 * rows] = (total[3 * rows:] + gv[mine]).astype(bf16)


def unpack_kernel(r0, rows, members, in_ref, *refs):
    outs, bufs, sem = refs[:4], refs[4:8], refs[8]
    tokens = bufs[0].shape[0]
    bf16 = jnp.bfloat16
    kinds = range(min(H, 2 * r0))
    query_sels = [selector(h, r0, rows, tokens, True, takes_fine(members)) for h in kinds]
    key_sels = [selector(h, r0, rows, tokens, True, True) for h in kinds]
    copies = []
    for i, base in enumerate((0, 1, 4, 5)):
        for h in range(H):
            sels = query_sels if i < 2 else key_sels
            part = jnp.concatenate([in_ref[h, (base + e) * rows:(base + e + 1) * rows] for e in (0, 2)], 0)
            bufs[i][:, h * HD:(h + 1) * HD] = dot_nn(sels[h % (2 * r0)], part).astype(bf16)
        copies.append(pltpu.make_async_copy(bufs[i], outs[i], sem.at[i]))
        copies[-1].start()
    for copy in copies:
        copy.wait()


def call(kernel, out_shape, scratch=(), limit=16, **more):
    return pl.pallas_call(
        kernel,
        out_shape=out_shape,
        scratch_shapes=list(scratch),
        compiler_params=pltpu.CompilerParams(vmem_limit_bytes=limit * 1024 * 1024),
        **more,
    )


def per_device(members, queries, keys, values, cotangent, doc_ids):
    G = members
    tokens = queries.shape[0]
    devices = 2 * H * G
    r0 = tokens * devices // (2 * SEG)
    rows = tokens // (2 * r0)
    bf16, f32 = jnp.bfloat16, jnp.float32
    shape = jax.ShapeDtypeStruct
    n = H * G * rows
    anywhere = pl.BlockSpec(memory_space=pltpu.HBM)
    wide = pltpu.VMEM((tokens, H * HD), bf16)
    message = (H, 8 * rows + DOC_ROWS, HD)

    packed = call(
        functools.partial(pack_kernel, r0, rows, G), shape(message, bf16),
        [wide] * 4 + [pltpu.VMEM((1, tokens), jnp.int32), pltpu.VMEM(message, bf16), pltpu.SemaphoreType.DMA((5 + H,))],
        limit=64, in_specs=[anywhere] * 5, out_specs=anywhere,
    )(queries, keys, values, cotangent, doc_ids.reshape(1, tokens))

    def to_head(x):
        return lax.all_to_all(x, "head", 0, 0, tiled=True)

    def to_member(x, g):
        return lax.ppermute(x, "member", [(i, i ^ g) for i in range(G)])

    def across(x):
        return lax.ppermute(x, "half", [(0, 1), (1, 0)])

    own = to_head(packed)
    queries_here = jnp.where(takes_fine(G), own[:, 2 * rows:4 * rows], own[:, :2 * rows])
    sent_across = jnp.where(lax.axis_index("half") == 0, own[:, 6 * rows:8 * rows], queries_here)
    docs = jnp.pad(own[:, 8 * rows], ((0, DOC_ROWS - H), (0, 0)))
    cross = across(jnp.concatenate([sent_across.reshape(-1, HD), docs], 0))
    swaps = [to_member(own[:, (2 if g == G // 2 else 4) * rows:], g) for g in range(1, G)]
    nd, lanes = tile_sizes(rows, G)
    nq = TILES * lanes
    tile = [shape(((u + 1) * nd, lanes), f32) for u in range(TILES) for _ in range(2)]
    key_rows, key_sums = pltpu.VMEM((n, HD), bf16), pltpu.VMEM((n, HD), f32)
    k1, k2, q_all, g_all, *rest = call(
        functools.partial(local_kernel, r0, rows, G),
        [shape((n, HD), bf16)] * 2 + [shape((nq, HD), bf16)] * 2 + [shape((8, nq), f32)]
        + [shape((HD, nq), f32)] * 2 + tile * 2,
        [key_rows] * 4, limit=32,
    )(own, *swaps)
    cross, k1 = lax.optimization_barrier((cross, k1))
    crosses = [cross] + [to_member(cross, g) for g in range(1, G)]
    sent = lambda g: (H, (6 if g == G // 2 else 4) * rows, HD)
    outs = call(
        functools.partial(finish_kernel, r0, rows, G),
        [shape((8, nq), f32), shape((H, 2 * rows, HD), bf16), shape((H, 4 * rows, HD), f32)]
        + [shape(sent(g), bf16) for g in range(1, G)],
        [pltpu.VMEM((nq, HD), bf16), pltpu.VMEM((HD, nq), f32), pltpu.VMEM((8, nq), f32)]
        + [key_rows] * 3 + [key_sums] * 4, limit=32,
    )(*crosses, q_all, g_all, *rest[:3], k1, k2, *rest[3:])
    far_stats = across(jnp.concatenate([outs[0]] + [to_member(outs[0], g) for g in range(1, G)], 0))
    products = call(
        functools.partial(far_kernel, r0, rows, G),
        [shape((G // 2, (TILES - u) * nd // G, lanes), f32) for u in range(TILES) for _ in range(2)],
    )(own, *crosses)
    swaps = [to_member(outs[2 + g], g) for g in range(1, G)]
    back = call(
        functools.partial(sum_kernel, rows, G), shape((H, 8 * rows, HD), bf16),
        [pltpu.VMEM((H * rows, HD), f32)] * 2,
    )(*crosses, far_stats, *products, outs[1], outs[2], *swaps)
    back = to_head(back)
    return tuple(call(
        functools.partial(unpack_kernel, r0, rows, G), [shape((tokens, H * HD), bf16)] * 4,
        [wide] * 4 + [pltpu.SemaphoreType.DMA((4,))],
        in_specs=[VMEM], out_specs=[anywhere] * 4,
    )(back))


def solution(mesh):
    members = mesh.shape["seq"] // (2 * H)
    parts = {"seq": [("half", 2), ("head", H), ("member", members)]}
    axes = [part for name in mesh.axis_names for part in parts.get(name, [(name, mesh.shape[name])])]
    inner = Mesh(mesh.devices.reshape([size for _, size in axes]), [name for name, _ in axes])
    split = ("dp", "half", "head", "member")
    in_specs = (P(split, None),) * 4 + (P(split),)
    return jax.shard_map(
        functools.partial(per_device, members), mesh=inner, in_specs=in_specs,
        out_specs=(P(split, None),) * 4, check_vma=False,
    )
```

```python
import functools

import jax
import jax.numpy as jnp
import numpy as np
from jax import lax
from jax.experimental import pallas as pl
from jax.experimental.pallas import tpu as pltpu
from jax.sharding import Mesh
from jax.sharding import PartitionSpec as P

H = 8
HD = 128
SEG = 1024

MASKED = -1e30
SCALE = HD ** -0.5
LOG2E = float(np.log2(np.e))
VMEM = pl.BlockSpec(memory_space=pltpu.VMEM)
DOC_ROWS = 16


def dot_nn(a, b):
    return lax.dot_general(a, b, (((1,), (0,)), ((), ())), preferred_element_type=jnp.float32)


def dot_nt(a, b):
    return lax.dot_general(a, b, (((1,), (1,)), ((), ())), preferred_element_type=jnp.float32)


def selector(head, r0, rows, tokens, transposed, fine_first=False):
    r1 = 2 * r0
    shape = (tokens, 2 * rows) if transposed else (2 * rows, tokens)
    k = lax.broadcasted_iota(jnp.int32, shape, 1 if transposed else 0)
    p = lax.broadcasted_iota(jnp.int32, shape, 0 if transposed else 1)
    coarse = head % r1
    other = (coarse + r0) % r1
    first, second = jnp.where(fine_first, other, coarse), jnp.where(fine_first, coarse, other)
    target = jnp.where(k < rows, r1 * k + first, r1 * (k - rows) + second)
    return (p == target).astype(jnp.float32).astype(jnp.bfloat16)


def takes_fine(members):
    return lax.axis_index("member") >= members // 2


def pack_kernel(r0, rows, members, q_in, k_in, v_in, g_in, doc_in, out, q_ref, k_ref, v_ref, g_ref, doc_ref, buf, sem):
    tokens = q_ref.shape[0]
    pairs = ((doc_in, doc_ref), (k_in, k_ref), (v_in, v_ref), (q_in, q_ref), (g_in, g_ref))
    copies = [pltpu.make_async_copy(src, dst, sem.at[i]) for i, (src, dst) in enumerate(pairs)]
    for copy in copies:
        copy.start()
    kinds = range(min(H, 2 * r0))
    key_sels = [selector(h, r0, rows, tokens, False) for h in kinds]
    query_sels = [selector(h, r0, rows, tokens, False, takes_fine(members)) for h in kinds]

    def pick(sels, h, ref):
        return dot_nn(sels[h % (2 * r0)], ref[:, h * HD:(h + 1) * HD]).astype(jnp.bfloat16)

    for copy in copies:
        copy.wait()
    docs = jnp.broadcast_to(doc_ref[...].astype(jnp.float32).astype(jnp.bfloat16), (DOC_ROWS, tokens))
    sends = []
    for h in range(H):
        for i, ref in enumerate((q_ref, g_ref)):
            x = pick(query_sels, h, ref)
            buf[h, i * rows:(1 + i) * rows] = x[:rows]
            buf[h, (2 + i) * rows:(3 + i) * rows] = x[rows:]
        for i, ref in enumerate((k_ref, v_ref)):
            x = pick(key_sels, h, ref)
            buf[h, (4 + i) * rows:(5 + i) * rows] = x[rows:]
            buf[h, (6 + i) * rows:(7 + i) * rows] = x[:rows]
        buf[h, 8 * rows:8 * rows + DOC_ROWS] = docs
        sends.append(pltpu.make_async_copy(buf.at[h], out.at[h], sem.at[5 + h]))
        sends[-1].start()
    for copy in sends:
        copy.wait()


TILES = 2


def tile_sizes(rows, members):
    per = H // TILES
    return per * members * rows, per * 2 * rows


def eye_matrix():
    shape = (HD, HD)
    same = lax.broadcasted_iota(jnp.int32, shape, 0) == lax.broadcasted_iota(jnp.int32, shape, 1)
    return same.astype(jnp.float32).astype(jnp.bfloat16)


def doc_cols(x):
    return dot_nn(x, jnp.ones((HD, HD), jnp.bfloat16))[:, 0:1]


def local_kernel(r0, rows, members, *refs):
    G = members
    r1 = 2 * r0
    own_ref, swap_refs = refs[0], refs[1:G]
    (k1, k2, q_all, g_all, stats, out_ref, gtt_ref), rest = refs[G:G + 7], refs[G + 7:]
    p_refs, dp_refs, (v1, v2, d1, d2) = rest[:2 * TILES], rest[2 * TILES:4 * TILES], rest[4 * TILES:]
    bf16, f32 = jnp.bfloat16, jnp.float32
    tokens = HD
    head = lax.axis_index("head")
    member = lax.axis_index("member")
    fine = takes_fine(G)
    partner = G // 2
    partner_ref = swap_refs[partner - 1]

    sel = selector(head, r0, rows, tokens, False)
    query_sel = jnp.where(fine, sel[rows:].astype(f32), sel[:rows].astype(f32)).astype(bf16)
    source_docs = []
    for j in range(H):
        for g in range(G):
            at = pl.ds((j * G + g) * rows, rows)
            ref, base = (own_ref, 4 * rows) if g == 0 else (swap_refs[g - 1], 2 * rows if g == partner else 0)
            k2[at] = ref[j, base:base + rows]
            v2[at] = ref[j, base + rows:base + 2 * rows]
            k1[at] = ref[j, base + 2 * rows:base + 3 * rows]
            v1[at] = ref[j, base + 3 * rows:base + 4 * rows]
            doc = ref[j, base + 4 * rows:base + 4 * rows + DOC_ROWS][0:1]
            if g in (0, partner):
                source_docs.append(doc)
            d1[at] = sel[:rows] * doc
            d2[at] = sel[rows:] * doc

    eye = eye_matrix()
    v1t, v2t = dot_nt(eye, v1[...]).astype(bf16), dot_nt(eye, v2[...]).astype(bf16)
    docs1, docs2 = doc_cols(d1[...]), doc_cols(d2[...])
    nd, lanes = tile_sizes(rows, G)
    per = H // TILES

    coarse = head % r1
    other = (coarse + r0) % r1
    lane = lax.broadcasted_iota(jnp.int32, (1, lanes), 1)
    qmember = member ^ (partner * ((lane // rows) % 2))
    qpos = (lane // (2 * rows)) * (G * tokens) + qmember * tokens + r1 * (lane % rows) + jnp.where(fine, other, coarse)
    kl = lax.broadcasted_iota(jnp.int32, (nd, 1), 0)
    kmember = member ^ ((kl // rows) % G)
    kpos = (kl // (rows * G)) * (G * tokens) + kmember * tokens + r1 * (kl % rows)
    causal1 = kpos + coarse <= qpos
    causal2 = kpos + other <= qpos
    both = jnp.where(fine, 0.0, 1.0)
    c = SCALE * LOG2E

    for u in range(TILES):
        nk = (u + 1) * nd
        x0 = u * nd
        src = range(u * per, (u + 1) * per)
        mine = slice(u * lanes, (u + 1) * lanes)
        gather = lambda lo: jnp.concatenate([ref[j, lo:lo + rows] for j in src for ref in (own_ref, partner_ref)], 0)
        qt, gt = gather(0), gather(rows)
        q_all[mine], g_all[mine] = qt, gt
        dq = jnp.concatenate([query_sel * source_docs[2 * j + e] for j in src for e in range(2)], 0)
        qdoc = dot_nt(jnp.ones((16, HD), bf16), dq)[0:1]

        def scores(key, docs, causal):
            s = jnp.where(docs == qdoc, dot_nt(key, qt), MASKED)
            if u:
                return jnp.concatenate([s[:x0], jnp.where(causal, s[x0:], MASKED)], 0)
            return jnp.where(causal, s, MASKED)

        s1 = scores(k1[0:nk], docs1[0:nk], causal1)
        s2 = scores(k2[0:nk], docs2[0:nk], causal2)
        top = jnp.maximum(jnp.max(s1, 0, keepdims=True), jnp.max(s2, 0, keepdims=True))
        base = top * c
        p1 = jnp.exp2(s1 * c - (base - both))
        p2 = jnp.exp2(s2 * c - base)
        stats[0:1, mine] = top
        stats[1:2, mine] = jnp.sum(p1, 0, keepdims=True) + jnp.sum(p2, 0, keepdims=True)
        stats[2:3, mine] = qdoc
        out_ref[:, mine] = dot_nn(v1t[:, :nk], p1.astype(bf16)) + dot_nn(v2t[:, :nk], p2.astype(bf16))
        gtt_ref[:, mine] = dot_nt(eye, gt)
        p_refs[2 * u][...], p_refs[2 * u + 1][...] = p1, p2
        dp_refs[2 * u][...], dp_refs[2 * u + 1][...] = dot_nt(v1[0:nk], gt), dot_nt(v2[0:nk], gt)


def finish_tile(u, r0, rows, members, parts, shared, products, results, scratch):
    G = members
    q_all, g_all, stats, local_out, gtt_ref, k1, k2 = shared
    far_stats, att, gq_ref, sums = results[0], results[1], results[2], results[3:]
    kx, vx, dx = scratch
    bf16 = jnp.bfloat16
    half = lax.axis_index("half")
    sel = selector(lax.axis_index("head"), r0, rows, HD, False)
    per = H // TILES
    for p, part in enumerate(parts):
        for j in range(per):
            for g, ref in enumerate(part):
                at = pl.ds(((p * per + j) * G + g) * rows, rows)
                kx[at] = ref[2 * j * rows:(2 * j + 1) * rows]
                vx[at] = ref[(2 * j + 1) * rows:(2 * j + 2) * rows]
                dx[at] = sel[:rows] * ref[2 * per * rows:2 * per * rows + DOC_ROWS][j:j + 1]
    eye = eye_matrix()
    nd, lanes = tile_sizes(rows, G)
    nk = (u + 1) * nd
    mine = slice(u * lanes, (u + 1) * lanes)
    c = SCALE * LOG2E
    keys_x, values_x = kx[...], vx[...]
    kxt, vxt = dot_nt(eye, keys_x).astype(bf16), dot_nt(eye, values_x).astype(bf16)
    docsx = doc_cols(dx[...]) + jnp.where((half == 0) | takes_fine(G), 1000.0, 0.0)
    qt, gt = q_all[mine], g_all[mine]
    top0, total0, qdoc = stats[0:1, mine], stats[1:2, mine], stats[2:3, mine]
    sx = jnp.where(docsx == qdoc, dot_nt(keys_x, qt), MASKED)
    top = jnp.maximum(top0, jnp.max(sx, 0, keepdims=True))
    px = jnp.exp2(sx * c - top * c)
    shrink = jnp.exp2(top0 * c - top * c)
    total = total0 * shrink + jnp.sum(px, 0, keepdims=True)
    inv = 1.0 / total
    local_inv = shrink * inv
    out = local_out[:, mine] * local_inv + dot_nn(vxt, px.astype(bf16)) * inv
    dot = jnp.sum(gtt_ref[:, mine] * out, 0, keepdims=True)
    far_stats[0:1] = top * c + jnp.log(total) * LOG2E
    far_stats[1:2] = dot
    att[...] = out.T.astype(bf16)
    ds = (px * inv * (dot_nt(values_x, gt) - dot)).astype(bf16)
    gq = dot_nn(kxt, ds)
    for i, k in enumerate((k1, k2)):
        w = products[i][...] * local_inv
        ds = (w * (products[2 + i][...] - dot)).astype(bf16)
        gq = gq + dot_nn(dot_nt(eye, k[0:nk]).astype(bf16), ds)
        sums[i][...] = dot_nn(ds, qt)
        sums[2 + i][...] = dot_nn(w.astype(bf16), gt)
    gq_ref[...] = (gq * SCALE).T.astype(bf16)


def last_tile_kernel(r0, rows, members, *refs):
    G = members
    finish_tile(1, r0, rows, G, [refs[:G]], refs[G:G + 7], refs[G + 7:G + 11], refs[G + 11:G + 18], refs[G + 18:])


def first_tile_kernel(r0, rows, members, *refs):
    G = members
    parts, refs = [refs[:G], refs[G:2 * G]], refs[2 * G:]
    shared, products, last, refs = refs[:7], refs[7:11], refs[11:18], refs[18:]
    far_stats, out_own, out_kv, out_swap, scratch = refs[0], refs[1], refs[2], refs[3:G + 2], refs[G + 2:]
    nd, lanes = tile_sizes(rows, G)
    first = (far_stats.at[:, 0:lanes],) + tuple(scratch[:6])
    finish_tile(0, r0, rows, G, parts, shared, products, first, scratch[6:])
    far_stats[:, lanes:] = last[0][...]
    partner, per = G // 2, H // TILES
    for j in range(H):
        att, gq = (first, last)[j // per][1:3]
        for e, ref in enumerate((out_own, out_swap[partner - 1])):
            lo = (2 * (j % per) + e) * rows
            ref[j, 0:rows] = att[lo:lo + rows]
            ref[j, rows:2 * rows] = gq[lo:lo + rows]
        for g in range(G):
            at = pl.ds((j * G + g) * rows, rows)
            gk1, gk2, gv1, gv2 = (last[3 + i][at] + first[3 + i][at] if j < per else last[3 + i][at] for i in range(4))
            ref = out_kv if g == 0 else out_swap[g - 1]
            base = 2 if g == partner else 0
            for i, part in enumerate((gk2 * SCALE, gv2, gk1 * SCALE, gv1), base):
                ref[j, i * rows:(i + 1) * rows] = part.astype(ref.dtype)


def far_rows(query_refs, g, members, u, rows, lo):
    pair = (query_refs[u * members + g], query_refs[u * members + (g ^ (members // 2))])
    return jnp.concatenate([ref[(2 * j + lo) * rows:(2 * j + lo + 1) * rows] for j in range(H // TILES) for ref in pair], 0)


def far_slots(members, body):
    for g in range(members):
        slot = lax.axis_index("member") ^ g

        @pl.when((lax.axis_index("half") == 0) & (slot < members // 2))
        def _(g=g, slot=slot):
            body(g, slot)


def far_kernel(r0, rows, members, own_ref, *refs):
    G = members
    query_refs, products = refs[:TILES * G], refs[TILES * G:]
    sel = selector(lax.axis_index("head"), r0, rows, HD, False)[:rows]
    per = H // TILES
    keys, values = (jnp.concatenate([own_ref[j, lo * rows:(lo + 1) * rows] for j in range(H)], 0) for lo in (6, 7))
    docs = doc_cols(jnp.concatenate([sel * own_ref[j, 8 * rows:8 * rows + DOC_ROWS][0:1] for j in range(H)], 0))

    def body(g, slot):
        for u in range(TILES):
            x0 = u * per * rows
            pair = (query_refs[u * G + g], query_refs[u * G + (g ^ (G // 2))])
            dq = jnp.concatenate([sel * ref[2 * per * rows:2 * per * rows + DOC_ROWS][j:j + 1]
                                  for j in range(per) for ref in pair], 0)
            qdoc = dot_nt(jnp.ones((16, HD), jnp.bfloat16), dq)[0:1]
            s = dot_nt(keys[x0:], far_rows(query_refs, g, G, u, rows, 0)) * (SCALE * LOG2E)
            products[2 * u][slot] = jnp.where(docs[x0:] == qdoc, s, MASKED)
            products[2 * u + 1][slot] = dot_nt(values[x0:], far_rows(query_refs, g, G, u, rows, 1))

    far_slots(G, body)


def far_grads(rows, members, query_refs, stat_ref, products, gk, gv):
    G = members
    per = H // TILES
    gk[...], gv[...] = jnp.zeros_like(gk), jnp.zeros_like(gv)

    def body(g, slot):
        for u in range(TILES):
            x0 = u * per * rows
            mine = slice(u * per * 2 * rows, (u + 1) * per * 2 * rows)
            lse, dot = (stat_ref[8 * g + i:8 * g + i + 1, mine] for i in range(2))
            p = jnp.exp2(products[2 * u][slot] - lse)
            ds = p * (products[2 * u + 1][slot] - dot)
            gk[x0:] += dot_nn(ds.astype(jnp.bfloat16), far_rows(query_refs, g, G, u, rows, 0)) * SCALE
            gv[x0:] += dot_nn(p.astype(jnp.bfloat16), far_rows(query_refs, g, G, u, rows, 1))

    far_slots(G, body)


def sum_kernel(rows, members, *refs):
    G = members
    query_refs, refs = refs[:TILES * G], refs[TILES * G:]
    stat_ref, products, refs = refs[0], refs[1:1 + 2 * TILES], refs[1 + 2 * TILES:]
    own_ref, kv_ref, swap_refs, (out_ref, gk, gv) = refs[0], refs[1], refs[2:G + 1], refs[G + 1:]
    f32, bf16 = jnp.float32, jnp.bfloat16
    far_grads(rows, G, query_refs, stat_ref, products, gk, gv)
    out_ref[:, 0:2 * rows] = own_ref[...]
    out_ref[:, 2 * rows:4 * rows] = swap_refs[G // 2 - 1][:, 0:2 * rows]
    for j in range(H):
        total = kv_ref[j]
        for g, ref in enumerate(swap_refs, 1):
            base = 2 * rows if g == G // 2 else 0
            total = total + ref[j, base:base + 4 * rows].astype(f32)
        mine = slice(j * rows, (j + 1) * rows)
        out_ref[j, 4 * rows:6 * rows] = total[:2 * rows].astype(bf16)
        out_ref[j, 6 * rows:7 * rows] = (total[2 * rows:3 * rows] + gk[mine]).astype(bf16)
        out_ref[j, 7 * rows:8 * rows] = (total[3 * rows:] + gv[mine]).astype(bf16)


def unpack_kernel(r0, rows, members, in_ref, *refs):
    outs, bufs, sem = refs[:4], refs[4:8], refs[8]
    tokens = bufs[0].shape[0]
    bf16 = jnp.bfloat16
    kinds = range(min(H, 2 * r0))
    query_sels = [selector(h, r0, rows, tokens, True, takes_fine(members)) for h in kinds]
    key_sels = [selector(h, r0, rows, tokens, True, True) for h in kinds]
    copies = []
    for i, base in enumerate((0, 1, 4, 5)):
        for h in range(H):
            sels = query_sels if i < 2 else key_sels
            part = jnp.concatenate([in_ref[h, (base + e) * rows:(base + e + 1) * rows] for e in (0, 2)], 0)
            bufs[i][:, h * HD:(h + 1) * HD] = dot_nn(sels[h % (2 * r0)], part).astype(bf16)
        copies.append(pltpu.make_async_copy(bufs[i], outs[i], sem.at[i]))
        copies[-1].start()
    for copy in copies:
        copy.wait()


def call(kernel, out_shape, scratch=(), limit=16, **more):
    return pl.pallas_call(
        kernel,
        out_shape=out_shape,
        scratch_shapes=list(scratch),
        compiler_params=pltpu.CompilerParams(vmem_limit_bytes=limit * 1024 * 1024),
        **more,
    )


def per_device(members, queries, keys, values, cotangent, doc_ids):
    G = members
    tokens = queries.shape[0]
    devices = 2 * H * G
    r0 = tokens * devices // (2 * SEG)
    rows = tokens // (2 * r0)
    bf16, f32 = jnp.bfloat16, jnp.float32
    shape = jax.ShapeDtypeStruct
    n = H * G * rows
    anywhere = pl.BlockSpec(memory_space=pltpu.HBM)
    wide = pltpu.VMEM((tokens, H * HD), bf16)
    message = (H, 8 * rows + DOC_ROWS, HD)

    packed = call(
        functools.partial(pack_kernel, r0, rows, G), shape(message, bf16),
        [wide] * 4 + [pltpu.VMEM((1, tokens), jnp.int32), pltpu.VMEM(message, bf16), pltpu.SemaphoreType.DMA((5 + H,))],
        limit=64, in_specs=[anywhere] * 5, out_specs=anywhere,
    )(queries, keys, values, cotangent, doc_ids.reshape(1, tokens))

    def to_head(x):
        return lax.all_to_all(x, "head", 0, 0, tiled=True)

    def to_member(x, g):
        return lax.ppermute(x, "member", [(i, i ^ g) for i in range(G)])

    def across(x):
        return lax.ppermute(x, "half", [(0, 1), (1, 0)])

    own = to_head(packed)
    queries_here = jnp.where(takes_fine(G), own[:, 2 * rows:4 * rows], own[:, :2 * rows])
    sent_across = jnp.where(lax.axis_index("half") == 0, own[:, 6 * rows:8 * rows], queries_here)
    per = H // TILES

    def part_across(u):
        at = slice(u * per, (u + 1) * per)
        docs = jnp.pad(own[at, 8 * rows], ((0, DOC_ROWS - per), (0, 0)))
        return across(jnp.concatenate([sent_across[at].reshape(-1, HD), docs], 0))

    upper, lower = part_across(1), part_across(0)
    swaps = [to_member(own[:, (2 if g == G // 2 else 4) * rows:], g) for g in range(1, G)]
    nd, lanes = tile_sizes(rows, G)
    nq = TILES * lanes
    tile = [shape(((u + 1) * nd, lanes), f32) for u in range(TILES) for _ in range(2)]
    key_rows = pltpu.VMEM((n, HD), bf16)
    k1, k2, q_all, g_all, stats, out, gtt, *products = call(
        functools.partial(local_kernel, r0, rows, G),
        [shape((n, HD), bf16)] * 2 + [shape((nq, HD), bf16)] * 2 + [shape((8, nq), f32)]
        + [shape((HD, nq), f32)] * 2 + tile * 2,
        [key_rows] * 4, limit=32,
    )(own, *swaps)
    shared = (q_all, g_all, stats, out, gtt, k1, k2)
    upper, k1 = lax.optimization_barrier((upper, k1))
    uppers = [upper] + [to_member(upper, g) for g in range(1, G)]
    rows_x, tile_rows = pltpu.VMEM((nd, HD), bf16), pltpu.VMEM((lanes, HD), bf16)
    last = call(
        functools.partial(last_tile_kernel, r0, rows, G),
        [shape((8, lanes), f32)] + [shape((lanes, HD), bf16)] * 2 + [shape((n, HD), f32)] * 4,
        [rows_x] * 3, limit=32,
    )(*uppers, *shared, *products[2:4], *products[6:8])
    lower, *last = lax.optimization_barrier((lower, *last))
    lowers = [lower] + [to_member(lower, g) for g in range(1, G)]
    sent = lambda g: (H, (6 if g == G // 2 else 4) * rows, HD)
    outs = call(
        functools.partial(first_tile_kernel, r0, rows, G),
        [shape((8, nq), f32), shape((H, 2 * rows, HD), bf16), shape((H, 4 * rows, HD), f32)]
        + [shape(sent(g), bf16) for g in range(1, G)],
        [tile_rows] * 2 + [pltpu.VMEM((nd, HD), f32)] * 4 + [key_rows] * 3, limit=32,
    )(*lowers, *uppers, *shared, *products[0:2], *products[4:6], *last)
    crosses = lowers + uppers
    far_stats = across(jnp.concatenate([outs[0]] + [to_member(outs[0], g) for g in range(1, G)], 0))
    products = call(
        functools.partial(far_kernel, r0, rows, G),
        [shape((G // 2, (TILES - u) * nd // G, lanes), f32) for u in range(TILES) for _ in range(2)],
    )(own, *crosses)
    swaps = [to_member(outs[2 + g], g) for g in range(1, G)]
    back = call(
        functools.partial(sum_kernel, rows, G), shape((H, 8 * rows, HD), bf16),
        [pltpu.VMEM((H * rows, HD), f32)] * 2,
    )(*crosses, far_stats, *products, outs[1], outs[2], *swaps)
    back = to_head(back)
    return tuple(call(
        functools.partial(unpack_kernel, r0, rows, G), [shape((tokens, H * HD), bf16)] * 4,
        [wide] * 4 + [pltpu.SemaphoreType.DMA((4,))],
        in_specs=[VMEM], out_specs=[anywhere] * 4,
    )(back))


def solution(mesh):
    members = mesh.shape["seq"] // (2 * H)
    parts = {"seq": [("half", 2), ("head", H), ("member", members)]}
    axes = [part for name in mesh.axis_names for part in parts.get(name, [(name, mesh.shape[name])])]
    inner = Mesh(mesh.devices.reshape([size for _, size in axes]), [name for name, _ in axes])
    split = ("dp", "half", "head", "member")
    in_specs = (P(split, None),) * 4 + (P(split),)
    return jax.shard_map(
        functools.partial(per_device, members), mesh=inner, in_specs=in_specs,
        out_specs=(P(split, None),) * 4, check_vma=False,
    )
```

```python
import functools

import jax
import jax.numpy as jnp
import numpy as np
from jax import lax
from jax.experimental import pallas as pl
from jax.experimental.pallas import tpu as pltpu
from jax.sharding import Mesh
from jax.sharding import PartitionSpec as P

H = 8
HD = 128
SEG = 1024

MASKED = -1e30
SCALE = HD ** -0.5
LOG2E = float(np.log2(np.e))
VMEM = pl.BlockSpec(memory_space=pltpu.VMEM)
DOC_ROWS = 16


def dot_nn(a, b):
    return lax.dot_general(a, b, (((1,), (0,)), ((), ())), preferred_element_type=jnp.float32)


def dot_nt(a, b):
    return lax.dot_general(a, b, (((1,), (1,)), ((), ())), preferred_element_type=jnp.float32)


def selector(head, r0, rows, tokens, transposed, fine_first=False):
    r1 = 2 * r0
    shape = (tokens, 2 * rows) if transposed else (2 * rows, tokens)
    k = lax.broadcasted_iota(jnp.int32, shape, 1 if transposed else 0)
    p = lax.broadcasted_iota(jnp.int32, shape, 0 if transposed else 1)
    coarse = head % r1
    other = (coarse + r0) % r1
    first, second = jnp.where(fine_first, other, coarse), jnp.where(fine_first, coarse, other)
    target = jnp.where(k < rows, r1 * k + first, r1 * (k - rows) + second)
    return (p == target).astype(jnp.float32).astype(jnp.bfloat16)


def takes_fine(members):
    return lax.axis_index("member") >= members // 2


def pack_kernel(r0, rows, members, q_in, k_in, v_in, g_in, doc_in, out, q_ref, k_ref, v_ref, g_ref, doc_ref, buf, sem):
    tokens = q_ref.shape[0]
    pairs = ((doc_in, doc_ref), (k_in, k_ref), (v_in, v_ref), (q_in, q_ref), (g_in, g_ref))
    copies = [pltpu.make_async_copy(src, dst, sem.at[i]) for i, (src, dst) in enumerate(pairs)]
    for copy in copies:
        copy.start()
    kinds = range(min(H, 2 * r0))
    key_sels = [selector(h, r0, rows, tokens, False) for h in kinds]
    query_sels = [selector(h, r0, rows, tokens, False, takes_fine(members)) for h in kinds]

    def pick(sels, h, ref):
        return dot_nn(sels[h % (2 * r0)], ref[:, h * HD:(h + 1) * HD]).astype(jnp.bfloat16)

    for copy in copies:
        copy.wait()
    docs = jnp.broadcast_to(doc_ref[...].astype(jnp.float32).astype(jnp.bfloat16), (DOC_ROWS, tokens))
    sends = []
    for h in range(H):
        for i, ref in enumerate((q_ref, g_ref)):
            x = pick(query_sels, h, ref)
            buf[h, i * rows:(1 + i) * rows] = x[:rows]
            buf[h, (2 + i) * rows:(3 + i) * rows] = x[rows:]
        for i, ref in enumerate((k_ref, v_ref)):
            x = pick(key_sels, h, ref)
            buf[h, (4 + i) * rows:(5 + i) * rows] = x[rows:]
            buf[h, (6 + i) * rows:(7 + i) * rows] = x[:rows]
        buf[h, 8 * rows:8 * rows + DOC_ROWS] = docs
        sends.append(pltpu.make_async_copy(buf.at[h], out.at[h], sem.at[5 + h]))
        sends[-1].start()
    for copy in sends:
        copy.wait()


TILES = 2


def tile_sizes(rows, members):
    per = H // TILES
    return per * members * rows, per * 2 * rows


def eye_matrix():
    shape = (HD, HD)
    same = lax.broadcasted_iota(jnp.int32, shape, 0) == lax.broadcasted_iota(jnp.int32, shape, 1)
    return same.astype(jnp.float32).astype(jnp.bfloat16)


def doc_cols(x):
    return dot_nn(x, jnp.ones((HD, HD), jnp.bfloat16))[:, 0:1]


def local_kernel(r0, rows, members, *refs):
    G = members
    r1 = 2 * r0
    own_ref, swap_refs = refs[0], refs[1:G]
    (k1, k2, q_all, g_all, stats, out_ref, gtt_ref), rest = refs[G:G + 7], refs[G + 7:]
    p_refs, dp_refs, (v1, v2, d1, d2) = rest[:2 * TILES], rest[2 * TILES:4 * TILES], rest[4 * TILES:]
    bf16, f32 = jnp.bfloat16, jnp.float32
    tokens = HD
    head = lax.axis_index("head")
    member = lax.axis_index("member")
    fine = takes_fine(G)
    partner = G // 2
    partner_ref = swap_refs[partner - 1]

    sel = selector(head, r0, rows, tokens, False)
    query_sel = jnp.where(fine, sel[rows:].astype(f32), sel[:rows].astype(f32)).astype(bf16)
    source_docs = []
    for j in range(H):
        for g in range(G):
            at = pl.ds((j * G + g) * rows, rows)
            ref, base = (own_ref, 4 * rows) if g == 0 else (swap_refs[g - 1], 2 * rows if g == partner else 0)
            k2[at] = ref[j, base:base + rows]
            v2[at] = ref[j, base + rows:base + 2 * rows]
            k1[at] = ref[j, base + 2 * rows:base + 3 * rows]
            v1[at] = ref[j, base + 3 * rows:base + 4 * rows]
            doc = ref[j, base + 4 * rows:base + 4 * rows + DOC_ROWS][0:1]
            if g in (0, partner):
                source_docs.append(doc)
            d1[at] = sel[:rows] * doc
            d2[at] = sel[rows:] * doc

    eye = eye_matrix()
    v1t, v2t = dot_nt(eye, v1[...]).astype(bf16), dot_nt(eye, v2[...]).astype(bf16)
    docs1, docs2 = doc_cols(d1[...]), doc_cols(d2[...])
    nd, lanes = tile_sizes(rows, G)
    per = H // TILES

    coarse = head % r1
    other = (coarse + r0) % r1
    lane = lax.broadcasted_iota(jnp.int32, (1, lanes), 1)
    qmember = member ^ (partner * ((lane // rows) % 2))
    qpos = (lane // (2 * rows)) * (G * tokens) + qmember * tokens + r1 * (lane % rows) + jnp.where(fine, other, coarse)
    kl = lax.broadcasted_iota(jnp.int32, (nd, 1), 0)
    kmember = member ^ ((kl // rows) % G)
    kpos = (kl // (rows * G)) * (G * tokens) + kmember * tokens + r1 * (kl % rows)
    causal1 = kpos + coarse <= qpos
    causal2 = kpos + other <= qpos
    both = jnp.where(fine, 0.0, 1.0)
    c = SCALE * LOG2E

    for u in range(TILES):
        nk = (u + 1) * nd
        x0 = u * nd
        src = range(u * per, (u + 1) * per)
        mine = slice(u * lanes, (u + 1) * lanes)
        gather = lambda lo: jnp.concatenate([ref[j, lo:lo + rows] for j in src for ref in (own_ref, partner_ref)], 0)
        qt, gt = gather(0), gather(rows)
        q_all[mine], g_all[mine] = qt, gt
        dq = jnp.concatenate([query_sel * source_docs[2 * j + e] for j in src for e in range(2)], 0)
        qdoc = dot_nt(jnp.ones((16, HD), bf16), dq)[0:1]

        def scores(key, docs, causal):
            s = jnp.where(docs == qdoc, dot_nt(key, qt), MASKED)
            if u:
                return jnp.concatenate([s[:x0], jnp.where(causal, s[x0:], MASKED)], 0)
            return jnp.where(causal, s, MASKED)

        s1 = scores(k1[0:nk], docs1[0:nk], causal1)
        s2 = scores(k2[0:nk], docs2[0:nk], causal2)
        top = jnp.maximum(jnp.max(s1, 0, keepdims=True), jnp.max(s2, 0, keepdims=True))
        base = top * c
        p1 = jnp.exp2(s1 * c - (base - both))
        p2 = jnp.exp2(s2 * c - base)
        stats[0:1, mine] = top
        stats[1:2, mine] = jnp.sum(p1, 0, keepdims=True) + jnp.sum(p2, 0, keepdims=True)
        stats[2:3, mine] = qdoc
        out_ref[:, mine] = dot_nn(v1t[:, :nk], p1.astype(bf16)) + dot_nn(v2t[:, :nk], p2.astype(bf16))
        gtt_ref[:, mine] = dot_nt(eye, gt)
        p_refs[2 * u][...], p_refs[2 * u + 1][...] = p1, p2
        dp_refs[2 * u][...], dp_refs[2 * u + 1][...] = dot_nt(v1[0:nk], gt), dot_nt(v2[0:nk], gt)


def finish_tile(u, r0, rows, members, parts, shared, products, results, scratch):
    G = members
    q_all, g_all, stats, local_out, gtt_ref, k1, k2 = shared
    far_stats, att, gq_ref, sums = results[0], results[1], results[2], results[3:]
    kx, vx, dx = scratch
    bf16 = jnp.bfloat16
    half = lax.axis_index("half")
    sel = selector(lax.axis_index("head"), r0, rows, HD, False)
    per = H // TILES
    for p, part in enumerate(parts):
        for j in range(per):
            for g, ref in enumerate(part):
                at = pl.ds(((p * per + j) * G + g) * rows, rows)
                kx[at] = ref[2 * j * rows:(2 * j + 1) * rows]
                vx[at] = ref[(2 * j + 1) * rows:(2 * j + 2) * rows]
                dx[at] = sel[:rows] * ref[2 * per * rows:2 * per * rows + DOC_ROWS][j:j + 1]
    eye = eye_matrix()
    nd, lanes = tile_sizes(rows, G)
    nk = (u + 1) * nd
    mine = slice(u * lanes, (u + 1) * lanes)
    c = SCALE * LOG2E
    keys_x, values_x = kx[...], vx[...]
    kxt, vxt = dot_nt(eye, keys_x).astype(bf16), dot_nt(eye, values_x).astype(bf16)
    docsx = doc_cols(dx[...]) + jnp.where((half == 0) | takes_fine(G), 1000.0, 0.0)
    qt, gt = q_all[mine], g_all[mine]
    top0, total0, qdoc = stats[0:1, mine], stats[1:2, mine], stats[2:3, mine]
    sx = jnp.where(docsx == qdoc, dot_nt(keys_x, qt), MASKED)
    top = jnp.maximum(top0, jnp.max(sx, 0, keepdims=True))
    px = jnp.exp2(sx * c - top * c)
    shrink = jnp.exp2(top0 * c - top * c)
    total = total0 * shrink + jnp.sum(px, 0, keepdims=True)
    inv = 1.0 / total
    local_inv = shrink * inv
    out = local_out[:, mine] * local_inv + dot_nn(vxt, px.astype(bf16)) * inv
    dot = jnp.sum(gtt_ref[:, mine] * out, 0, keepdims=True)
    far_stats[0:1] = top * c + jnp.log(total) * LOG2E
    far_stats[1:2] = dot
    att[...] = out.T.astype(bf16)
    ds = (px * inv * (dot_nt(values_x, gt) - dot)).astype(bf16)
    gq = dot_nn(kxt, ds)
    for i, k in enumerate((k1, k2)):
        w = products[i][...] * local_inv
        ds = (w * (products[2 + i][...] - dot)).astype(bf16)
        gq = gq + dot_nn(dot_nt(eye, k[0:nk]).astype(bf16), ds)
        sums[i][...] = dot_nn(ds, qt)
        sums[2 + i][...] = dot_nn(w.astype(bf16), gt)
    gq_ref[...] = (gq * SCALE).T.astype(bf16)


def last_tile_kernel(r0, rows, members, *refs):
    G = members
    finish_tile(1, r0, rows, G, [refs[:G]], refs[G:G + 7], refs[G + 7:G + 11], refs[G + 11:G + 18], refs[G + 18:])


def first_tile_kernel(r0, rows, members, *refs):
    G = members
    parts, refs = [refs[:G], refs[G:2 * G]], refs[2 * G:]
    shared, products, last, refs = refs[:7], refs[7:11], refs[11:18], refs[18:]
    far_stats, out_own, out_kv, out_swap, scratch = refs[0], refs[1], refs[2], refs[3:G + 2], refs[G + 2:]
    nd, lanes = tile_sizes(rows, G)
    first = (far_stats.at[:, 0:lanes],) + tuple(scratch[:6])
    finish_tile(0, r0, rows, G, parts, shared, products, first, scratch[6:])
    far_stats[:, lanes:] = last[0][...]
    partner, per = G // 2, H // TILES
    for j in range(H):
        att, gq = (first, last)[j // per][1:3]
        for e, ref in enumerate((out_own, out_swap[partner - 1])):
            lo = (2 * (j % per) + e) * rows
            ref[j, 0:rows] = att[lo:lo + rows]
            ref[j, rows:2 * rows] = gq[lo:lo + rows]
        for g in range(G):
            at = pl.ds((j * G + g) * rows, rows)
            gk1, gk2, gv1, gv2 = (last[3 + i][at] + first[3 + i][at] if j < per else last[3 + i][at] for i in range(4))
            ref = out_kv if g == 0 else out_swap[g - 1]
            base = 2 if g == partner else 0
            for i, part in enumerate((gk2 * SCALE, gv2, gk1 * SCALE, gv1), base):
                ref[j, i * rows:(i + 1) * rows] = part.astype(ref.dtype)


def far_rows(query_refs, g, members, u, rows, lo):
    pair = (query_refs[u * members + g], query_refs[u * members + (g ^ (members // 2))])
    return jnp.concatenate([ref[(2 * j + lo) * rows:(2 * j + lo + 1) * rows] for j in range(H // TILES) for ref in pair], 0)


def far_slots(members, body):
    for g in range(members):
        slot = lax.axis_index("member") ^ g

        @pl.when((lax.axis_index("half") == 0) & (slot < members // 2))
        def _(g=g, slot=slot):
            body(g, slot)


def far_kernel(r0, rows, members, own_ref, *refs):
    G = members
    query_refs, products = refs[:TILES * G], refs[TILES * G:]
    sel = selector(lax.axis_index("head"), r0, rows, HD, False)[:rows]
    per = H // TILES
    keys, values = (jnp.concatenate([own_ref[j, lo * rows:(lo + 1) * rows] for j in range(H)], 0) for lo in (6, 7))
    docs = doc_cols(jnp.concatenate([sel * own_ref[j, 8 * rows:8 * rows + DOC_ROWS][0:1] for j in range(H)], 0))

    def body(g, slot):
        for u in range(TILES):
            x0 = u * per * rows
            pair = (query_refs[u * G + g], query_refs[u * G + (g ^ (G // 2))])
            dq = jnp.concatenate([sel * ref[2 * per * rows:2 * per * rows + DOC_ROWS][j:j + 1]
                                  for j in range(per) for ref in pair], 0)
            qdoc = dot_nt(jnp.ones((16, HD), jnp.bfloat16), dq)[0:1]
            s = dot_nt(keys[x0:], far_rows(query_refs, g, G, u, rows, 0)) * (SCALE * LOG2E)
            products[2 * u][slot] = jnp.where(docs[x0:] == qdoc, s, MASKED)
            products[2 * u + 1][slot] = dot_nt(values[x0:], far_rows(query_refs, g, G, u, rows, 1))

    far_slots(G, body)


def far_grads(rows, members, query_refs, stat_ref, products, gk, gv):
    G = members
    per = H // TILES
    gk[...], gv[...] = jnp.zeros_like(gk), jnp.zeros_like(gv)

    def body(g, slot):
        for u in range(TILES):
            x0 = u * per * rows
            mine = slice(u * per * 2 * rows, (u + 1) * per * 2 * rows)
            lse, dot = (stat_ref[8 * g + i:8 * g + i + 1, mine] for i in range(2))
            p = jnp.exp2(products[2 * u][slot] - lse)
            ds = p * (products[2 * u + 1][slot] - dot)
            gk[x0:] += dot_nn(ds.astype(jnp.bfloat16), far_rows(query_refs, g, G, u, rows, 0)) * SCALE
            gv[x0:] += dot_nn(p.astype(jnp.bfloat16), far_rows(query_refs, g, G, u, rows, 1))

    far_slots(G, body)


def sum_kernel(rows, members, *refs):
    G = members
    query_refs, refs = refs[:TILES * G], refs[TILES * G:]
    stat_ref, products, refs = refs[0], refs[1:1 + 2 * TILES], refs[1 + 2 * TILES:]
    own_ref, kv_ref, swap_refs, (out_ref, gk, gv) = refs[0], refs[1], refs[2:G + 1], refs[G + 1:]
    f32, bf16 = jnp.float32, jnp.bfloat16
    far_grads(rows, G, query_refs, stat_ref, products, gk, gv)
    out_ref[:, 0:2 * rows] = own_ref[...]
    out_ref[:, 2 * rows:4 * rows] = swap_refs[G // 2 - 1][:, 0:2 * rows]
    for j in range(H):
        total = kv_ref[j]
        for g, ref in enumerate(swap_refs, 1):
            base = 2 * rows if g == G // 2 else 0
            total = total + ref[j, base:base + 4 * rows].astype(f32)
        mine = slice(j * rows, (j + 1) * rows)
        out_ref[j, 4 * rows:6 * rows] = total[:2 * rows].astype(bf16)
        out_ref[j, 6 * rows:7 * rows] = (total[2 * rows:3 * rows] + gk[mine]).astype(bf16)
        out_ref[j, 7 * rows:8 * rows] = (total[3 * rows:] + gv[mine]).astype(bf16)


def unpack_kernel(r0, rows, members, in_ref, *refs):
    outs, bufs, sem = refs[:4], refs[4:8], refs[8]
    tokens = bufs[0].shape[0]
    bf16 = jnp.bfloat16
    kinds = range(min(H, 2 * r0))
    query_sels = [selector(h, r0, rows, tokens, True, takes_fine(members)) for h in kinds]
    key_sels = [selector(h, r0, rows, tokens, True, True) for h in kinds]
    copies = []
    for i, base in enumerate((0, 1, 4, 5)):
        for h in range(H):
            sels = query_sels if i < 2 else key_sels
            part = jnp.concatenate([in_ref[h, (base + e) * rows:(base + e + 1) * rows] for e in (0, 2)], 0)
            bufs[i][:, h * HD:(h + 1) * HD] = dot_nn(sels[h % (2 * r0)], part).astype(bf16)
        copies.append(pltpu.make_async_copy(bufs[i], outs[i], sem.at[i]))
        copies[-1].start()
    for copy in copies:
        copy.wait()


def call(kernel, out_shape, scratch=(), limit=16, **more):
    return pl.pallas_call(
        kernel,
        out_shape=out_shape,
        scratch_shapes=list(scratch),
        compiler_params=pltpu.CompilerParams(vmem_limit_bytes=limit * 1024 * 1024),
        **more,
    )


def per_device(members, queries, keys, values, cotangent, doc_ids):
    G = members
    tokens = queries.shape[0]
    devices = 2 * H * G
    r0 = tokens * devices // (2 * SEG)
    rows = tokens // (2 * r0)
    bf16, f32 = jnp.bfloat16, jnp.float32
    shape = jax.ShapeDtypeStruct
    n = H * G * rows
    anywhere = pl.BlockSpec(memory_space=pltpu.HBM)
    wide = pltpu.VMEM((tokens, H * HD), bf16)
    message = (H, 8 * rows + DOC_ROWS, HD)

    packed = call(
        functools.partial(pack_kernel, r0, rows, G), shape(message, bf16),
        [wide] * 4 + [pltpu.VMEM((1, tokens), jnp.int32), pltpu.VMEM(message, bf16), pltpu.SemaphoreType.DMA((5 + H,))],
        limit=64, in_specs=[anywhere] * 5, out_specs=anywhere,
    )(queries, keys, values, cotangent, doc_ids.reshape(1, tokens))

    def to_head(x):
        return lax.all_to_all(x, "head", 0, 0, tiled=True)

    def to_member(x, g):
        return lax.ppermute(x, "member", [(i, i ^ g) for i in range(G)])

    def across(x):
        return lax.ppermute(x, "half", [(0, 1), (1, 0)])

    own = to_head(packed)
    queries_here = jnp.where(takes_fine(G), own[:, 2 * rows:4 * rows], own[:, :2 * rows])
    sent_across = jnp.where(lax.axis_index("half") == 0, own[:, 6 * rows:8 * rows], queries_here)
    per = H // TILES

    def part_across(u):
        at = slice(u * per, (u + 1) * per)
        docs = jnp.pad(own[at, 8 * rows], ((0, DOC_ROWS - per), (0, 0)))
        return across(jnp.concatenate([sent_across[at].reshape(-1, HD), docs], 0))

    upper, lower = part_across(1), part_across(0)
    swaps = [to_member(own[:, (2 if g == G // 2 else 4) * rows:], g) for g in range(1, G)]
    nd, lanes = tile_sizes(rows, G)
    nq = TILES * lanes
    tile = [shape(((u + 1) * nd, lanes), f32) for u in range(TILES) for _ in range(2)]
    key_rows = pltpu.VMEM((n, HD), bf16)
    k1, k2, q_all, g_all, stats, out, gtt, *products = call(
        functools.partial(local_kernel, r0, rows, G),
        [shape((n, HD), bf16)] * 2 + [shape((nq, HD), bf16)] * 2 + [shape((8, nq), f32)]
        + [shape((HD, nq), f32)] * 2 + tile * 2,
        [key_rows] * 4, limit=32,
    )(own, *swaps)
    shared = (q_all, g_all, stats, out, gtt, k1, k2)
    upper, k1 = lax.optimization_barrier((upper, k1))
    uppers = [upper] + [to_member(upper, g) for g in range(1, G)]
    rows_x, tile_rows = pltpu.VMEM((nd, HD), bf16), pltpu.VMEM((lanes, HD), bf16)
    last = call(
        functools.partial(last_tile_kernel, r0, rows, G),
        [shape((8, lanes), f32)] + [shape((lanes, HD), bf16)] * 2 + [shape((n, HD), f32)] * 4,
        [rows_x] * 3, limit=32,
    )(*uppers, *shared, *products[2:4], *products[6:8])
    lowers = [lower] + [to_member(lower, g) for g in range(1, G)]
    sent = lambda g: (H, (6 if g == G // 2 else 4) * rows, HD)
    outs = call(
        functools.partial(first_tile_kernel, r0, rows, G),
        [shape((8, nq), f32), shape((H, 2 * rows, HD), bf16), shape((H, 4 * rows, HD), f32)]
        + [shape(sent(g), bf16) for g in range(1, G)],
        [tile_rows] * 2 + [pltpu.VMEM((nd, HD), f32)] * 4 + [key_rows] * 3, limit=32,
    )(*lowers, *uppers, *shared, *products[0:2], *products[4:6], *last)
    crosses = lowers + uppers
    far_stats = across(jnp.concatenate([outs[0]] + [to_member(outs[0], g) for g in range(1, G)], 0))
    products = call(
        functools.partial(far_kernel, r0, rows, G),
        [shape((G // 2, (TILES - u) * nd // G, lanes), f32) for u in range(TILES) for _ in range(2)],
    )(own, *crosses)
    swaps = [to_member(outs[2 + g], g) for g in range(1, G)]
    back = call(
        functools.partial(sum_kernel, rows, G), shape((H, 8 * rows, HD), bf16),
        [pltpu.VMEM((H * rows, HD), f32)] * 2,
    )(*crosses, far_stats, *products, outs[1], outs[2], *swaps)
    back = to_head(back)
    return tuple(call(
        functools.partial(unpack_kernel, r0, rows, G), [shape((tokens, H * HD), bf16)] * 4,
        [wide] * 4 + [pltpu.SemaphoreType.DMA((4,))],
        in_specs=[VMEM], out_specs=[anywhere] * 4,
    )(back))


def solution(mesh):
    members = mesh.shape["seq"] // (2 * H)
    parts = {"seq": [("half", 2), ("head", H), ("member", members)]}
    axes = [part for name in mesh.axis_names for part in parts.get(name, [(name, mesh.shape[name])])]
    inner = Mesh(mesh.devices.reshape([size for _, size in axes]), [name for name, _ in axes])
    split = ("dp", "half", "head", "member")
    in_specs = (P(split, None),) * 4 + (P(split),)
    return jax.shard_map(
        functools.partial(per_device, members), mesh=inner, in_specs=in_specs,
        out_specs=(P(split, None),) * 4, check_vma=False,
    )
```

```python
import functools

import jax
import jax.numpy as jnp
import numpy as np
from jax import lax
from jax.experimental import pallas as pl
from jax.experimental.pallas import tpu as pltpu
from jax.sharding import Mesh
from jax.sharding import PartitionSpec as P

H = 8
HD = 128
SEG = 1024

MASKED = -1e30
SCALE = HD ** -0.5
LOG2E = float(np.log2(np.e))
VMEM = pl.BlockSpec(memory_space=pltpu.VMEM)
DOC_ROWS = 16


def dot_nn(a, b):
    return lax.dot_general(a, b, (((1,), (0,)), ((), ())), preferred_element_type=jnp.float32)


def dot_nt(a, b):
    return lax.dot_general(a, b, (((1,), (1,)), ((), ())), preferred_element_type=jnp.float32)


def selector(head, r0, rows, tokens, transposed, fine_first=False):
    r1 = 2 * r0
    shape = (tokens, 2 * rows) if transposed else (2 * rows, tokens)
    k = lax.broadcasted_iota(jnp.int32, shape, 1 if transposed else 0)
    p = lax.broadcasted_iota(jnp.int32, shape, 0 if transposed else 1)
    coarse = head % r1
    other = (coarse + r0) % r1
    first, second = jnp.where(fine_first, other, coarse), jnp.where(fine_first, coarse, other)
    target = jnp.where(k < rows, r1 * k + first, r1 * (k - rows) + second)
    return (p == target).astype(jnp.float32).astype(jnp.bfloat16)


def takes_fine(members):
    return lax.axis_index("member") >= members // 2


def pack_kernel(r0, rows, members, q_in, k_in, v_in, g_in, doc_in, out, q_ref, k_ref, v_ref, g_ref, doc_ref, buf, sem):
    tokens = q_ref.shape[0]
    pairs = ((doc_in, doc_ref), (k_in, k_ref), (v_in, v_ref), (q_in, q_ref), (g_in, g_ref))
    copies = [pltpu.make_async_copy(src, dst, sem.at[i]) for i, (src, dst) in enumerate(pairs)]
    for copy in copies:
        copy.start()
    kinds = range(min(H, 2 * r0))
    key_sels = [selector(h, r0, rows, tokens, False) for h in kinds]
    query_sels = [selector(h, r0, rows, tokens, False, takes_fine(members)) for h in kinds]

    def pick(sels, h, ref):
        return dot_nn(sels[h % (2 * r0)], ref[:, h * HD:(h + 1) * HD]).astype(jnp.bfloat16)

    for copy in copies:
        copy.wait()
    docs = jnp.broadcast_to(doc_ref[...].astype(jnp.float32).astype(jnp.bfloat16), (DOC_ROWS, tokens))
    sends = []
    for h in range(H):
        for i, ref in enumerate((q_ref, g_ref)):
            x = pick(query_sels, h, ref)
            buf[h, i * rows:(1 + i) * rows] = x[:rows]
            buf[h, (2 + i) * rows:(3 + i) * rows] = x[rows:]
        for i, ref in enumerate((k_ref, v_ref)):
            x = pick(key_sels, h, ref)
            buf[h, (4 + i) * rows:(5 + i) * rows] = x[rows:]
            buf[h, (6 + i) * rows:(7 + i) * rows] = x[:rows]
        buf[h, 8 * rows:8 * rows + DOC_ROWS] = docs
        sends.append(pltpu.make_async_copy(buf.at[h], out.at[h], sem.at[5 + h]))
        sends[-1].start()
    for copy in sends:
        copy.wait()


TILES = 2


def tile_sizes(rows, members):
    per = H // TILES
    return per * members * rows, per * 2 * rows


def eye_matrix():
    shape = (HD, HD)
    same = lax.broadcasted_iota(jnp.int32, shape, 0) == lax.broadcasted_iota(jnp.int32, shape, 1)
    return same.astype(jnp.float32).astype(jnp.bfloat16)


def doc_cols(x):
    return dot_nn(x, jnp.ones((HD, HD), jnp.bfloat16))[:, 0:1]


def local_kernel(r0, rows, members, *refs):
    G = members
    r1 = 2 * r0
    own_ref, swap_refs = refs[0], refs[1:G]
    (k1, k2, q_all, g_all, stats, out_ref, gtt_ref), rest = refs[G:G + 7], refs[G + 7:]
    p_refs, dp_refs, (v1, v2, d1, d2) = rest[:2 * TILES], rest[2 * TILES:4 * TILES], rest[4 * TILES:]
    bf16, f32 = jnp.bfloat16, jnp.float32
    tokens = HD
    head = lax.axis_index("head")
    member = lax.axis_index("member")
    fine = takes_fine(G)
    partner = G // 2
    partner_ref = swap_refs[partner - 1]

    sel = selector(head, r0, rows, tokens, False)
    query_sel = jnp.where(fine, sel[rows:].astype(f32), sel[:rows].astype(f32)).astype(bf16)
    source_docs = []
    for j in range(H):
        for g in range(G):
            at = pl.ds((j * G + g) * rows, rows)
            ref, base = (own_ref, 4 * rows) if g == 0 else (swap_refs[g - 1], 2 * rows if g == partner else 0)
            k2[at] = ref[j, base:base + rows]
            v2[at] = ref[j, base + rows:base + 2 * rows]
            k1[at] = ref[j, base + 2 * rows:base + 3 * rows]
            v1[at] = ref[j, base + 3 * rows:base + 4 * rows]
            doc = ref[j, base + 4 * rows:base + 4 * rows + DOC_ROWS][0:1]
            if g in (0, partner):
                source_docs.append(doc)
            d1[at] = sel[:rows] * doc
            d2[at] = sel[rows:] * doc

    eye = eye_matrix()
    v1t, v2t = dot_nt(eye, v1[...]).astype(bf16), dot_nt(eye, v2[...]).astype(bf16)
    docs1, docs2 = doc_cols(d1[...]), doc_cols(d2[...])
    nd, lanes = tile_sizes(rows, G)
    per = H // TILES

    coarse = head % r1
    other = (coarse + r0) % r1
    lane = lax.broadcasted_iota(jnp.int32, (1, lanes), 1)
    qmember = member ^ (partner * ((lane // rows) % 2))
    qpos = (lane // (2 * rows)) * (G * tokens) + qmember * tokens + r1 * (lane % rows) + jnp.where(fine, other, coarse)
    kl = lax.broadcasted_iota(jnp.int32, (nd, 1), 0)
    kmember = member ^ ((kl // rows) % G)
    kpos = (kl // (rows * G)) * (G * tokens) + kmember * tokens + r1 * (kl % rows)
    causal1 = kpos + coarse <= qpos
    causal2 = kpos + other <= qpos
    both = jnp.where(fine, 0.0, 1.0)
    c = SCALE * LOG2E

    for u in range(TILES):
        nk = (u + 1) * nd
        x0 = u * nd
        src = range(u * per, (u + 1) * per)
        mine = slice(u * lanes, (u + 1) * lanes)
        gather = lambda lo: jnp.concatenate([ref[j, lo:lo + rows] for j in src for ref in (own_ref, partner_ref)], 0)
        qt, gt = gather(0), gather(rows)
        q_all[mine], g_all[mine] = qt, gt
        dq = jnp.concatenate([query_sel * source_docs[2 * j + e] for j in src for e in range(2)], 0)
        qdoc = dot_nt(jnp.ones((16, HD), bf16), dq)[0:1]

        def scores(key, docs, causal):
            s = jnp.where(docs == qdoc, dot_nt(key, qt), MASKED)
            if u:
                return jnp.concatenate([s[:x0], jnp.where(causal, s[x0:], MASKED)], 0)
            return jnp.where(causal, s, MASKED)

        s1 = scores(k1[0:nk], docs1[0:nk], causal1)
        s2 = scores(k2[0:nk], docs2[0:nk], causal2)
        top = jnp.maximum(jnp.max(s1, 0, keepdims=True), jnp.max(s2, 0, keepdims=True))
        base = top * c
        p1 = jnp.exp2(s1 * c - (base - both))
        p2 = jnp.exp2(s2 * c - base)
        stats[0:1, mine] = top
        stats[1:2, mine] = jnp.sum(p1, 0, keepdims=True) + jnp.sum(p2, 0, keepdims=True)
        stats[2:3, mine] = qdoc
        out_ref[:, mine] = dot_nn(v1t[:, :nk], p1.astype(bf16)) + dot_nn(v2t[:, :nk], p2.astype(bf16))
        gtt_ref[:, mine] = dot_nt(eye, gt)
        p_refs[2 * u][...], p_refs[2 * u + 1][...] = p1, p2
        dp_refs[2 * u][...], dp_refs[2 * u + 1][...] = dot_nt(v1[0:nk], gt), dot_nt(v2[0:nk], gt)


def finish_tile(u, r0, rows, members, parts, shared, products, results, scratch):
    G = members
    q_all, g_all, stats, local_out, gtt_ref, k1, k2 = shared
    far_stats, att, gq_ref, sums = results[0], results[1], results[2], results[3:]
    kx, vx, dx, px, out_x, gq_x, tops = scratch
    bf16 = jnp.bfloat16
    far = (lax.axis_index("half") == 1) & jnp.logical_not(takes_fine(G))
    sel = selector(lax.axis_index("head"), r0, rows, HD, False)
    per = H // TILES
    eye = eye_matrix()
    nd, lanes = tile_sizes(rows, G)
    nk = (u + 1) * nd
    mine = slice(u * lanes, (u + 1) * lanes)
    c = SCALE * LOG2E
    qt, gt = q_all[mine], g_all[mine]
    top0, total0, qdoc = stats[0:1, mine], stats[1:2, mine], stats[2:3, mine]
    tops[0:1], tops[1:2] = top0, jnp.zeros_like(top0)
    out_x[...], gq_x[...] = jnp.zeros_like(out_x), jnp.zeros_like(gq_x)

    @pl.when(far)
    def _():
        for p, part in enumerate(parts):
            for j in range(per):
                for g, ref in enumerate(part):
                    at = pl.ds(((p * per + j) * G + g) * rows, rows)
                    kx[at] = ref[2 * j * rows:(2 * j + 1) * rows]
                    vx[at] = ref[(2 * j + 1) * rows:(2 * j + 2) * rows]
                    dx[at] = sel[:rows] * ref[2 * per * rows:2 * per * rows + DOC_ROWS][j:j + 1]
        sx = jnp.where(doc_cols(dx[...]) == qdoc, dot_nt(kx[...], qt), MASKED)
        top = jnp.maximum(top0, jnp.max(sx, 0, keepdims=True))
        p = jnp.exp2(sx * c - top * c)
        px[...] = p
        tops[0:1], tops[1:2] = top, jnp.sum(p, 0, keepdims=True)
        out_x[...] = dot_nn(dot_nt(eye, vx[...]).astype(bf16), p.astype(bf16))

    top = tops[0:1]
    shrink = jnp.exp2(top0 * c - top * c)
    total = total0 * shrink + tops[1:2]
    inv = 1.0 / total
    local_inv = shrink * inv
    out = local_out[:, mine] * local_inv + out_x[...] * inv
    dot = jnp.sum(gtt_ref[:, mine] * out, 0, keepdims=True)
    lse = top * c + jnp.log(total) * LOG2E
    chunks = lanes // HD
    for i in range(chunks):
        far_stats[u * chunks + i:u * chunks + i + 1] = lse[:, i * HD:(i + 1) * HD]
        far_stats[4 + u * chunks + i:5 + u * chunks + i] = dot[:, i * HD:(i + 1) * HD]
    att[...] = out.T.astype(bf16)

    @pl.when(far)
    def _():
        ds = (px[...] * inv * (dot_nt(vx[...], gt) - dot)).astype(bf16)
        gq_x[...] = dot_nn(dot_nt(eye, kx[...]).astype(bf16), ds)

    gq = gq_x[...]
    for i, k in enumerate((k1, k2)):
        w = products[i][...] * local_inv
        ds = (w * (products[2 + i][...] - dot)).astype(bf16)
        gq = gq + dot_nn(dot_nt(eye, k[0:nk]).astype(bf16), ds)
        sums[i][...] = dot_nn(ds, qt)
        sums[2 + i][...] = dot_nn(w.astype(bf16), gt)
    gq_ref[...] = (gq * SCALE).T.astype(bf16)


def last_tile_kernel(r0, rows, members, *refs):
    G = members
    finish_tile(1, r0, rows, G, [refs[:G]], refs[G:G + 7], refs[G + 7:G + 11], refs[G + 11:G + 18], refs[G + 18:])


def first_tile_kernel(r0, rows, members, *refs):
    G = members
    parts, refs = [refs[:G], refs[G:2 * G]], refs[2 * G:]
    shared, products, last, refs = refs[:7], refs[7:11], refs[11:18], refs[18:]
    far_stats, out_own, out_kv, out_swap, scratch = refs[0], refs[1], refs[2], refs[3:G + 2], refs[G + 2:]
    nd, lanes = tile_sizes(rows, G)
    first = (far_stats,) + tuple(scratch[:6])
    far_stats[...] = last[0][...]
    finish_tile(0, r0, rows, G, parts, shared, products, first, scratch[6:])
    partner, per = G // 2, H // TILES
    for j in range(H):
        att, gq = (first, last)[j // per][1:3]
        for e, ref in enumerate((out_own, out_swap[partner - 1])):
            lo = (2 * (j % per) + e) * rows
            ref[j, 0:rows] = att[lo:lo + rows]
            ref[j, rows:2 * rows] = gq[lo:lo + rows]
        for g in range(G):
            at = pl.ds((j * G + g) * rows, rows)
            gk1, gk2, gv1, gv2 = (last[3 + i][at] + first[3 + i][at] if j < per else last[3 + i][at] for i in range(4))
            ref = out_kv if g == 0 else out_swap[g - 1]
            base = 2 if g == partner else 0
            for i, part in enumerate((gk2 * SCALE, gv2, gk1 * SCALE, gv1), base):
                ref[j, i * rows:(i + 1) * rows] = part.astype(ref.dtype)


def far_rows(query_refs, g, members, u, rows, lo):
    pair = (query_refs[u * members + g], query_refs[u * members + (g ^ (members // 2))])
    return jnp.concatenate([ref[(2 * j + lo) * rows:(2 * j + lo + 1) * rows] for j in range(H // TILES) for ref in pair], 0)


def far_slots(members, body):
    for g in range(members):
        slot = lax.axis_index("member") ^ g

        @pl.when((lax.axis_index("half") == 0) & (slot < members // 2))
        def _(g=g, slot=slot):
            body(g, slot)


def far_kernel(r0, rows, members, own_ref, *refs):
    G = members
    query_refs, products = refs[:TILES * G], refs[TILES * G:]
    sel = selector(lax.axis_index("head"), r0, rows, HD, False)[:rows]
    per = H // TILES
    keys, values = (jnp.concatenate([own_ref[j, lo * rows:(lo + 1) * rows] for j in range(H)], 0) for lo in (6, 7))
    docs = doc_cols(jnp.concatenate([sel * own_ref[j, 8 * rows:8 * rows + DOC_ROWS][0:1] for j in range(H)], 0))

    def body(g, slot):
        for u in range(TILES):
            x0 = u * per * rows
            pair = (query_refs[u * G + g], query_refs[u * G + (g ^ (G // 2))])
            dq = jnp.concatenate([sel * ref[2 * per * rows:2 * per * rows + DOC_ROWS][j:j + 1]
                                  for j in range(per) for ref in pair], 0)
            qdoc = dot_nt(jnp.ones((16, HD), jnp.bfloat16), dq)[0:1]
            s = dot_nt(keys[x0:], far_rows(query_refs, g, G, u, rows, 0)) * (SCALE * LOG2E)
            products[2 * u][slot] = jnp.where(docs[x0:] == qdoc, s, MASKED)
            products[2 * u + 1][slot] = dot_nt(values[x0:], far_rows(query_refs, g, G, u, rows, 1))

    far_slots(G, body)


def far_grads(rows, members, query_refs, stat_ref, products, gk, gv):
    G = members
    per = H // TILES
    gk[...], gv[...] = jnp.zeros_like(gk), jnp.zeros_like(gv)

    def body(g, slot):
        for u in range(TILES):
            x0 = u * per * rows
            chunks = per * 2 * rows // HD
            lse, dot = (jnp.concatenate([stat_ref[at + i:at + i + 1] for i in range(chunks)], 1)
                        for at in (8 * g + u * chunks, 8 * g + 4 + u * chunks))
            p = jnp.exp2(products[2 * u][slot] - lse)
            ds = p * (products[2 * u + 1][slot] - dot)
            gk[x0:] += dot_nn(ds.astype(jnp.bfloat16), far_rows(query_refs, g, G, u, rows, 0)) * SCALE
            gv[x0:] += dot_nn(p.astype(jnp.bfloat16), far_rows(query_refs, g, G, u, rows, 1))

    far_slots(G, body)


def sum_kernel(rows, members, *refs):
    G = members
    query_refs, refs = refs[:TILES * G], refs[TILES * G:]
    stat_ref, products, refs = refs[0], refs[1:1 + 2 * TILES], refs[1 + 2 * TILES:]
    own_ref, kv_ref, swap_refs, (out_ref, gk, gv) = refs[0], refs[1], refs[2:G + 1], refs[G + 1:]
    f32, bf16 = jnp.float32, jnp.bfloat16
    far_grads(rows, G, query_refs, stat_ref, products, gk, gv)
    out_ref[:, 0:2 * rows] = own_ref[...]
    out_ref[:, 2 * rows:4 * rows] = swap_refs[G // 2 - 1][:, 0:2 * rows]
    for j in range(H):
        total = kv_ref[j]
        for g, ref in enumerate(swap_refs, 1):
            base = 2 * rows if g == G // 2 else 0
            total = total + ref[j, base:base + 4 * rows].astype(f32)
        mine = slice(j * rows, (j + 1) * rows)
        out_ref[j, 4 * rows:6 * rows] = total[:2 * rows].astype(bf16)
        out_ref[j, 6 * rows:7 * rows] = (total[2 * rows:3 * rows] + gk[mine]).astype(bf16)
        out_ref[j, 7 * rows:8 * rows] = (total[3 * rows:] + gv[mine]).astype(bf16)


def unpack_kernel(r0, rows, members, in_ref, *refs):
    outs, bufs, sem = refs[:4], refs[4:8], refs[8]
    tokens = bufs[0].shape[0]
    bf16 = jnp.bfloat16
    kinds = range(min(H, 2 * r0))
    query_sels = [selector(h, r0, rows, tokens, True, takes_fine(members)) for h in kinds]
    key_sels = [selector(h, r0, rows, tokens, True, True) for h in kinds]
    copies = []
    for i, base in enumerate((0, 1, 4, 5)):
        for h in range(H):
            sels = query_sels if i < 2 else key_sels
            part = jnp.concatenate([in_ref[h, (base + e) * rows:(base + e + 1) * rows] for e in (0, 2)], 0)
            bufs[i][:, h * HD:(h + 1) * HD] = dot_nn(sels[h % (2 * r0)], part).astype(bf16)
        copies.append(pltpu.make_async_copy(bufs[i], outs[i], sem.at[i]))
        copies[-1].start()
    for copy in copies:
        copy.wait()


def call(kernel, out_shape, scratch=(), limit=16, **more):
    return pl.pallas_call(
        kernel,
        out_shape=out_shape,
        scratch_shapes=list(scratch),
        compiler_params=pltpu.CompilerParams(vmem_limit_bytes=limit * 1024 * 1024),
        **more,
    )


def per_device(members, queries, keys, values, cotangent, doc_ids):
    G = members
    tokens = queries.shape[0]
    devices = 2 * H * G
    r0 = tokens * devices // (2 * SEG)
    rows = tokens // (2 * r0)
    bf16, f32 = jnp.bfloat16, jnp.float32
    shape = jax.ShapeDtypeStruct
    n = H * G * rows
    anywhere = pl.BlockSpec(memory_space=pltpu.HBM)
    wide = pltpu.VMEM((tokens, H * HD), bf16)
    message = (H, 8 * rows + DOC_ROWS, HD)

    packed = call(
        functools.partial(pack_kernel, r0, rows, G), shape(message, bf16),
        [wide] * 4 + [pltpu.VMEM((1, tokens), jnp.int32), pltpu.VMEM(message, bf16), pltpu.SemaphoreType.DMA((5 + H,))],
        limit=64, in_specs=[anywhere] * 5, out_specs=anywhere,
    )(queries, keys, values, cotangent, doc_ids.reshape(1, tokens))

    def to_head(x):
        return lax.all_to_all(x, "head", 0, 0, tiled=True)

    def to_member(x, g):
        return lax.ppermute(x, "member", [(i, i ^ g) for i in range(G)])

    def across(x):
        return lax.ppermute(x, "half", [(0, 1), (1, 0)])

    own = to_head(packed)
    queries_here = jnp.where(takes_fine(G), own[:, 2 * rows:4 * rows], own[:, :2 * rows])
    sent_across = jnp.where(lax.axis_index("half") == 0, own[:, 6 * rows:8 * rows], queries_here)
    per = H // TILES

    def part_across(u):
        at = slice(u * per, (u + 1) * per)
        docs = jnp.pad(own[at, 8 * rows], ((0, DOC_ROWS - per), (0, 0)))
        return across(jnp.concatenate([sent_across[at].reshape(-1, HD), docs], 0))

    upper, lower = part_across(1), part_across(0)
    swaps = [to_member(own[:, (2 if g == G // 2 else 4) * rows:], g) for g in range(1, G)]
    nd, lanes = tile_sizes(rows, G)
    nq = TILES * lanes
    tile = [shape(((u + 1) * nd, lanes), f32) for u in range(TILES) for _ in range(2)]
    key_rows = pltpu.VMEM((n, HD), bf16)
    k1, k2, q_all, g_all, stats, out, gtt, *products = call(
        functools.partial(local_kernel, r0, rows, G),
        [shape((n, HD), bf16)] * 2 + [shape((nq, HD), bf16)] * 2 + [shape((8, nq), f32)]
        + [shape((HD, nq), f32)] * 2 + tile * 2,
        [key_rows] * 4, limit=32,
    )(own, *swaps)
    shared = (q_all, g_all, stats, out, gtt, k1, k2)
    upper, k1 = lax.optimization_barrier((upper, k1))
    uppers = [upper] + [to_member(upper, g) for g in range(1, G)]
    tile_rows, tile_columns = pltpu.VMEM((lanes, HD), bf16), pltpu.VMEM((HD, lanes), f32)
    far_scratch = lambda keys: [pltpu.VMEM((keys, HD), bf16)] * 3 + [pltpu.VMEM((keys, lanes), f32)] + [tile_columns] * 2 + [
        pltpu.VMEM((8, lanes), f32)]
    last = call(
        functools.partial(last_tile_kernel, r0, rows, G),
        [shape((8, HD), f32)] + [shape((lanes, HD), bf16)] * 2 + [shape((n, HD), f32)] * 4,
        far_scratch(nd), limit=32,
    )(*uppers, *shared, *products[2:4], *products[6:8])
    lowers = [lower] + [to_member(lower, g) for g in range(1, G)]
    sent = lambda g: (H, (6 if g == G // 2 else 4) * rows, HD)
    outs = call(
        functools.partial(first_tile_kernel, r0, rows, G),
        [shape((8, HD), f32), shape((H, 2 * rows, HD), bf16), shape((H, 4 * rows, HD), f32)]
        + [shape(sent(g), bf16) for g in range(1, G)],
        [tile_rows] * 2 + [pltpu.VMEM((nd, HD), f32)] * 4 + far_scratch(n), limit=32,
    )(*lowers, *uppers, *shared, *products[0:2], *products[4:6], *last)
    crosses = lowers + uppers
    far_stats = across(jnp.concatenate([outs[0]] + [to_member(outs[0], g) for g in range(1, G)], 0))
    products = call(
        functools.partial(far_kernel, r0, rows, G),
        [shape((G // 2, (TILES - u) * nd // G, lanes), f32) for u in range(TILES) for _ in range(2)],
    )(own, *crosses)
    swaps = [to_member(outs[2 + g], g) for g in range(1, G)]
    back = call(
        functools.partial(sum_kernel, rows, G), shape((H, 8 * rows, HD), bf16),
        [pltpu.VMEM((H * rows, HD), f32)] * 2,
    )(*crosses, far_stats, *products, outs[1], outs[2], *swaps)
    back = to_head(back)
    return tuple(call(
        functools.partial(unpack_kernel, r0, rows, G), [shape((tokens, H * HD), bf16)] * 4,
        [wide] * 4 + [pltpu.SemaphoreType.DMA((4,))],
        in_specs=[VMEM], out_specs=[anywhere] * 4,
    )(back))


def solution(mesh):
    members = mesh.shape["seq"] // (2 * H)
    parts = {"seq": [("half", 2), ("head", H), ("member", members)]}
    axes = [part for name in mesh.axis_names for part in parts.get(name, [(name, mesh.shape[name])])]
    inner = Mesh(mesh.devices.reshape([size for _, size in axes]), [name for name, _ in axes])
    split = ("dp", "half", "head", "member")
    in_specs = (P(split, None),) * 4 + (P(split),)
    return jax.shard_map(
        functools.partial(per_device, members), mesh=inner, in_specs=in_specs,
        out_specs=(P(split, None),) * 4, check_vma=False,
    )
```

```python
import functools

import jax
import jax.numpy as jnp
import numpy as np
from jax import lax
from jax.experimental import pallas as pl
from jax.experimental.pallas import tpu as pltpu
from jax.sharding import Mesh
from jax.sharding import PartitionSpec as P

H = 8
HD = 128
SEG = 1024

MASKED = -1e30
SCALE = HD ** -0.5
LOG2E = float(np.log2(np.e))
VMEM = pl.BlockSpec(memory_space=pltpu.VMEM)
DOC_ROWS = 16


def dot_nn(a, b):
    return lax.dot_general(a, b, (((1,), (0,)), ((), ())), preferred_element_type=jnp.float32)


def dot_nt(a, b):
    return lax.dot_general(a, b, (((1,), (1,)), ((), ())), preferred_element_type=jnp.float32)


def selector(head, r0, rows, tokens, transposed, fine_first=False):
    r1 = 2 * r0
    shape = (tokens, 2 * rows) if transposed else (2 * rows, tokens)
    k = lax.broadcasted_iota(jnp.int32, shape, 1 if transposed else 0)
    p = lax.broadcasted_iota(jnp.int32, shape, 0 if transposed else 1)
    coarse = head % r1
    other = (coarse + r0) % r1
    first, second = jnp.where(fine_first, other, coarse), jnp.where(fine_first, coarse, other)
    target = jnp.where(k < rows, r1 * k + first, r1 * (k - rows) + second)
    return (p == target).astype(jnp.float32).astype(jnp.bfloat16)


def takes_fine(members):
    return lax.axis_index("member") >= members // 2


def pack_kernel(r0, rows, members, q_in, k_in, v_in, g_in, doc_in, out, q_ref, k_ref, v_ref, g_ref, doc_ref, buf, sem):
    tokens = q_ref.shape[0]
    pairs = ((doc_in, doc_ref), (k_in, k_ref), (v_in, v_ref), (q_in, q_ref), (g_in, g_ref))
    copies = [pltpu.make_async_copy(src, dst, sem.at[i]) for i, (src, dst) in enumerate(pairs)]
    for copy in copies:
        copy.start()
    kinds = range(min(H, 2 * r0))
    key_sels = [selector(h, r0, rows, tokens, False) for h in kinds]
    query_sels = [selector(h, r0, rows, tokens, False, takes_fine(members)) for h in kinds]

    def pick(sels, h, ref):
        return dot_nn(sels[h % (2 * r0)], ref[:, h * HD:(h + 1) * HD]).astype(jnp.bfloat16)

    for copy in copies:
        copy.wait()
    docs = jnp.broadcast_to(doc_ref[...].astype(jnp.float32).astype(jnp.bfloat16), (DOC_ROWS, tokens))
    sends = []
    for h in range(H):
        for i, ref in enumerate((q_ref, g_ref)):
            x = pick(query_sels, h, ref)
            buf[h, i * rows:(1 + i) * rows] = x[:rows]
            buf[h, (2 + i) * rows:(3 + i) * rows] = x[rows:]
        for i, ref in enumerate((k_ref, v_ref)):
            x = pick(key_sels, h, ref)
            buf[h, (4 + i) * rows:(5 + i) * rows] = x[rows:]
            buf[h, (6 + i) * rows:(7 + i) * rows] = x[:rows]
        buf[h, 8 * rows:8 * rows + DOC_ROWS] = docs
        sends.append(pltpu.make_async_copy(buf.at[h], out.at[h], sem.at[5 + h]))
        sends[-1].start()
    for copy in sends:
        copy.wait()


TILES = 2


def tile_sizes(rows, members):
    per = H // TILES
    return per * members * rows, per * 2 * rows


def eye_matrix():
    shape = (HD, HD)
    same = lax.broadcasted_iota(jnp.int32, shape, 0) == lax.broadcasted_iota(jnp.int32, shape, 1)
    return same.astype(jnp.float32).astype(jnp.bfloat16)


def doc_cols(x):
    return dot_nn(x, jnp.ones((HD, HD), jnp.bfloat16))[:, 0:1]


def local_kernel(r0, rows, members, *refs):
    G = members
    r1 = 2 * r0
    own_ref, swap_refs = refs[0], refs[1:G]
    (k1, k2, q_all, g_all, stats, out_ref, gtt_ref), rest = refs[G:G + 7], refs[G + 7:]
    p_refs, dp_refs, (v1, v2, d1, d2) = rest[:2 * TILES], rest[2 * TILES:4 * TILES], rest[4 * TILES:]
    bf16, f32 = jnp.bfloat16, jnp.float32
    tokens = HD
    head = lax.axis_index("head")
    member = lax.axis_index("member")
    fine = takes_fine(G)
    partner = G // 2
    partner_ref = swap_refs[partner - 1]

    sel = selector(head, r0, rows, tokens, False)
    query_sel = jnp.where(fine, sel[rows:].astype(f32), sel[:rows].astype(f32)).astype(bf16)
    source_docs = []
    for j in range(H):
        for g in range(G):
            at = pl.ds((j * G + g) * rows, rows)
            ref, base = (own_ref, 4 * rows) if g == 0 else (swap_refs[g - 1], 2 * rows if g == partner else 0)
            k2[at] = ref[j, base:base + rows]
            v2[at] = ref[j, base + rows:base + 2 * rows]
            k1[at] = ref[j, base + 2 * rows:base + 3 * rows]
            v1[at] = ref[j, base + 3 * rows:base + 4 * rows]
            doc = ref[j, base + 4 * rows:base + 4 * rows + DOC_ROWS][0:1]
            if g in (0, partner):
                source_docs.append(doc)
            d1[at] = sel[:rows] * doc
            d2[at] = sel[rows:] * doc

    eye = eye_matrix()
    v1t, v2t = dot_nt(eye, v1[...]).astype(bf16), dot_nt(eye, v2[...]).astype(bf16)
    docs1, docs2 = doc_cols(d1[...]), doc_cols(d2[...])
    nd, lanes = tile_sizes(rows, G)
    per = H // TILES

    coarse = head % r1
    other = (coarse + r0) % r1
    lane = lax.broadcasted_iota(jnp.int32, (1, lanes), 1)
    qmember = member ^ (partner * ((lane // rows) % 2))
    qpos = (lane // (2 * rows)) * (G * tokens) + qmember * tokens + r1 * (lane % rows) + jnp.where(fine, other, coarse)
    kl = lax.broadcasted_iota(jnp.int32, (nd, 1), 0)
    kmember = member ^ ((kl // rows) % G)
    kpos = (kl // (rows * G)) * (G * tokens) + kmember * tokens + r1 * (kl % rows)
    causal1 = kpos + coarse <= qpos
    causal2 = kpos + other <= qpos
    both = jnp.where(fine, 0.0, 1.0)
    c = SCALE * LOG2E

    for u in range(TILES):
        nk = (u + 1) * nd
        x0 = u * nd
        src = range(u * per, (u + 1) * per)
        mine = slice(u * lanes, (u + 1) * lanes)
        gather = lambda lo: jnp.concatenate([ref[j, lo:lo + rows] for j in src for ref in (own_ref, partner_ref)], 0)
        qt, gt = gather(0), gather(rows)
        q_all[mine], g_all[mine] = qt, gt
        dq = jnp.concatenate([query_sel * source_docs[2 * j + e] for j in src for e in range(2)], 0)
        qdoc = dot_nt(jnp.ones((16, HD), bf16), dq)[0:1]

        def scores(key, docs, causal):
            s = jnp.where(docs == qdoc, dot_nt(key, qt), MASKED)
            if u:
                return jnp.concatenate([s[:x0], jnp.where(causal, s[x0:], MASKED)], 0)
            return jnp.where(causal, s, MASKED)

        s1 = scores(k1[0:nk], docs1[0:nk], causal1)
        s2 = scores(k2[0:nk], docs2[0:nk], causal2)
        top = jnp.maximum(jnp.max(s1, 0, keepdims=True), jnp.max(s2, 0, keepdims=True))
        base = top * c
        p1 = jnp.exp2(s1 * c - (base - both))
        p2 = jnp.exp2(s2 * c - base)
        stats[0:1, mine] = top
        stats[1:2, mine] = jnp.sum(p1, 0, keepdims=True) + jnp.sum(p2, 0, keepdims=True)
        stats[2:3, mine] = qdoc
        out_ref[:, mine] = dot_nn(v1t[:, :nk], p1.astype(bf16)) + dot_nn(v2t[:, :nk], p2.astype(bf16))
        gtt_ref[:, mine] = dot_nt(eye, gt)
        p_refs[2 * u][...], p_refs[2 * u + 1][...] = p1, p2
        dp_refs[2 * u][...], dp_refs[2 * u + 1][...] = dot_nt(v1[0:nk], gt), dot_nt(v2[0:nk], gt)


def finish_tile(u, r0, rows, members, parts, shared, products, results, scratch):
    far = (lax.axis_index("half") == 1) & jnp.logical_not(takes_fine(members))
    for branch, with_far in ((far, True), (jnp.logical_not(far), False)):
        pl.when(branch)(functools.partial(
            tile_body, u, r0, rows, members, with_far, parts, shared, products, results, scratch))


def tile_body(u, r0, rows, members, with_far, parts, shared, products, results, scratch):
    G = members
    q_all, g_all, stats, local_out, gtt_ref, k1, k2 = shared
    far_stats, att, gq_ref, sums = results[0], results[1], results[2], results[3:]
    kx, vx, dx = scratch
    bf16 = jnp.bfloat16
    per = H // TILES
    eye = eye_matrix()
    nd, lanes = tile_sizes(rows, G)
    nk = (u + 1) * nd
    mine = slice(u * lanes, (u + 1) * lanes)
    c = SCALE * LOG2E
    qt, gt = q_all[mine], g_all[mine]
    top, total, out = stats[0:1, mine], stats[1:2, mine], local_out[:, mine]
    if with_far:
        sel = selector(lax.axis_index("head"), r0, rows, HD, False)
        for p, part in enumerate(parts):
            for j in range(per):
                for g, ref in enumerate(part):
                    at = pl.ds(((p * per + j) * G + g) * rows, rows)
                    kx[at] = ref[2 * j * rows:(2 * j + 1) * rows]
                    vx[at] = ref[(2 * j + 1) * rows:(2 * j + 2) * rows]
                    dx[at] = sel[:rows] * ref[2 * per * rows:2 * per * rows + DOC_ROWS][j:j + 1]
        keys_x, values_x = kx[...], vx[...]
        kxt, vxt = dot_nt(eye, keys_x).astype(bf16), dot_nt(eye, values_x).astype(bf16)
        sx = jnp.where(doc_cols(dx[...]) == stats[2:3, mine], dot_nt(keys_x, qt), MASKED)
        local_top = top
        top = jnp.maximum(local_top, jnp.max(sx, 0, keepdims=True))
        px = jnp.exp2(sx * c - top * c)
        shrink = jnp.exp2(local_top * c - top * c)
        total = total * shrink + jnp.sum(px, 0, keepdims=True)
        inv = 1.0 / total
        local_inv = shrink * inv
        out = out * local_inv + dot_nn(vxt, px.astype(bf16)) * inv
    else:
        local_inv = 1.0 / total
        out = out * local_inv
    dot = jnp.sum(gtt_ref[:, mine] * out, 0, keepdims=True)
    lse = top * c + jnp.log(total) * LOG2E
    chunks = lanes // HD
    for i in range(chunks):
        far_stats[u * chunks + i:u * chunks + i + 1] = lse[:, i * HD:(i + 1) * HD]
        far_stats[4 + u * chunks + i:5 + u * chunks + i] = dot[:, i * HD:(i + 1) * HD]
    att[...] = out.T.astype(bf16)
    gq = 0.0
    if with_far:
        ds = (px * inv * (dot_nt(values_x, gt) - dot)).astype(bf16)
        gq = dot_nn(kxt, ds)
    for i, k in enumerate((k1, k2)):
        w = products[i][...] * local_inv
        ds = (w * (products[2 + i][...] - dot)).astype(bf16)
        gq = gq + dot_nn(dot_nt(eye, k[0:nk]).astype(bf16), ds)
        sums[i][...] = dot_nn(ds, qt)
        sums[2 + i][...] = dot_nn(w.astype(bf16), gt)
    gq_ref[...] = (gq * SCALE).T.astype(bf16)


def last_tile_kernel(r0, rows, members, *refs):
    G = members
    finish_tile(1, r0, rows, G, [refs[:G]], refs[G:G + 7], refs[G + 7:G + 11], refs[G + 11:G + 18], refs[G + 18:])


def first_tile_kernel(r0, rows, members, *refs):
    G = members
    parts, refs = [refs[:G], refs[G:2 * G]], refs[2 * G:]
    shared, products, last, refs = refs[:7], refs[7:11], refs[11:18], refs[18:]
    far_stats, out_own, out_kv, out_swap, scratch = refs[0], refs[1], refs[2], refs[3:G + 2], refs[G + 2:]
    nd, lanes = tile_sizes(rows, G)
    first = (far_stats,) + tuple(scratch[:6])
    far_stats[...] = last[0][...]
    finish_tile(0, r0, rows, G, parts, shared, products, first, scratch[6:])
    partner, per = G // 2, H // TILES
    for j in range(H):
        att, gq = (first, last)[j // per][1:3]
        for e, ref in enumerate((out_own, out_swap[partner - 1])):
            lo = (2 * (j % per) + e) * rows
            ref[j, 0:rows] = att[lo:lo + rows]
            ref[j, rows:2 * rows] = gq[lo:lo + rows]
        for g in range(G):
            at = pl.ds((j * G + g) * rows, rows)
            gk1, gk2, gv1, gv2 = (last[3 + i][at] + first[3 + i][at] if j < per else last[3 + i][at] for i in range(4))
            ref = out_kv if g == 0 else out_swap[g - 1]
            base = 2 if g == partner else 0
            for i, part in enumerate((gk2 * SCALE, gv2, gk1 * SCALE, gv1), base):
                ref[j, i * rows:(i + 1) * rows] = part.astype(ref.dtype)


def far_rows(query_refs, g, members, u, rows, lo):
    pair = (query_refs[u * members + g], query_refs[u * members + (g ^ (members // 2))])
    return jnp.concatenate([ref[(2 * j + lo) * rows:(2 * j + lo + 1) * rows] for j in range(H // TILES) for ref in pair], 0)


def far_slots(members, body):
    for g in range(members):
        slot = lax.axis_index("member") ^ g

        @pl.when((lax.axis_index("half") == 0) & (slot < members // 2))
        def _(g=g, slot=slot):
            body(g, slot)


def far_kernel(r0, rows, members, own_ref, *refs):
    G = members
    query_refs, products = refs[:TILES * G], refs[TILES * G:]
    sel = selector(lax.axis_index("head"), r0, rows, HD, False)[:rows]
    per = H // TILES
    keys, values = (jnp.concatenate([own_ref[j, lo * rows:(lo + 1) * rows] for j in range(H)], 0) for lo in (6, 7))
    docs = doc_cols(jnp.concatenate([sel * own_ref[j, 8 * rows:8 * rows + DOC_ROWS][0:1] for j in range(H)], 0))

    def body(g, slot):
        for u in range(TILES):
            x0 = u * per * rows
            pair = (query_refs[u * G + g], query_refs[u * G + (g ^ (G // 2))])
            dq = jnp.concatenate([sel * ref[2 * per * rows:2 * per * rows + DOC_ROWS][j:j + 1]
                                  for j in range(per) for ref in pair], 0)
            qdoc = dot_nt(jnp.ones((16, HD), jnp.bfloat16), dq)[0:1]
            s = dot_nt(keys[x0:], far_rows(query_refs, g, G, u, rows, 0)) * (SCALE * LOG2E)
            products[2 * u][slot] = jnp.where(docs[x0:] == qdoc, s, MASKED)
            products[2 * u + 1][slot] = dot_nt(values[x0:], far_rows(query_refs, g, G, u, rows, 1))

    far_slots(G, body)


def far_grads(rows, members, query_refs, stat_ref, products, gk, gv):
    G = members
    per = H // TILES
    gk[...], gv[...] = jnp.zeros_like(gk), jnp.zeros_like(gv)

    def body(g, slot):
        for u in range(TILES):
            x0 = u * per * rows
            chunks = per * 2 * rows // HD
            lse, dot = (jnp.concatenate([stat_ref[at + i:at + i + 1] for i in range(chunks)], 1)
                        for at in (8 * g + u * chunks, 8 * g + 4 + u * chunks))
            p = jnp.exp2(products[2 * u][slot] - lse)
            ds = p * (products[2 * u + 1][slot] - dot)
            gk[x0:] += dot_nn(ds.astype(jnp.bfloat16), far_rows(query_refs, g, G, u, rows, 0)) * SCALE
            gv[x0:] += dot_nn(p.astype(jnp.bfloat16), far_rows(query_refs, g, G, u, rows, 1))

    far_slots(G, body)


def sum_kernel(rows, members, *refs):
    G = members
    query_refs, refs = refs[:TILES * G], refs[TILES * G:]
    stat_ref, products, refs = refs[0], refs[1:1 + 2 * TILES], refs[1 + 2 * TILES:]
    own_ref, kv_ref, swap_refs, (out_ref, gk, gv) = refs[0], refs[1], refs[2:G + 1], refs[G + 1:]
    f32, bf16 = jnp.float32, jnp.bfloat16
    far_grads(rows, G, query_refs, stat_ref, products, gk, gv)
    out_ref[:, 0:2 * rows] = own_ref[...]
    out_ref[:, 2 * rows:4 * rows] = swap_refs[G // 2 - 1][:, 0:2 * rows]
    for j in range(H):
        total = kv_ref[j]
        for g, ref in enumerate(swap_refs, 1):
            base = 2 * rows if g == G // 2 else 0
            total = total + ref[j, base:base + 4 * rows].astype(f32)
        mine = slice(j * rows, (j + 1) * rows)
        out_ref[j, 4 * rows:6 * rows] = total[:2 * rows].astype(bf16)
        out_ref[j, 6 * rows:7 * rows] = (total[2 * rows:3 * rows] + gk[mine]).astype(bf16)
        out_ref[j, 7 * rows:8 * rows] = (total[3 * rows:] + gv[mine]).astype(bf16)


def unpack_kernel(r0, rows, members, in_ref, *refs):
    outs, bufs, sem = refs[:4], refs[4:8], refs[8]
    tokens = bufs[0].shape[0]
    bf16 = jnp.bfloat16
    kinds = range(min(H, 2 * r0))
    query_sels = [selector(h, r0, rows, tokens, True, takes_fine(members)) for h in kinds]
    key_sels = [selector(h, r0, rows, tokens, True, True) for h in kinds]
    copies = []
    for i, base in enumerate((0, 1, 4, 5)):
        for h in range(H):
            sels = query_sels if i < 2 else key_sels
            part = jnp.concatenate([in_ref[h, (base + e) * rows:(base + e + 1) * rows] for e in (0, 2)], 0)
            bufs[i][:, h * HD:(h + 1) * HD] = dot_nn(sels[h % (2 * r0)], part).astype(bf16)
        copies.append(pltpu.make_async_copy(bufs[i], outs[i], sem.at[i]))
        copies[-1].start()
    for copy in copies:
        copy.wait()


def call(kernel, out_shape, scratch=(), limit=16, **more):
    return pl.pallas_call(
        kernel,
        out_shape=out_shape,
        scratch_shapes=list(scratch),
        compiler_params=pltpu.CompilerParams(vmem_limit_bytes=limit * 1024 * 1024),
        **more,
    )


def per_device(members, queries, keys, values, cotangent, doc_ids):
    G = members
    tokens = queries.shape[0]
    devices = 2 * H * G
    r0 = tokens * devices // (2 * SEG)
    rows = tokens // (2 * r0)
    bf16, f32 = jnp.bfloat16, jnp.float32
    shape = jax.ShapeDtypeStruct
    n = H * G * rows
    anywhere = pl.BlockSpec(memory_space=pltpu.HBM)
    wide = pltpu.VMEM((tokens, H * HD), bf16)
    message = (H, 8 * rows + DOC_ROWS, HD)

    packed = call(
        functools.partial(pack_kernel, r0, rows, G), shape(message, bf16),
        [wide] * 4 + [pltpu.VMEM((1, tokens), jnp.int32), pltpu.VMEM(message, bf16), pltpu.SemaphoreType.DMA((5 + H,))],
        limit=64, in_specs=[anywhere] * 5, out_specs=anywhere,
    )(queries, keys, values, cotangent, doc_ids.reshape(1, tokens))

    def to_head(x):
        return lax.all_to_all(x, "head", 0, 0, tiled=True)

    def to_member(x, g):
        return lax.ppermute(x, "member", [(i, i ^ g) for i in range(G)])

    def across(x):
        return lax.ppermute(x, "half", [(0, 1), (1, 0)])

    def back_across(x):
        return lax.ppermute(x, "half", [(1, 0)])

    own = to_head(packed)
    queries_here = jnp.where(takes_fine(G), own[:, 2 * rows:4 * rows], own[:, :2 * rows])
    sent_across = jnp.where(lax.axis_index("half") == 0, own[:, 6 * rows:8 * rows], queries_here)
    per = H // TILES

    def part_across(u):
        at = slice(u * per, (u + 1) * per)
        docs = jnp.pad(own[at, 8 * rows], ((0, DOC_ROWS - per), (0, 0)))
        return across(jnp.concatenate([sent_across[at].reshape(-1, HD), docs], 0))

    upper, lower = part_across(1), part_across(0)
    swaps = [to_member(own[:, (2 if g == G // 2 else 4) * rows:], g) for g in range(1, G)]
    nd, lanes = tile_sizes(rows, G)
    nq = TILES * lanes
    tile = [shape(((u + 1) * nd, lanes), f32) for u in range(TILES) for _ in range(2)]
    key_rows = pltpu.VMEM((n, HD), bf16)
    k1, k2, q_all, g_all, stats, out, gtt, *products = call(
        functools.partial(local_kernel, r0, rows, G),
        [shape((n, HD), bf16)] * 2 + [shape((nq, HD), bf16)] * 2 + [shape((8, nq), f32)]
        + [shape((HD, nq), f32)] * 2 + tile * 2,
        [key_rows] * 4, limit=32,
    )(own, *swaps)
    shared = (q_all, g_all, stats, out, gtt, k1, k2)
    upper, k1 = lax.optimization_barrier((upper, k1))
    uppers = [upper] + [to_member(upper, g) for g in range(1, G)]
    tile_rows = pltpu.VMEM((lanes, HD), bf16)
    far_scratch = lambda keys: [pltpu.VMEM((keys, HD), bf16)] * 3
    last = call(
        functools.partial(last_tile_kernel, r0, rows, G),
        [shape((8, HD), f32)] + [shape((lanes, HD), bf16)] * 2 + [shape((n, HD), f32)] * 4,
        far_scratch(nd), limit=32,
    )(*uppers, *shared, *products[2:4], *products[6:8])
    lowers = [lower] + [to_member(lower, g) for g in range(1, G)]
    sent = lambda g: (H, (6 if g == G // 2 else 4) * rows, HD)
    outs = call(
        functools.partial(first_tile_kernel, r0, rows, G),
        [shape((8, HD), f32), shape((H, 2 * rows, HD), bf16), shape((H, 4 * rows, HD), f32)]
        + [shape(sent(g), bf16) for g in range(1, G)],
        [tile_rows] * 2 + [pltpu.VMEM((nd, HD), f32)] * 4 + far_scratch(n), limit=32,
    )(*lowers, *uppers, *shared, *products[0:2], *products[4:6], *last)
    crosses = lowers + uppers
    far_stats = back_across(jnp.concatenate([outs[0]] + [to_member(outs[0], g) for g in range(1, G)], 0))
    products = call(
        functools.partial(far_kernel, r0, rows, G),
        [shape((G // 2, (TILES - u) * nd // G, lanes), f32) for u in range(TILES) for _ in range(2)],
    )(own, *crosses)
    swaps = [to_member(outs[2 + g], g) for g in range(1, G)]
    back = call(
        functools.partial(sum_kernel, rows, G), shape((H, 8 * rows, HD), bf16),
        [pltpu.VMEM((H * rows, HD), f32)] * 2,
    )(*crosses, far_stats, *products, outs[1], outs[2], *swaps)
    back = to_head(back)
    return tuple(call(
        functools.partial(unpack_kernel, r0, rows, G), [shape((tokens, H * HD), bf16)] * 4,
        [wide] * 4 + [pltpu.SemaphoreType.DMA((4,))],
        in_specs=[VMEM], out_specs=[anywhere] * 4,
    )(back))


def solution(mesh):
    members = mesh.shape["seq"] // (2 * H)
    parts = {"seq": [("half", 2), ("head", H), ("member", members)]}
    axes = [part for name in mesh.axis_names for part in parts.get(name, [(name, mesh.shape[name])])]
    inner = Mesh(mesh.devices.reshape([size for _, size in axes]), [name for name, _ in axes])
    split = ("dp", "half", "head", "member")
    in_specs = (P(split, None),) * 4 + (P(split),)
    return jax.shard_map(
        functools.partial(per_device, members), mesh=inner, in_specs=in_specs,
        out_specs=(P(split, None),) * 4, check_vma=False,
    )
```

```python
import functools

import jax
import jax.numpy as jnp
import numpy as np
from jax import lax
from jax.experimental import pallas as pl
from jax.experimental.pallas import tpu as pltpu
from jax.sharding import Mesh
from jax.sharding import PartitionSpec as P

H = 8
HD = 128
SEG = 1024

MASKED = -1e30
SCALE = HD ** -0.5
LOG2E = float(np.log2(np.e))
VMEM = pl.BlockSpec(memory_space=pltpu.VMEM)
DOC_ROWS = 16


def dot_nn(a, b):
    return lax.dot_general(a, b, (((1,), (0,)), ((), ())), preferred_element_type=jnp.float32)


def dot_nt(a, b):
    return lax.dot_general(a, b, (((1,), (1,)), ((), ())), preferred_element_type=jnp.float32)


def selector(head, r0, rows, tokens, transposed, fine_first=False):
    r1 = 2 * r0
    shape = (tokens, 2 * rows) if transposed else (2 * rows, tokens)
    k = lax.broadcasted_iota(jnp.int32, shape, 1 if transposed else 0)
    p = lax.broadcasted_iota(jnp.int32, shape, 0 if transposed else 1)
    coarse = head % r1
    other = (coarse + r0) % r1
    first, second = jnp.where(fine_first, other, coarse), jnp.where(fine_first, coarse, other)
    target = jnp.where(k < rows, r1 * k + first, r1 * (k - rows) + second)
    return (p == target).astype(jnp.float32).astype(jnp.bfloat16)


def takes_fine(members):
    return lax.axis_index("member") >= members // 2


def pack_kernel(r0, rows, members, q_in, k_in, v_in, g_in, doc_in, out, q_ref, k_ref, v_ref, g_ref, doc_ref, buf, sem):
    tokens = q_ref.shape[0]
    pairs = ((doc_in, doc_ref), (k_in, k_ref), (v_in, v_ref), (q_in, q_ref), (g_in, g_ref))
    copies = [pltpu.make_async_copy(src, dst, sem.at[i]) for i, (src, dst) in enumerate(pairs)]
    for copy in copies:
        copy.start()
    kinds = range(min(H, 2 * r0))
    key_sels = [selector(h, r0, rows, tokens, False) for h in kinds]
    query_sels = [selector(h, r0, rows, tokens, False, takes_fine(members)) for h in kinds]

    def pick(sels, h, ref):
        return dot_nn(sels[h % (2 * r0)], ref[:, h * HD:(h + 1) * HD]).astype(jnp.bfloat16)

    for copy in copies:
        copy.wait()
    docs = jnp.broadcast_to(doc_ref[...].astype(jnp.float32).astype(jnp.bfloat16), (DOC_ROWS, tokens))
    sends = []
    for h in range(H):
        for i, ref in enumerate((q_ref, g_ref)):
            x = pick(query_sels, h, ref)
            buf[h, i * rows:(1 + i) * rows] = x[:rows]
            buf[h, (2 + i) * rows:(3 + i) * rows] = x[rows:]
        for i, ref in enumerate((k_ref, v_ref)):
            x = pick(key_sels, h, ref)
            buf[h, (4 + i) * rows:(5 + i) * rows] = x[rows:]
            buf[h, (6 + i) * rows:(7 + i) * rows] = x[:rows]
        buf[h, 8 * rows:8 * rows + DOC_ROWS] = docs
        sends.append(pltpu.make_async_copy(buf.at[h], out.at[h], sem.at[5 + h]))
        sends[-1].start()
    for copy in sends:
        copy.wait()


TILES = 2


def tile_sizes(rows, members):
    per = H // TILES
    return per * members * rows, per * 2 * rows


def eye_matrix():
    shape = (HD, HD)
    same = lax.broadcasted_iota(jnp.int32, shape, 0) == lax.broadcasted_iota(jnp.int32, shape, 1)
    return same.astype(jnp.float32).astype(jnp.bfloat16)


def doc_cols(x):
    return dot_nn(x, jnp.ones((HD, HD), jnp.bfloat16))[:, 0:1]


def local_kernel(r0, rows, members, *refs):
    G = members
    r1 = 2 * r0
    own_ref, swap_refs = refs[0], refs[1:G]
    (k1, k2, q_all, g_all, stats, out_ref, gtt_ref), rest = refs[G:G + 7], refs[G + 7:]
    p_refs, dp_refs, (v1, v2, d1, d2) = rest[:2 * TILES], rest[2 * TILES:4 * TILES], rest[4 * TILES:]
    bf16, f32 = jnp.bfloat16, jnp.float32
    tokens = HD
    head = lax.axis_index("head")
    member = lax.axis_index("member")
    fine = takes_fine(G)
    partner = G // 2
    partner_ref = swap_refs[partner - 1]

    sel = selector(head, r0, rows, tokens, False)
    query_sel = jnp.where(fine, sel[rows:].astype(f32), sel[:rows].astype(f32)).astype(bf16)
    source_docs = []
    for j in range(H):
        for g in range(G):
            at = pl.ds((j * G + g) * rows, rows)
            ref, base = (own_ref, 4 * rows) if g == 0 else (swap_refs[g - 1], 2 * rows if g == partner else 0)
            k2[at] = ref[j, base:base + rows]
            v2[at] = ref[j, base + rows:base + 2 * rows]
            k1[at] = ref[j, base + 2 * rows:base + 3 * rows]
            v1[at] = ref[j, base + 3 * rows:base + 4 * rows]
            doc = ref[j, base + 4 * rows:base + 4 * rows + DOC_ROWS][0:1]
            if g in (0, partner):
                source_docs.append(doc)
            d1[at] = sel[:rows] * doc
            d2[at] = sel[rows:] * doc

    eye = eye_matrix()
    v1t, v2t = dot_nt(eye, v1[...]).astype(bf16), dot_nt(eye, v2[...]).astype(bf16)
    docs1, docs2 = doc_cols(d1[...]), doc_cols(d2[...])
    nd, lanes = tile_sizes(rows, G)
    per = H // TILES

    coarse = head % r1
    other = (coarse + r0) % r1
    lane = lax.broadcasted_iota(jnp.int32, (1, lanes), 1)
    qmember = member ^ (partner * ((lane // rows) % 2))
    qpos = (lane // (2 * rows)) * (G * tokens) + qmember * tokens + r1 * (lane % rows) + jnp.where(fine, other, coarse)
    kl = lax.broadcasted_iota(jnp.int32, (nd, 1), 0)
    kmember = member ^ ((kl // rows) % G)
    kpos = (kl // (rows * G)) * (G * tokens) + kmember * tokens + r1 * (kl % rows)
    causal1 = kpos + coarse <= qpos
    causal2 = kpos + other <= qpos
    both = jnp.where(fine, 0.0, 1.0)
    c = SCALE * LOG2E

    for u in range(TILES):
        nk = (u + 1) * nd
        x0 = u * nd
        src = range(u * per, (u + 1) * per)
        mine = slice(u * lanes, (u + 1) * lanes)
        gather = lambda lo: jnp.concatenate([ref[j, lo:lo + rows] for j in src for ref in (own_ref, partner_ref)], 0)
        qt, gt = gather(0), gather(rows)
        q_all[mine], g_all[mine] = qt, gt
        dq = jnp.concatenate([query_sel * source_docs[2 * j + e] for j in src for e in range(2)], 0)
        qdoc = dot_nt(jnp.ones((16, HD), bf16), dq)[0:1]

        def scores(key, docs, causal):
            s = jnp.where(docs == qdoc, dot_nt(key, qt), MASKED)
            if u:
                return jnp.concatenate([s[:x0], jnp.where(causal, s[x0:], MASKED)], 0)
            return jnp.where(causal, s, MASKED)

        s1 = scores(k1[0:nk], docs1[0:nk], causal1)
        s2 = scores(k2[0:nk], docs2[0:nk], causal2)
        top = jnp.maximum(jnp.max(s1, 0, keepdims=True), jnp.max(s2, 0, keepdims=True))
        base = top * c
        p1 = jnp.exp2(s1 * c - (base - both))
        p2 = jnp.exp2(s2 * c - base)
        stats[0:1, mine] = top
        stats[1:2, mine] = jnp.sum(p1, 0, keepdims=True) + jnp.sum(p2, 0, keepdims=True)
        stats[2:3, mine] = qdoc
        out_ref[:, mine] = dot_nn(v1t[:, :nk], p1.astype(bf16)) + dot_nn(v2t[:, :nk], p2.astype(bf16))
        gtt_ref[:, mine] = dot_nt(eye, gt)
        p_refs[2 * u][...], p_refs[2 * u + 1][...] = p1, p2
        dp_refs[2 * u][...], dp_refs[2 * u + 1][...] = dot_nt(v1[0:nk], gt), dot_nt(v2[0:nk], gt)


def finish_tile(u, r0, rows, members, parts, shared, products, results, scratch):
    far = (lax.axis_index("half") == 1) & jnp.logical_not(takes_fine(members))
    for branch, with_far in ((far, True), (jnp.logical_not(far), False)):
        pl.when(branch)(functools.partial(
            tile_body, u, r0, rows, members, with_far, parts, shared, products, results, scratch))


def tile_body(u, r0, rows, members, with_far, parts, shared, products, results, scratch):
    G = members
    q_all, g_all, stats, local_out, gtt_ref, k1, k2 = shared
    far_stats, att, gq_ref, sums = results[0], results[1], results[2], results[3:]
    kx, vx, dx = scratch
    bf16 = jnp.bfloat16
    per = H // TILES
    eye = eye_matrix()
    nd, lanes = tile_sizes(rows, G)
    nk = (u + 1) * nd
    mine = slice(u * lanes, (u + 1) * lanes)
    c = SCALE * LOG2E
    qt, gt = q_all[mine], g_all[mine]
    top, total, out = stats[0:1, mine], stats[1:2, mine], local_out[:, mine]
    if with_far:
        sel = selector(lax.axis_index("head"), r0, rows, HD, False)
        for p, part in enumerate(parts):
            for j in range(per):
                for g, ref in enumerate(part):
                    at = pl.ds(((p * per + j) * G + g) * rows, rows)
                    kx[at] = ref[2 * j * rows:(2 * j + 1) * rows]
                    vx[at] = ref[(2 * j + 1) * rows:(2 * j + 2) * rows]
                    dx[at] = sel[:rows] * ref[2 * per * rows:2 * per * rows + DOC_ROWS][j:j + 1]
        keys_x, values_x = kx[...], vx[...]
        kxt, vxt = dot_nt(eye, keys_x).astype(bf16), dot_nt(eye, values_x).astype(bf16)
        sx = jnp.where(doc_cols(dx[...]) == stats[2:3, mine], dot_nt(keys_x, qt), MASKED)
        local_top = top
        top = jnp.maximum(local_top, jnp.max(sx, 0, keepdims=True))
        px = jnp.exp2(sx * c - top * c)
        shrink = jnp.exp2(local_top * c - top * c)
        total = total * shrink + jnp.sum(px, 0, keepdims=True)
        inv = 1.0 / total
        local_inv = shrink * inv
        out = out * local_inv + dot_nn(vxt, px.astype(bf16)) * inv
    else:
        local_inv = 1.0 / total
        out = out * local_inv
    dot = jnp.sum(gtt_ref[:, mine] * out, 0, keepdims=True)
    lse = top * c + jnp.log(total) * LOG2E
    chunks = lanes // HD
    for i in range(chunks):
        far_stats[u * chunks + i:u * chunks + i + 1] = lse[:, i * HD:(i + 1) * HD]
        far_stats[4 + u * chunks + i:5 + u * chunks + i] = dot[:, i * HD:(i + 1) * HD]
    att[...] = out.T.astype(bf16)
    gq = 0.0
    if with_far:
        ds = (px * inv * (dot_nt(values_x, gt) - dot)).astype(bf16)
        gq = dot_nn(kxt, ds)
    for i, k in enumerate((k1, k2)):
        w = products[i][...] * local_inv
        ds = (w * (products[2 + i][...] - dot)).astype(bf16)
        gq = gq + dot_nn(dot_nt(eye, k[0:nk]).astype(bf16), ds)
        sums[i][...] = dot_nn(ds, qt)
        sums[2 + i][...] = dot_nn(w.astype(bf16), gt)
    gq_ref[...] = (gq * SCALE).T.astype(bf16)


def last_tile_kernel(r0, rows, members, *refs):
    G = members
    finish_tile(1, r0, rows, G, [refs[:G]], refs[G:G + 7], refs[G + 7:G + 11], refs[G + 11:G + 18], refs[G + 18:])


def first_tile_kernel(r0, rows, members, *refs):
    G = members
    parts, refs = [refs[:G], refs[G:2 * G]], refs[2 * G:]
    shared, products, last, refs = refs[:7], refs[7:11], refs[11:18], refs[18:]
    far_stats, out_own, out_kv, out_swap, scratch = refs[0], refs[1], refs[2], refs[3:G + 2], refs[G + 2:]
    nd, lanes = tile_sizes(rows, G)
    first = (far_stats,) + tuple(scratch[:6])
    far_stats[...] = last[0][...]
    finish_tile(0, r0, rows, G, parts, shared, products, first, scratch[6:])
    partner, per = G // 2, H // TILES
    for j in range(H):
        att, gq = (first, last)[j // per][1:3]
        for e, ref in enumerate((out_own, out_swap[partner - 1])):
            lo = (2 * (j % per) + e) * rows
            ref[j, 0:rows] = att[lo:lo + rows]
            ref[j, rows:2 * rows] = gq[lo:lo + rows]
        for g in range(G):
            at = pl.ds((j * G + g) * rows, rows)
            gk1, gk2, gv1, gv2 = (last[3 + i][at] + first[3 + i][at] if j < per else last[3 + i][at] for i in range(4))
            ref = out_kv if g == 0 else out_swap[g - 1]
            base = 2 if g == partner else 0
            for i, part in enumerate((gk2 * SCALE, gv2, gk1 * SCALE, gv1), base):
                ref[j, i * rows:(i + 1) * rows] = part.astype(ref.dtype)


def far_rows(query_refs, g, members, u, rows, lo):
    pair = (query_refs[u * members + g], query_refs[u * members + (g ^ (members // 2))])
    return jnp.concatenate([ref[(2 * j + lo) * rows:(2 * j + lo + 1) * rows] for j in range(H // TILES) for ref in pair], 0)


def far_slots(members, body):
    for g in range(members):
        slot = lax.axis_index("member") ^ g

        @pl.when((lax.axis_index("half") == 0) & (slot < members // 2))
        def _(g=g, slot=slot):
            body(g, slot)


def far_kernel(r0, rows, members, own_ref, *refs):
    G = members
    query_refs, products = refs[:TILES * G], refs[TILES * G:]
    sel = selector(lax.axis_index("head"), r0, rows, HD, False)[:rows]
    per = H // TILES
    keys, values = (jnp.concatenate([own_ref[j, lo * rows:(lo + 1) * rows] for j in range(H)], 0) for lo in (6, 7))
    docs = doc_cols(jnp.concatenate([sel * own_ref[j, 8 * rows:8 * rows + DOC_ROWS][0:1] for j in range(H)], 0))

    def body(g, slot):
        for u in range(TILES):
            x0 = u * per * rows
            pair = (query_refs[u * G + g], query_refs[u * G + (g ^ (G // 2))])
            dq = jnp.concatenate([sel * ref[2 * per * rows:2 * per * rows + DOC_ROWS][j:j + 1]
                                  for j in range(per) for ref in pair], 0)
            qdoc = dot_nt(jnp.ones((16, HD), jnp.bfloat16), dq)[0:1]
            s = dot_nt(keys[x0:], far_rows(query_refs, g, G, u, rows, 0)) * (SCALE * LOG2E)
            products[2 * u][slot] = jnp.where(docs[x0:] == qdoc, s, MASKED)
            products[2 * u + 1][slot] = dot_nt(values[x0:], far_rows(query_refs, g, G, u, rows, 1))

    far_slots(G, body)


def far_grads(rows, members, query_refs, stat_ref, products, gk, gv):
    G = members
    per = H // TILES
    gk[...], gv[...] = jnp.zeros_like(gk), jnp.zeros_like(gv)

    def body(g, slot):
        for u in range(TILES):
            x0 = u * per * rows
            chunks = per * 2 * rows // HD
            lse, dot = (jnp.concatenate([stat_ref[at + i:at + i + 1] for i in range(chunks)], 1)
                        for at in (8 * g + u * chunks, 8 * g + 4 + u * chunks))
            p = jnp.exp2(products[2 * u][slot] - lse)
            ds = p * (products[2 * u + 1][slot] - dot)
            gk[x0:] += dot_nn(ds.astype(jnp.bfloat16), far_rows(query_refs, g, G, u, rows, 0)) * SCALE
            gv[x0:] += dot_nn(p.astype(jnp.bfloat16), far_rows(query_refs, g, G, u, rows, 1))

    far_slots(G, body)


def sum_kernel(rows, members, *refs):
    G = members
    query_refs, refs = refs[:TILES * G], refs[TILES * G:]
    stat_ref, products, refs = refs[0], refs[1:1 + 2 * TILES], refs[1 + 2 * TILES:]
    own_ref, kv_ref, swap_refs, (out_ref, gk, gv) = refs[0], refs[1], refs[2:G + 1], refs[G + 1:]
    f32, bf16 = jnp.float32, jnp.bfloat16
    far_grads(rows, G, query_refs, stat_ref, products, gk, gv)
    out_ref[:, 0:2 * rows] = own_ref[...]
    out_ref[:, 2 * rows:4 * rows] = swap_refs[G // 2 - 1][:, 0:2 * rows]
    for j in range(H):
        total = kv_ref[j]
        for g, ref in enumerate(swap_refs, 1):
            base = 2 * rows if g == G // 2 else 0
            total = total + ref[j, base:base + 4 * rows].astype(f32)
        mine = slice(j * rows, (j + 1) * rows)
        out_ref[j, 4 * rows:6 * rows] = total[:2 * rows].astype(bf16)
        out_ref[j, 6 * rows:7 * rows] = (total[2 * rows:3 * rows] + gk[mine]).astype(bf16)
        out_ref[j, 7 * rows:8 * rows] = (total[3 * rows:] + gv[mine]).astype(bf16)


def unpack_kernel(r0, rows, members, in_ref, *refs):
    outs, bufs, sem = refs[:4], refs[4:8], refs[8]
    tokens = bufs[0].shape[0]
    bf16 = jnp.bfloat16
    kinds = range(min(H, 2 * r0))
    query_sels = [selector(h, r0, rows, tokens, True, takes_fine(members)) for h in kinds]
    key_sels = [selector(h, r0, rows, tokens, True, True) for h in kinds]
    copies = []
    for i, base in enumerate((0, 1, 4, 5)):
        for h in range(H):
            sels = query_sels if i < 2 else key_sels
            part = jnp.concatenate([in_ref[h, (base + e) * rows:(base + e + 1) * rows] for e in (0, 2)], 0)
            bufs[i][:, h * HD:(h + 1) * HD] = dot_nn(sels[h % (2 * r0)], part).astype(bf16)
        copies.append(pltpu.make_async_copy(bufs[i], outs[i], sem.at[i]))
        copies[-1].start()
    for copy in copies:
        copy.wait()


def call(kernel, out_shape, scratch=(), limit=16, **more):
    return pl.pallas_call(
        kernel,
        out_shape=out_shape,
        scratch_shapes=list(scratch),
        compiler_params=pltpu.CompilerParams(vmem_limit_bytes=limit * 1024 * 1024),
        **more,
    )


def per_device(members, queries, keys, values, cotangent, doc_ids):
    G = members
    tokens = queries.shape[0]
    devices = 2 * H * G
    r0 = tokens * devices // (2 * SEG)
    rows = tokens // (2 * r0)
    bf16, f32 = jnp.bfloat16, jnp.float32
    shape = jax.ShapeDtypeStruct
    n = H * G * rows
    anywhere = pl.BlockSpec(memory_space=pltpu.HBM)
    wide = pltpu.VMEM((tokens, H * HD), bf16)
    message = (H, 8 * rows + DOC_ROWS, HD)

    packed = call(
        functools.partial(pack_kernel, r0, rows, G), shape(message, bf16),
        [wide] * 4 + [pltpu.VMEM((1, tokens), jnp.int32), pltpu.VMEM(message, bf16), pltpu.SemaphoreType.DMA((5 + H,))],
        limit=64, in_specs=[anywhere] * 5, out_specs=anywhere,
    )(queries, keys, values, cotangent, doc_ids.reshape(1, tokens))

    def to_head(x):
        return lax.all_to_all(x, "head", 0, 0, tiled=True)

    def to_member(x, g):
        return lax.ppermute(x, "member", [(i, i ^ g) for i in range(G)])

    def across(x):
        return lax.ppermute(x, "half", [(0, 1), (1, 0)])

    own = to_head(packed)
    queries_here = jnp.where(takes_fine(G), own[:, 2 * rows:4 * rows], own[:, :2 * rows])
    sent_across = jnp.where(lax.axis_index("half") == 0, own[:, 6 * rows:8 * rows], queries_here)
    per = H // TILES

    def part_across(u):
        at = slice(u * per, (u + 1) * per)
        docs = jnp.pad(own[at, 8 * rows], ((0, DOC_ROWS - per), (0, 0)))
        return across(jnp.concatenate([sent_across[at].reshape(-1, HD), docs], 0))

    upper, lower = part_across(1), part_across(0)
    swaps = [to_member(own[:, (2 if g == G // 2 else 4) * rows:], g) for g in range(1, G)]
    nd, lanes = tile_sizes(rows, G)
    nq = TILES * lanes
    tile = [shape(((u + 1) * nd, lanes), f32) for u in range(TILES) for _ in range(2)]
    key_rows = pltpu.VMEM((n, HD), bf16)
    k1, k2, q_all, g_all, stats, out, gtt, *products = call(
        functools.partial(local_kernel, r0, rows, G),
        [shape((n, HD), bf16)] * 2 + [shape((nq, HD), bf16)] * 2 + [shape((8, nq), f32)]
        + [shape((HD, nq), f32)] * 2 + tile * 2,
        [key_rows] * 4, limit=32,
    )(own, *swaps)
    shared = (q_all, g_all, stats, out, gtt, k1, k2)
    upper, k1 = lax.optimization_barrier((upper, k1))
    uppers = [upper] + [to_member(upper, g) for g in range(1, G)]
    tile_rows = pltpu.VMEM((lanes, HD), bf16)
    far_scratch = lambda keys: [pltpu.VMEM((keys, HD), bf16)] * 3
    last = call(
        functools.partial(last_tile_kernel, r0, rows, G),
        [shape((8, HD), f32)] + [shape((lanes, HD), bf16)] * 2 + [shape((n, HD), f32)] * 4,
        far_scratch(nd), limit=32,
    )(*uppers, *shared, *products[2:4], *products[6:8])
    lowers = [lower] + [to_member(lower, g) for g in range(1, G)]
    sent = lambda g: (H, (6 if g == G // 2 else 4) * rows, HD)
    outs = call(
        functools.partial(first_tile_kernel, r0, rows, G),
        [shape((8, HD), f32), shape((H, 2 * rows, HD), bf16), shape((H, 4 * rows, HD), f32)]
        + [shape(sent(g), bf16) for g in range(1, G)],
        [tile_rows] * 2 + [pltpu.VMEM((nd, HD), f32)] * 4 + far_scratch(n), limit=32,
    )(*lowers, *uppers, *shared, *products[0:2], *products[4:6], *last)
    crosses = lowers + uppers
    far_stats = across(jnp.concatenate([outs[0]] + [to_member(outs[0], g) for g in range(1, G)], 0))
    products = call(
        functools.partial(far_kernel, r0, rows, G),
        [shape((G // 2, (TILES - u) * nd // G, lanes), f32) for u in range(TILES) for _ in range(2)],
    )(own, *crosses)
    swaps = [to_member(outs[2 + g], g) for g in range(1, G)]
    back = call(
        functools.partial(sum_kernel, rows, G), shape((H, 8 * rows, HD), bf16),
        [pltpu.VMEM((H * rows, HD), f32)] * 2,
    )(*crosses, far_stats, *products, outs[1], outs[2], *swaps)
    back = to_head(back)
    return tuple(call(
        functools.partial(unpack_kernel, r0, rows, G), [shape((tokens, H * HD), bf16)] * 4,
        [wide] * 4 + [pltpu.SemaphoreType.DMA((4,))],
        in_specs=[VMEM], out_specs=[anywhere] * 4,
    )(back))


def solution(mesh):
    members = mesh.shape["seq"] // (2 * H)
    parts = {"seq": [("half", 2), ("head", H), ("member", members)]}
    axes = [part for name in mesh.axis_names for part in parts.get(name, [(name, mesh.shape[name])])]
    inner = Mesh(mesh.devices.reshape([size for _, size in axes]), [name for name, _ in axes])
    split = ("dp", "half", "head", "member")
    in_specs = (P(split, None),) * 4 + (P(split),)
    return jax.shard_map(
        functools.partial(per_device, members), mesh=inner, in_specs=in_specs,
        out_specs=(P(split, None),) * 4, check_vma=False,
    )
```

```python
import functools

import jax
import jax.numpy as jnp
import numpy as np
from jax import lax
from jax.experimental import pallas as pl
from jax.experimental.pallas import tpu as pltpu
from jax.sharding import Mesh
from jax.sharding import PartitionSpec as P

H = 8
HD = 128
SEG = 1024

MASKED = -1e30
SCALE = HD ** -0.5
LOG2E = float(np.log2(np.e))
VMEM = pl.BlockSpec(memory_space=pltpu.VMEM)
DOC_ROWS = 16


def dot_nn(a, b):
    return lax.dot_general(a, b, (((1,), (0,)), ((), ())), preferred_element_type=jnp.float32)


def dot_nt(a, b):
    return lax.dot_general(a, b, (((1,), (1,)), ((), ())), preferred_element_type=jnp.float32)


def selector(head, r0, rows, tokens, transposed, fine_first=False):
    r1 = 2 * r0
    shape = (tokens, 2 * rows) if transposed else (2 * rows, tokens)
    k = lax.broadcasted_iota(jnp.int32, shape, 1 if transposed else 0)
    p = lax.broadcasted_iota(jnp.int32, shape, 0 if transposed else 1)
    coarse = head % r1
    other = (coarse + r0) % r1
    first, second = jnp.where(fine_first, other, coarse), jnp.where(fine_first, coarse, other)
    target = jnp.where(k < rows, r1 * k + first, r1 * (k - rows) + second)
    return (p == target).astype(jnp.float32).astype(jnp.bfloat16)


def takes_fine(members):
    return lax.axis_index("member") >= members // 2


def column_chunks():
    return [((h, h + 1), slice(h * HD, (h + 2) * HD)) for h in range(0, H, 2)]


def pack_kernel(r0, rows, members, q_in, k_in, v_in, g_in, doc_in, out, q_ref, k_ref, v_ref, g_ref, doc_ref, buf, sem):
    tokens = q_ref.shape[0]
    pairs = ((q_in, q_ref), (g_in, g_ref), (k_in, k_ref), (v_in, v_ref))
    copies = [[pltpu.make_async_copy(doc_in, doc_ref, sem.at[0])]]
    for i, (_, cols) in enumerate(column_chunks()):
        copies.append([pltpu.make_async_copy(src.at[:, cols], dst.at[:, cols], sem.at[1 + 4 * i + k])
                       for k, (src, dst) in enumerate(pairs)])
    for copy in sum(copies, []):
        copy.start()
    kinds = range(min(H, 2 * r0))
    key_sels = [selector(h, r0, rows, tokens, False) for h in kinds]
    query_sels = [selector(h, r0, rows, tokens, False, takes_fine(members)) for h in kinds]

    def pick(sels, h, ref):
        return dot_nn(sels[h % (2 * r0)], ref[:, h * HD:(h + 1) * HD]).astype(jnp.bfloat16)

    copies[0][0].wait()
    docs = jnp.broadcast_to(doc_ref[...].astype(jnp.float32).astype(jnp.bfloat16), (DOC_ROWS, tokens))
    sends = []
    for group, (heads, _) in zip(copies[1:], column_chunks()):
        for copy in group:
            copy.wait()
        for h in heads:
            for i, ref in enumerate((q_ref, g_ref)):
                x = pick(query_sels, h, ref)
                buf[h, i * rows:(1 + i) * rows] = x[:rows]
                buf[h, (2 + i) * rows:(3 + i) * rows] = x[rows:]
            for i, ref in enumerate((k_ref, v_ref)):
                x = pick(key_sels, h, ref)
                buf[h, (4 + i) * rows:(5 + i) * rows] = x[rows:]
                buf[h, (6 + i) * rows:(7 + i) * rows] = x[:rows]
            buf[h, 8 * rows:8 * rows + DOC_ROWS] = docs
            sends.append(pltpu.make_async_copy(buf.at[h], out.at[h], sem.at[1 + 2 * H + h]))
            sends[-1].start()
    for copy in sends:
        copy.wait()


TILES = 2


def tile_sizes(rows, members):
    per = H // TILES
    return per * members * rows, per * 2 * rows


def eye_matrix():
    shape = (HD, HD)
    same = lax.broadcasted_iota(jnp.int32, shape, 0) == lax.broadcasted_iota(jnp.int32, shape, 1)
    return same.astype(jnp.float32).astype(jnp.bfloat16)


def doc_cols(x):
    return dot_nn(x, jnp.ones((HD, HD), jnp.bfloat16))[:, 0:1]


def local_kernel(r0, rows, members, *refs):
    G = members
    r1 = 2 * r0
    own_ref, swap_refs = refs[0], refs[1:G]
    (k1, k2, q_all, g_all, stats, out_ref, gtt_ref), rest = refs[G:G + 7], refs[G + 7:]
    p_refs, dp_refs, (v1, v2, d1, d2) = rest[:2 * TILES], rest[2 * TILES:4 * TILES], rest[4 * TILES:]
    bf16, f32 = jnp.bfloat16, jnp.float32
    tokens = HD
    head = lax.axis_index("head")
    member = lax.axis_index("member")
    fine = takes_fine(G)
    partner = G // 2
    partner_ref = swap_refs[partner - 1]

    sel = selector(head, r0, rows, tokens, False)
    query_sel = jnp.where(fine, sel[rows:].astype(f32), sel[:rows].astype(f32)).astype(bf16)
    source_docs = []
    for j in range(H):
        for g in range(G):
            at = pl.ds((j * G + g) * rows, rows)
            ref, base = (own_ref, 4 * rows) if g == 0 else (swap_refs[g - 1], 2 * rows if g == partner else 0)
            k2[at] = ref[j, base:base + rows]
            v2[at] = ref[j, base + rows:base + 2 * rows]
            k1[at] = ref[j, base + 2 * rows:base + 3 * rows]
            v1[at] = ref[j, base + 3 * rows:base + 4 * rows]
            doc = ref[j, base + 4 * rows:base + 4 * rows + DOC_ROWS][0:1]
            if g in (0, partner):
                source_docs.append(doc)
            d1[at] = sel[:rows] * doc
            d2[at] = sel[rows:] * doc

    eye = eye_matrix()
    v1t, v2t = dot_nt(eye, v1[...]).astype(bf16), dot_nt(eye, v2[...]).astype(bf16)
    docs1, docs2 = doc_cols(d1[...]), doc_cols(d2[...])
    nd, lanes = tile_sizes(rows, G)
    per = H // TILES

    coarse = head % r1
    other = (coarse + r0) % r1
    lane = lax.broadcasted_iota(jnp.int32, (1, lanes), 1)
    qmember = member ^ (partner * ((lane // rows) % 2))
    qpos = (lane // (2 * rows)) * (G * tokens) + qmember * tokens + r1 * (lane % rows) + jnp.where(fine, other, coarse)
    kl = lax.broadcasted_iota(jnp.int32, (nd, 1), 0)
    kmember = member ^ ((kl // rows) % G)
    kpos = (kl // (rows * G)) * (G * tokens) + kmember * tokens + r1 * (kl % rows)
    causal1 = kpos + coarse <= qpos
    causal2 = kpos + other <= qpos
    both = jnp.where(fine, 0.0, 1.0)
    c = SCALE * LOG2E

    for u in range(TILES):
        nk = (u + 1) * nd
        x0 = u * nd
        src = range(u * per, (u + 1) * per)
        mine = slice(u * lanes, (u + 1) * lanes)
        gather = lambda lo: jnp.concatenate([ref[j, lo:lo + rows] for j in src for ref in (own_ref, partner_ref)], 0)
        qt, gt = gather(0), gather(rows)
        q_all[mine], g_all[mine] = qt, gt
        dq = jnp.concatenate([query_sel * source_docs[2 * j + e] for j in src for e in range(2)], 0)
        qdoc = dot_nt(jnp.ones((16, HD), bf16), dq)[0:1]

        def scores(key, docs, causal):
            s = jnp.where(docs == qdoc, dot_nt(key, qt), MASKED)
            if u:
                return jnp.concatenate([s[:x0], jnp.where(causal, s[x0:], MASKED)], 0)
            return jnp.where(causal, s, MASKED)

        s1 = scores(k1[0:nk], docs1[0:nk], causal1)
        s2 = scores(k2[0:nk], docs2[0:nk], causal2)
        top = jnp.maximum(jnp.max(s1, 0, keepdims=True), jnp.max(s2, 0, keepdims=True))
        base = top * c
        p1 = jnp.exp2(s1 * c - (base - both))
        p2 = jnp.exp2(s2 * c - base)
        stats[0:1, mine] = top
        stats[1:2, mine] = jnp.sum(p1, 0, keepdims=True) + jnp.sum(p2, 0, keepdims=True)
        stats[2:3, mine] = qdoc
        out_ref[:, mine] = dot_nn(v1t[:, :nk], p1.astype(bf16)) + dot_nn(v2t[:, :nk], p2.astype(bf16))
        gtt_ref[:, mine] = dot_nt(eye, gt)
        p_refs[2 * u][...], p_refs[2 * u + 1][...] = p1, p2
        dp_refs[2 * u][...], dp_refs[2 * u + 1][...] = dot_nt(v1[0:nk], gt), dot_nt(v2[0:nk], gt)


def finish_tile(u, r0, rows, members, parts, shared, products, results, scratch):
    far = (lax.axis_index("half") == 1) & jnp.logical_not(takes_fine(members))
    for branch, with_far in ((far, True), (jnp.logical_not(far), False)):
        pl.when(branch)(functools.partial(
            tile_body, u, r0, rows, members, with_far, parts, shared, products, results, scratch))


def tile_body(u, r0, rows, members, with_far, parts, shared, products, results, scratch):
    G = members
    q_all, g_all, stats, local_out, gtt_ref, k1, k2 = shared
    far_stats, att, gq_ref, sums = results[0], results[1], results[2], results[3:]
    kx, vx, dx = scratch
    bf16 = jnp.bfloat16
    per = H // TILES
    eye = eye_matrix()
    nd, lanes = tile_sizes(rows, G)
    nk = (u + 1) * nd
    mine = slice(u * lanes, (u + 1) * lanes)
    c = SCALE * LOG2E
    qt, gt = q_all[mine], g_all[mine]
    top, total, out = stats[0:1, mine], stats[1:2, mine], local_out[:, mine]
    if with_far:
        sel = selector(lax.axis_index("head"), r0, rows, HD, False)
        for p, part in enumerate(parts):
            for j in range(per):
                for g, ref in enumerate(part):
                    at = pl.ds(((p * per + j) * G + g) * rows, rows)
                    kx[at] = ref[2 * j * rows:(2 * j + 1) * rows]
                    vx[at] = ref[(2 * j + 1) * rows:(2 * j + 2) * rows]
                    dx[at] = sel[:rows] * ref[2 * per * rows:2 * per * rows + DOC_ROWS][j:j + 1]
        keys_x, values_x = kx[...], vx[...]
        kxt, vxt = dot_nt(eye, keys_x).astype(bf16), dot_nt(eye, values_x).astype(bf16)
        sx = jnp.where(doc_cols(dx[...]) == stats[2:3, mine], dot_nt(keys_x, qt), MASKED)
        local_top = top
        top = jnp.maximum(local_top, jnp.max(sx, 0, keepdims=True))
        px = jnp.exp2(sx * c - top * c)
        shrink = jnp.exp2(local_top * c - top * c)
        total = total * shrink + jnp.sum(px, 0, keepdims=True)
        inv = 1.0 / total
        local_inv = shrink * inv
        out = out * local_inv + dot_nn(vxt, px.astype(bf16)) * inv
    else:
        local_inv = 1.0 / total
        out = out * local_inv
    dot = jnp.sum(gtt_ref[:, mine] * out, 0, keepdims=True)
    lse = top * c + jnp.log(total) * LOG2E
    chunks = lanes // HD
    for i in range(chunks):
        far_stats[u * chunks + i:u * chunks + i + 1] = lse[:, i * HD:(i + 1) * HD]
        far_stats[4 + u * chunks + i:5 + u * chunks + i] = dot[:, i * HD:(i + 1) * HD]
    att[...] = out.T.astype(bf16)
    gq = 0.0
    if with_far:
        ds = (px * inv * (dot_nt(values_x, gt) - dot)).astype(bf16)
        gq = dot_nn(kxt, ds)
    for i, k in enumerate((k1, k2)):
        w = products[i][...] * local_inv
        ds = (w * (products[2 + i][...] - dot)).astype(bf16)
        gq = gq + dot_nn(dot_nt(eye, k[0:nk]).astype(bf16), ds)
        sums[i][...] = dot_nn(ds, qt)
        sums[2 + i][...] = dot_nn(w.astype(bf16), gt)
    gq_ref[...] = (gq * SCALE).T.astype(bf16)


def last_tile_kernel(r0, rows, members, *refs):
    G = members
    finish_tile(1, r0, rows, G, [refs[:G]], refs[G:G + 7], refs[G + 7:G + 11], refs[G + 11:G + 18], refs[G + 18:])


def first_tile_kernel(r0, rows, members, *refs):
    G = members
    parts, refs = [refs[:G], refs[G:2 * G]], refs[2 * G:]
    shared, products, last, refs = refs[:7], refs[7:11], refs[11:18], refs[18:]
    far_stats, out_own, out_kv, out_swap, scratch = refs[0], refs[1], refs[2], refs[3:G + 2], refs[G + 2:]
    nd, lanes = tile_sizes(rows, G)
    first = (far_stats,) + tuple(scratch[:6])
    far_stats[...] = last[0][...]
    finish_tile(0, r0, rows, G, parts, shared, products, first, scratch[6:])
    partner, per = G // 2, H // TILES
    for j in range(H):
        att, gq = (first, last)[j // per][1:3]
        for e, ref in enumerate((out_own, out_swap[partner - 1])):
            lo = (2 * (j % per) + e) * rows
            ref[j, 0:rows] = att[lo:lo + rows]
            ref[j, rows:2 * rows] = gq[lo:lo + rows]
        for g in range(G):
            at = pl.ds((j * G + g) * rows, rows)
            gk1, gk2, gv1, gv2 = (last[3 + i][at] + first[3 + i][at] if j < per else last[3 + i][at] for i in range(4))
            ref = out_kv if g == 0 else out_swap[g - 1]
            base = 2 if g == partner else 0
            for i, part in enumerate((gk2 * SCALE, gv2, gk1 * SCALE, gv1), base):
                ref[j, i * rows:(i + 1) * rows] = part.astype(ref.dtype)


def far_rows(query_refs, g, members, u, rows, lo):
    pair = (query_refs[u * members + g], query_refs[u * members + (g ^ (members // 2))])
    return jnp.concatenate([ref[(2 * j + lo) * rows:(2 * j + lo + 1) * rows] for j in range(H // TILES) for ref in pair], 0)


def far_slots(members, body):
    for g in range(members):
        slot = lax.axis_index("member") ^ g

        @pl.when((lax.axis_index("half") == 0) & (slot < members // 2))
        def _(g=g, slot=slot):
            body(g, slot)


def far_kernel(r0, rows, members, own_ref, *refs):
    G = members
    query_refs, products = refs[:TILES * G], refs[TILES * G:]
    sel = selector(lax.axis_index("head"), r0, rows, HD, False)[:rows]
    per = H // TILES
    keys, values = (jnp.concatenate([own_ref[j, lo * rows:(lo + 1) * rows] for j in range(H)], 0) for lo in (6, 7))
    docs = doc_cols(jnp.concatenate([sel * own_ref[j, 8 * rows:8 * rows + DOC_ROWS][0:1] for j in range(H)], 0))

    def body(g, slot):
        for u in range(TILES):
            x0 = u * per * rows
            pair = (query_refs[u * G + g], query_refs[u * G + (g ^ (G // 2))])
            dq = jnp.concatenate([sel * ref[2 * per * rows:2 * per * rows + DOC_ROWS][j:j + 1]
                                  for j in range(per) for ref in pair], 0)
            qdoc = dot_nt(jnp.ones((16, HD), jnp.bfloat16), dq)[0:1]
            s = dot_nt(keys[x0:], far_rows(query_refs, g, G, u, rows, 0)) * (SCALE * LOG2E)
            products[2 * u][slot] = jnp.where(docs[x0:] == qdoc, s, MASKED)
            products[2 * u + 1][slot] = dot_nt(values[x0:], far_rows(query_refs, g, G, u, rows, 1))

    far_slots(G, body)


def far_grads(rows, members, query_refs, stat_ref, products, gk, gv):
    G = members
    per = H // TILES
    gk[...], gv[...] = jnp.zeros_like(gk), jnp.zeros_like(gv)

    def body(g, slot):
        for u in range(TILES):
            x0 = u * per * rows
            chunks = per * 2 * rows // HD
            lse, dot = (jnp.concatenate([stat_ref[at + i:at + i + 1] for i in range(chunks)], 1)
                        for at in (8 * g + u * chunks, 8 * g + 4 + u * chunks))
            p = jnp.exp2(products[2 * u][slot] - lse)
            ds = p * (products[2 * u + 1][slot] - dot)
            gk[x0:] += dot_nn(ds.astype(jnp.bfloat16), far_rows(query_refs, g, G, u, rows, 0)) * SCALE
            gv[x0:] += dot_nn(p.astype(jnp.bfloat16), far_rows(query_refs, g, G, u, rows, 1))

    far_slots(G, body)


def sum_kernel(rows, members, *refs):
    G = members
    query_refs, refs = refs[:TILES * G], refs[TILES * G:]
    stat_ref, products, refs = refs[0], refs[1:1 + 2 * TILES], refs[1 + 2 * TILES:]
    own_ref, kv_ref, swap_refs, (out_ref, gk, gv) = refs[0], refs[1], refs[2:G + 1], refs[G + 1:]
    f32, bf16 = jnp.float32, jnp.bfloat16
    far_grads(rows, G, query_refs, stat_ref, products, gk, gv)
    out_ref[:, 0:2 * rows] = own_ref[...]
    out_ref[:, 2 * rows:4 * rows] = swap_refs[G // 2 - 1][:, 0:2 * rows]
    for j in range(H):
        total = kv_ref[j]
        for g, ref in enumerate(swap_refs, 1):
            base = 2 * rows if g == G // 2 else 0
            total = total + ref[j, base:base + 4 * rows].astype(f32)
        mine = slice(j * rows, (j + 1) * rows)
        out_ref[j, 4 * rows:6 * rows] = total[:2 * rows].astype(bf16)
        out_ref[j, 6 * rows:7 * rows] = (total[2 * rows:3 * rows] + gk[mine]).astype(bf16)
        out_ref[j, 7 * rows:8 * rows] = (total[3 * rows:] + gv[mine]).astype(bf16)


def unpack_kernel(r0, rows, members, in_ref, *refs):
    outs, bufs, sem = refs[:4], refs[4:8], refs[8]
    tokens = bufs[0].shape[0]
    bf16 = jnp.bfloat16
    kinds = range(min(H, 2 * r0))
    query_sels = [selector(h, r0, rows, tokens, True, takes_fine(members)) for h in kinds]
    key_sels = [selector(h, r0, rows, tokens, True, True) for h in kinds]
    copies = []
    for heads, cols in column_chunks():
        for i, base in enumerate((0, 1, 4, 5)):
            sels = query_sels if i < 2 else key_sels
            for h in heads:
                part = jnp.concatenate([in_ref[h, (base + e) * rows:(base + e + 1) * rows] for e in (0, 2)], 0)
                bufs[i][:, h * HD:(h + 1) * HD] = dot_nn(sels[h % (2 * r0)], part).astype(bf16)
            copies.append(pltpu.make_async_copy(bufs[i].at[:, cols], outs[i].at[:, cols], sem.at[len(copies)]))
            copies[-1].start()
    for copy in copies:
        copy.wait()


def call(kernel, out_shape, scratch=(), limit=16, **more):
    return pl.pallas_call(
        kernel,
        out_shape=out_shape,
        scratch_shapes=list(scratch),
        compiler_params=pltpu.CompilerParams(vmem_limit_bytes=limit * 1024 * 1024),
        **more,
    )


def per_device(members, queries, keys, values, cotangent, doc_ids):
    G = members
    tokens = queries.shape[0]
    devices = 2 * H * G
    r0 = tokens * devices // (2 * SEG)
    rows = tokens // (2 * r0)
    bf16, f32 = jnp.bfloat16, jnp.float32
    shape = jax.ShapeDtypeStruct
    n = H * G * rows
    anywhere = pl.BlockSpec(memory_space=pltpu.HBM)
    wide = pltpu.VMEM((tokens, H * HD), bf16)
    message = (H, 8 * rows + DOC_ROWS, HD)

    packed = call(
        functools.partial(pack_kernel, r0, rows, G), shape(message, bf16),
        [wide] * 4 + [pltpu.VMEM((1, tokens), jnp.int32), pltpu.VMEM(message, bf16), pltpu.SemaphoreType.DMA((1 + 3 * H,))],
        limit=64, in_specs=[anywhere] * 5, out_specs=anywhere,
    )(queries, keys, values, cotangent, doc_ids.reshape(1, tokens))

    def to_head(x):
        return lax.all_to_all(x, "head", 0, 0, tiled=True)

    def to_member(x, g):
        return lax.ppermute(x, "member", [(i, i ^ g) for i in range(G)])

    def across(x):
        return lax.ppermute(x, "half", [(0, 1), (1, 0)])

    own = to_head(packed)
    queries_here = jnp.where(takes_fine(G), own[:, 2 * rows:4 * rows], own[:, :2 * rows])
    sent_across = jnp.where(lax.axis_index("half") == 0, own[:, 6 * rows:8 * rows], queries_here)
    per = H // TILES

    def part_across(u):
        at = slice(u * per, (u + 1) * per)
        docs = jnp.pad(own[at, 8 * rows], ((0, DOC_ROWS - per), (0, 0)))
        return across(jnp.concatenate([sent_across[at].reshape(-1, HD), docs], 0))

    upper, lower = part_across(1), part_across(0)
    swaps = [to_member(own[:, (2 if g == G // 2 else 4) * rows:], g) for g in range(1, G)]
    nd, lanes = tile_sizes(rows, G)
    nq = TILES * lanes
    tile = [shape(((u + 1) * nd, lanes), f32) for u in range(TILES) for _ in range(2)]
    key_rows = pltpu.VMEM((n, HD), bf16)
    k1, k2, q_all, g_all, stats, out, gtt, *products = call(
        functools.partial(local_kernel, r0, rows, G),
        [shape((n, HD), bf16)] * 2 + [shape((nq, HD), bf16)] * 2 + [shape((8, nq), f32)]
        + [shape((HD, nq), f32)] * 2 + tile * 2,
        [key_rows] * 4, limit=32,
    )(own, *swaps)
    shared = (q_all, g_all, stats, out, gtt, k1, k2)
    upper, k1 = lax.optimization_barrier((upper, k1))
    uppers = [upper] + [to_member(upper, g) for g in range(1, G)]
    tile_rows = pltpu.VMEM((lanes, HD), bf16)
    far_scratch = lambda keys: [pltpu.VMEM((keys, HD), bf16)] * 3
    last = call(
        functools.partial(last_tile_kernel, r0, rows, G),
        [shape((8, HD), f32)] + [shape((lanes, HD), bf16)] * 2 + [shape((n, HD), f32)] * 4,
        far_scratch(nd), limit=32,
    )(*uppers, *shared, *products[2:4], *products[6:8])
    lowers = [lower] + [to_member(lower, g) for g in range(1, G)]
    sent = lambda g: (H, (6 if g == G // 2 else 4) * rows, HD)
    outs = call(
        functools.partial(first_tile_kernel, r0, rows, G),
        [shape((8, HD), f32), shape((H, 2 * rows, HD), bf16), shape((H, 4 * rows, HD), f32)]
        + [shape(sent(g), bf16) for g in range(1, G)],
        [tile_rows] * 2 + [pltpu.VMEM((nd, HD), f32)] * 4 + far_scratch(n), limit=32,
    )(*lowers, *uppers, *shared, *products[0:2], *products[4:6], *last)
    crosses = lowers + uppers
    far_stats = across(jnp.concatenate([outs[0]] + [to_member(outs[0], g) for g in range(1, G)], 0))
    products = call(
        functools.partial(far_kernel, r0, rows, G),
        [shape((G // 2, (TILES - u) * nd // G, lanes), f32) for u in range(TILES) for _ in range(2)],
    )(own, *crosses)
    swaps = [to_member(outs[2 + g], g) for g in range(1, G)]
    back = call(
        functools.partial(sum_kernel, rows, G), shape((H, 8 * rows, HD), bf16),
        [pltpu.VMEM((H * rows, HD), f32)] * 2,
    )(*crosses, far_stats, *products, outs[1], outs[2], *swaps)
    back = to_head(back)
    return tuple(call(
        functools.partial(unpack_kernel, r0, rows, G), [shape((tokens, H * HD), bf16)] * 4,
        [wide] * 4 + [pltpu.SemaphoreType.DMA((2 * H,))],
        in_specs=[VMEM], out_specs=[anywhere] * 4,
    )(back))


def solution(mesh):
    members = mesh.shape["seq"] // (2 * H)
    parts = {"seq": [("half", 2), ("head", H), ("member", members)]}
    axes = [part for name in mesh.axis_names for part in parts.get(name, [(name, mesh.shape[name])])]
    inner = Mesh(mesh.devices.reshape([size for _, size in axes]), [name for name, _ in axes])
    split = ("dp", "half", "head", "member")
    in_specs = (P(split, None),) * 4 + (P(split),)
    return jax.shard_map(
        functools.partial(per_device, members), mesh=inner, in_specs=in_specs,
        out_specs=(P(split, None),) * 4, check_vma=False,
    )
```

```python
import functools

import jax
import jax.numpy as jnp
import numpy as np
from jax import lax
from jax.experimental import pallas as pl
from jax.experimental.pallas import tpu as pltpu
from jax.sharding import Mesh
from jax.sharding import PartitionSpec as P

H = 8
HD = 128
SEG = 1024

MASKED = -1e30
SCALE = HD ** -0.5
LOG2E = float(np.log2(np.e))
VMEM = pl.BlockSpec(memory_space=pltpu.VMEM)
DOC_ROWS = 16


def dot_nn(a, b):
    return lax.dot_general(a, b, (((1,), (0,)), ((), ())), preferred_element_type=jnp.float32)


def dot_nt(a, b):
    return lax.dot_general(a, b, (((1,), (1,)), ((), ())), preferred_element_type=jnp.float32)


def selector(head, r0, rows, tokens, transposed, fine_first=False):
    r1 = 2 * r0
    shape = (tokens, 2 * rows) if transposed else (2 * rows, tokens)
    k = lax.broadcasted_iota(jnp.int32, shape, 1 if transposed else 0)
    p = lax.broadcasted_iota(jnp.int32, shape, 0 if transposed else 1)
    coarse = head % r1
    other = (coarse + r0) % r1
    first, second = jnp.where(fine_first, other, coarse), jnp.where(fine_first, coarse, other)
    target = jnp.where(k < rows, r1 * k + first, r1 * (k - rows) + second)
    return (p == target).astype(jnp.float32).astype(jnp.bfloat16)


def takes_fine(members):
    return lax.axis_index("member") >= members // 2


def pack_kernel(r0, rows, members, q_in, k_in, v_in, g_in, doc_in, out, q_ref, k_ref, v_ref, g_ref, doc_ref, buf, sem):
    tokens = q_ref.shape[0]
    pairs = ((doc_in, doc_ref), (k_in, k_ref), (v_in, v_ref), (q_in, q_ref), (g_in, g_ref))
    copies = [pltpu.make_async_copy(src, dst, sem.at[i]) for i, (src, dst) in enumerate(pairs)]
    for copy in copies:
        copy.start()
    kinds = range(min(H, 2 * r0))
    key_sels = [selector(h, r0, rows, tokens, False) for h in kinds]
    query_sels = [selector(h, r0, rows, tokens, False, takes_fine(members)) for h in kinds]

    def pick(sels, h, ref):
        return dot_nn(sels[h % (2 * r0)], ref[:, h * HD:(h + 1) * HD]).astype(jnp.bfloat16)

    for copy in copies:
        copy.wait()
    docs = jnp.broadcast_to(doc_ref[...].astype(jnp.float32).astype(jnp.bfloat16), (DOC_ROWS, tokens))
    sends = []
    for h in range(H):
        for i, ref in enumerate((q_ref, g_ref)):
            x = pick(query_sels, h, ref)
            buf[h, i * rows:(1 + i) * rows] = x[:rows]
            buf[h, (2 + i) * rows:(3 + i) * rows] = x[rows:]
        for i, ref in enumerate((k_ref, v_ref)):
            x = pick(key_sels, h, ref)
            buf[h, (4 + i) * rows:(5 + i) * rows] = x[rows:]
            buf[h, (6 + i) * rows:(7 + i) * rows] = x[:rows]
        buf[h, 8 * rows:8 * rows + DOC_ROWS] = docs
        sends.append(pltpu.make_async_copy(buf.at[h], out.at[h], sem.at[5 + h]))
        sends[-1].start()
    for copy in sends:
        copy.wait()


TILES = 2


def tile_sizes(rows, members):
    per = H // TILES
    return per * members * rows, per * 2 * rows


def eye_matrix():
    shape = (HD, HD)
    same = lax.broadcasted_iota(jnp.int32, shape, 0) == lax.broadcasted_iota(jnp.int32, shape, 1)
    return same.astype(jnp.float32).astype(jnp.bfloat16)


def doc_cols(x):
    return dot_nn(x, jnp.ones((HD, HD), jnp.bfloat16))[:, 0:1]


def local_kernel(r0, rows, members, *refs):
    G = members
    r1 = 2 * r0
    own_ref, swap_refs = refs[0], refs[1:G]
    (k1, k2, q_all, g_all, stats, out_ref, gtt_ref), rest = refs[G:G + 7], refs[G + 7:]
    p_refs, dp_refs, (v1, v2, d1, d2) = rest[:2 * TILES], rest[2 * TILES:4 * TILES], rest[4 * TILES:]
    bf16, f32 = jnp.bfloat16, jnp.float32
    tokens = HD
    head = lax.axis_index("head")
    member = lax.axis_index("member")
    fine = takes_fine(G)
    partner = G // 2
    partner_ref = swap_refs[partner - 1]

    sel = selector(head, r0, rows, tokens, False)
    query_sel = jnp.where(fine, sel[rows:].astype(f32), sel[:rows].astype(f32)).astype(bf16)
    source_docs = []
    for j in range(H):
        for g in range(G):
            at = pl.ds((j * G + g) * rows, rows)
            ref, base = (own_ref, 4 * rows) if g == 0 else (swap_refs[g - 1], 2 * rows if g == partner else 0)
            k2[at] = ref[j, base:base + rows]
            v2[at] = ref[j, base + rows:base + 2 * rows]
            k1[at] = ref[j, base + 2 * rows:base + 3 * rows]
            v1[at] = ref[j, base + 3 * rows:base + 4 * rows]
            doc = ref[j, base + 4 * rows:base + 4 * rows + DOC_ROWS][0:1]
            if g in (0, partner):
                source_docs.append(doc)
            d1[at] = sel[:rows] * doc
            d2[at] = sel[rows:] * doc

    eye = eye_matrix()
    v1t, v2t = dot_nt(eye, v1[...]).astype(bf16), dot_nt(eye, v2[...]).astype(bf16)
    docs1, docs2 = doc_cols(d1[...]), doc_cols(d2[...])
    nd, lanes = tile_sizes(rows, G)
    per = H // TILES

    coarse = head % r1
    other = (coarse + r0) % r1
    lane = lax.broadcasted_iota(jnp.int32, (1, lanes), 1)
    qmember = member ^ (partner * ((lane // rows) % 2))
    qpos = (lane // (2 * rows)) * (G * tokens) + qmember * tokens + r1 * (lane % rows) + jnp.where(fine, other, coarse)
    kl = lax.broadcasted_iota(jnp.int32, (nd, 1), 0)
    kmember = member ^ ((kl // rows) % G)
    kpos = (kl // (rows * G)) * (G * tokens) + kmember * tokens + r1 * (kl % rows)
    causal1 = kpos + coarse <= qpos
    causal2 = kpos + other <= qpos
    both = jnp.where(fine, 0.0, 1.0)
    c = SCALE * LOG2E

    for u in range(TILES):
        nk = (u + 1) * nd
        x0 = u * nd
        src = range(u * per, (u + 1) * per)
        mine = slice(u * lanes, (u + 1) * lanes)
        gather = lambda lo: jnp.concatenate([ref[j, lo:lo + rows] for j in src for ref in (own_ref, partner_ref)], 0)
        qt, gt = gather(0), gather(rows)
        q_all[mine], g_all[mine] = qt, gt
        dq = jnp.concatenate([query_sel * source_docs[2 * j + e] for j in src for e in range(2)], 0)
        qdoc = dot_nt(jnp.ones((16, HD), bf16), dq)[0:1]

        def scores(key, docs, causal):
            s = jnp.where(docs == qdoc, dot_nt(key, qt), MASKED)
            if u:
                return jnp.concatenate([s[:x0], jnp.where(causal, s[x0:], MASKED)], 0)
            return jnp.where(causal, s, MASKED)

        s1 = scores(k1[0:nk], docs1[0:nk], causal1)
        s2 = scores(k2[0:nk], docs2[0:nk], causal2)
        top = jnp.maximum(jnp.max(s1, 0, keepdims=True), jnp.max(s2, 0, keepdims=True))
        base = top * c
        p1 = jnp.exp2(s1 * c - (base - both))
        p2 = jnp.exp2(s2 * c - base)
        stats[0:1, mine] = top
        stats[1:2, mine] = jnp.sum(p1, 0, keepdims=True) + jnp.sum(p2, 0, keepdims=True)
        stats[2:3, mine] = qdoc
        out_ref[:, mine] = dot_nn(v1t[:, :nk], p1.astype(bf16)) + dot_nn(v2t[:, :nk], p2.astype(bf16))
        gtt_ref[:, mine] = dot_nt(eye, gt)
        p_refs[2 * u][...], p_refs[2 * u + 1][...] = p1, p2
        dp_refs[2 * u][...], dp_refs[2 * u + 1][...] = dot_nt(v1[0:nk], gt), dot_nt(v2[0:nk], gt)


def finish_tile(u, r0, rows, members, parts, shared, products, results, scratch):
    far = (lax.axis_index("half") == 1) & jnp.logical_not(takes_fine(members))
    for branch, with_far in ((far, True), (jnp.logical_not(far), False)):
        pl.when(branch)(functools.partial(
            tile_body, u, r0, rows, members, with_far, parts, shared, products, results, scratch))


def tile_body(u, r0, rows, members, with_far, parts, shared, products, results, scratch):
    G = members
    q_all, g_all, stats, local_out, gtt_ref, k1, k2 = shared
    far_stats, att, gq_ref, sums = results[0], results[1], results[2], results[3:]
    kx, vx, dx = scratch
    bf16 = jnp.bfloat16
    per = H // TILES
    eye = eye_matrix()
    nd, lanes = tile_sizes(rows, G)
    nk = (u + 1) * nd
    mine = slice(u * lanes, (u + 1) * lanes)
    c = SCALE * LOG2E
    qt, gt = q_all[mine], g_all[mine]
    top, total, out = stats[0:1, mine], stats[1:2, mine], local_out[:, mine]
    if with_far:
        sel = selector(lax.axis_index("head"), r0, rows, HD, False)
        for p, part in enumerate(parts):
            for j in range(per):
                for g, ref in enumerate(part):
                    at = pl.ds(((p * per + j) * G + g) * rows, rows)
                    kx[at] = ref[2 * j * rows:(2 * j + 1) * rows]
                    vx[at] = ref[(2 * j + 1) * rows:(2 * j + 2) * rows]
                    dx[at] = sel[:rows] * ref[2 * per * rows:2 * per * rows + DOC_ROWS][j:j + 1]
        keys_x, values_x = kx[...], vx[...]
        kxt, vxt = dot_nt(eye, keys_x).astype(bf16), dot_nt(eye, values_x).astype(bf16)
        sx = jnp.where(doc_cols(dx[...]) == stats[2:3, mine], dot_nt(keys_x, qt), MASKED)
        local_top = top
        top = jnp.maximum(local_top, jnp.max(sx, 0, keepdims=True))
        px = jnp.exp2(sx * c - top * c)
        shrink = jnp.exp2(local_top * c - top * c)
        total = total * shrink + jnp.sum(px, 0, keepdims=True)
        inv = 1.0 / total
        local_inv = shrink * inv
        out = out * local_inv + dot_nn(vxt, px.astype(bf16)) * inv
    else:
        local_inv = 1.0 / total
        out = out * local_inv
    dot = jnp.sum(gtt_ref[:, mine] * out, 0, keepdims=True)
    lse = top * c + jnp.log(total) * LOG2E
    chunks = lanes // HD
    for i in range(chunks):
        far_stats[u * chunks + i:u * chunks + i + 1] = lse[:, i * HD:(i + 1) * HD]
        far_stats[4 + u * chunks + i:5 + u * chunks + i] = dot[:, i * HD:(i + 1) * HD]
    att[...] = out.T.astype(bf16)
    gq = 0.0
    if with_far:
        ds = (px * inv * (dot_nt(values_x, gt) - dot)).astype(bf16)
        gq = dot_nn(kxt, ds)
    for i, k in enumerate((k1, k2)):
        w = products[i][...] * local_inv
        ds = (w * (products[2 + i][...] - dot)).astype(bf16)
        gq = gq + dot_nn(dot_nt(eye, k[0:nk]).astype(bf16), ds)
        sums[i][...] = dot_nn(ds, qt)
        sums[2 + i][...] = dot_nn(w.astype(bf16), gt)
    gq_ref[...] = (gq * SCALE).T.astype(bf16)


def last_tile_kernel(r0, rows, members, *refs):
    G = members
    finish_tile(1, r0, rows, G, [refs[:G]], refs[G:G + 7], refs[G + 7:G + 11], refs[G + 11:G + 18], refs[G + 18:])


def first_tile_kernel(r0, rows, members, *refs):
    G = members
    parts, refs = [refs[:G], refs[G:2 * G]], refs[2 * G:]
    shared, products, last, refs = refs[:7], refs[7:11], refs[11:18], refs[18:]
    far_stats, out_own, out_kv, out_swap, scratch = refs[0], refs[1], refs[2], refs[3:G + 2], refs[G + 2:]
    nd, lanes = tile_sizes(rows, G)
    first = (far_stats,) + tuple(scratch[:6])
    far_stats[...] = last[0][...]
    finish_tile(0, r0, rows, G, parts, shared, products, first, scratch[6:])
    partner, per = G // 2, H // TILES
    for j in range(H):
        att, gq = (first, last)[j // per][1:3]
        for e, ref in enumerate((out_own, out_swap[partner - 1])):
            lo = (2 * (j % per) + e) * rows
            ref[j, 0:rows] = att[lo:lo + rows]
            ref[j, rows:2 * rows] = gq[lo:lo + rows]
        for g in range(G):
            at = pl.ds((j * G + g) * rows, rows)
            gk1, gk2, gv1, gv2 = (last[3 + i][at] + first[3 + i][at] if j < per else last[3 + i][at] for i in range(4))
            ref = out_kv if g == 0 else out_swap[g - 1]
            base = 2 if g == partner else 0
            for i, part in enumerate((gk2 * SCALE, gv2, gk1 * SCALE, gv1), base):
                ref[j, i * rows:(i + 1) * rows] = part.astype(ref.dtype)


def far_rows(query_refs, g, members, u, rows, lo):
    pair = (query_refs[u * members + g], query_refs[u * members + (g ^ (members // 2))])
    return jnp.concatenate([ref[(2 * j + lo) * rows:(2 * j + lo + 1) * rows] for j in range(H // TILES) for ref in pair], 0)


def far_slots(members, body):
    for g in range(members):
        slot = lax.axis_index("member") ^ g

        @pl.when((lax.axis_index("half") == 0) & (slot < members // 2))
        def _(g=g, slot=slot):
            body(g, slot)


def far_kernel(r0, rows, members, own_ref, *refs):
    G = members
    query_refs, products = refs[:TILES * G], refs[TILES * G:]
    sel = selector(lax.axis_index("head"), r0, rows, HD, False)[:rows]
    per = H // TILES
    keys, values = (jnp.concatenate([own_ref[j, lo * rows:(lo + 1) * rows] for j in range(H)], 0) for lo in (6, 7))
    docs = doc_cols(jnp.concatenate([sel * own_ref[j, 8 * rows:8 * rows + DOC_ROWS][0:1] for j in range(H)], 0))

    def body(g, slot):
        for u in range(TILES):
            x0 = u * per * rows
            pair = (query_refs[u * G + g], query_refs[u * G + (g ^ (G // 2))])
            dq = jnp.concatenate([sel * ref[2 * per * rows:2 * per * rows + DOC_ROWS][j:j + 1]
                                  for j in range(per) for ref in pair], 0)
            qdoc = dot_nt(jnp.ones((16, HD), jnp.bfloat16), dq)[0:1]
            s = dot_nt(keys[x0:], far_rows(query_refs, g, G, u, rows, 0)) * (SCALE * LOG2E)
            products[2 * u][slot] = jnp.where(docs[x0:] == qdoc, s, MASKED)
            products[2 * u + 1][slot] = dot_nt(values[x0:], far_rows(query_refs, g, G, u, rows, 1))

    far_slots(G, body)


def far_grads(rows, members, query_refs, stat_ref, products, gk, gv):
    G = members
    per = H // TILES
    gk[...], gv[...] = jnp.zeros_like(gk), jnp.zeros_like(gv)

    def body(g, slot):
        for u in range(TILES):
            x0 = u * per * rows
            chunks = per * 2 * rows // HD
            lse, dot = (jnp.concatenate([stat_ref[at + i:at + i + 1] for i in range(chunks)], 1)
                        for at in (8 * g + u * chunks, 8 * g + 4 + u * chunks))
            p = jnp.exp2(products[2 * u][slot] - lse)
            ds = p * (products[2 * u + 1][slot] - dot)
            gk[x0:] += dot_nn(ds.astype(jnp.bfloat16), far_rows(query_refs, g, G, u, rows, 0)) * SCALE
            gv[x0:] += dot_nn(p.astype(jnp.bfloat16), far_rows(query_refs, g, G, u, rows, 1))

    far_slots(G, body)


def sum_kernel(rows, members, *refs):
    G = members
    query_refs, refs = refs[:TILES * G], refs[TILES * G:]
    stat_ref, products, refs = refs[0], refs[1:1 + 2 * TILES], refs[1 + 2 * TILES:]
    own_ref, kv_ref, swap_refs, (out_ref, gk, gv) = refs[0], refs[1], refs[2:G + 1], refs[G + 1:]
    f32, bf16 = jnp.float32, jnp.bfloat16
    far_grads(rows, G, query_refs, stat_ref, products, gk, gv)
    out_ref[:, 0:2 * rows] = own_ref[...]
    out_ref[:, 2 * rows:4 * rows] = swap_refs[G // 2 - 1][:, 0:2 * rows]
    for j in range(H):
        total = kv_ref[j]
        for g, ref in enumerate(swap_refs, 1):
            base = 2 * rows if g == G // 2 else 0
            total = total + ref[j, base:base + 4 * rows].astype(f32)
        mine = slice(j * rows, (j + 1) * rows)
        out_ref[j, 4 * rows:6 * rows] = total[:2 * rows].astype(bf16)
        out_ref[j, 6 * rows:7 * rows] = (total[2 * rows:3 * rows] + gk[mine]).astype(bf16)
        out_ref[j, 7 * rows:8 * rows] = (total[3 * rows:] + gv[mine]).astype(bf16)


def unpack_kernel(r0, rows, members, in_ref, *refs):
    outs, bufs, sem = refs[:4], refs[4:8], refs[8]
    tokens = bufs[0].shape[0]
    bf16 = jnp.bfloat16
    kinds = range(min(H, 2 * r0))
    query_sels = [selector(h, r0, rows, tokens, True, takes_fine(members)) for h in kinds]
    key_sels = [selector(h, r0, rows, tokens, True, True) for h in kinds]
    copies = []
    for i, base in enumerate((0, 1, 4, 5)):
        for h in range(H):
            sels = query_sels if i < 2 else key_sels
            part = jnp.concatenate([in_ref[h, (base + e) * rows:(base + e + 1) * rows] for e in (0, 2)], 0)
            bufs[i][:, h * HD:(h + 1) * HD] = dot_nn(sels[h % (2 * r0)], part).astype(bf16)
        copies.append(pltpu.make_async_copy(bufs[i], outs[i], sem.at[i]))
        copies[-1].start()
    for copy in copies:
        copy.wait()


def call(kernel, out_shape, scratch=(), limit=16, **more):
    return pl.pallas_call(
        kernel,
        out_shape=out_shape,
        scratch_shapes=list(scratch),
        compiler_params=pltpu.CompilerParams(vmem_limit_bytes=limit * 1024 * 1024),
        **more,
    )


def per_device(members, queries, keys, values, cotangent, doc_ids):
    G = members
    tokens = queries.shape[0]
    devices = 2 * H * G
    r0 = tokens * devices // (2 * SEG)
    rows = tokens // (2 * r0)
    bf16, f32 = jnp.bfloat16, jnp.float32
    shape = jax.ShapeDtypeStruct
    n = H * G * rows
    anywhere = pl.BlockSpec(memory_space=pltpu.HBM)
    wide = pltpu.VMEM((tokens, H * HD), bf16)
    message = (H, 8 * rows + DOC_ROWS, HD)

    packed = call(
        functools.partial(pack_kernel, r0, rows, G), shape(message, bf16),
        [wide] * 4 + [pltpu.VMEM((1, tokens), jnp.int32), pltpu.VMEM(message, bf16), pltpu.SemaphoreType.DMA((5 + H,))],
        limit=64, in_specs=[anywhere] * 5, out_specs=anywhere,
    )(queries, keys, values, cotangent, doc_ids.reshape(1, tokens))

    def to_head(x):
        return lax.all_to_all(x, "head", 0, 0, tiled=True)

    def to_member(x, g):
        return lax.ppermute(x, "member", [(i, i ^ g) for i in range(G)])

    def across(x):
        return lax.ppermute(x, "half", [(0, 1), (1, 0)])

    own = to_head(packed)
    queries_here = jnp.where(takes_fine(G), own[:, 2 * rows:4 * rows], own[:, :2 * rows])
    sent_across = jnp.where(lax.axis_index("half") == 0, own[:, 6 * rows:8 * rows], queries_here)
    per = H // TILES

    def part_across(u):
        at = slice(u * per, (u + 1) * per)
        docs = jnp.pad(own[at, 8 * rows], ((0, DOC_ROWS - per), (0, 0)))
        return across(jnp.concatenate([sent_across[at].reshape(-1, HD), docs], 0))

    upper, lower = part_across(1), part_across(0)
    swaps = [to_member(own[:, (2 if g == G // 2 else 4) * rows:], g) for g in range(1, G)]
    nd, lanes = tile_sizes(rows, G)
    nq = TILES * lanes
    tile = [shape(((u + 1) * nd, lanes), f32) for u in range(TILES) for _ in range(2)]
    key_rows = pltpu.VMEM((n, HD), bf16)
    k1, k2, q_all, g_all, stats, out, gtt, *products = call(
        functools.partial(local_kernel, r0, rows, G),
        [shape((n, HD), bf16)] * 2 + [shape((nq, HD), bf16)] * 2 + [shape((8, nq), f32)]
        + [shape((HD, nq), f32)] * 2 + tile * 2,
        [key_rows] * 4, limit=32,
    )(own, *swaps)
    shared = (q_all, g_all, stats, out, gtt, k1, k2)
    upper, k1 = lax.optimization_barrier((upper, k1))
    uppers = [upper] + [to_member(upper, g) for g in range(1, G)]
    tile_rows = pltpu.VMEM((lanes, HD), bf16)
    far_scratch = lambda keys: [pltpu.VMEM((keys, HD), bf16)] * 3
    last = call(
        functools.partial(last_tile_kernel, r0, rows, G),
        [shape((8, HD), f32)] + [shape((lanes, HD), bf16)] * 2 + [shape((n, HD), f32)] * 4,
        far_scratch(nd), limit=32,
    )(*uppers, *shared, *products[2:4], *products[6:8])
    lowers = [lower] + [to_member(lower, g) for g in range(1, G)]
    sent = lambda g: (H, (6 if g == G // 2 else 4) * rows, HD)
    outs = call(
        functools.partial(first_tile_kernel, r0, rows, G),
        [shape((8, HD), f32), shape((H, 2 * rows, HD), bf16), shape((H, 4 * rows, HD), f32)]
        + [shape(sent(g), bf16) for g in range(1, G)],
        [tile_rows] * 2 + [pltpu.VMEM((nd, HD), f32)] * 4 + far_scratch(n), limit=32,
    )(*lowers, *uppers, *shared, *products[0:2], *products[4:6], *last)
    crosses = lowers + uppers
    hops = [to_member(outs[0], g) for g in range(1, G)]
    far_stats = across(jnp.concatenate([outs[0]] + hops, 0))
    products = call(
        functools.partial(far_kernel, r0, rows, G),
        [shape((G // 2, (TILES - u) * nd // G, lanes), f32) for u in range(TILES) for _ in range(2)],
    )(own, *crosses)
    sends, _ = lax.optimization_barrier((list(outs[3:]), hops))
    swaps = [to_member(x, g) for g, x in enumerate(sends, 1)]
    back = call(
        functools.partial(sum_kernel, rows, G), shape((H, 8 * rows, HD), bf16),
        [pltpu.VMEM((H * rows, HD), f32)] * 2,
    )(*crosses, far_stats, *products, outs[1], outs[2], *swaps)
    back = to_head(back)
    return tuple(call(
        functools.partial(unpack_kernel, r0, rows, G), [shape((tokens, H * HD), bf16)] * 4,
        [wide] * 4 + [pltpu.SemaphoreType.DMA((4,))],
        in_specs=[VMEM], out_specs=[anywhere] * 4,
    )(back))


def solution(mesh):
    members = mesh.shape["seq"] // (2 * H)
    parts = {"seq": [("half", 2), ("head", H), ("member", members)]}
    axes = [part for name in mesh.axis_names for part in parts.get(name, [(name, mesh.shape[name])])]
    inner = Mesh(mesh.devices.reshape([size for _, size in axes]), [name for name, _ in axes])
    split = ("dp", "half", "head", "member")
    in_specs = (P(split, None),) * 4 + (P(split),)
    return jax.shard_map(
        functools.partial(per_device, members), mesh=inner, in_specs=in_specs,
        out_specs=(P(split, None),) * 4, check_vma=False,
    )
```

```python
import functools

import jax
import jax.numpy as jnp
import numpy as np
from jax import lax
from jax.experimental import pallas as pl
from jax.experimental.pallas import tpu as pltpu
from jax.sharding import Mesh
from jax.sharding import PartitionSpec as P

H = 8
HD = 128
SEG = 1024

MASKED = -1e30
SCALE = HD ** -0.5
LOG2E = float(np.log2(np.e))
VMEM = pl.BlockSpec(memory_space=pltpu.VMEM)
DOC_ROWS = 16


def dot_nn(a, b):
    return lax.dot_general(a, b, (((1,), (0,)), ((), ())), preferred_element_type=jnp.float32)


def dot_nt(a, b):
    return lax.dot_general(a, b, (((1,), (1,)), ((), ())), preferred_element_type=jnp.float32)


def selector(head, r0, rows, tokens, transposed, fine_first=False):
    r1 = 2 * r0
    shape = (tokens, 2 * rows) if transposed else (2 * rows, tokens)
    k = lax.broadcasted_iota(jnp.int32, shape, 1 if transposed else 0)
    p = lax.broadcasted_iota(jnp.int32, shape, 0 if transposed else 1)
    coarse = head % r1
    other = (coarse + r0) % r1
    first, second = jnp.where(fine_first, other, coarse), jnp.where(fine_first, coarse, other)
    target = jnp.where(k < rows, r1 * k + first, r1 * (k - rows) + second)
    return (p == target).astype(jnp.float32).astype(jnp.bfloat16)


def takes_fine(members):
    return lax.axis_index("member") >= members // 2


def pack_kernel(r0, rows, members, q_in, k_in, v_in, g_in, doc_in, out, q_ref, k_ref, v_ref, g_ref, doc_ref, buf, sem):
    tokens = q_ref.shape[0]
    pairs = ((doc_in, doc_ref), (k_in, k_ref), (v_in, v_ref), (q_in, q_ref), (g_in, g_ref))
    copies = [pltpu.make_async_copy(src, dst, sem.at[i]) for i, (src, dst) in enumerate(pairs)]
    for copy in copies:
        copy.start()
    kinds = range(min(H, 2 * r0))
    key_sels = [selector(h, r0, rows, tokens, False) for h in kinds]
    query_sels = [selector(h, r0, rows, tokens, False, takes_fine(members)) for h in kinds]

    def pick(sels, h, ref):
        return dot_nn(sels[h % (2 * r0)], ref[:, h * HD:(h + 1) * HD]).astype(jnp.bfloat16)

    for copy in copies:
        copy.wait()
    docs = jnp.broadcast_to(doc_ref[...].astype(jnp.float32).astype(jnp.bfloat16), (DOC_ROWS, tokens))
    sends = []
    for h in range(H):
        for i, ref in enumerate((q_ref, g_ref)):
            x = pick(query_sels, h, ref)
            buf[h, i * rows:(1 + i) * rows] = x[:rows]
            buf[h, (2 + i) * rows:(3 + i) * rows] = x[rows:]
        for i, ref in enumerate((k_ref, v_ref)):
            x = pick(key_sels, h, ref)
            buf[h, (4 + i) * rows:(5 + i) * rows] = x[rows:]
            buf[h, (6 + i) * rows:(7 + i) * rows] = x[:rows]
        buf[h, 8 * rows:8 * rows + DOC_ROWS] = docs
        sends.append(pltpu.make_async_copy(buf.at[h], out.at[h], sem.at[5 + h]))
        sends[-1].start()
    for copy in sends:
        copy.wait()


TILES = 2


def tile_sizes(rows, members):
    per = H // TILES
    return per * members * rows, per * 2 * rows


def eye_matrix():
    shape = (HD, HD)
    same = lax.broadcasted_iota(jnp.int32, shape, 0) == lax.broadcasted_iota(jnp.int32, shape, 1)
    return same.astype(jnp.float32).astype(jnp.bfloat16)


def doc_cols(x):
    return dot_nn(x, jnp.ones((HD, HD), jnp.bfloat16))[:, 0:1]


def local_kernel(r0, rows, members, *refs):
    G = members
    r1 = 2 * r0
    own_ref, swap_refs = refs[0], refs[1:G]
    (k1, k2, q_all, g_all, stats, out_ref, gtt_ref), rest = refs[G:G + 7], refs[G + 7:]
    p_refs, dp_refs, (v1, v2, d1, d2) = rest[:2 * TILES], rest[2 * TILES:4 * TILES], rest[4 * TILES:]
    bf16, f32 = jnp.bfloat16, jnp.float32
    tokens = HD
    head = lax.axis_index("head")
    member = lax.axis_index("member")
    fine = takes_fine(G)
    partner = G // 2
    partner_ref = swap_refs[partner - 1]

    sel = selector(head, r0, rows, tokens, False)
    query_sel = jnp.where(fine, sel[rows:].astype(f32), sel[:rows].astype(f32)).astype(bf16)
    source_docs = []
    for j in range(H):
        for g in range(G):
            at = pl.ds((j * G + g) * rows, rows)
            ref, base = (own_ref, 4 * rows) if g == 0 else (swap_refs[g - 1], 2 * rows if g == partner else 0)
            k2[at] = ref[j, base:base + rows]
            v2[at] = ref[j, base + rows:base + 2 * rows]
            k1[at] = ref[j, base + 2 * rows:base + 3 * rows]
            v1[at] = ref[j, base + 3 * rows:base + 4 * rows]
            doc = ref[j, base + 4 * rows:base + 4 * rows + DOC_ROWS][0:1]
            if g in (0, partner):
                source_docs.append(doc)
            d1[at] = sel[:rows] * doc
            d2[at] = sel[rows:] * doc

    eye = eye_matrix()
    v1t, v2t = dot_nt(eye, v1[...]).astype(bf16), dot_nt(eye, v2[...]).astype(bf16)
    docs1, docs2 = doc_cols(d1[...]), doc_cols(d2[...])
    nd, lanes = tile_sizes(rows, G)
    per = H // TILES

    coarse = head % r1
    other = (coarse + r0) % r1
    lane = lax.broadcasted_iota(jnp.int32, (1, lanes), 1)
    qmember = member ^ (partner * ((lane // rows) % 2))
    qpos = (lane // (2 * rows)) * (G * tokens) + qmember * tokens + r1 * (lane % rows) + jnp.where(fine, other, coarse)
    kl = lax.broadcasted_iota(jnp.int32, (nd, 1), 0)
    kmember = member ^ ((kl // rows) % G)
    kpos = (kl // (rows * G)) * (G * tokens) + kmember * tokens + r1 * (kl % rows)
    causal1 = kpos + coarse <= qpos
    causal2 = kpos + other <= qpos
    both = jnp.where(fine, 0.0, 1.0)
    c = SCALE * LOG2E

    for u in range(TILES):
        nk = (u + 1) * nd
        x0 = u * nd
        src = range(u * per, (u + 1) * per)
        mine = slice(u * lanes, (u + 1) * lanes)
        gather = lambda lo: jnp.concatenate([ref[j, lo:lo + rows] for j in src for ref in (own_ref, partner_ref)], 0)
        qt, gt = gather(0), gather(rows)
        q_all[mine], g_all[mine] = qt, gt
        dq = jnp.concatenate([query_sel * source_docs[2 * j + e] for j in src for e in range(2)], 0)
        qdoc = dot_nt(jnp.ones((16, HD), bf16), dq)[0:1]

        def scores(key, docs, causal):
            s = jnp.where(docs == qdoc, dot_nt(key, qt), MASKED)
            if u:
                return jnp.concatenate([s[:x0], jnp.where(causal, s[x0:], MASKED)], 0)
            return jnp.where(causal, s, MASKED)

        s1 = scores(k1[0:nk], docs1[0:nk], causal1)
        s2 = scores(k2[0:nk], docs2[0:nk], causal2)
        top = jnp.maximum(jnp.max(s1, 0, keepdims=True), jnp.max(s2, 0, keepdims=True))
        base = top * c
        p1 = jnp.exp2(s1 * c - (base - both))
        p2 = jnp.exp2(s2 * c - base)
        stats[0:1, mine] = top
        stats[1:2, mine] = jnp.sum(p1, 0, keepdims=True) + jnp.sum(p2, 0, keepdims=True)
        stats[2:3, mine] = qdoc
        out_ref[:, mine] = dot_nn(v1t[:, :nk], p1.astype(bf16)) + dot_nn(v2t[:, :nk], p2.astype(bf16))
        gtt_ref[:, mine] = dot_nt(eye, gt)
        p_refs[2 * u][...], p_refs[2 * u + 1][...] = p1, p2
        dp_refs[2 * u][...], dp_refs[2 * u + 1][...] = dot_nt(v1[0:nk], gt), dot_nt(v2[0:nk], gt)


def finish_tile(u, r0, rows, members, parts, shared, products, results, scratch):
    far = (lax.axis_index("half") == 1) & jnp.logical_not(takes_fine(members))
    for branch, with_far in ((far, True), (jnp.logical_not(far), False)):
        pl.when(branch)(functools.partial(
            tile_body, u, r0, rows, members, with_far, parts, shared, products, results, scratch))


def tile_body(u, r0, rows, members, with_far, parts, shared, products, results, scratch):
    G = members
    q_all, g_all, stats, local_out, gtt_ref, k1, k2 = shared
    far_stats, att, gq_ref, sums = results[0], results[1], results[2], results[3:]
    kx, vx, dx = scratch
    bf16 = jnp.bfloat16
    per = H // TILES
    eye = eye_matrix()
    nd, lanes = tile_sizes(rows, G)
    nk = (u + 1) * nd
    mine = slice(u * lanes, (u + 1) * lanes)
    c = SCALE * LOG2E
    qt, gt = q_all[mine], g_all[mine]
    top, total, out = stats[0:1, mine], stats[1:2, mine], local_out[:, mine]
    if with_far:
        sel = selector(lax.axis_index("head"), r0, rows, HD, False)
        for p, part in enumerate(parts):
            for j in range(per):
                for g, ref in enumerate(part):
                    at = pl.ds(((p * per + j) * G + g) * rows, rows)
                    kx[at] = ref[2 * j * rows:(2 * j + 1) * rows]
                    vx[at] = ref[(2 * j + 1) * rows:(2 * j + 2) * rows]
                    source = (TILES - len(parts) + p) * per + j
                    dx[at] = sel[:rows] * parts[-1][g][2 * per * rows:2 * per * rows + DOC_ROWS][source:source + 1]
        keys_x, values_x = kx[...], vx[...]
        kxt, vxt = dot_nt(eye, keys_x).astype(bf16), dot_nt(eye, values_x).astype(bf16)
        sx = jnp.where(doc_cols(dx[...]) == stats[2:3, mine], dot_nt(keys_x, qt), MASKED)
        local_top = top
        top = jnp.maximum(local_top, jnp.max(sx, 0, keepdims=True))
        px = jnp.exp2(sx * c - top * c)
        shrink = jnp.exp2(local_top * c - top * c)
        total = total * shrink + jnp.sum(px, 0, keepdims=True)
        inv = 1.0 / total
        local_inv = shrink * inv
        out = out * local_inv + dot_nn(vxt, px.astype(bf16)) * inv
    else:
        local_inv = 1.0 / total
        out = out * local_inv
    dot = jnp.sum(gtt_ref[:, mine] * out, 0, keepdims=True)
    lse = top * c + jnp.log(total) * LOG2E
    chunks = lanes // HD
    for i in range(chunks):
        far_stats[u * chunks + i:u * chunks + i + 1] = lse[:, i * HD:(i + 1) * HD]
        far_stats[4 + u * chunks + i:5 + u * chunks + i] = dot[:, i * HD:(i + 1) * HD]
    att[...] = out.T.astype(bf16)
    gq = 0.0
    if with_far:
        ds = (px * inv * (dot_nt(values_x, gt) - dot)).astype(bf16)
        gq = dot_nn(kxt, ds)
    for i, k in enumerate((k1, k2)):
        w = products[i][...] * local_inv
        ds = (w * (products[2 + i][...] - dot)).astype(bf16)
        gq = gq + dot_nn(dot_nt(eye, k[0:nk]).astype(bf16), ds)
        sums[i][...] = dot_nn(ds, qt)
        sums[2 + i][...] = dot_nn(w.astype(bf16), gt)
    gq_ref[...] = (gq * SCALE).T.astype(bf16)


def last_tile_kernel(r0, rows, members, *refs):
    G = members
    finish_tile(1, r0, rows, G, [refs[:G]], refs[G:G + 7], refs[G + 7:G + 11], refs[G + 11:G + 18], refs[G + 18:])


def first_tile_kernel(r0, rows, members, *refs):
    G = members
    parts, refs = [refs[:G], refs[G:2 * G]], refs[2 * G:]
    shared, products, last, refs = refs[:7], refs[7:11], refs[11:18], refs[18:]
    far_stats, out_own, out_kv, out_swap, scratch = refs[0], refs[1], refs[2], refs[3:G + 2], refs[G + 2:]
    nd, lanes = tile_sizes(rows, G)
    first = (far_stats,) + tuple(scratch[:6])
    far_stats[...] = last[0][...]
    finish_tile(0, r0, rows, G, parts, shared, products, first, scratch[6:])
    partner, per = G // 2, H // TILES
    for j in range(H):
        att, gq = (first, last)[j // per][1:3]
        for e, ref in enumerate((out_own, out_swap[partner - 1])):
            lo = (2 * (j % per) + e) * rows
            ref[j, 0:rows] = att[lo:lo + rows]
            ref[j, rows:2 * rows] = gq[lo:lo + rows]
        for g in range(G):
            at = pl.ds((j * G + g) * rows, rows)
            gk1, gk2, gv1, gv2 = (last[3 + i][at] + first[3 + i][at] if j < per else last[3 + i][at] for i in range(4))
            ref = out_kv if g == 0 else out_swap[g - 1]
            base = 2 if g == partner else 0
            for i, part in enumerate((gk2 * SCALE, gv2, gk1 * SCALE, gv1), base):
                ref[j, i * rows:(i + 1) * rows] = part.astype(ref.dtype)


def far_rows(query_refs, g, members, u, rows, lo):
    pair = (query_refs[u * members + g], query_refs[u * members + (g ^ (members // 2))])
    return jnp.concatenate([ref[(2 * j + lo) * rows:(2 * j + lo + 1) * rows] for j in range(H // TILES) for ref in pair], 0)


def far_slots(members, body):
    for g in range(members):
        slot = lax.axis_index("member") ^ g

        @pl.when((lax.axis_index("half") == 0) & (slot < members // 2))
        def _(g=g, slot=slot):
            body(g, slot)


def far_kernel(r0, rows, members, own_ref, *refs):
    G = members
    query_refs, products = refs[:TILES * G], refs[TILES * G:]
    sel = selector(lax.axis_index("head"), r0, rows, HD, False)[:rows]
    per = H // TILES
    keys, values = (jnp.concatenate([own_ref[j, lo * rows:(lo + 1) * rows] for j in range(H)], 0) for lo in (6, 7))
    docs = doc_cols(jnp.concatenate([sel * own_ref[j, 8 * rows:8 * rows + DOC_ROWS][0:1] for j in range(H)], 0))

    def body(g, slot):
        for u in range(TILES):
            x0 = u * per * rows
            pair = (query_refs[G + g], query_refs[G + (g ^ (G // 2))])
            dq = jnp.concatenate([sel * ref[2 * per * rows:2 * per * rows + DOC_ROWS][j:j + 1]
                                  for j in range(u * per, (u + 1) * per) for ref in pair], 0)
            qdoc = dot_nt(jnp.ones((16, HD), jnp.bfloat16), dq)[0:1]
            s = dot_nt(keys[x0:], far_rows(query_refs, g, G, u, rows, 0)) * (SCALE * LOG2E)
            products[2 * u][slot] = jnp.where(docs[x0:] == qdoc, s, MASKED)
            products[2 * u + 1][slot] = dot_nt(values[x0:], far_rows(query_refs, g, G, u, rows, 1))

    far_slots(G, body)


def far_grads(rows, members, query_refs, stat_ref, products, gk, gv):
    G = members
    per = H // TILES
    gk[...], gv[...] = jnp.zeros_like(gk), jnp.zeros_like(gv)

    def body(g, slot):
        for u in range(TILES):
            x0 = u * per * rows
            chunks = per * 2 * rows // HD
            lse, dot = (jnp.concatenate([stat_ref[at + i:at + i + 1] for i in range(chunks)], 1)
                        for at in (8 * g + u * chunks, 8 * g + 4 + u * chunks))
            p = jnp.exp2(products[2 * u][slot] - lse)
            ds = p * (products[2 * u + 1][slot] - dot)
            gk[x0:] += dot_nn(ds.astype(jnp.bfloat16), far_rows(query_refs, g, G, u, rows, 0)) * SCALE
            gv[x0:] += dot_nn(p.astype(jnp.bfloat16), far_rows(query_refs, g, G, u, rows, 1))

    far_slots(G, body)


def sum_kernel(rows, members, *refs):
    G = members
    query_refs, refs = refs[:TILES * G], refs[TILES * G:]
    stat_ref, products, refs = refs[0], refs[1:1 + 2 * TILES], refs[1 + 2 * TILES:]
    own_ref, kv_ref, swap_refs, (out_ref, gk, gv) = refs[0], refs[1], refs[2:G + 1], refs[G + 1:]
    f32, bf16 = jnp.float32, jnp.bfloat16
    far_grads(rows, G, query_refs, stat_ref, products, gk, gv)
    out_ref[:, 0:2 * rows] = own_ref[...]
    out_ref[:, 2 * rows:4 * rows] = swap_refs[G // 2 - 1][:, 0:2 * rows]
    for j in range(H):
        total = kv_ref[j]
        for g, ref in enumerate(swap_refs, 1):
            base = 2 * rows if g == G // 2 else 0
            total = total + ref[j, base:base + 4 * rows].astype(f32)
        mine = slice(j * rows, (j + 1) * rows)
        out_ref[j, 4 * rows:6 * rows] = total[:2 * rows].astype(bf16)
        out_ref[j, 6 * rows:7 * rows] = (total[2 * rows:3 * rows] + gk[mine]).astype(bf16)
        out_ref[j, 7 * rows:8 * rows] = (total[3 * rows:] + gv[mine]).astype(bf16)


def unpack_kernel(r0, rows, members, in_ref, *refs):
    outs, bufs, sem = refs[:4], refs[4:8], refs[8]
    tokens = bufs[0].shape[0]
    bf16 = jnp.bfloat16
    kinds = range(min(H, 2 * r0))
    query_sels = [selector(h, r0, rows, tokens, True, takes_fine(members)) for h in kinds]
    key_sels = [selector(h, r0, rows, tokens, True, True) for h in kinds]
    copies = []
    for i, base in enumerate((0, 1, 4, 5)):
        for h in range(H):
            sels = query_sels if i < 2 else key_sels
            part = jnp.concatenate([in_ref[h, (base + e) * rows:(base + e + 1) * rows] for e in (0, 2)], 0)
            bufs[i][:, h * HD:(h + 1) * HD] = dot_nn(sels[h % (2 * r0)], part).astype(bf16)
        copies.append(pltpu.make_async_copy(bufs[i], outs[i], sem.at[i]))
        copies[-1].start()
    for copy in copies:
        copy.wait()


def call(kernel, out_shape, scratch=(), limit=16, **more):
    return pl.pallas_call(
        kernel,
        out_shape=out_shape,
        scratch_shapes=list(scratch),
        compiler_params=pltpu.CompilerParams(vmem_limit_bytes=limit * 1024 * 1024),
        **more,
    )


def per_device(members, queries, keys, values, cotangent, doc_ids):
    G = members
    tokens = queries.shape[0]
    devices = 2 * H * G
    r0 = tokens * devices // (2 * SEG)
    rows = tokens // (2 * r0)
    bf16, f32 = jnp.bfloat16, jnp.float32
    shape = jax.ShapeDtypeStruct
    n = H * G * rows
    anywhere = pl.BlockSpec(memory_space=pltpu.HBM)
    wide = pltpu.VMEM((tokens, H * HD), bf16)
    message = (H, 8 * rows + DOC_ROWS, HD)

    packed = call(
        functools.partial(pack_kernel, r0, rows, G), shape(message, bf16),
        [wide] * 4 + [pltpu.VMEM((1, tokens), jnp.int32), pltpu.VMEM(message, bf16), pltpu.SemaphoreType.DMA((5 + H,))],
        limit=64, in_specs=[anywhere] * 5, out_specs=anywhere,
    )(queries, keys, values, cotangent, doc_ids.reshape(1, tokens))

    def to_head(x):
        return lax.all_to_all(x, "head", 0, 0, tiled=True)

    def to_member(x, g):
        return lax.ppermute(x, "member", [(i, i ^ g) for i in range(G)])

    def across(x):
        return lax.ppermute(x, "half", [(0, 1), (1, 0)])

    own = to_head(packed)
    queries_here = jnp.where(takes_fine(G), own[:, 2 * rows:4 * rows], own[:, :2 * rows])
    sent_across = jnp.where(lax.axis_index("half") == 0, own[:, 6 * rows:8 * rows], queries_here)
    per = H // TILES

    docs = jnp.pad(own[:, 8 * rows], ((0, DOC_ROWS - H), (0, 0)))
    upper = across(jnp.concatenate([sent_across[per:].reshape(-1, HD), docs], 0))
    lower = across(sent_across[:per].reshape(-1, HD))
    swaps = [to_member(own[:, (2 if g == G // 2 else 4) * rows:], g) for g in range(1, G)]
    nd, lanes = tile_sizes(rows, G)
    nq = TILES * lanes
    tile = [shape(((u + 1) * nd, lanes), f32) for u in range(TILES) for _ in range(2)]
    key_rows = pltpu.VMEM((n, HD), bf16)
    k1, k2, q_all, g_all, stats, out, gtt, *products = call(
        functools.partial(local_kernel, r0, rows, G),
        [shape((n, HD), bf16)] * 2 + [shape((nq, HD), bf16)] * 2 + [shape((8, nq), f32)]
        + [shape((HD, nq), f32)] * 2 + tile * 2,
        [key_rows] * 4, limit=32,
    )(own, *swaps)
    shared = (q_all, g_all, stats, out, gtt, k1, k2)
    upper, k1 = lax.optimization_barrier((upper, k1))
    uppers = [upper] + [to_member(upper, g) for g in range(1, G)]
    tile_rows = pltpu.VMEM((lanes, HD), bf16)
    far_scratch = lambda keys: [pltpu.VMEM((keys, HD), bf16)] * 3
    last = call(
        functools.partial(last_tile_kernel, r0, rows, G),
        [shape((8, HD), f32)] + [shape((lanes, HD), bf16)] * 2 + [shape((n, HD), f32)] * 4,
        far_scratch(nd), limit=32,
    )(*uppers, *shared, *products[2:4], *products[6:8])
    lowers = [lower] + [to_member(lower, g) for g in range(1, G)]
    sent = lambda g: (H, (6 if g == G // 2 else 4) * rows, HD)
    outs = call(
        functools.partial(first_tile_kernel, r0, rows, G),
        [shape((8, HD), f32), shape((H, 2 * rows, HD), bf16), shape((H, 4 * rows, HD), f32)]
        + [shape(sent(g), bf16) for g in range(1, G)],
        [tile_rows] * 2 + [pltpu.VMEM((nd, HD), f32)] * 4 + far_scratch(n), limit=32,
    )(*lowers, *uppers, *shared, *products[0:2], *products[4:6], *last)
    crosses = lowers + uppers
    hops = [to_member(outs[0], g) for g in range(1, G)]
    far_stats = across(jnp.concatenate([outs[0]] + hops, 0))
    products = call(
        functools.partial(far_kernel, r0, rows, G),
        [shape((G // 2, (TILES - u) * nd // G, lanes), f32) for u in range(TILES) for _ in range(2)],
    )(own, *crosses)
    sends, _ = lax.optimization_barrier((list(outs[3:]), hops))
    swaps = [to_member(x, g) for g, x in enumerate(sends, 1)]
    back = call(
        functools.partial(sum_kernel, rows, G), shape((H, 8 * rows, HD), bf16),
        [pltpu.VMEM((H * rows, HD), f32)] * 2,
    )(*crosses, far_stats, *products, outs[1], outs[2], *swaps)
    back = to_head(back)
    return tuple(call(
        functools.partial(unpack_kernel, r0, rows, G), [shape((tokens, H * HD), bf16)] * 4,
        [wide] * 4 + [pltpu.SemaphoreType.DMA((4,))],
        in_specs=[VMEM], out_specs=[anywhere] * 4,
    )(back))


def solution(mesh):
    members = mesh.shape["seq"] // (2 * H)
    parts = {"seq": [("half", 2), ("head", H), ("member", members)]}
    axes = [part for name in mesh.axis_names for part in parts.get(name, [(name, mesh.shape[name])])]
    inner = Mesh(mesh.devices.reshape([size for _, size in axes]), [name for name, _ in axes])
    split = ("dp", "half", "head", "member")
    in_specs = (P(split, None),) * 4 + (P(split),)
    return jax.shard_map(
        functools.partial(per_device, members), mesh=inner, in_specs=in_specs,
        out_specs=(P(split, None),) * 4, check_vma=False,
    )
```

```python
import functools

import jax
import jax.numpy as jnp
import numpy as np
from jax import lax
from jax.experimental import pallas as pl
from jax.experimental.pallas import tpu as pltpu
from jax.sharding import Mesh
from jax.sharding import PartitionSpec as P

H = 8
HD = 128
SEG = 1024

MASKED = -1e30
SCALE = HD ** -0.5
LOG2E = float(np.log2(np.e))
VMEM = pl.BlockSpec(memory_space=pltpu.VMEM)
DOC_ROWS = 16


def dot_nn(a, b):
    return lax.dot_general(a, b, (((1,), (0,)), ((), ())), preferred_element_type=jnp.float32)


def dot_nt(a, b):
    return lax.dot_general(a, b, (((1,), (1,)), ((), ())), preferred_element_type=jnp.float32)


def selector(head, r0, rows, tokens, transposed, fine_first=False):
    r1 = 2 * r0
    shape = (tokens, 2 * rows) if transposed else (2 * rows, tokens)
    k = lax.broadcasted_iota(jnp.int32, shape, 1 if transposed else 0)
    p = lax.broadcasted_iota(jnp.int32, shape, 0 if transposed else 1)
    coarse = head % r1
    other = (coarse + r0) % r1
    first, second = jnp.where(fine_first, other, coarse), jnp.where(fine_first, coarse, other)
    target = jnp.where(k < rows, r1 * k + first, r1 * (k - rows) + second)
    return (p == target).astype(jnp.float32).astype(jnp.bfloat16)


def takes_fine(members):
    return lax.axis_index("member") >= members // 2


def pack_kernel(r0, rows, members, q_in, k_in, v_in, g_in, doc_in, out, q_ref, k_ref, v_ref, g_ref, doc_ref, buf, sem):
    tokens = q_ref.shape[0]
    pairs = ((doc_in, doc_ref), (k_in, k_ref), (v_in, v_ref), (q_in, q_ref), (g_in, g_ref))
    copies = [pltpu.make_async_copy(src, dst, sem.at[i]) for i, (src, dst) in enumerate(pairs)]
    for copy in copies:
        copy.start()
    kinds = range(min(H, 2 * r0))
    key_sels = [selector(h, r0, rows, tokens, False) for h in kinds]
    query_sels = [selector(h, r0, rows, tokens, False, takes_fine(members)) for h in kinds]

    def pick(sels, h, ref):
        return dot_nn(sels[h % (2 * r0)], ref[:, h * HD:(h + 1) * HD]).astype(jnp.bfloat16)

    for copy in copies:
        copy.wait()
    docs = jnp.broadcast_to(doc_ref[...].astype(jnp.float32).astype(jnp.bfloat16), (DOC_ROWS, tokens))
    sends = []
    for h in range(H):
        for i, ref in enumerate((q_ref, g_ref)):
            x = pick(query_sels, h, ref)
            buf[h, i * rows:(1 + i) * rows] = x[:rows]
            buf[h, (2 + i) * rows:(3 + i) * rows] = x[rows:]
        for i, ref in enumerate((k_ref, v_ref)):
            x = pick(key_sels, h, ref)
            buf[h, (4 + i) * rows:(5 + i) * rows] = x[rows:]
            buf[h, (6 + i) * rows:(7 + i) * rows] = x[:rows]
        buf[h, 8 * rows:8 * rows + DOC_ROWS] = docs
        sends.append(pltpu.make_async_copy(buf.at[h], out.at[h], sem.at[5 + h]))
        sends[-1].start()
    for copy in sends:
        copy.wait()


TILES = 2


def tile_sizes(rows, members):
    per = H // TILES
    return per * members * rows, per * 2 * rows


def eye_matrix():
    shape = (HD, HD)
    same = lax.broadcasted_iota(jnp.int32, shape, 0) == lax.broadcasted_iota(jnp.int32, shape, 1)
    return same.astype(jnp.float32).astype(jnp.bfloat16)


def doc_cols(x):
    return dot_nn(x, jnp.ones((HD, HD), jnp.bfloat16))[:, 0:1]


def local_kernel(r0, rows, members, *refs):
    G = members
    r1 = 2 * r0
    own_ref, swap_refs = refs[0], refs[1:G]
    (k1, k2, q_all, g_all, stats, out_ref, gtt_ref), rest = refs[G:G + 7], refs[G + 7:]
    p_refs, dp_refs, (v1, v2, d1, d2) = rest[:2 * TILES], rest[2 * TILES:4 * TILES], rest[4 * TILES:]
    bf16, f32 = jnp.bfloat16, jnp.float32
    tokens = HD
    head = lax.axis_index("head")
    member = lax.axis_index("member")
    fine = takes_fine(G)
    partner = G // 2
    partner_ref = swap_refs[partner - 1]

    sel = selector(head, r0, rows, tokens, False)
    query_sel = jnp.where(fine, sel[rows:].astype(f32), sel[:rows].astype(f32)).astype(bf16)
    source_docs = []
    for j in range(H):
        for g in range(G):
            at = pl.ds((j * G + g) * rows, rows)
            ref, base = (own_ref, 4 * rows) if g == 0 else (swap_refs[g - 1], 2 * rows if g == partner else 0)
            k2[at] = ref[j, base:base + rows]
            v2[at] = ref[j, base + rows:base + 2 * rows]
            k1[at] = ref[j, base + 2 * rows:base + 3 * rows]
            v1[at] = ref[j, base + 3 * rows:base + 4 * rows]
            doc = ref[j, base + 4 * rows:base + 4 * rows + DOC_ROWS][0:1]
            if g in (0, partner):
                source_docs.append(doc)
            d1[at] = sel[:rows] * doc
            d2[at] = sel[rows:] * doc

    eye = eye_matrix()
    v1t, v2t = dot_nt(eye, v1[...]).astype(bf16), dot_nt(eye, v2[...]).astype(bf16)
    docs1, docs2 = doc_cols(d1[...]), doc_cols(d2[...])
    nd, lanes = tile_sizes(rows, G)
    per = H // TILES

    coarse = head % r1
    other = (coarse + r0) % r1
    lane = lax.broadcasted_iota(jnp.int32, (1, lanes), 1)
    qmember = member ^ (partner * ((lane // rows) % 2))
    qpos = (lane // (2 * rows)) * (G * tokens) + qmember * tokens + r1 * (lane % rows) + jnp.where(fine, other, coarse)
    kl = lax.broadcasted_iota(jnp.int32, (nd, 1), 0)
    kmember = member ^ ((kl // rows) % G)
    kpos = (kl // (rows * G)) * (G * tokens) + kmember * tokens + r1 * (kl % rows)
    causal1 = kpos + coarse <= qpos
    causal2 = kpos + other <= qpos
    both = jnp.where(fine, 0.0, 1.0)
    c = SCALE * LOG2E

    for u in range(TILES):
        nk = (u + 1) * nd
        x0 = u * nd
        src = range(u * per, (u + 1) * per)
        mine = slice(u * lanes, (u + 1) * lanes)
        gather = lambda lo: jnp.concatenate([ref[j, lo:lo + rows] for j in src for ref in (own_ref, partner_ref)], 0)
        qt, gt = gather(0), gather(rows)
        q_all[mine], g_all[mine] = qt, gt
        dq = jnp.concatenate([query_sel * source_docs[2 * j + e] for j in src for e in range(2)], 0)
        qdoc = dot_nt(jnp.ones((16, HD), bf16), dq)[0:1]

        def scores(key, docs, causal):
            s = jnp.where(docs == qdoc, dot_nt(key, qt), MASKED)
            if u:
                return jnp.concatenate([s[:x0], jnp.where(causal, s[x0:], MASKED)], 0)
            return jnp.where(causal, s, MASKED)

        s1 = scores(k1[0:nk], docs1[0:nk], causal1)
        s2 = scores(k2[0:nk], docs2[0:nk], causal2)
        top = jnp.maximum(jnp.max(s1, 0, keepdims=True), jnp.max(s2, 0, keepdims=True))
        base = top * c
        p1 = jnp.exp2(s1 * c - (base - both))
        p2 = jnp.exp2(s2 * c - base)
        stats[0:1, mine] = top
        stats[1:2, mine] = jnp.sum(p1, 0, keepdims=True) + jnp.sum(p2, 0, keepdims=True)
        stats[2:3, mine] = qdoc
        out_ref[:, mine] = dot_nn(v1t[:, :nk], p1.astype(bf16)) + dot_nn(v2t[:, :nk], p2.astype(bf16))
        gtt_ref[:, mine] = dot_nt(eye, gt)
        p_refs[2 * u][...], p_refs[2 * u + 1][...] = p1, p2
        dp_refs[2 * u][...], dp_refs[2 * u + 1][...] = dot_nt(v1[0:nk], gt), dot_nt(v2[0:nk], gt)


def finish_tile(u, r0, rows, members, parts, shared, products, results):
    far = (lax.axis_index("half") == 1) & jnp.logical_not(takes_fine(members))
    for branch, with_far in ((far, True), (jnp.logical_not(far), False)):
        pl.when(branch)(functools.partial(
            tile_body, u, r0, rows, members, with_far, parts, shared, products, results))


def tile_body(u, r0, rows, members, with_far, parts, shared, products, results):
    G = members
    q_all, g_all, stats, local_out, gtt_ref, k1, k2 = shared
    far_stats, att, gq_ref, sums = results[0], results[1], results[2], results[3:]
    bf16 = jnp.bfloat16
    per = H // TILES
    eye = eye_matrix()
    nd, lanes = tile_sizes(rows, G)
    nk = (u + 1) * nd
    mine = slice(u * lanes, (u + 1) * lanes)
    c = SCALE * LOG2E
    qt, gt = q_all[mine], g_all[mine]
    top, total, out = stats[0:1, mine], stats[1:2, mine], local_out[:, mine]
    if with_far:
        sel = selector(lax.axis_index("head"), r0, rows, HD, False)
        size = per * rows
        keys_x, values_x = (jnp.concatenate([ref[lo:lo + size] for part in parts for ref in part], 0) for lo in (0, size))
        first = TILES - len(parts)
        docs_x = jnp.concatenate([sel[:rows] * ref[2 * size:2 * size + DOC_ROWS][source:source + 1]
                                  for p in range(first, TILES) for ref in parts[-1]
                                  for source in range(p * per, (p + 1) * per)], 0)
        kxt, vxt = dot_nt(eye, keys_x).astype(bf16), dot_nt(eye, values_x).astype(bf16)
        sx = jnp.where(doc_cols(docs_x) == stats[2:3, mine], dot_nt(keys_x, qt), MASKED)
        local_top = top
        top = jnp.maximum(local_top, jnp.max(sx, 0, keepdims=True))
        px = jnp.exp2(sx * c - top * c)
        shrink = jnp.exp2(local_top * c - top * c)
        total = total * shrink + jnp.sum(px, 0, keepdims=True)
        inv = 1.0 / total
        local_inv = shrink * inv
        out = out * local_inv + dot_nn(vxt, px.astype(bf16)) * inv
    else:
        local_inv = 1.0 / total
        out = out * local_inv
    dot = jnp.sum(gtt_ref[:, mine] * out, 0, keepdims=True)
    lse = top * c + jnp.log(total) * LOG2E
    chunks = lanes // HD
    for i in range(chunks):
        far_stats[u * chunks + i:u * chunks + i + 1] = lse[:, i * HD:(i + 1) * HD]
        far_stats[4 + u * chunks + i:5 + u * chunks + i] = dot[:, i * HD:(i + 1) * HD]
    att[...] = out.T.astype(bf16)
    gq = 0.0
    if with_far:
        ds = (px * inv * (dot_nt(values_x, gt) - dot)).astype(bf16)
        gq = dot_nn(kxt, ds)
    for i, k in enumerate((k1, k2)):
        w = products[i][...] * local_inv
        ds = (w * (products[2 + i][...] - dot)).astype(bf16)
        gq = gq + dot_nn(dot_nt(eye, k[0:nk]).astype(bf16), ds)
        sums[i][...] = dot_nn(ds, qt)
        sums[2 + i][...] = dot_nn(w.astype(bf16), gt)
    gq_ref[...] = (gq * SCALE).T.astype(bf16)


def last_tile_kernel(r0, rows, members, *refs):
    G = members
    finish_tile(1, r0, rows, G, [refs[:G]], refs[G:G + 7], refs[G + 7:G + 11], refs[G + 11:G + 18])


def first_tile_kernel(r0, rows, members, *refs):
    G = members
    parts, refs = [refs[:G], refs[G:2 * G]], refs[2 * G:]
    shared, products, last, refs = refs[:7], refs[7:11], refs[11:18], refs[18:]
    far_stats, out_own, out_kv, out_swap, scratch = refs[0], refs[1], refs[2], refs[3:G + 2], refs[G + 2:]
    nd, lanes = tile_sizes(rows, G)
    first = (far_stats,) + tuple(scratch[:6])
    far_stats[...] = last[0][...]
    finish_tile(0, r0, rows, G, parts, shared, products, first)
    partner, per = G // 2, H // TILES
    for j in range(H):
        att, gq = (first, last)[j // per][1:3]
        for e, ref in enumerate((out_own, out_swap[partner - 1])):
            lo = (2 * (j % per) + e) * rows
            ref[j, 0:rows] = att[lo:lo + rows]
            ref[j, rows:2 * rows] = gq[lo:lo + rows]
        for g in range(G):
            at = pl.ds((j * G + g) * rows, rows)
            gk1, gk2, gv1, gv2 = (last[3 + i][at] + first[3 + i][at] if j < per else last[3 + i][at] for i in range(4))
            ref = out_kv if g == 0 else out_swap[g - 1]
            base = 2 if g == partner else 0
            for i, part in enumerate((gk2 * SCALE, gv2, gk1 * SCALE, gv1), base):
                ref[j, i * rows:(i + 1) * rows] = part.astype(ref.dtype)


def far_rows(query_refs, g, members, u, rows, lo):
    size = H // TILES * rows
    pair = (query_refs[u * members + g], query_refs[u * members + (g ^ (members // 2))])
    return jnp.concatenate([ref[at:at + rows] for at in range(lo * size, (lo + 1) * size, rows) for ref in pair], 0)


def far_slots(members, body):
    for g in range(members):
        slot = lax.axis_index("member") ^ g

        @pl.when((lax.axis_index("half") == 0) & (slot < members // 2))
        def _(g=g, slot=slot):
            body(g, slot)


def far_kernel(r0, rows, members, own_ref, *refs):
    G = members
    query_refs, products = refs[:TILES * G], refs[TILES * G:]
    sel = selector(lax.axis_index("head"), r0, rows, HD, False)[:rows]
    per = H // TILES
    keys, values = (jnp.concatenate([own_ref[j, lo * rows:(lo + 1) * rows] for j in range(H)], 0) for lo in (6, 7))
    docs = doc_cols(jnp.concatenate([sel * own_ref[j, 8 * rows:8 * rows + DOC_ROWS][0:1] for j in range(H)], 0))

    def body(g, slot):
        for u in range(TILES):
            x0 = u * per * rows
            pair = (query_refs[G + g], query_refs[G + (g ^ (G // 2))])
            dq = jnp.concatenate([sel * ref[2 * per * rows:2 * per * rows + DOC_ROWS][j:j + 1]
                                  for j in range(u * per, (u + 1) * per) for ref in pair], 0)
            qdoc = dot_nt(jnp.ones((16, HD), jnp.bfloat16), dq)[0:1]
            s = dot_nt(keys[x0:], far_rows(query_refs, g, G, u, rows, 0)) * (SCALE * LOG2E)
            products[2 * u][slot] = jnp.where(docs[x0:] == qdoc, s, MASKED)
            products[2 * u + 1][slot] = dot_nt(values[x0:], far_rows(query_refs, g, G, u, rows, 1))

    far_slots(G, body)


def far_grads(rows, members, query_refs, stat_ref, products, gk, gv):
    G = members
    per = H // TILES
    gk[...], gv[...] = jnp.zeros_like(gk), jnp.zeros_like(gv)

    def body(g, slot):
        for u in range(TILES):
            x0 = u * per * rows
            chunks = per * 2 * rows // HD
            lse, dot = (jnp.concatenate([stat_ref[at + i:at + i + 1] for i in range(chunks)], 1)
                        for at in (8 * g + u * chunks, 8 * g + 4 + u * chunks))
            p = jnp.exp2(products[2 * u][slot] - lse)
            ds = p * (products[2 * u + 1][slot] - dot)
            gk[x0:] += dot_nn(ds.astype(jnp.bfloat16), far_rows(query_refs, g, G, u, rows, 0)) * SCALE
            gv[x0:] += dot_nn(p.astype(jnp.bfloat16), far_rows(query_refs, g, G, u, rows, 1))

    far_slots(G, body)


def sum_kernel(rows, members, *refs):
    G = members
    query_refs, refs = refs[:TILES * G], refs[TILES * G:]
    stat_ref, products, refs = refs[0], refs[1:1 + 2 * TILES], refs[1 + 2 * TILES:]
    own_ref, kv_ref, swap_refs, (out_ref, gk, gv) = refs[0], refs[1], refs[2:G + 1], refs[G + 1:]
    f32, bf16 = jnp.float32, jnp.bfloat16
    far_grads(rows, G, query_refs, stat_ref, products, gk, gv)
    out_ref[:, 0:2 * rows] = own_ref[...]
    out_ref[:, 2 * rows:4 * rows] = swap_refs[G // 2 - 1][:, 0:2 * rows]
    for j in range(H):
        total = kv_ref[j]
        for g, ref in enumerate(swap_refs, 1):
            base = 2 * rows if g == G // 2 else 0
            total = total + ref[j, base:base + 4 * rows].astype(f32)
        mine = slice(j * rows, (j + 1) * rows)
        out_ref[j, 4 * rows:6 * rows] = total[:2 * rows].astype(bf16)
        out_ref[j, 6 * rows:7 * rows] = (total[2 * rows:3 * rows] + gk[mine]).astype(bf16)
        out_ref[j, 7 * rows:8 * rows] = (total[3 * rows:] + gv[mine]).astype(bf16)


def unpack_kernel(r0, rows, members, in_ref, *refs):
    outs, bufs, sem = refs[:4], refs[4:8], refs[8]
    tokens = bufs[0].shape[0]
    bf16 = jnp.bfloat16
    kinds = range(min(H, 2 * r0))
    query_sels = [selector(h, r0, rows, tokens, True, takes_fine(members)) for h in kinds]
    key_sels = [selector(h, r0, rows, tokens, True, True) for h in kinds]
    copies = []
    for i, base in enumerate((0, 1, 4, 5)):
        for h in range(H):
            sels = query_sels if i < 2 else key_sels
            part = jnp.concatenate([in_ref[h, (base + e) * rows:(base + e + 1) * rows] for e in (0, 2)], 0)
            bufs[i][:, h * HD:(h + 1) * HD] = dot_nn(sels[h % (2 * r0)], part).astype(bf16)
        copies.append(pltpu.make_async_copy(bufs[i], outs[i], sem.at[i]))
        copies[-1].start()
    for copy in copies:
        copy.wait()


def call(kernel, out_shape, scratch=(), limit=16, **more):
    return pl.pallas_call(
        kernel,
        out_shape=out_shape,
        scratch_shapes=list(scratch),
        compiler_params=pltpu.CompilerParams(vmem_limit_bytes=limit * 1024 * 1024),
        **more,
    )


def per_device(members, queries, keys, values, cotangent, doc_ids):
    G = members
    tokens = queries.shape[0]
    devices = 2 * H * G
    r0 = tokens * devices // (2 * SEG)
    rows = tokens // (2 * r0)
    bf16, f32 = jnp.bfloat16, jnp.float32
    shape = jax.ShapeDtypeStruct
    n = H * G * rows
    anywhere = pl.BlockSpec(memory_space=pltpu.HBM)
    wide = pltpu.VMEM((tokens, H * HD), bf16)
    message = (H, 8 * rows + DOC_ROWS, HD)

    packed = call(
        functools.partial(pack_kernel, r0, rows, G), shape(message, bf16),
        [wide] * 4 + [pltpu.VMEM((1, tokens), jnp.int32), pltpu.VMEM(message, bf16), pltpu.SemaphoreType.DMA((5 + H,))],
        limit=64, in_specs=[anywhere] * 5, out_specs=anywhere,
    )(queries, keys, values, cotangent, doc_ids.reshape(1, tokens))

    def to_head(x):
        return lax.all_to_all(x, "head", 0, 0, tiled=True)

    def to_member(x, g):
        return lax.ppermute(x, "member", [(i, i ^ g) for i in range(G)])

    def across(x):
        return lax.ppermute(x, "half", [(0, 1), (1, 0)])

    own = to_head(packed)
    queries_here = jnp.where(takes_fine(G), own[:, 2 * rows:4 * rows], own[:, :2 * rows])
    sent_across = jnp.where(lax.axis_index("half") == 0, own[:, 6 * rows:8 * rows], queries_here)
    per = H // TILES

    docs = jnp.pad(own[:, 8 * rows], ((0, DOC_ROWS - H), (0, 0)))
    def part(at):
        return [sent_across[at, lo * rows:(lo + 1) * rows].reshape(-1, HD) for lo in range(2)]

    upper = across(jnp.concatenate(part(slice(per, H)) + [docs], 0))
    lower = across(jnp.concatenate(part(slice(0, per)), 0))
    swaps = [to_member(own[:, (2 if g == G // 2 else 4) * rows:], g) for g in range(1, G)]
    nd, lanes = tile_sizes(rows, G)
    nq = TILES * lanes
    tile = [shape(((u + 1) * nd, lanes), f32) for u in range(TILES) for _ in range(2)]
    key_rows = pltpu.VMEM((n, HD), bf16)
    k1, k2, q_all, g_all, stats, out, gtt, *products = call(
        functools.partial(local_kernel, r0, rows, G),
        [shape((n, HD), bf16)] * 2 + [shape((nq, HD), bf16)] * 2 + [shape((8, nq), f32)]
        + [shape((HD, nq), f32)] * 2 + tile * 2,
        [key_rows] * 4, limit=32,
    )(own, *swaps)
    shared = (q_all, g_all, stats, out, gtt, k1, k2)
    upper, k1 = lax.optimization_barrier((upper, k1))
    uppers = [upper] + [to_member(upper, g) for g in range(1, G)]
    tile_rows = pltpu.VMEM((lanes, HD), bf16)
    last = call(
        functools.partial(last_tile_kernel, r0, rows, G),
        [shape((8, HD), f32)] + [shape((lanes, HD), bf16)] * 2 + [shape((n, HD), f32)] * 4,
        limit=32,
    )(*uppers, *shared, *products[2:4], *products[6:8])
    lowers = [lower] + [to_member(lower, g) for g in range(1, G)]
    sent = lambda g: (H, (6 if g == G // 2 else 4) * rows, HD)
    outs = call(
        functools.partial(first_tile_kernel, r0, rows, G),
        [shape((8, HD), f32), shape((H, 2 * rows, HD), bf16), shape((H, 4 * rows, HD), f32)]
        + [shape(sent(g), bf16) for g in range(1, G)],
        [tile_rows] * 2 + [pltpu.VMEM((nd, HD), f32)] * 4, limit=32,
    )(*lowers, *uppers, *shared, *products[0:2], *products[4:6], *last)
    crosses = lowers + uppers
    hops = [to_member(outs[0], g) for g in range(1, G)]
    far_stats = across(jnp.concatenate([outs[0]] + hops, 0))
    products = call(
        functools.partial(far_kernel, r0, rows, G),
        [shape((G // 2, (TILES - u) * nd // G, lanes), f32) for u in range(TILES) for _ in range(2)],
    )(own, *crosses)
    sends, _ = lax.optimization_barrier((list(outs[3:]), hops))
    swaps = [to_member(x, g) for g, x in enumerate(sends, 1)]
    back = call(
        functools.partial(sum_kernel, rows, G), shape((H, 8 * rows, HD), bf16),
        [pltpu.VMEM((H * rows, HD), f32)] * 2,
    )(*crosses, far_stats, *products, outs[1], outs[2], *swaps)
    back = to_head(back)
    return tuple(call(
        functools.partial(unpack_kernel, r0, rows, G), [shape((tokens, H * HD), bf16)] * 4,
        [wide] * 4 + [pltpu.SemaphoreType.DMA((4,))],
        in_specs=[VMEM], out_specs=[anywhere] * 4,
    )(back))


def solution(mesh):
    members = mesh.shape["seq"] // (2 * H)
    parts = {"seq": [("half", 2), ("head", H), ("member", members)]}
    axes = [part for name in mesh.axis_names for part in parts.get(name, [(name, mesh.shape[name])])]
    inner = Mesh(mesh.devices.reshape([size for _, size in axes]), [name for name, _ in axes])
    split = ("dp", "half", "head", "member")
    in_specs = (P(split, None),) * 4 + (P(split),)
    return jax.shard_map(
        functools.partial(per_device, members), mesh=inner, in_specs=in_specs,
        out_specs=(P(split, None),) * 4, check_vma=False,
    )
```

```python
import functools

import jax
import jax.numpy as jnp
import numpy as np
from jax import lax
from jax.experimental import pallas as pl
from jax.experimental.pallas import tpu as pltpu
from jax.sharding import Mesh
from jax.sharding import PartitionSpec as P

H = 8
HD = 128
SEG = 1024

MASKED = -1e30
SCALE = HD ** -0.5
LOG2E = float(np.log2(np.e))
VMEM = pl.BlockSpec(memory_space=pltpu.VMEM)
DOC_ROWS = 16


def dot_nn(a, b):
    return lax.dot_general(a, b, (((1,), (0,)), ((), ())), preferred_element_type=jnp.float32)


def dot_nt(a, b):
    return lax.dot_general(a, b, (((1,), (1,)), ((), ())), preferred_element_type=jnp.float32)


def selector(head, r0, rows, tokens, transposed, fine_first=False):
    r1 = 2 * r0
    shape = (tokens, 2 * rows) if transposed else (2 * rows, tokens)
    k = lax.broadcasted_iota(jnp.int32, shape, 1 if transposed else 0)
    p = lax.broadcasted_iota(jnp.int32, shape, 0 if transposed else 1)
    coarse = head % r1
    other = (coarse + r0) % r1
    first, second = jnp.where(fine_first, other, coarse), jnp.where(fine_first, coarse, other)
    target = jnp.where(k < rows, r1 * k + first, r1 * (k - rows) + second)
    return (p == target).astype(jnp.float32).astype(jnp.bfloat16)


def takes_fine(members):
    return lax.axis_index("member") >= members // 2


def pack_kernel(r0, rows, members, q_in, k_in, v_in, g_in, doc_in, out, q_ref, k_ref, v_ref, g_ref, doc_ref, buf, sem):
    tokens = q_ref.shape[0]
    pairs = ((doc_in, doc_ref), (k_in, k_ref), (v_in, v_ref), (q_in, q_ref), (g_in, g_ref))
    copies = [pltpu.make_async_copy(src, dst, sem.at[i]) for i, (src, dst) in enumerate(pairs)]
    for copy in copies:
        copy.start()
    kinds = range(min(H, 2 * r0))
    key_sels = [selector(h, r0, rows, tokens, False) for h in kinds]
    query_sels = [selector(h, r0, rows, tokens, False, takes_fine(members)) for h in kinds]

    def pick(sels, h, ref):
        return dot_nn(sels[h % (2 * r0)], ref[:, h * HD:(h + 1) * HD]).astype(jnp.bfloat16)

    for copy in copies:
        copy.wait()
    docs = jnp.broadcast_to(doc_ref[...].astype(jnp.float32).astype(jnp.bfloat16), (DOC_ROWS, tokens))
    sends = []
    for h in range(H):
        for i, ref in enumerate((q_ref, g_ref)):
            x = pick(query_sels, h, ref)
            buf[h, i * rows:(1 + i) * rows] = x[:rows]
            buf[h, (2 + i) * rows:(3 + i) * rows] = x[rows:]
        for i, ref in enumerate((k_ref, v_ref)):
            x = pick(key_sels, h, ref)
            buf[h, (4 + i) * rows:(5 + i) * rows] = x[rows:]
            buf[h, (6 + i) * rows:(7 + i) * rows] = x[:rows]
        buf[h, 8 * rows:8 * rows + DOC_ROWS] = docs
        sends.append(pltpu.make_async_copy(buf.at[h], out.at[h], sem.at[5 + h]))
        sends[-1].start()
    for copy in sends:
        copy.wait()


TILES = 2


def tile_sizes(rows, members):
    per = H // TILES
    return per * members * rows, per * 2 * rows


def eye_matrix():
    shape = (HD, HD)
    same = lax.broadcasted_iota(jnp.int32, shape, 0) == lax.broadcasted_iota(jnp.int32, shape, 1)
    return same.astype(jnp.float32).astype(jnp.bfloat16)


def doc_cols(x):
    return dot_nn(x, jnp.ones((HD, HD), jnp.bfloat16))[:, 0:1]


def local_kernel(r0, rows, members, *refs):
    G = members
    r1 = 2 * r0
    own_ref, swap_refs = refs[0], refs[1:G]
    (k1t, k2t, q_all, g_all, stats, out_ref, gtt_ref), rest = refs[G:G + 7], refs[G + 7:]
    p_refs, dp_refs, (v1, v2, d1, d2, k1, k2) = rest[:2 * TILES], rest[2 * TILES:4 * TILES], rest[4 * TILES:]
    bf16, f32 = jnp.bfloat16, jnp.float32
    tokens = HD
    head = lax.axis_index("head")
    member = lax.axis_index("member")
    fine = takes_fine(G)
    partner = G // 2
    partner_ref = swap_refs[partner - 1]

    sel = selector(head, r0, rows, tokens, False)
    query_sel = jnp.where(fine, sel[rows:].astype(f32), sel[:rows].astype(f32)).astype(bf16)
    source_docs = []
    for j in range(H):
        for g in range(G):
            at = pl.ds((j * G + g) * rows, rows)
            ref, base = (own_ref, 4 * rows) if g == 0 else (swap_refs[g - 1], 2 * rows if g == partner else 0)
            k2[at] = ref[j, base:base + rows]
            v2[at] = ref[j, base + rows:base + 2 * rows]
            k1[at] = ref[j, base + 2 * rows:base + 3 * rows]
            v1[at] = ref[j, base + 3 * rows:base + 4 * rows]
            doc = ref[j, base + 4 * rows:base + 4 * rows + DOC_ROWS][0:1]
            if g in (0, partner):
                source_docs.append(doc)
            d1[at] = sel[:rows] * doc
            d2[at] = sel[rows:] * doc

    eye = eye_matrix()
    k1t[...], k2t[...] = dot_nt(eye, k1[...]).astype(bf16), dot_nt(eye, k2[...]).astype(bf16)
    v1t, v2t = dot_nt(eye, v1[...]).astype(bf16), dot_nt(eye, v2[...]).astype(bf16)
    docs1, docs2 = doc_cols(d1[...]), doc_cols(d2[...])
    nd, lanes = tile_sizes(rows, G)
    per = H // TILES

    coarse = head % r1
    other = (coarse + r0) % r1
    lane = lax.broadcasted_iota(jnp.int32, (1, lanes), 1)
    qmember = member ^ (partner * ((lane // rows) % 2))
    qpos = (lane // (2 * rows)) * (G * tokens) + qmember * tokens + r1 * (lane % rows) + jnp.where(fine, other, coarse)
    kl = lax.broadcasted_iota(jnp.int32, (nd, 1), 0)
    kmember = member ^ ((kl // rows) % G)
    kpos = (kl // (rows * G)) * (G * tokens) + kmember * tokens + r1 * (kl % rows)
    causal1 = kpos + coarse <= qpos
    causal2 = kpos + other <= qpos
    both = jnp.where(fine, 0.0, 1.0)
    c = SCALE * LOG2E

    for u in range(TILES):
        nk = (u + 1) * nd
        x0 = u * nd
        src = range(u * per, (u + 1) * per)
        mine = slice(u * lanes, (u + 1) * lanes)
        gather = lambda lo: jnp.concatenate([ref[j, lo:lo + rows] for j in src for ref in (own_ref, partner_ref)], 0)
        qt, gt = gather(0), gather(rows)
        q_all[mine], g_all[mine] = qt, gt
        dq = jnp.concatenate([query_sel * source_docs[2 * j + e] for j in src for e in range(2)], 0)
        qdoc = dot_nt(jnp.ones((16, HD), bf16), dq)[0:1]

        def scores(key, docs, causal):
            s = jnp.where(docs == qdoc, dot_nt(key, qt), MASKED)
            if u:
                return jnp.concatenate([s[:x0], jnp.where(causal, s[x0:], MASKED)], 0)
            return jnp.where(causal, s, MASKED)

        s1 = scores(k1[0:nk], docs1[0:nk], causal1)
        s2 = scores(k2[0:nk], docs2[0:nk], causal2)
        top = jnp.maximum(jnp.max(s1, 0, keepdims=True), jnp.max(s2, 0, keepdims=True))
        base = top * c
        p1 = jnp.exp2(s1 * c - (base - both))
        p2 = jnp.exp2(s2 * c - base)
        stats[0:1, mine] = top
        stats[1:2, mine] = jnp.sum(p1, 0, keepdims=True) + jnp.sum(p2, 0, keepdims=True)
        stats[2:3, mine] = qdoc
        out_ref[:, mine] = dot_nn(v1t[:, :nk], p1.astype(bf16)) + dot_nn(v2t[:, :nk], p2.astype(bf16))
        gtt_ref[:, mine] = dot_nt(eye, gt)
        p_refs[2 * u][...], p_refs[2 * u + 1][...] = p1, p2
        dp_refs[2 * u][...], dp_refs[2 * u + 1][...] = dot_nt(v1[0:nk], gt), dot_nt(v2[0:nk], gt)


def finish_tile(u, r0, rows, members, parts, shared, products, results):
    far = (lax.axis_index("half") == 1) & jnp.logical_not(takes_fine(members))
    for branch, with_far in ((far, True), (jnp.logical_not(far), False)):
        pl.when(branch)(functools.partial(
            tile_body, u, r0, rows, members, with_far, parts, shared, products, results))


def tile_body(u, r0, rows, members, with_far, parts, shared, products, results):
    G = members
    q_all, g_all, stats, local_out, gtt_ref, k1, k2 = shared
    far_stats, att, gq_ref, sums = results[0], results[1], results[2], results[3:]
    bf16 = jnp.bfloat16
    per = H // TILES
    eye = eye_matrix()
    nd, lanes = tile_sizes(rows, G)
    nk = (u + 1) * nd
    mine = slice(u * lanes, (u + 1) * lanes)
    c = SCALE * LOG2E
    qt, gt = q_all[mine], g_all[mine]
    top, total, out = stats[0:1, mine], stats[1:2, mine], local_out[:, mine]
    if with_far:
        sel = selector(lax.axis_index("head"), r0, rows, HD, False)
        size = per * rows
        keys_x, values_x = (jnp.concatenate([ref[lo:lo + size] for part in parts for ref in part], 0) for lo in (0, size))
        first = TILES - len(parts)
        docs_x = jnp.concatenate([sel[:rows] * ref[2 * size:2 * size + DOC_ROWS][source:source + 1]
                                  for p in range(first, TILES) for ref in parts[-1]
                                  for source in range(p * per, (p + 1) * per)], 0)
        kxt, vxt = dot_nt(eye, keys_x).astype(bf16), dot_nt(eye, values_x).astype(bf16)
        sx = jnp.where(doc_cols(docs_x) == stats[2:3, mine], dot_nt(keys_x, qt), MASKED)
        local_top = top
        top = jnp.maximum(local_top, jnp.max(sx, 0, keepdims=True))
        px = jnp.exp2(sx * c - top * c)
        shrink = jnp.exp2(local_top * c - top * c)
        total = total * shrink + jnp.sum(px, 0, keepdims=True)
        inv = 1.0 / total
        local_inv = shrink * inv
        out = out * local_inv + dot_nn(vxt, px.astype(bf16)) * inv
    else:
        local_inv = 1.0 / total
        out = out * local_inv
    dot = jnp.sum(gtt_ref[:, mine] * out, 0, keepdims=True)
    lse = top * c + jnp.log(total) * LOG2E
    chunks = lanes // HD
    for i in range(chunks):
        far_stats[u * chunks + i:u * chunks + i + 1] = lse[:, i * HD:(i + 1) * HD]
        far_stats[4 + u * chunks + i:5 + u * chunks + i] = dot[:, i * HD:(i + 1) * HD]
    att[...] = out.T.astype(bf16)
    gq = 0.0
    if with_far:
        ds = (px * inv * (dot_nt(values_x, gt) - dot)).astype(bf16)
        gq = dot_nn(kxt, ds)
    for i, k in enumerate((k1, k2)):
        w = products[i][...] * local_inv
        ds = (w * (products[2 + i][...] - dot)).astype(bf16)
        gq = gq + dot_nn(k[:, 0:nk], ds)
        sums[i][...] = dot_nn(ds, qt)
        sums[2 + i][...] = dot_nn(w.astype(bf16), gt)
    gq_ref[...] = (gq * SCALE).T.astype(bf16)


def last_tile_kernel(r0, rows, members, *refs):
    G = members
    finish_tile(1, r0, rows, G, [refs[:G]], refs[G:G + 7], refs[G + 7:G + 11], refs[G + 11:G + 18])


def first_tile_kernel(r0, rows, members, *refs):
    G = members
    parts, refs = [refs[:G], refs[G:2 * G]], refs[2 * G:]
    shared, products, last, refs = refs[:7], refs[7:11], refs[11:18], refs[18:]
    far_stats, out_own, out_kv, out_swap, scratch = refs[0], refs[1], refs[2], refs[3:G + 2], refs[G + 2:]
    nd, lanes = tile_sizes(rows, G)
    first = (far_stats,) + tuple(scratch[:6])
    far_stats[...] = last[0][...]
    finish_tile(0, r0, rows, G, parts, shared, products, first)
    partner, per = G // 2, H // TILES
    for j in range(H):
        att, gq = (first, last)[j // per][1:3]
        for e, ref in enumerate((out_own, out_swap[partner - 1])):
            lo = (2 * (j % per) + e) * rows
            ref[j, 0:rows] = att[lo:lo + rows]
            ref[j, rows:2 * rows] = gq[lo:lo + rows]
        for g in range(G):
            at = pl.ds((j * G + g) * rows, rows)
            gk1, gk2, gv1, gv2 = (last[3 + i][at] + first[3 + i][at] if j < per else last[3 + i][at] for i in range(4))
            ref = out_kv if g == 0 else out_swap[g - 1]
            base = 2 if g == partner else 0
            for i, part in enumerate((gk2 * SCALE, gv2, gk1 * SCALE, gv1), base):
                ref[j, i * rows:(i + 1) * rows] = part.astype(ref.dtype)


def far_rows(query_refs, g, members, u, rows, lo):
    size = H // TILES * rows
    pair = (query_refs[u * members + g], query_refs[u * members + (g ^ (members // 2))])
    return jnp.concatenate([ref[at:at + rows] for at in range(lo * size, (lo + 1) * size, rows) for ref in pair], 0)


def far_slots(members, body):
    for g in range(members):
        slot = lax.axis_index("member") ^ g

        @pl.when((lax.axis_index("half") == 0) & (slot < members // 2))
        def _(g=g, slot=slot):
            body(g, slot)


def far_kernel(r0, rows, members, own_ref, *refs):
    G = members
    query_refs, products = refs[:TILES * G], refs[TILES * G:]
    sel = selector(lax.axis_index("head"), r0, rows, HD, False)[:rows]
    per = H // TILES
    keys, values = (jnp.concatenate([own_ref[j, lo * rows:(lo + 1) * rows] for j in range(H)], 0) for lo in (6, 7))
    docs = doc_cols(jnp.concatenate([sel * own_ref[j, 8 * rows:8 * rows + DOC_ROWS][0:1] for j in range(H)], 0))

    def body(g, slot):
        for u in range(TILES):
            x0 = u * per * rows
            pair = (query_refs[G + g], query_refs[G + (g ^ (G // 2))])
            dq = jnp.concatenate([sel * ref[2 * per * rows:2 * per * rows + DOC_ROWS][j:j + 1]
                                  for j in range(u * per, (u + 1) * per) for ref in pair], 0)
            qdoc = dot_nt(jnp.ones((16, HD), jnp.bfloat16), dq)[0:1]
            s = dot_nt(keys[x0:], far_rows(query_refs, g, G, u, rows, 0)) * (SCALE * LOG2E)
            products[2 * u][slot] = jnp.where(docs[x0:] == qdoc, s, MASKED)
            products[2 * u + 1][slot] = dot_nt(values[x0:], far_rows(query_refs, g, G, u, rows, 1))

    far_slots(G, body)


def far_grads(rows, members, query_refs, stat_ref, products, gk, gv):
    G = members
    per = H // TILES
    gk[...], gv[...] = jnp.zeros_like(gk), jnp.zeros_like(gv)

    def body(g, slot):
        for u in range(TILES):
            x0 = u * per * rows
            chunks = per * 2 * rows // HD
            lse, dot = (jnp.concatenate([stat_ref[at + i:at + i + 1] for i in range(chunks)], 1)
                        for at in (8 * g + u * chunks, 8 * g + 4 + u * chunks))
            p = jnp.exp2(products[2 * u][slot] - lse)
            ds = p * (products[2 * u + 1][slot] - dot)
            gk[x0:] += dot_nn(ds.astype(jnp.bfloat16), far_rows(query_refs, g, G, u, rows, 0)) * SCALE
            gv[x0:] += dot_nn(p.astype(jnp.bfloat16), far_rows(query_refs, g, G, u, rows, 1))

    far_slots(G, body)


def sum_kernel(rows, members, *refs):
    G = members
    query_refs, refs = refs[:TILES * G], refs[TILES * G:]
    stat_ref, products, refs = refs[0], refs[1:1 + 2 * TILES], refs[1 + 2 * TILES:]
    own_ref, kv_ref, swap_refs, (out_ref, gk, gv) = refs[0], refs[1], refs[2:G + 1], refs[G + 1:]
    f32, bf16 = jnp.float32, jnp.bfloat16
    far_grads(rows, G, query_refs, stat_ref, products, gk, gv)
    out_ref[:, 0:2 * rows] = own_ref[...]
    out_ref[:, 2 * rows:4 * rows] = swap_refs[G // 2 - 1][:, 0:2 * rows]
    for j in range(H):
        total = kv_ref[j]
        for g, ref in enumerate(swap_refs, 1):
            base = 2 * rows if g == G // 2 else 0
            total = total + ref[j, base:base + 4 * rows].astype(f32)
        mine = slice(j * rows, (j + 1) * rows)
        out_ref[j, 4 * rows:6 * rows] = total[:2 * rows].astype(bf16)
        out_ref[j, 6 * rows:7 * rows] = (total[2 * rows:3 * rows] + gk[mine]).astype(bf16)
        out_ref[j, 7 * rows:8 * rows] = (total[3 * rows:] + gv[mine]).astype(bf16)


def unpack_kernel(r0, rows, members, in_ref, *refs):
    outs, bufs, sem = refs[:4], refs[4:8], refs[8]
    tokens = bufs[0].shape[0]
    bf16 = jnp.bfloat16
    kinds = range(min(H, 2 * r0))
    query_sels = [selector(h, r0, rows, tokens, True, takes_fine(members)) for h in kinds]
    key_sels = [selector(h, r0, rows, tokens, True, True) for h in kinds]
    copies = []
    for i, base in enumerate((0, 1, 4, 5)):
        for h in range(H):
            sels = query_sels if i < 2 else key_sels
            part = jnp.concatenate([in_ref[h, (base + e) * rows:(base + e + 1) * rows] for e in (0, 2)], 0)
            bufs[i][:, h * HD:(h + 1) * HD] = dot_nn(sels[h % (2 * r0)], part).astype(bf16)
        copies.append(pltpu.make_async_copy(bufs[i], outs[i], sem.at[i]))
        copies[-1].start()
    for copy in copies:
        copy.wait()


def call(kernel, out_shape, scratch=(), limit=16, **more):
    return pl.pallas_call(
        kernel,
        out_shape=out_shape,
        scratch_shapes=list(scratch),
        compiler_params=pltpu.CompilerParams(vmem_limit_bytes=limit * 1024 * 1024),
        **more,
    )


def per_device(members, queries, keys, values, cotangent, doc_ids):
    G = members
    tokens = queries.shape[0]
    devices = 2 * H * G
    r0 = tokens * devices // (2 * SEG)
    rows = tokens // (2 * r0)
    bf16, f32 = jnp.bfloat16, jnp.float32
    shape = jax.ShapeDtypeStruct
    n = H * G * rows
    anywhere = pl.BlockSpec(memory_space=pltpu.HBM)
    wide = pltpu.VMEM((tokens, H * HD), bf16)
    message = (H, 8 * rows + DOC_ROWS, HD)

    packed = call(
        functools.partial(pack_kernel, r0, rows, G), shape(message, bf16),
        [wide] * 4 + [pltpu.VMEM((1, tokens), jnp.int32), pltpu.VMEM(message, bf16), pltpu.SemaphoreType.DMA((5 + H,))],
        limit=64, in_specs=[anywhere] * 5, out_specs=anywhere,
    )(queries, keys, values, cotangent, doc_ids.reshape(1, tokens))

    def to_head(x):
        return lax.all_to_all(x, "head", 0, 0, tiled=True)

    def to_member(x, g):
        return lax.ppermute(x, "member", [(i, i ^ g) for i in range(G)])

    def across(x):
        return lax.ppermute(x, "half", [(0, 1), (1, 0)])

    own = to_head(packed)
    queries_here = jnp.where(takes_fine(G), own[:, 2 * rows:4 * rows], own[:, :2 * rows])
    sent_across = jnp.where(lax.axis_index("half") == 0, own[:, 6 * rows:8 * rows], queries_here)
    per = H // TILES

    docs = jnp.pad(own[:, 8 * rows], ((0, DOC_ROWS - H), (0, 0)))
    def part(at):
        return [sent_across[at, lo * rows:(lo + 1) * rows].reshape(-1, HD) for lo in range(2)]

    upper = across(jnp.concatenate(part(slice(per, H)) + [docs], 0))
    lower = across(jnp.concatenate(part(slice(0, per)), 0))
    swaps = [to_member(own[:, (2 if g == G // 2 else 4) * rows:], g) for g in range(1, G)]
    nd, lanes = tile_sizes(rows, G)
    nq = TILES * lanes
    tile = [shape(((u + 1) * nd, lanes), f32) for u in range(TILES) for _ in range(2)]
    key_rows = pltpu.VMEM((n, HD), bf16)
    k1, k2, q_all, g_all, stats, out, gtt, *products = call(
        functools.partial(local_kernel, r0, rows, G),
        [shape((HD, n), bf16)] * 2 + [shape((nq, HD), bf16)] * 2 + [shape((8, nq), f32)]
        + [shape((HD, nq), f32)] * 2 + tile * 2,
        [key_rows] * 6, limit=32,
    )(own, *swaps)
    shared = (q_all, g_all, stats, out, gtt, k1, k2)
    upper, k1 = lax.optimization_barrier((upper, k1))
    uppers = [upper] + [to_member(upper, g) for g in range(1, G)]
    tile_rows = pltpu.VMEM((lanes, HD), bf16)
    last = call(
        functools.partial(last_tile_kernel, r0, rows, G),
        [shape((8, HD), f32)] + [shape((lanes, HD), bf16)] * 2 + [shape((n, HD), f32)] * 4,
        limit=32,
    )(*uppers, *shared, *products[2:4], *products[6:8])
    lowers = [lower] + [to_member(lower, g) for g in range(1, G)]
    sent = lambda g: (H, (6 if g == G // 2 else 4) * rows, HD)
    outs = call(
        functools.partial(first_tile_kernel, r0, rows, G),
        [shape((8, HD), f32), shape((H, 2 * rows, HD), bf16), shape((H, 4 * rows, HD), f32)]
        + [shape(sent(g), bf16) for g in range(1, G)],
        [tile_rows] * 2 + [pltpu.VMEM((nd, HD), f32)] * 4, limit=32,
    )(*lowers, *uppers, *shared, *products[0:2], *products[4:6], *last)
    crosses = lowers + uppers
    hops = [to_member(outs[0], g) for g in range(1, G)]
    far_stats = across(jnp.concatenate([outs[0]] + hops, 0))
    products = call(
        functools.partial(far_kernel, r0, rows, G),
        [shape((G // 2, (TILES - u) * nd // G, lanes), f32) for u in range(TILES) for _ in range(2)],
    )(own, *crosses)
    sends, _ = lax.optimization_barrier((list(outs[3:]), hops))
    swaps = [to_member(x, g) for g, x in enumerate(sends, 1)]
    back = call(
        functools.partial(sum_kernel, rows, G), shape((H, 8 * rows, HD), bf16),
        [pltpu.VMEM((H * rows, HD), f32)] * 2,
    )(*crosses, far_stats, *products, outs[1], outs[2], *swaps)
    back = to_head(back)
    return tuple(call(
        functools.partial(unpack_kernel, r0, rows, G), [shape((tokens, H * HD), bf16)] * 4,
        [wide] * 4 + [pltpu.SemaphoreType.DMA((4,))],
        in_specs=[VMEM], out_specs=[anywhere] * 4,
    )(back))


def solution(mesh):
    members = mesh.shape["seq"] // (2 * H)
    parts = {"seq": [("half", 2), ("head", H), ("member", members)]}
    axes = [part for name in mesh.axis_names for part in parts.get(name, [(name, mesh.shape[name])])]
    inner = Mesh(mesh.devices.reshape([size for _, size in axes]), [name for name, _ in axes])
    split = ("dp", "half", "head", "member")
    in_specs = (P(split, None),) * 4 + (P(split),)
    return jax.shard_map(
        functools.partial(per_device, members), mesh=inner, in_specs=in_specs,
        out_specs=(P(split, None),) * 4, check_vma=False,
    )
```

```python
import functools

import jax
import jax.numpy as jnp
import numpy as np
from jax import lax
from jax.experimental import pallas as pl
from jax.experimental.pallas import tpu as pltpu
from jax.sharding import Mesh
from jax.sharding import PartitionSpec as P

H = 8
HD = 128
SEG = 1024

MASKED = -1e30
SCALE = HD ** -0.5
LOG2E = float(np.log2(np.e))
VMEM = pl.BlockSpec(memory_space=pltpu.VMEM)
DOC_ROWS = 16


def dot_nn(a, b):
    return lax.dot_general(a, b, (((1,), (0,)), ((), ())), preferred_element_type=jnp.float32)


def dot_nt(a, b):
    return lax.dot_general(a, b, (((1,), (1,)), ((), ())), preferred_element_type=jnp.float32)


def selector(head, r0, rows, tokens, transposed, fine_first=False):
    r1 = 2 * r0
    shape = (tokens, 2 * rows) if transposed else (2 * rows, tokens)
    k = lax.broadcasted_iota(jnp.int32, shape, 1 if transposed else 0)
    p = lax.broadcasted_iota(jnp.int32, shape, 0 if transposed else 1)
    coarse = head % r1
    other = (coarse + r0) % r1
    first, second = jnp.where(fine_first, other, coarse), jnp.where(fine_first, coarse, other)
    target = jnp.where(k < rows, r1 * k + first, r1 * (k - rows) + second)
    return (p == target).astype(jnp.float32).astype(jnp.bfloat16)


def takes_fine(members):
    return lax.axis_index("member") >= members // 2


def column_chunks():
    return [((h, h + 1), slice(h * HD, (h + 2) * HD)) for h in range(0, H, 2)]


def pack_kernel(r0, rows, members, q_in, k_in, v_in, g_in, doc_in, out, q_ref, k_ref, v_ref, g_ref, doc_ref, buf, sem):
    tokens = q_ref.shape[0]
    pairs = ((doc_in, doc_ref), (k_in, k_ref), (v_in, v_ref), (q_in, q_ref), (g_in, g_ref))
    copies = [pltpu.make_async_copy(src, dst, sem.at[i]) for i, (src, dst) in enumerate(pairs)]
    for copy in copies:
        copy.start()
    kinds = range(min(H, 2 * r0))
    key_sels = [selector(h, r0, rows, tokens, False) for h in kinds]
    query_sels = [selector(h, r0, rows, tokens, False, takes_fine(members)) for h in kinds]

    def pick(sels, h, ref):
        return dot_nn(sels[h % (2 * r0)], ref[:, h * HD:(h + 1) * HD]).astype(jnp.bfloat16)

    for copy in copies:
        copy.wait()
    docs = jnp.broadcast_to(doc_ref[...].astype(jnp.float32).astype(jnp.bfloat16), (DOC_ROWS, tokens))
    sends = []
    for h in range(H):
        for i, ref in enumerate((q_ref, g_ref)):
            x = pick(query_sels, h, ref)
            buf[h, i * rows:(1 + i) * rows] = x[:rows]
            buf[h, (2 + i) * rows:(3 + i) * rows] = x[rows:]
        for i, ref in enumerate((k_ref, v_ref)):
            x = pick(key_sels, h, ref)
            buf[h, (4 + i) * rows:(5 + i) * rows] = x[rows:]
            buf[h, (6 + i) * rows:(7 + i) * rows] = x[:rows]
        buf[h, 8 * rows:8 * rows + DOC_ROWS] = docs
        sends.append(pltpu.make_async_copy(buf.at[h], out.at[h], sem.at[5 + h]))
        sends[-1].start()
    for copy in sends:
        copy.wait()


TILES = 2


def tile_sizes(rows, members):
    per = H // TILES
    return per * members * rows, per * 2 * rows


def eye_matrix():
    shape = (HD, HD)
    same = lax.broadcasted_iota(jnp.int32, shape, 0) == lax.broadcasted_iota(jnp.int32, shape, 1)
    return same.astype(jnp.float32).astype(jnp.bfloat16)


def doc_cols(x):
    return dot_nn(x, jnp.ones((HD, HD), jnp.bfloat16))[:, 0:1]


def local_kernel(r0, rows, members, *refs):
    G = members
    r1 = 2 * r0
    own_ref, swap_refs = refs[0], refs[1:G]
    (k1, k2, q_all, g_all, stats, out_ref, gtt_ref), rest = refs[G:G + 7], refs[G + 7:]
    p_refs, dp_refs, (v1, v2, d1, d2) = rest[:2 * TILES], rest[2 * TILES:4 * TILES], rest[4 * TILES:]
    bf16, f32 = jnp.bfloat16, jnp.float32
    tokens = HD
    head = lax.axis_index("head")
    member = lax.axis_index("member")
    fine = takes_fine(G)
    partner = G // 2
    partner_ref = swap_refs[partner - 1]

    sel = selector(head, r0, rows, tokens, False)
    query_sel = jnp.where(fine, sel[rows:].astype(f32), sel[:rows].astype(f32)).astype(bf16)
    source_docs = []
    for j in range(H):
        for g in range(G):
            at = pl.ds((j * G + g) * rows, rows)
            ref, base = (own_ref, 4 * rows) if g == 0 else (swap_refs[g - 1], 2 * rows if g == partner else 0)
            k2[at] = ref[j, base:base + rows]
            v2[at] = ref[j, base + rows:base + 2 * rows]
            k1[at] = ref[j, base + 2 * rows:base + 3 * rows]
            v1[at] = ref[j, base + 3 * rows:base + 4 * rows]
            doc = ref[j, base + 4 * rows:base + 4 * rows + DOC_ROWS][0:1]
            if g in (0, partner):
                source_docs.append(doc)
            d1[at] = sel[:rows] * doc
            d2[at] = sel[rows:] * doc

    eye = eye_matrix()
    v1t, v2t = dot_nt(eye, v1[...]).astype(bf16), dot_nt(eye, v2[...]).astype(bf16)
    docs1, docs2 = doc_cols(d1[...]), doc_cols(d2[...])
    nd, lanes = tile_sizes(rows, G)
    per = H // TILES

    coarse = head % r1
    other = (coarse + r0) % r1
    lane = lax.broadcasted_iota(jnp.int32, (1, lanes), 1)
    qmember = member ^ (partner * ((lane // rows) % 2))
    qpos = (lane // (2 * rows)) * (G * tokens) + qmember * tokens + r1 * (lane % rows) + jnp.where(fine, other, coarse)
    kl = lax.broadcasted_iota(jnp.int32, (nd, 1), 0)
    kmember = member ^ ((kl // rows) % G)
    kpos = (kl // (rows * G)) * (G * tokens) + kmember * tokens + r1 * (kl % rows)
    causal1 = kpos + coarse <= qpos
    causal2 = kpos + other <= qpos
    both = jnp.where(fine, 0.0, 1.0)
    c = SCALE * LOG2E

    for u in range(TILES):
        nk = (u + 1) * nd
        x0 = u * nd
        src = range(u * per, (u + 1) * per)
        mine = slice(u * lanes, (u + 1) * lanes)
        gather = lambda lo: jnp.concatenate([ref[j, lo:lo + rows] for j in src for ref in (own_ref, partner_ref)], 0)
        qt, gt = gather(0), gather(rows)
        q_all[mine], g_all[mine] = qt, gt
        dq = jnp.concatenate([query_sel * source_docs[2 * j + e] for j in src for e in range(2)], 0)
        qdoc = dot_nt(jnp.ones((16, HD), bf16), dq)[0:1]

        def scores(key, docs, causal):
            s = jnp.where(docs == qdoc, dot_nt(key, qt), MASKED)
            if u:
                return jnp.concatenate([s[:x0], jnp.where(causal, s[x0:], MASKED)], 0)
            return jnp.where(causal, s, MASKED)

        s1 = scores(k1[0:nk], docs1[0:nk], causal1)
        s2 = scores(k2[0:nk], docs2[0:nk], causal2)
        top = jnp.maximum(jnp.max(s1, 0, keepdims=True), jnp.max(s2, 0, keepdims=True))
        base = top * c
        p1 = jnp.exp2(s1 * c - (base - both))
        p2 = jnp.exp2(s2 * c - base)
        stats[0:1, mine] = top
        stats[1:2, mine] = jnp.sum(p1, 0, keepdims=True) + jnp.sum(p2, 0, keepdims=True)
        stats[2:3, mine] = qdoc
        out_ref[:, mine] = dot_nn(v1t[:, :nk], p1.astype(bf16)) + dot_nn(v2t[:, :nk], p2.astype(bf16))
        gtt_ref[:, mine] = dot_nt(eye, gt)
        p_refs[2 * u][...], p_refs[2 * u + 1][...] = p1, p2
        dp_refs[2 * u][...], dp_refs[2 * u + 1][...] = dot_nt(v1[0:nk], gt), dot_nt(v2[0:nk], gt)


def finish_tile(u, r0, rows, members, parts, shared, products, results):
    far = (lax.axis_index("half") == 1) & jnp.logical_not(takes_fine(members))
    for branch, with_far in ((far, True), (jnp.logical_not(far), False)):
        pl.when(branch)(functools.partial(
            tile_body, u, r0, rows, members, with_far, parts, shared, products, results))


def tile_body(u, r0, rows, members, with_far, parts, shared, products, results):
    G = members
    q_all, g_all, stats, local_out, gtt_ref, k1, k2 = shared
    far_stats, att, gq_ref, sums = results[0], results[1], results[2], results[3:]
    bf16 = jnp.bfloat16
    per = H // TILES
    eye = eye_matrix()
    nd, lanes = tile_sizes(rows, G)
    nk = (u + 1) * nd
    mine = slice(u * lanes, (u + 1) * lanes)
    c = SCALE * LOG2E
    qt, gt = q_all[mine], g_all[mine]
    top, total, out = stats[0:1, mine], stats[1:2, mine], local_out[:, mine]
    if with_far:
        sel = selector(lax.axis_index("head"), r0, rows, HD, False)
        size = per * rows
        keys_x, values_x = (jnp.concatenate([ref[lo:lo + size] for part in parts for ref in part], 0) for lo in (0, size))
        first = TILES - len(parts)
        docs_x = jnp.concatenate([sel[:rows] * ref[2 * size:2 * size + DOC_ROWS][source:source + 1]
                                  for p in range(first, TILES) for ref in parts[-1]
                                  for source in range(p * per, (p + 1) * per)], 0)
        kxt, vxt = dot_nt(eye, keys_x).astype(bf16), dot_nt(eye, values_x).astype(bf16)
        sx = jnp.where(doc_cols(docs_x) == stats[2:3, mine], dot_nt(keys_x, qt), MASKED)
        local_top = top
        top = jnp.maximum(local_top, jnp.max(sx, 0, keepdims=True))
        px = jnp.exp2(sx * c - top * c)
        shrink = jnp.exp2(local_top * c - top * c)
        total = total * shrink + jnp.sum(px, 0, keepdims=True)
        inv = 1.0 / total
        local_inv = shrink * inv
        out = out * local_inv + dot_nn(vxt, px.astype(bf16)) * inv
    else:
        local_inv = 1.0 / total
        out = out * local_inv
    dot = jnp.sum(gtt_ref[:, mine] * out, 0, keepdims=True)
    lse = top * c + jnp.log(total) * LOG2E
    chunks = lanes // HD
    for i in range(chunks):
        far_stats[u * chunks + i:u * chunks + i + 1] = lse[:, i * HD:(i + 1) * HD]
        far_stats[4 + u * chunks + i:5 + u * chunks + i] = dot[:, i * HD:(i + 1) * HD]
    att[...] = out.T.astype(bf16)
    gq = 0.0
    if with_far:
        ds = (px * inv * (dot_nt(values_x, gt) - dot)).astype(bf16)
        gq = dot_nn(kxt, ds)
    for i, k in enumerate((k1, k2)):
        w = products[i][...] * local_inv
        ds = (w * (products[2 + i][...] - dot)).astype(bf16)
        gq = gq + dot_nn(dot_nt(eye, k[0:nk]).astype(bf16), ds)
        sums[i][...] = dot_nn(ds, qt)
        sums[2 + i][...] = dot_nn(w.astype(bf16), gt)
    gq_ref[...] = (gq * SCALE).T.astype(bf16)


def last_tile_kernel(r0, rows, members, *refs):
    G = members
    finish_tile(1, r0, rows, G, [refs[:G]], refs[G:G + 7], refs[G + 7:G + 11], refs[G + 11:G + 18])


def first_tile_kernel(r0, rows, members, *refs):
    G = members
    parts, refs = [refs[:G], refs[G:2 * G]], refs[2 * G:]
    shared, products, last, refs = refs[:7], refs[7:11], refs[11:18], refs[18:]
    far_stats, out_own, out_kv, out_swap, scratch = refs[0], refs[1], refs[2], refs[3:G + 2], refs[G + 2:]
    nd, lanes = tile_sizes(rows, G)
    first = (far_stats,) + tuple(scratch[:6])
    far_stats[...] = last[0][...]
    finish_tile(0, r0, rows, G, parts, shared, products, first)
    partner, per = G // 2, H // TILES
    for j in range(H):
        att, gq = (first, last)[j // per][1:3]
        for e, ref in enumerate((out_own, out_swap[partner - 1])):
            lo = (2 * (j % per) + e) * rows
            ref[j, 0:rows] = att[lo:lo + rows]
            ref[j, rows:2 * rows] = gq[lo:lo + rows]
        for g in range(G):
            at = pl.ds((j * G + g) * rows, rows)
            gk1, gk2, gv1, gv2 = (last[3 + i][at] + first[3 + i][at] if j < per else last[3 + i][at] for i in range(4))
            ref = out_kv if g == 0 else out_swap[g - 1]
            base = 2 if g == partner else 0
            for i, part in enumerate((gk2 * SCALE, gv2, gk1 * SCALE, gv1), base):
                ref[j, i * rows:(i + 1) * rows] = part.astype(ref.dtype)


def far_rows(query_refs, g, members, u, rows, lo):
    size = H // TILES * rows
    pair = (query_refs[u * members + g], query_refs[u * members + (g ^ (members // 2))])
    return jnp.concatenate([ref[at:at + rows] for at in range(lo * size, (lo + 1) * size, rows) for ref in pair], 0)


def far_slots(members, body):
    for g in range(members):
        slot = lax.axis_index("member") ^ g

        @pl.when((lax.axis_index("half") == 0) & (slot < members // 2))
        def _(g=g, slot=slot):
            body(g, slot)


def far_kernel(r0, rows, members, own_ref, *refs):
    G = members
    query_refs, products = refs[:TILES * G], refs[TILES * G:]
    sel = selector(lax.axis_index("head"), r0, rows, HD, False)[:rows]
    per = H // TILES
    keys, values = (jnp.concatenate([own_ref[j, lo * rows:(lo + 1) * rows] for j in range(H)], 0) for lo in (6, 7))
    docs = doc_cols(jnp.concatenate([sel * own_ref[j, 8 * rows:8 * rows + DOC_ROWS][0:1] for j in range(H)], 0))

    def body(g, slot):
        for u in range(TILES):
            x0 = u * per * rows
            pair = (query_refs[G + g], query_refs[G + (g ^ (G // 2))])
            dq = jnp.concatenate([sel * ref[2 * per * rows:2 * per * rows + DOC_ROWS][j:j + 1]
                                  for j in range(u * per, (u + 1) * per) for ref in pair], 0)
            qdoc = dot_nt(jnp.ones((16, HD), jnp.bfloat16), dq)[0:1]
            s = dot_nt(keys[x0:], far_rows(query_refs, g, G, u, rows, 0)) * (SCALE * LOG2E)
            products[2 * u][slot] = jnp.where(docs[x0:] == qdoc, s, MASKED)
            products[2 * u + 1][slot] = dot_nt(values[x0:], far_rows(query_refs, g, G, u, rows, 1))

    far_slots(G, body)


def far_grads(rows, members, query_refs, stat_ref, products, gk, gv):
    G = members
    per = H // TILES
    gk[...], gv[...] = jnp.zeros_like(gk), jnp.zeros_like(gv)

    def body(g, slot):
        for u in range(TILES):
            x0 = u * per * rows
            chunks = per * 2 * rows // HD
            lse, dot = (jnp.concatenate([stat_ref[at + i:at + i + 1] for i in range(chunks)], 1)
                        for at in (8 * g + u * chunks, 8 * g + 4 + u * chunks))
            p = jnp.exp2(products[2 * u][slot] - lse)
            ds = p * (products[2 * u + 1][slot] - dot)
            gk[x0:] += dot_nn(ds.astype(jnp.bfloat16), far_rows(query_refs, g, G, u, rows, 0)) * SCALE
            gv[x0:] += dot_nn(p.astype(jnp.bfloat16), far_rows(query_refs, g, G, u, rows, 1))

    far_slots(G, body)


def sum_kernel(rows, members, *refs):
    G = members
    query_refs, refs = refs[:TILES * G], refs[TILES * G:]
    stat_ref, products, refs = refs[0], refs[1:1 + 2 * TILES], refs[1 + 2 * TILES:]
    own_ref, kv_ref, swap_refs, (out_ref, gk, gv) = refs[0], refs[1], refs[2:G + 1], refs[G + 1:]
    f32, bf16 = jnp.float32, jnp.bfloat16
    far_grads(rows, G, query_refs, stat_ref, products, gk, gv)
    out_ref[:, 0:2 * rows] = own_ref[...]
    out_ref[:, 2 * rows:4 * rows] = swap_refs[G // 2 - 1][:, 0:2 * rows]
    for j in range(H):
        total = kv_ref[j]
        for g, ref in enumerate(swap_refs, 1):
            base = 2 * rows if g == G // 2 else 0
            total = total + ref[j, base:base + 4 * rows].astype(f32)
        mine = slice(j * rows, (j + 1) * rows)
        out_ref[j, 4 * rows:6 * rows] = total[:2 * rows].astype(bf16)
        out_ref[j, 6 * rows:7 * rows] = (total[2 * rows:3 * rows] + gk[mine]).astype(bf16)
        out_ref[j, 7 * rows:8 * rows] = (total[3 * rows:] + gv[mine]).astype(bf16)


def unpack_kernel(r0, rows, members, in_ref, *refs):
    outs, bufs, sem = refs[:4], refs[4:8], refs[8]
    tokens = bufs[0].shape[0]
    bf16 = jnp.bfloat16
    kinds = range(min(H, 2 * r0))
    query_sels = [selector(h, r0, rows, tokens, True, takes_fine(members)) for h in kinds]
    key_sels = [selector(h, r0, rows, tokens, True, True) for h in kinds]
    copies = []
    for heads, cols in column_chunks():
        for i, base in enumerate((0, 1, 4, 5)):
            sels = query_sels if i < 2 else key_sels
            for h in heads:
                part = jnp.concatenate([in_ref[h, (base + e) * rows:(base + e + 1) * rows] for e in (0, 2)], 0)
                bufs[i][:, h * HD:(h + 1) * HD] = dot_nn(sels[h % (2 * r0)], part).astype(bf16)
            copies.append(pltpu.make_async_copy(bufs[i].at[:, cols], outs[i].at[:, cols], sem.at[len(copies)]))
            copies[-1].start()
    for copy in copies:
        copy.wait()


def call(kernel, out_shape, scratch=(), limit=16, **more):
    return pl.pallas_call(
        kernel,
        out_shape=out_shape,
        scratch_shapes=list(scratch),
        compiler_params=pltpu.CompilerParams(vmem_limit_bytes=limit * 1024 * 1024),
        **more,
    )


def per_device(members, queries, keys, values, cotangent, doc_ids):
    G = members
    tokens = queries.shape[0]
    devices = 2 * H * G
    r0 = tokens * devices // (2 * SEG)
    rows = tokens // (2 * r0)
    bf16, f32 = jnp.bfloat16, jnp.float32
    shape = jax.ShapeDtypeStruct
    n = H * G * rows
    anywhere = pl.BlockSpec(memory_space=pltpu.HBM)
    wide = pltpu.VMEM((tokens, H * HD), bf16)
    message = (H, 8 * rows + DOC_ROWS, HD)

    packed = call(
        functools.partial(pack_kernel, r0, rows, G), shape(message, bf16),
        [wide] * 4 + [pltpu.VMEM((1, tokens), jnp.int32), pltpu.VMEM(message, bf16), pltpu.SemaphoreType.DMA((5 + H,))],
        limit=64, in_specs=[anywhere] * 5, out_specs=anywhere,
    )(queries, keys, values, cotangent, doc_ids.reshape(1, tokens))

    def to_head(x):
        return lax.all_to_all(x, "head", 0, 0, tiled=True)

    def to_member(x, g):
        return lax.ppermute(x, "member", [(i, i ^ g) for i in range(G)])

    def across(x):
        return lax.ppermute(x, "half", [(0, 1), (1, 0)])

    own = to_head(packed)
    queries_here = jnp.where(takes_fine(G), own[:, 2 * rows:4 * rows], own[:, :2 * rows])
    sent_across = jnp.where(lax.axis_index("half") == 0, own[:, 6 * rows:8 * rows], queries_here)
    per = H // TILES

    docs = jnp.pad(own[:, 8 * rows], ((0, DOC_ROWS - H), (0, 0)))
    def part(at):
        return [sent_across[at, lo * rows:(lo + 1) * rows].reshape(-1, HD) for lo in range(2)]

    upper = across(jnp.concatenate(part(slice(per, H)) + [docs], 0))
    lower = across(jnp.concatenate(part(slice(0, per)), 0))
    swaps = [to_member(own[:, (2 if g == G // 2 else 4) * rows:], g) for g in range(1, G)]
    nd, lanes = tile_sizes(rows, G)
    nq = TILES * lanes
    tile = [shape(((u + 1) * nd, lanes), f32) for u in range(TILES) for _ in range(2)]
    key_rows = pltpu.VMEM((n, HD), bf16)
    k1, k2, q_all, g_all, stats, out, gtt, *products = call(
        functools.partial(local_kernel, r0, rows, G),
        [shape((n, HD), bf16)] * 2 + [shape((nq, HD), bf16)] * 2 + [shape((8, nq), f32)]
        + [shape((HD, nq), f32)] * 2 + tile * 2,
        [key_rows] * 4, limit=32,
    )(own, *swaps)
    shared = (q_all, g_all, stats, out, gtt, k1, k2)
    upper, k1 = lax.optimization_barrier((upper, k1))
    uppers = [upper] + [to_member(upper, g) for g in range(1, G)]
    tile_rows = pltpu.VMEM((lanes, HD), bf16)
    last = call(
        functools.partial(last_tile_kernel, r0, rows, G),
        [shape((8, HD), f32)] + [shape((lanes, HD), bf16)] * 2 + [shape((n, HD), f32)] * 4,
        limit=32,
    )(*uppers, *shared, *products[2:4], *products[6:8])
    lowers = [lower] + [to_member(lower, g) for g in range(1, G)]
    sent = lambda g: (H, (6 if g == G // 2 else 4) * rows, HD)
    outs = call(
        functools.partial(first_tile_kernel, r0, rows, G),
        [shape((8, HD), f32), shape((H, 2 * rows, HD), bf16), shape((H, 4 * rows, HD), f32)]
        + [shape(sent(g), bf16) for g in range(1, G)],
        [tile_rows] * 2 + [pltpu.VMEM((nd, HD), f32)] * 4, limit=32,
    )(*lowers, *uppers, *shared, *products[0:2], *products[4:6], *last)
    crosses = lowers + uppers
    hops = [to_member(outs[0], g) for g in range(1, G)]
    far_stats = across(jnp.concatenate([outs[0]] + hops, 0))
    products = call(
        functools.partial(far_kernel, r0, rows, G),
        [shape((G // 2, (TILES - u) * nd // G, lanes), f32) for u in range(TILES) for _ in range(2)],
    )(own, *crosses)
    sends, _ = lax.optimization_barrier((list(outs[3:]), hops))
    swaps = [to_member(x, g) for g, x in enumerate(sends, 1)]
    back = call(
        functools.partial(sum_kernel, rows, G), shape((H, 8 * rows, HD), bf16),
        [pltpu.VMEM((H * rows, HD), f32)] * 2,
    )(*crosses, far_stats, *products, outs[1], outs[2], *swaps)
    back = to_head(back)
    return tuple(call(
        functools.partial(unpack_kernel, r0, rows, G), [shape((tokens, H * HD), bf16)] * 4,
        [wide] * 4 + [pltpu.SemaphoreType.DMA((2 * H,))],
        in_specs=[VMEM], out_specs=[anywhere] * 4,
    )(back))


def solution(mesh):
    members = mesh.shape["seq"] // (2 * H)
    parts = {"seq": [("half", 2), ("head", H), ("member", members)]}
    axes = [part for name in mesh.axis_names for part in parts.get(name, [(name, mesh.shape[name])])]
    inner = Mesh(mesh.devices.reshape([size for _, size in axes]), [name for name, _ in axes])
    split = ("dp", "half", "head", "member")
    in_specs = (P(split, None),) * 4 + (P(split),)
    return jax.shard_map(
        functools.partial(per_device, members), mesh=inner, in_specs=in_specs,
        out_specs=(P(split, None),) * 4, check_vma=False,
    )
```
